32 devices in a mesh: groups: 2 (over x), expert: 16 (over z, y, core).
Axes of the slice: x: 2, y: 2, z: 4, core: 2. Of those that a mesh axis runs over, the one named last changes fastest.
Arguments:
- hidden_in: bfloat16 [4096, 7168], P(('groups', 'expert')), parts along dimension 0, may hold values from -6 to 6
- out_grads: bfloat16 [4096, 8, 2048], P(('groups', 'expert')), parts along dimension 0, may hold values from -6 to 6
- routes: int32 [4096, 8], P(('groups', 'expert')), parts along dimension 0, may hold values from 0 to 63, all different within a row; in each aligned block of 128 rows (0 to 127, 128 to 255, ...) at most 24 rows name the same one
- segments: int32 [4096], P(('groups', 'expert')), parts along dimension 0, may hold values from 0 to 31, as said below
- in_proj: bfloat16 [64, 7168], replicated, may hold values from -0.0625 to 0.0625
- out_proj: bfloat16 [64, 64, 2048], P('expert'), may hold values from -0.125 to 0.125
Outputs:
- example_grads: bfloat16 [64, 64, 4096], P(('groups', 'expert')), parts along dimension 0
The draws below stay inside these ranges and needn't reach their ends.
There are 2 independent parts, one for each index of `groups`. The reference program is written for one: setup_inputs(seed, part) draws one part's arguments, and reference() takes and returns one part's arrays. A program takes and returns all parts, laid end to end along the dimension named above; an argument that names none is the same for every part. Nothing has to cross between parts.
Inputs may be any that keep to these rules, and one draw needn't show every extreme that they name: `routes`: each row names 8 different experts. Within the rows of one index of expert (aligned blocks of 128 rows) no expert is named more than 24 times, a bound that some block reaches. `segments`: tokens k * 128 to (k + 1) * 128 - 1 belong to examples k * 2 to k * 2 + 1, each of which has at least one token; ids never fall.
All inputs are finite; a program needn't handle non-finite values.
Results may differ from the reference program's by a relative error of at most 0.0058.
Values may be sent and summed in bfloat16 or wider, within the bound.
No kernel may reach another device: no remote copies, remote signals or barrier semaphores. Data moves between devices by JAX's collectives and lax.ppermute only.
A program may use at most 128 MiB of HBM per device.

```python
import math
import jax
import jax.numpy as jnp
import numpy as np
from jax import lax

D = 7168
FF = 2048
TOP = 8
R = 64
TOK_DEV = 128
SEG_DEV = 2
EXPERTS = 64
TOKENS = 2048
EXAMPLES = 32
CAP = 24
N_EXPERT = 16


def draw_segments(key, part):
    key = jax.random.fold_in(key, 7)
    keys = jax.random.split(key, N_EXPERT)

    def one_block(block_key):
        shuffled = jax.random.permutation(block_key, TOK_DEV - 1) + 1
        cuts = jnp.sort(shuffled[:SEG_DEV - 1])
        position = jnp.arange(TOK_DEV)
        return jnp.sum((position[:, None] >= cuts[None, :]).astype(jnp.int32), axis=1)
    local = jax.vmap(one_block)(keys)
    offsets = jnp.arange(N_EXPERT, dtype=jnp.int32)[:, None] * SEG_DEV
    return (local + offsets).reshape(TOKENS).astype(jnp.int32)


def steps_of(stream_key, shape, pieces, least, top_value):
    def one(dim, blocks):
        draws = jax.random.uniform(jax.random.fold_in(jax.random.fold_in(stream_key, 6), dim), (blocks,), jnp.float32, least / len(pieces), top_value / len(pieces))
        return jnp.repeat(jnp.exp(draws), shape[dim] // blocks).reshape((-1,) + (1,) * (len(shape) - dim - 1))

    factor_of = one(*pieces[0])
    for cut in pieces[1:]:
        factor_of = factor_of * one(*cut)
    return factor_of


def routed_block(own_key, own, number, rows, number_of, top, bound, slope):
    ranking = jax.random.permutation(own_key, number_of)
    packed, usual = load_shares(number_of, rows * top, bound, slope, True), load_shares(number_of, rows * top, bound, slope, False)
    places = jnp.arange(number_of)

    def named(sizes, turn):
        used = int((sizes > 0).sum())
        fixed = max(1, used // 4)
        shifted = fixed + (places - fixed + turn * (used - fixed)) % max(1, number_of - fixed)
        return jnp.zeros((number_of,), jnp.int32).at[ranking[jnp.where(places < fixed, places, shifted)]].set(jnp.asarray(sizes, jnp.int32))

    sizes = jnp.where(number % 4 == 0, named(packed, number // 4), named(usual, number - number // 4 - 1))
    mixed = jax.random.permutation(jax.random.fold_in(own, 3), number_of)
    source_of, taker = mixed[0:number_of // 2 * 2:2], mixed[1:number_of // 2 * 2:2]
    slack = jnp.minimum(sizes[source_of] - 1, bound - sizes[taker]) // 2
    slack = jnp.where((source_of == ranking[0]) | (taker == ranking[0]) | (sizes[taker] == 0), 0, jnp.maximum(slack, 0))
    shifted = jax.random.randint(jax.random.fold_in(own, 4), (number_of // 2,), 0, 1 << 20) % (slack + 1)
    sizes = sizes.at[source_of].add(-shifted).at[taker].add(shifted)
    labels = jnp.searchsorted(jnp.cumsum(sizes), jnp.arange(rows * top), side="right").astype(jnp.int32)
    grid = labels.reshape(top, rows).T
    grid = grid[jax.random.permutation(jax.random.fold_in(own, 1), rows)]
    turn = jax.random.randint(jax.random.fold_in(own, 2), (rows, 1), 0, top)
    return jnp.take_along_axis(grid, (jnp.arange(top)[None, :] + turn) % top, axis=1)


def load_shares(amount, total, reach, skew, full):
    weights = [(1 << 20) // math.isqrt(rank ** skew) + 1 for rank in range(1, amount + 1)]
    largest = reach if full else min(reach, max(-(-total // amount), total * weights[0] // sum(weights)))
    least = 1 if total - largest >= amount - 1 else 0
    given, rest = [largest] + [least] * (amount - 1), total - largest - least * (amount - 1)
    while rest > 0:
        candidates = [i for i in range(1, amount) if given[i] < largest] or [i for i in range(1, amount) if given[i] < reach]
        mass, left = sum([weights[i] for i in candidates]), rest
        for i in candidates:
            extra = min(reach - given[i], max(1, left * weights[i] // mass), rest)
            given[i] = given[i] + extra
            rest = rest - extra
    return np.array(given)


def scatter_about(rng, dims, spread, most, shards=(), kind=jnp.bfloat16):
    factor_of = steps_of(rng, dims, shards, -0.22, 0.18) if shards else 1.0
    array = jax.random.normal(rng, dims, jnp.float32) * spread * factor_of
    return jnp.minimum(jnp.maximum(array, -most), most).astype(kind)


def setup_inputs(seed: int = 0, part: int = 0) -> dict:
    key_list = jax.random.split(jax.random.key(seed), 7)
    own_keys = jax.random.split(jax.random.fold_in(key_list[6], part), 7)
    hidden_in = scatter_about(own_keys[0], (TOKENS, D), 1.0, 6.0, ((0, 16),))
    out_grads = scatter_about(own_keys[1], (TOKENS, TOP, FF), 1.0, 6.0, ((0, 16),))
    routes_keys = jax.random.split(jax.random.fold_in(own_keys[2], 1), TOKENS // TOK_DEV)
    routes_turns = jax.random.permutation(jax.random.fold_in(own_keys[2], 3), TOKENS // TOK_DEV)
    routes = jax.vmap(lambda own, number: routed_block(jax.random.fold_in(own_keys[2], 2), own, number, TOK_DEV, EXPERTS, TOP, CAP, 2))(routes_keys, routes_turns).reshape((TOKENS, TOP))
    segments = draw_segments(jax.random.fold_in(jax.random.fold_in(key_list[6], part), 71), part)
    in_proj = scatter_about(key_list[4], (R, D), D ** -0.5, 0.0625)
    out_proj = scatter_about(key_list[5], (EXPERTS, R, FF), FF ** -0.5, 0.125, ((0, 16),))
    return {"hidden_in": hidden_in, "out_grads": out_grads, "routes": routes, "segments": segments, "in_proj": in_proj, "out_proj": out_proj}


def reference(hidden_in, out_grads, routes, segments, in_proj, out_proj):
    projected = lax.dot_general(hidden_in, in_proj, (((1,), (1,)), ((), ())), preferred_element_type=jnp.float32).astype(jnp.bfloat16)
    pair_count = TOKENS * TOP
    slot_count = N_EXPERT * CAP
    flat_routes = routes.reshape(pair_count).astype(jnp.int32)
    ordering = jnp.argsort(flat_routes, stable=True).astype(jnp.int32)
    sorted_routes = flat_routes[ordering]
    counts = jnp.bincount(flat_routes, length=EXPERTS).astype(jnp.int32)
    starts = (jnp.cumsum(counts) - counts).astype(jnp.int32)
    within = jnp.arange(pair_count, dtype=jnp.int32) - starts[sorted_routes]
    slot_table = jnp.full((EXPERTS * slot_count,), pair_count, jnp.int32).at[sorted_routes * slot_count + within].set(ordering)
    grad_rows = out_grads.reshape(pair_count, FF)

    def per_expert(expert_id):
        picked = lax.dynamic_slice_in_dim(slot_table, (expert_id * slot_count).astype(jnp.int32), slot_count)
        rows = jnp.take(grad_rows, picked, axis=0, mode="fill", fill_value=0)
        weight = lax.dynamic_index_in_dim(out_proj, expert_id, 0, keepdims=False)
        reduced = lax.dot_general(rows, weight, (((1,), (1,)), ((), ())), preferred_element_type=jnp.float32).astype(jnp.bfloat16)
        token_ids = picked // TOP
        factor = jnp.take(projected, token_ids, axis=0, mode="fill", fill_value=0)
        example = jnp.take(segments, token_ids, axis=0, mode="fill", fill_value=0)
        outer = reduced.astype(jnp.float32)[:, :, None] * factor.astype(jnp.float32)[:, None, :]
        outer = outer.reshape(slot_count, R * R)
        return jax.ops.segment_sum(outer, example, num_segments=EXAMPLES)

    blocks = lax.map(per_expert, jnp.arange(EXPERTS, dtype=jnp.int32))
    return jnp.transpose(blocks, (1, 0, 2)).astype(jnp.bfloat16)
```

```python
import functools

import jax
import jax.numpy as jnp
from jax import lax
from jax.experimental import pallas as pl
from jax.experimental.pallas import tpu as pltpu
from jax.sharding import PartitionSpec as P

SEG_DEV = 2
ROWS = 256


def reduce_kernel(tops, tokens, rank, grads_ref, routes_ref, weight_ref, basis_ref, out_ref, held):
    step = pl.program_id(0)
    dense = lax.dot_general(
        grads_ref[...], weight_ref[...], (((1,), (1,)), ((), ())), preferred_element_type=jnp.float32
    )
    first = step * (ROWS // rank)
    lanes = first + lax.broadcasted_iota(jnp.int32, (tokens, ROWS), 1) // rank
    total = jnp.zeros((tokens, ROWS), jnp.float32)
    for k in range(tops):
        rows = pl.ds(k * tokens, tokens)
        chosen = routes_ref[rows, :]
        chosen = jnp.concatenate([chosen] * (ROWS // 128), axis=1)
        total = total + jnp.where(chosen == lanes, dense[k * tokens : (k + 1) * tokens], 0.0)
    held[pl.ds(pl.multiple_of(step * ROWS, ROWS), ROWS), :] = total.T

    @pl.when(step == pl.num_programs(0) - 1)
    def _():
        experts = out_ref.shape[1]
        for pair in range(rank // 2):
            left = held[pl.ds(2 * pair, experts, stride=rank), :]
            right = held[pl.ds(2 * pair + 1, experts, stride=rank), :]
            both = jnp.concatenate([left, right], axis=1).astype(jnp.bfloat16)
            block = jnp.dot(both, basis_ref[...], preferred_element_type=jnp.float32)
            block = block.astype(jnp.bfloat16)
            for s in range(SEG_DEV):
                out_ref[s, :, pl.ds(pair * 2 * rank, 2 * rank)] = block[
                    :, s * 2 * rank : (s + 1) * 2 * rank
                ]


def local(hidden_in, out_grads, routes, segments, in_proj, out_proj):
    tokens, tops = routes.shape
    exp_here, rank, width = out_proj.shape
    experts = exp_here * lax.axis_size("expert")
    pairs = tokens * tops
    gathered = lax.all_gather(out_proj.reshape(exp_here * rank, width), "expert", axis=0, tiled=True)
    projected = lax.dot_general(
        hidden_in, in_proj, (((1,), (1,)), ((), ())), preferred_element_type=jnp.float32
    ).astype(jnp.bfloat16)
    local_seg = segments - lax.axis_index("expert") * SEG_DEV
    seg_mask = (local_seg[:, None] == jnp.arange(SEG_DEV, dtype=jnp.int32)[None, :]).astype(
        jnp.bfloat16
    )
    spread = seg_mask[:, :, None] * projected[:, None, :]
    parity = jnp.eye(2, dtype=jnp.bfloat16)
    basis = (parity[:, None, None, :, None] * spread[None, :, :, None, :]).reshape(
        2 * tokens, SEG_DEV * 2 * rank
    )
    grads = jnp.swapaxes(out_grads, 0, 1).reshape(pairs, width)
    chosen = jnp.broadcast_to(routes.T.reshape(pairs, 1), (pairs, 128))
    steps = experts * rank // ROWS
    return pl.pallas_call(
        functools.partial(reduce_kernel, tops, tokens, rank),
        grid=(steps,),
        out_shape=jax.ShapeDtypeStruct((SEG_DEV, experts, rank * rank), jnp.bfloat16),
        in_specs=[
            pl.BlockSpec((pairs, width), lambda i: (0, 0)),
            pl.BlockSpec((pairs, 128), lambda i: (0, 0)),
            pl.BlockSpec((ROWS, width), lambda i: (i, 0)),
            pl.BlockSpec((2 * tokens, SEG_DEV * 2 * rank), lambda i: (0, 0)),
        ],
        out_specs=pl.BlockSpec((SEG_DEV, experts, rank * rank), lambda i: (0, 0, 0)),
        scratch_shapes=[pltpu.VMEM((experts * rank, tokens), jnp.float32)],
        compiler_params=pltpu.CompilerParams(vmem_limit_bytes=56 * 1024 * 1024),
        cost_estimate=pl.CostEstimate(
            flops=2 * pairs * width * experts * rank,
            bytes_accessed=experts * rank * width * 2,
            transcendentals=0,
        ),
    )(grads, chosen, gathered, basis)


def solution(mesh):
    placed = (
        P(("groups", "expert"), None),
        P(("groups", "expert"), None, None),
        P(("groups", "expert"), None),
        P(("groups", "expert")),
        P(),
        P("expert", None, None),
    )
    return jax.shard_map(
        local,
        mesh=mesh,
        in_specs=placed,
        out_specs=P(("groups", "expert"), None, None),
        check_vma=False,
    )
```

```python
import functools

import jax
import jax.numpy as jnp
from jax import lax
from jax.experimental import pallas as pl
from jax.experimental.pallas import tpu as pltpu
from jax.sharding import PartitionSpec as P

SEG_DEV = 2
LANES = 128
CORES = 2
SIDES = 2
QUAD = 4
BOTH = ("groups", "expert")


def partial_kernel(plan, rank, fresh, bases_ref, tidx_ref, widx_ref, *refs):
    blocks, units, new_blocks = plan["blocks"], plan["units"], plan["new_blocks"]
    token_refs = refs[:blocks]
    weight_refs = refs[blocks : blocks + units]
    routes_ref = refs[blocks + units]
    acc_in = None if fresh else refs[blocks + units + 1]
    acc_out = refs[blocks + units + (1 if fresh else 2)]
    token_vmem, weight_vmem, sems = refs[-3:]
    copies = [
        pltpu.make_async_copy(ref, token_vmem.at[i], sems.at[i]) for i, ref in enumerate(token_refs)
    ] + [
        pltpu.make_async_copy(ref, weight_vmem.at[i], sems.at[blocks + i])
        for i, ref in enumerate(weight_refs)
    ]
    for copy in copies:
        copy.start()
    if fresh:
        acc_out[...] = jnp.zeros_like(acc_out)
    else:
        acc_out[...] = acc_in[...]
    for copy in copies:
        copy.wait()
    rows, width = token_vmem.shape[1:]
    cols = weight_vmem.shape[1]
    lane = lax.broadcasted_iota(jnp.int32, (1, LANES), 1) // rank
    per_tile = LANES // rank
    half = cols // CORES

    def step(i, carry):
        t, w = tidx_ref[i], widx_ref[i]
        dense = lax.dot_general(
            token_vmem[t],
            weight_vmem[w],
            (((1,), (1,)), ((), ())),
            preferred_element_type=jnp.float32,
        )
        here = pl.ds(pl.multiple_of(t * rows, rows), rows)
        chosen = routes_ref[here, :]
        total = acc_out[here, :]
        for j in range(cols // LANES):
            core, tile = divmod(j, half // LANES)
            expert = bases_ref[w * CORES + core] + tile * per_tile + lane
            total = total + jnp.where(
                chosen == expert, dense[:, j * LANES : (j + 1) * LANES], 0.0
            )
        acc_out[here, :] = total
        return carry

    lax.fori_loop(0, len(plan["steps"]), step, 0)


def accumulate(tokens, units, bases, routes, acc, steps, rank):
    rows, width = tokens[0].shape
    cols = units[0].shape[0]
    plan = {"blocks": len(tokens), "units": len(units), "steps": steps, "new_blocks": 0}
    fresh = acc is None
    total_rows = routes.shape[0]
    smem = pl.BlockSpec(memory_space=pltpu.SMEM)
    vmem = pl.BlockSpec(memory_space=pltpu.VMEM)
    hbm = pl.BlockSpec(memory_space=pl.ANY)
    tidx = jnp.array([t for t, _ in steps], jnp.int32)
    widx = jnp.array([w for _, w in steps], jnp.int32)
    operands = [jnp.stack(bases).reshape(-1), tidx, widx, *tokens, *units, routes]
    specs = [smem] * 3 + [hbm] * (len(tokens) + len(units)) + [vmem]
    aliases = {}
    if not fresh:
        aliases = {len(operands): 0}
        operands.append(acc)
        specs.append(vmem)
    return pl.pallas_call(
        functools.partial(partial_kernel, plan, rank, fresh),
        out_shape=jax.ShapeDtypeStruct((total_rows, LANES), jnp.float32),
        in_specs=specs,
        out_specs=vmem,
        scratch_shapes=[
            pltpu.VMEM((len(tokens), rows, width), jnp.bfloat16),
            pltpu.VMEM((len(units), cols, width), jnp.bfloat16),
            pltpu.SemaphoreType.DMA((len(tokens) + len(units),)),
        ],
        input_output_aliases=aliases,
        compiler_params=pltpu.CompilerParams(vmem_limit_bytes=40 * 1024 * 1024),
        cost_estimate=pl.CostEstimate(
            flops=2 * rows * cols * width * len(steps),
            bytes_accessed=(len(tokens) * rows + len(units) * cols) * width * 2,
            transcendentals=0,
        ),
    )(*operands)


def fold_kernel(rank, acc_ref, own_ref, *send_refs):
    half = own_ref.shape[0]
    low = lax.broadcasted_iota(jnp.int32, (half, LANES), 1) < rank
    for i, out in enumerate([own_ref, *send_refs]):
        one = acc_ref[2 * half * i : 2 * half * i + half, :]
        two = acc_ref[2 * half * i + half : 2 * half * (i + 1), :]
        one = one + pltpu.roll(one, rank, 1)
        two = two + pltpu.roll(two, rank, 1)
        out[...] = jnp.where(low, one, two).astype(out.dtype)


def fold(acc, rank):
    half = acc.shape[0] // QUAD // 2
    vmem = pl.BlockSpec(memory_space=pltpu.VMEM)
    return pl.pallas_call(
        functools.partial(fold_kernel, rank),
        out_shape=[jax.ShapeDtypeStruct((half, LANES), jnp.float32)]
        + [jax.ShapeDtypeStruct((half, LANES), jnp.bfloat16)] * (QUAD - 1),
        in_specs=[vmem],
        out_specs=[vmem] * QUAD,
        compiler_params=pltpu.CompilerParams(vmem_limit_bytes=16 * 1024 * 1024),
    )(acc)


def blocks_kernel(tops, rank, routes_ref, basis_ref, own_ref, b_ref, c_ref, d_ref, out_ref, pairs, turned, spread):
    half = own_ref.shape[0]
    tokens = 2 * half // tops
    total = own_ref[...]
    for ref in (b_ref, c_ref, d_ref):
        total = total + ref[...].astype(jnp.float32)
    total = total.astype(jnp.bfloat16).astype(jnp.float32)
    pairs[0:half, :] = total
    pairs[half : 2 * half, :] = pltpu.roll(total, rank, 1)
    for k in range(tops):
        turned[k] = pairs[pl.ds(k, tokens, stride=tops), :].T[0:rank, :]
    experts = out_ref.shape[1]

    def expand(tile, carry):
        first = pl.multiple_of(tile * 8, 8)
        ids = first + lax.broadcasted_iota(jnp.int32, (8, tokens), 0)
        masks = [routes_ref[k : k + 1, :] == ids for k in range(tops)]
        for r in range(rank):
            value = jnp.zeros((8, tokens), jnp.float32)
            for k in range(tops):
                value = jnp.where(masks[k], turned[k, r : r + 1, :], value)
            spread[r, pl.ds(first, 8), :] = value
        return carry

    lax.fori_loop(0, experts // 8, expand, 0)
    for pair in range(rank // 2):
        both = jnp.concatenate([spread[2 * pair], spread[2 * pair + 1]], axis=1)
        block = jnp.dot(
            both.astype(jnp.bfloat16), basis_ref[...], preferred_element_type=jnp.float32
        ).astype(jnp.bfloat16)
        for s in range(SEG_DEV):
            out_ref[s, :, pl.ds(pair * 2 * rank, 2 * rank)] = block[
                :, s * 2 * rank : (s + 1) * 2 * rank
            ]


def local(hidden_in, out_grads, routes, segments, in_proj, out_proj):
    tokens, tops = routes.shape
    exp_here, rank, width = out_proj.shape
    owners, groups = lax.axis_size("expert"), lax.axis_size("groups")
    experts = exp_here * owners
    pairs = tokens * tops
    quarter = width // QUAD
    group, index = lax.axis_index("groups"), lax.axis_index("expert")
    mine = (group % SIDES) * CORES + index % CORES

    def swap(array, side, bit):
        table = [
            (g * owners + e, (g ^ side) * owners + (e ^ bit))
            for g in range(groups)
            for e in range(owners)
        ]
        return lax.ppermute(array, BOTH, table)

    def onward(array):
        return lax.ppermute(
            array, "expert", [(e, (e + 2 * CORES) % owners) for e in range(owners)]
        )

    def columns(array, who):
        return lax.dynamic_slice_in_dim(array, who * quarter, quarter, axis=array.ndim - 1)

    weights = out_proj.reshape(exp_here * rank, width)
    other = swap(columns(weights, mine ^ 1), 0, 1)
    unit = jnp.concatenate([columns(weights, mine), other], axis=0)

    part = tokens // 2

    def token_block(who, turn):
        piece = lax.dynamic_slice(
            out_grads, (turn * part, 0, who * quarter), (part, tops, quarter)
        )
        return piece.reshape(part * tops, quarter)

    own_blocks = [token_block(mine, h) for h in range(2)]
    core_blocks = [swap(token_block(mine ^ 1, h), 0, 1) for h in range(2)]
    side_plan = [(2, 0, 0), (2, 0, 1), (3, 1, 0), (3, 1, 1)]

    all_routes = jnp.concatenate(
        [routes.reshape(pairs)]
        + [swap(routes, side, bit).reshape(pairs) for side, bit in ((0, 1), (1, 0), (1, 1))]
    )
    wide_routes = jnp.broadcast_to(all_routes[:, None], (QUAD * pairs, LANES))

    def base_of(chip):
        return [
            (chip * CORES + index % CORES) * exp_here,
            (chip * CORES + 1 - index % CORES) * exp_here,
        ]

    chip = index // CORES
    chips = owners // CORES
    slots = chips // 2
    block_list = own_blocks + core_blocks
    unit_list, base_list = [unit], [base_of(chip)]
    acc = None
    done_units = 0
    line = unit
    sent = None
    for slot in range(max(slots, len(side_plan))):
        known = len(block_list)
        before = done_units
        if slot < len(side_plan):
            flip, bit, turn = side_plan[slot]
            piece = token_block(mine ^ flip, turn)
            if sent is not None:
                piece, sent = lax.optimization_barrier((piece, sent))
            sent = swap(piece, 1, bit)
            block_list.append(sent)
        if slot < slots:
            at = (chip - 2 * slot) % chips
            unit_list.append(swap(line, 0, CORES))
            base_list.append(base_of(at ^ 1))
            if slot + 1 < slots:
                line = onward(line)
                unit_list.append(line)
                base_list.append(base_of((chip - 2 * (slot + 1)) % chips))
        done_units = len(unit_list)
        steps = [(t, w) for t in range(known) for w in range(before, done_units)]
        steps += [(t, w) for t in range(known, len(block_list)) for w in range(done_units)]
        acc = accumulate(
            block_list,
            unit_list,
            [b for pair in base_list for b in pair],
            wide_routes,
            acc,
            steps,
            rank,
        )

    own, for_core, for_side, for_diagonal = fold(acc, rank)
    from_core = swap(for_core, 0, 1)
    from_side = swap(for_side, 1, 0)
    from_diagonal = swap(for_diagonal, 1, 1)

    projected = lax.dot_general(
        hidden_in, in_proj, (((1,), (1,)), ((), ())), preferred_element_type=jnp.float32
    ).astype(jnp.bfloat16)
    local_seg = segments - index * SEG_DEV
    seg_mask = (local_seg[:, None] == jnp.arange(SEG_DEV, dtype=jnp.int32)[None, :]).astype(
        jnp.bfloat16
    )
    picked = seg_mask[:, :, None] * projected[:, None, :]
    parity = jnp.eye(2, dtype=jnp.bfloat16)
    basis = (parity[:, None, None, :, None] * picked[None, :, :, None, :]).reshape(
        2 * tokens, SEG_DEV * 2 * rank
    )
    vmem = pl.BlockSpec(memory_space=pltpu.VMEM)
    return pl.pallas_call(
        functools.partial(blocks_kernel, tops, rank),
        out_shape=jax.ShapeDtypeStruct((SEG_DEV, experts, rank * rank), jnp.bfloat16),
        in_specs=[vmem] * 6,
        out_specs=vmem,
        scratch_shapes=[
            pltpu.VMEM((pairs, LANES), jnp.float32),
            pltpu.VMEM((tops, rank, tokens), jnp.float32),
            pltpu.VMEM((rank, experts, tokens), jnp.float32),
        ],
        compiler_params=pltpu.CompilerParams(vmem_limit_bytes=40 * 1024 * 1024),
        cost_estimate=pl.CostEstimate(
            flops=2 * rank * experts * tokens * SEG_DEV * 2 * rank,
            bytes_accessed=2 * SEG_DEV * experts * rank * rank,
            transcendentals=0,
        ),
    )(routes.T, basis, own, from_core, from_side, from_diagonal)


def solution(mesh):
    placed = (
        P(("groups", "expert"), None),
        P(("groups", "expert"), None, None),
        P(("groups", "expert"), None),
        P(("groups", "expert")),
        P(),
        P("expert", None, None),
    )
    return jax.shard_map(
        local,
        mesh=mesh,
        in_specs=placed,
        out_specs=P(("groups", "expert"), None, None),
        check_vma=False,
    )
```

```python
import functools

import jax
import jax.numpy as jnp
from jax import lax
from jax.experimental import pallas as pl
from jax.experimental.pallas import tpu as pltpu
from jax.sharding import PartitionSpec as P

SEG_DEV = 2
LANES = 128
CORES = 2
SIDES = 2
QUAD = 4
CHUNKS = 4
BOTH = ("groups", "expert")
MIB = 1024 * 1024
VMEM = pl.BlockSpec(memory_space=pltpu.VMEM)
SMEM = pl.BlockSpec(memory_space=pltpu.SMEM)
HBM = pl.BlockSpec(memory_space=pl.ANY)
QUICK = pl.CostEstimate(flops=1, bytes_accessed=1, transcendentals=0)


def columns_of(ref, who, width):
    return ref.at[..., pl.ds(pl.multiple_of(who * width, width), width)]


def weights_kernel(who_ref, weight_ref, grads_ref, mine_ref, core_ref, chunk_ref, stage, sems):
    width = mine_ref.shape[0]
    part = chunk_ref.shape[0]
    one = pltpu.make_async_copy(columns_of(weight_ref, who_ref[1], width), stage.at[0], sems.at[0])
    two = pltpu.make_async_copy(columns_of(weight_ref, who_ref[0], width), stage.at[1], sems.at[1])
    cut = pltpu.make_async_copy(
        columns_of(grads_ref.at[pl.ds(0, part)], who_ref[2], width), chunk_ref, sems.at[2]
    )
    one.start()
    two.start()
    cut.start()
    one.wait()
    core_ref[...] = stage[0].T
    two.wait()
    mine_ref[...] = stage[1].T
    cut.wait()


def tokens_kernel(plan, who_ref, grads_ref, *refs):
    outs, sems = refs[:-1], refs[-1]
    copies = []
    for i, (out, (who, first)) in enumerate(zip(outs, plan)):
        part, _, width = out.shape
        source = columns_of(grads_ref.at[pl.ds(first, part)], who_ref[who], width)
        copies.append(pltpu.make_async_copy(source, out, sems.at[i]))
    for copy in copies:
        copy.start()
    for copy in copies:
        copy.wait()


def partial_kernel(rank, loops, new_tokens, new_units, fresh, who_ref, bases_ref, routes_ref, *refs):
    token_refs, refs = refs[: len(new_tokens)], refs[len(new_tokens) :]
    unit_refs, refs = refs[: len(new_units)], refs[len(new_units) :]
    if fresh:
        grads_ref, tokens, units, total, stage, sem = refs
        width = units.shape[1]
        copy = pltpu.make_async_copy(columns_of(grads_ref, who_ref[0], width), stage, sem)
        copy.start()
        total[...] = jnp.zeros_like(total)
        copy.wait()
        pairs = stage.shape[0] * stage.shape[1]
        tokens[0:pairs, :] = stage[...].reshape(pairs, width)
    else:
        tokens, units, total = refs[3:6]
    for ref, first in zip(token_refs, new_tokens):
        tokens[first : first + ref.shape[0], :] = ref[...]
    for ref, place in zip(unit_refs, new_units):
        units[place] = ref[...]
    cols = units.shape[2]
    lane = lax.broadcasted_iota(jnp.int32, (1, LANES), 1) // rank
    per_tile = LANES // rank
    for rows, first_t, count_t, first_w, count_w, both in loops:

        def step(i, carry, rows=rows, first_t=first_t, count_t=count_t, first_w=first_w, both=both):
            here = pl.ds(pl.multiple_of((first_t + i % count_t) * rows, rows), rows)
            place = first_w + (i // count_t) * both
            chosen = routes_ref[here, :]
            grads = tokens[here, :]
            added = total[here, :]
            for more in range(both):
                dense = jnp.dot(grads, units[place + more], preferred_element_type=jnp.float32)
                base = bases_ref[place + more]
                for j in range(cols // LANES):
                    added = added + jnp.where(
                        chosen == base + j * per_tile + lane,
                        dense[:, j * LANES : (j + 1) * LANES],
                        0.0,
                    )
            total[here, :] = added
            return carry

        lax.fori_loop(0, count_t * count_w // both, step, 0)


def accumulate(state, who, bases, routes, tokens, units, loops, rank, grads=None, places=0):
    fresh = state is None
    operands = [who, bases, routes, *[a for a, _ in tokens], *[a for a, _ in units]]
    specs = [SMEM, SMEM] + [VMEM] * (len(operands) - 2)
    scratch = []
    if fresh:
        operands.append(grads)
        specs.append(HBM)
        count, tops, whole = grads.shape
        width = whole // QUAD
        scratch = [pltpu.VMEM((count, tops, width), jnp.bfloat16), pltpu.SemaphoreType.DMA]
        shapes = [
            jax.ShapeDtypeStruct((routes.shape[0], width), jnp.bfloat16),
            jax.ShapeDtypeStruct((places, *units[0][0].shape), jnp.bfloat16),
            jax.ShapeDtypeStruct((routes.shape[0], LANES), jnp.float32),
        ]
        aliases = {}
    else:
        aliases = {len(operands) + i: i for i in range(3)}
        operands += state
        specs += [VMEM] * 3
        shapes = [jax.ShapeDtypeStruct(a.shape, a.dtype) for a in state]
    return pl.pallas_call(
        functools.partial(
            partial_kernel, rank, loops, [f for _, f in tokens], [p for _, p in units], fresh
        ),
        out_shape=shapes,
        in_specs=specs,
        out_specs=[VMEM] * 3,
        scratch_shapes=scratch,
        input_output_aliases=aliases,
        compiler_params=pltpu.CompilerParams(vmem_limit_bytes=36 * MIB),
        cost_estimate=QUICK,
    )(*operands)


def fold_kernel(rank, total_ref, own_ref, *send_refs):
    half = own_ref.shape[0]
    low = lax.broadcasted_iota(jnp.int32, (half, LANES), 1) < rank
    for i, out in enumerate([own_ref, *send_refs]):
        one = total_ref[2 * half * i : 2 * half * i + half, :]
        two = total_ref[2 * half * i + half : 2 * half * (i + 1), :]
        one = one + pltpu.roll(one, rank, 1)
        two = two + pltpu.roll(two, rank, 1)
        out[...] = jnp.where(low, one, two).astype(out.dtype)


def fold(total, rank):
    half = total.shape[0] // QUAD // 2
    return pl.pallas_call(
        functools.partial(fold_kernel, rank),
        out_shape=[jax.ShapeDtypeStruct((half, LANES), jnp.float32)]
        + [jax.ShapeDtypeStruct((half, LANES), jnp.bfloat16)] * (QUAD - 1),
        in_specs=[VMEM],
        out_specs=[VMEM] * QUAD,
        compiler_params=pltpu.CompilerParams(vmem_limit_bytes=16 * MIB),
        cost_estimate=QUICK,
    )(total)


def blocks_kernel(
    tops, rank, routes_ref, basis_ref, own_ref, b_ref, c_ref, d_ref, out_ref, pairs, turned, spread
):
    half = own_ref.shape[0]
    tokens = 2 * half // tops
    total = own_ref[...]
    for ref in (b_ref, c_ref, d_ref):
        total = total + ref[...].astype(jnp.float32)
    total = total.astype(jnp.bfloat16).astype(jnp.float32)
    pairs[0:half, :] = total
    pairs[half : 2 * half, :] = pltpu.roll(total, rank, 1)
    for k in range(tops):
        turned[k] = pairs[pl.ds(k, tokens, stride=tops), :].T[0:rank, :]
    experts = out_ref.shape[1]

    def expand(tile, carry):
        first = pl.multiple_of(tile * 8, 8)
        ids = first + lax.broadcasted_iota(jnp.int32, (8, tokens), 0)
        masks = [routes_ref[k : k + 1, :] == ids for k in range(tops)]
        for r in range(rank):
            value = jnp.zeros((8, tokens), jnp.float32)
            for k in range(tops):
                value = jnp.where(masks[k], turned[k, r : r + 1, :], value)
            spread[r, pl.ds(first, 8), :] = value
        return carry

    lax.fori_loop(0, experts // 8, expand, 0)
    for pair in range(rank // 2):
        both = jnp.concatenate([spread[2 * pair], spread[2 * pair + 1]], axis=1)
        block = jnp.dot(
            both.astype(jnp.bfloat16), basis_ref[...], preferred_element_type=jnp.float32
        ).astype(jnp.bfloat16)
        for s in range(SEG_DEV):
            out_ref[s, :, pl.ds(pair * 2 * rank, 2 * rank)] = block[
                :, s * 2 * rank : (s + 1) * 2 * rank
            ]


def local(hidden_in, out_grads, routes, segments, in_proj, out_proj):
    tokens, tops = routes.shape
    exp_here, rank, width = out_proj.shape
    owners, groups = lax.axis_size("expert"), lax.axis_size("groups")
    experts = exp_here * owners
    pairs = tokens * tops
    quarter = width // QUAD
    cols = exp_here * rank
    group, index = lax.axis_index("groups"), lax.axis_index("expert")
    core, chip = index % CORES, index // CORES
    chips = owners // CORES
    slots = chips // 2
    mine = (group % SIDES) * CORES + core
    who = jnp.stack([mine, mine ^ 1, mine ^ 2, mine ^ 3]).astype(jnp.int32)

    def swap(array, side, bit):
        table = [
            (g * owners + e, (g ^ side) * owners + (e ^ bit))
            for g in range(groups)
            for e in range(owners)
        ]
        return lax.ppermute(array, BOTH, table)

    def onward(array):
        return lax.ppermute(
            array, "expert", [(e, (e + 2 * CORES) % owners) for e in range(owners)]
        )

    def tie(*arrays):
        return lax.optimization_barrier(arrays)

    part = tokens // 2
    rows = part * tops
    chunk_shape = jax.ShapeDtypeStruct((part, tops, quarter), jnp.bfloat16)
    unit_shape = jax.ShapeDtypeStruct((quarter, cols), jnp.bfloat16)
    mine_unit, core_unit, first_chunk = pl.pallas_call(
        weights_kernel,
        out_shape=[unit_shape, unit_shape, chunk_shape],
        in_specs=[SMEM, HBM, HBM],
        out_specs=[VMEM, VMEM, HBM],
        scratch_shapes=[
            pltpu.VMEM((2, cols, quarter), jnp.bfloat16),
            pltpu.SemaphoreType.DMA((3,)),
        ],
        compiler_params=pltpu.CompilerParams(vmem_limit_bytes=16 * MIB),
        cost_estimate=QUICK,
    )(who, out_proj.reshape(cols, width), out_grads)
    other_unit = swap(core_unit, 0, 1)
    chunks = {0: swap(first_chunk.reshape(rows, quarter), 1, 0)}
    later_who, later_first, _ = tie(who, out_grads, mine_unit)
    for_core, *cut = pl.pallas_call(
        functools.partial(tokens_kernel, [(1, 0), (2, part), (3, 0), (3, part)]),
        out_shape=[jax.ShapeDtypeStruct((tokens, tops, quarter), jnp.bfloat16)] + [chunk_shape] * 3,
        in_specs=[SMEM, HBM],
        out_specs=[HBM] * 4,
        scratch_shapes=[pltpu.SemaphoreType.DMA((4,))],
        compiler_params=pltpu.CompilerParams(vmem_limit_bytes=16 * MIB),
        cost_estimate=QUICK,
    )(later_who, later_first)
    cut = [None] + [piece.reshape(rows, quarter) for piece in cut]
    chunks[1] = swap(cut[1], 1, 0)
    from_core = swap(for_core.reshape(pairs, quarter), 0, 1)

    all_routes = jnp.concatenate(
        [routes.reshape(pairs)]
        + [swap(routes, side, bit).reshape(pairs) for side, bit in ((0, 1), (1, 0), (1, 1))]
    )
    wide_routes = jnp.broadcast_to(all_routes[:, None], (QUAD * pairs, LANES))

    base_list = [(chip * CORES + core) * exp_here, (chip * CORES + 1 - core) * exp_here]
    for slot in range(slots):
        here = (chip - 2 * slot) % chips
        after = (chip - 2 * (slot + 1)) % chips
        for flip in (0, 1):
            at_core = core ^ flip
            base_list.append(((here ^ 1) * CORES + at_core) * exp_here)
            if slot + 1 < slots:
                base_list.append((after * CORES + at_core) * exp_here)
    bases = jnp.stack(base_list).astype(jnp.int32)
    places = len(base_list)

    line = [mine_unit, other_unit]
    across = [swap(line[0], 0, CORES), swap(line[1], 0, CORES)]
    ahead = [onward(line[0]), onward(line[1])]
    call = functools.partial(accumulate, who=who, bases=bases, routes=wide_routes, rank=rank)
    own_blocks = pairs // rows
    state = call(
        None,
        tokens=[],
        units=[(line[0], 0), (line[1], 1)],
        loops=[(pairs, 0, 1, 0, 2, 1)],
        grads=out_grads,
        places=places,
    )
    known_units = 2
    known_blocks = own_blocks

    def block_loops(first_w, count_w):
        double = known_blocks // 2
        loops = [(2 * rows, 0, double, first_w, count_w, 1)]
        if known_blocks % 2:
            loops.append((rows, known_blocks - 1, 1, first_w, count_w, 1))
        return loops

    state = call(
        state,
        tokens=[(from_core, pairs)],
        units=[],
        loops=[(pairs, 1, 1, 0, 2, 1)],
    )
    known_blocks = 2 * own_blocks
    for slot in range(slots):
        for chain in range(2):
            arrived = [(across[chain], known_units)]
            count = 1
            if slot + 1 < slots:
                line[chain], *state = tie(ahead[chain], *state)
                if slot + 2 < slots:
                    ahead[chain] = onward(line[chain])
                across[chain] = swap(line[chain], 0, CORES)
                arrived.append((line[chain], known_units + 1))
                count = 2
            state = call(state, tokens=[], units=arrived, loops=block_loops(known_units, count))
            known_units += count
            take = slot if (chain == 0 and slot < CHUNKS - 1) else None
            if slot == slots - 1 and chain == 1:
                take = CHUNKS - 1
            if take is not None:
                if take + 2 < CHUNKS:
                    nxt, chunk, *state = tie(cut[take + 2], chunks[take], *state)
                    chunks[take + 2] = swap(nxt, 1, 1)
                    chunks[take] = chunk
                state = call(
                    state,
                    tokens=[(chunks[take], known_blocks * rows)],
                    units=[],
                    loops=[(rows, known_blocks, 1, 0, known_units // 2 * 2, 2)]
                    + ([(rows, known_blocks, 1, known_units - 1, 1, 1)] if known_units % 2 else []),
                )
                known_blocks += 1

    own, for_core, for_side, for_diagonal = fold(state[2], rank)
    from_core = swap(for_core, 0, 1)
    from_side = swap(for_side, 1, 0)
    from_diagonal = swap(for_diagonal, 1, 1)

    projected = lax.dot_general(
        hidden_in, in_proj, (((1,), (1,)), ((), ())), preferred_element_type=jnp.float32
    ).astype(jnp.bfloat16)
    local_seg = segments - index * SEG_DEV
    seg_mask = (local_seg[:, None] == jnp.arange(SEG_DEV, dtype=jnp.int32)[None, :]).astype(
        jnp.bfloat16
    )
    picked = seg_mask[:, :, None] * projected[:, None, :]
    parity = jnp.eye(2, dtype=jnp.bfloat16)
    basis = (parity[:, None, None, :, None] * picked[None, :, :, None, :]).reshape(
        2 * tokens, SEG_DEV * 2 * rank
    )
    return pl.pallas_call(
        functools.partial(blocks_kernel, tops, rank),
        out_shape=jax.ShapeDtypeStruct((SEG_DEV, experts, rank * rank), jnp.bfloat16),
        in_specs=[VMEM] * 6,
        out_specs=VMEM,
        scratch_shapes=[
            pltpu.VMEM((pairs, LANES), jnp.float32),
            pltpu.VMEM((tops, rank, tokens), jnp.float32),
            pltpu.VMEM((rank, experts, tokens), jnp.float32),
        ],
        compiler_params=pltpu.CompilerParams(vmem_limit_bytes=40 * MIB),
        cost_estimate=QUICK,
    )(routes.T, basis, own, from_core, from_side, from_diagonal)


def solution(mesh):
    placed = (
        P(("groups", "expert"), None),
        P(("groups", "expert"), None, None),
        P(("groups", "expert"), None),
        P(("groups", "expert")),
        P(),
        P("expert", None, None),
    )
    return jax.shard_map(
        local,
        mesh=mesh,
        in_specs=placed,
        out_specs=P(("groups", "expert"), None, None),
        check_vma=False,
    )
```

```python
import functools

import jax
import jax.numpy as jnp
import numpy as np
from jax import lax
from jax.experimental import pallas as pl
from jax.experimental.pallas import tpu as pltpu
from jax.sharding import PartitionSpec as P

SEG_DEV = 2
CORES = 2
SIDES = 2
QUAD = 4
CHUNKS = 4
BOTH = ("groups", "expert")
MIB = 1024 * 1024
VMEM = pl.BlockSpec(memory_space=pltpu.VMEM)
SMEM = pl.BlockSpec(memory_space=pltpu.SMEM)
HBM = pl.BlockSpec(memory_space=pltpu.HBM)
QUICK = pl.CostEstimate(flops=1, bytes_accessed=1, transcendentals=0)


def columns_of(ref, who, width):
    return ref.at[..., pl.ds(pl.multiple_of(who * width, width), width)]


def cut_kernel(plan, who_ref, *refs):
    sources, outs, sems = refs[:2], refs[2:-1], refs[-1]
    copies = []
    for i, (out, (source, who, first)) in enumerate(zip(outs, plan)):
        part = out.shape[0]
        block = columns_of(sources[source].at[pl.ds(first, part)], who_ref[who], out.shape[-1])
        copies.append(pltpu.make_async_copy(block, out, sems.at[i]))
    for copy in copies:
        copy.start()
    for copy in copies:
        copy.wait()


def cut(plan, shapes, who, weights, grads):
    return pl.pallas_call(
        functools.partial(cut_kernel, plan),
        out_shape=[jax.ShapeDtypeStruct(shape, jnp.bfloat16) for shape in shapes],
        in_specs=[SMEM, HBM, HBM],
        out_specs=[HBM] * len(plan),
        scratch_shapes=[pltpu.SemaphoreType.DMA((len(plan),))],
        compiler_params=pltpu.CompilerParams(vmem_limit_bytes=4 * MIB),
        cost_estimate=QUICK,
    )(who, weights, grads)


def basis_kernel(hidden_ref, proj_ref, segment_ref, out_ref):
    projected = lax.dot_general(
        hidden_ref[...], proj_ref[...], (((1,), (1,)), ((), ())), preferred_element_type=jnp.float32
    )
    zero = jnp.zeros_like(projected)
    picked = [jnp.where(segment_ref[...] == s, projected, zero) for s in range(SEG_DEV)]
    even = jnp.concatenate([b for p in picked for b in (p, zero)], axis=1)
    odd = jnp.concatenate([b for p in picked for b in (zero, p)], axis=1)
    out_ref[...] = jnp.concatenate([even, odd], axis=0).astype(out_ref.dtype)


def partial_kernel(
    rank, loops, new_tokens, new_units, fresh, sends, who_ref, bases_ref, routes_ref, *refs
):
    token_refs, refs = refs[: len(new_tokens)], refs[len(new_tokens) :]
    unit_refs, refs = refs[: len(new_units)], refs[len(new_units) :]
    if fresh:
        grads_ref, tokens, units, total, stage, sem = refs
        width = units.shape[2]
        copy = pltpu.make_async_copy(columns_of(grads_ref, who_ref[0], width), stage, sem)
        copy.start()
        total[...] = jnp.zeros_like(total)
        copy.wait()
        pairs = stage.shape[0] * stage.shape[1]
        tokens[0:pairs, :] = stage[...].reshape(pairs, width)
        send_refs = ()
    else:
        tokens, units, total = refs[3:6]
        send_refs = refs[6:]
    for ref, first in zip(token_refs, new_tokens):
        tokens[first : first + ref.shape[0], :] = ref[...]
    for ref, place in zip(unit_refs, new_units):
        units[place] = ref[...]
    cols, width = units.shape[1:]
    rows = total.shape[2]
    for first_t, count_t, first_w, count_w, together in loops:

        def step(i, carry, first_t=first_t, count_t=count_t, first_w=first_w, together=together):
            t = first_t + i % count_t
            w = first_w + (i // count_t) * together
            here = pl.ds(pl.multiple_of(t * rows, rows), rows)
            dense = lax.dot_general(
                units[pl.ds(w, together)].reshape(together * cols, width),
                tokens[here, :],
                (((1,), (1,)), ((), ())),
                preferred_element_type=jnp.float32,
            )
            chosen = routes_ref[pl.ds(t, 1), :]
            value = total[t]
            for more in range(together):
                base = bases_ref[w + more]
                for expert in range(cols // rank):
                    first = more * cols + expert * rank
                    value = jnp.where(chosen == base + expert, dense[first : first + rank], value)
            total[t] = value
            return carry

        lax.fori_loop(0, count_t * (count_w // together), step, 0)
    for ref, first in zip(send_refs, sends):
        ref[...] = total[first : first + ref.shape[0]].astype(ref.dtype)


def accumulate(
    state, who, bases, routes, tokens, units, loops, rank, grads=None, places=0, sends=()
):
    fresh = state is None
    operands = [who, bases, routes, *[a for a, _ in tokens], *[a for a, _ in units]]
    specs = [SMEM, SMEM] + [VMEM] * (len(operands) - 2)
    scratch = []
    blocks, rows = routes.shape
    if fresh:
        operands.append(grads)
        specs.append(HBM)
        count, tops, whole = grads.shape
        width = whole // QUAD
        scratch = [pltpu.VMEM((count, tops, width), jnp.bfloat16), pltpu.SemaphoreType.DMA]
        shapes = [
            jax.ShapeDtypeStruct((blocks * rows, width), jnp.bfloat16),
            jax.ShapeDtypeStruct((places, *units[0][0].shape), jnp.bfloat16),
            jax.ShapeDtypeStruct((blocks, rank, rows), jnp.float32),
        ]
        aliases = {}
    else:
        aliases = {len(operands) + i: i for i in range(3)}
        operands += state
        specs += [VMEM] * 3
        shapes = [jax.ShapeDtypeStruct(a.shape, a.dtype) for a in state]
    shapes += [jax.ShapeDtypeStruct((blocks // QUAD, rank, rows), jnp.bfloat16)] * len(sends)
    return pl.pallas_call(
        functools.partial(
            partial_kernel,
            rank,
            loops,
            [f for _, f in tokens],
            [p for _, p in units],
            fresh,
            sends,
        ),
        out_shape=shapes,
        in_specs=specs,
        out_specs=[VMEM] * len(shapes),
        scratch_shapes=scratch,
        input_output_aliases=aliases,
        compiler_params=pltpu.CompilerParams(vmem_limit_bytes=24 * MIB),
        cost_estimate=QUICK,
    )(*operands)


def blocks_kernel(
    tops, rank, routes_ref, basis_ref, own_ref, b_ref, c_ref, d_ref, out_ref, pairs, turned, spread
):
    halves, _, rows = b_ref.shape
    tokens = halves * rows // tops
    for h in range(halves):
        value = own_ref[h]
        for ref in (b_ref, c_ref, d_ref):
            value = value + ref[h].astype(jnp.float32)
        value = value.astype(jnp.bfloat16).astype(jnp.float32)
        pairs[h * rows : (h + 1) * rows, 0:rank] = value.T
    for k in range(tops):
        turned[k] = pairs[pl.ds(k, tokens, stride=tops), :].T[0:rank, :]
    experts = out_ref.shape[1]

    def expand(tile, carry):
        first = pl.multiple_of(tile * 8, 8)
        ids = first + lax.broadcasted_iota(jnp.int32, (8, tokens), 0)
        masks = [routes_ref[k : k + 1, :] == ids for k in range(tops)]
        for r in range(rank):
            value = jnp.zeros((8, tokens), jnp.float32)
            for k in range(tops):
                value = jnp.where(masks[k], turned[k, r : r + 1, :], value)
            spread[r, pl.ds(first, 8), :] = value
        return carry

    lax.fori_loop(0, experts // 8, expand, 0)
    for pair in range(rank // 2):
        both = jnp.concatenate([spread[2 * pair], spread[2 * pair + 1]], axis=1)
        block = jnp.dot(
            both.astype(jnp.bfloat16), basis_ref[...], preferred_element_type=jnp.float32
        ).astype(jnp.bfloat16)
        for s in range(SEG_DEV):
            out_ref[s, :, pl.ds(pair * 2 * rank, 2 * rank)] = block[
                :, s * 2 * rank : (s + 1) * 2 * rank
            ]


def local(hidden_in, out_grads, routes, segments, in_proj, out_proj):
    tokens, tops = routes.shape
    exp_here, rank, width = out_proj.shape
    owners, groups = lax.axis_size("expert"), lax.axis_size("groups")
    experts = exp_here * owners
    pairs = tokens * tops
    quarter = width // QUAD
    cols = exp_here * rank
    group, index = lax.axis_index("groups"), lax.axis_index("expert")
    core = index % CORES
    slots = owners // CORES // 2
    mine = (group % SIDES) * CORES + core
    who = jnp.stack([mine, mine ^ 1, mine ^ 2, mine ^ 3]).astype(jnp.int32)
    ring = [0, *range(1, slots, 2), *range((slots - 1) // 2 * 2, 0, -2)]
    following = {a: b for a, b in zip(ring, ring[1:] + ring[:1])}
    before = {b: a for a, b in following.items()}

    def swap(array, side, bit):
        table = [
            (g * owners + e, (g ^ side) * owners + (e ^ bit))
            for g in range(groups)
            for e in range(owners)
        ]
        return lax.ppermute(array, BOTH, table)

    def onward(array):
        wide = 2 * CORES
        table = [(e, following[e // wide] * wide + e % wide) for e in range(owners)]
        return lax.ppermute(array, "expert", table)

    def tie(*arrays):
        return lax.optimization_barrier(arrays)

    rows_of = []
    for e in range(owners):
        z, y, c = e // (2 * CORES), e // CORES % 2, e % CORES
        named = [(z, y, c), (z, y, 1 - c)]
        here = z
        for slot in range(slots):
            after = before[here]
            for flip in (0, 1):
                named.append((here, 1 - y, c ^ flip))
                if slot + 1 < slots:
                    named.append((after, y, c ^ flip))
            here = after
        rows_of.append([((a * 2 + b) * CORES + d) * exp_here for a, b, d in named])
    places = len(rows_of[0])
    bases = lax.dynamic_index_in_dim(
        jnp.asarray(np.array(rows_of, np.int32)), index, axis=0, keepdims=False
    )

    part = tokens // 2
    rows = part * tops
    flat_routes = routes.reshape(1, pairs)
    around = [swap(flat_routes, side, bit) for side, bit in ((0, 1), (1, 0), (1, 1))]
    all_routes = jnp.concatenate([flat_routes, *around], axis=0).reshape(QUAD * pairs // rows, rows)

    weights = out_proj.reshape(cols, width)
    unit_shape, chunk_shape = (cols, quarter), (part, tops, quarter)
    mine_unit, core_unit, first_chunk = cut(
        [(0, 0, 0), (0, 1, 0), (1, 2, 0)],
        [unit_shape, unit_shape, chunk_shape],
        who,
        weights,
        out_grads,
    )
    other_unit = swap(core_unit, 0, 1)
    later_who, _ = tie(who, mine_unit)
    for_core, *pieces = cut(
        [(1, 1, 0), (1, 2, part), (1, 3, 0), (1, 3, part)],
        [(tokens, tops, quarter)] + [chunk_shape] * 3,
        later_who,
        weights,
        out_grads,
    )
    pieces = [first_chunk, *pieces]
    chunks = [
        swap(piece.reshape(rows, quarter), 1, bit) for piece, bit in zip(pieces, (0, 0, 1, 1))
    ]
    from_core = swap(for_core.reshape(pairs, quarter), 0, 1)

    basis = pl.pallas_call(
        basis_kernel,
        out_shape=jax.ShapeDtypeStruct((2 * tokens, SEG_DEV * 2 * rank), jnp.bfloat16),
        in_specs=[VMEM] * 3,
        out_specs=VMEM,
        compiler_params=pltpu.CompilerParams(vmem_limit_bytes=16 * MIB),
        cost_estimate=QUICK,
    )(hidden_in, in_proj, (segments - index * SEG_DEV).reshape(tokens, 1))

    line = [mine_unit, other_unit]
    across = [swap(line[0], 0, CORES), swap(line[1], 0, CORES)]
    ahead = [onward(line[0]), onward(line[1])]
    call = functools.partial(accumulate, who=who, bases=bases, routes=all_routes, rank=rank)
    own_blocks = pairs // rows
    state = call(
        None,
        tokens=[],
        units=[(line[0], 0), (line[1], 1)],
        loops=[(0, own_blocks, 0, 2, 2)],
        grads=out_grads,
        places=places,
    )
    basis, *state = tie(basis, *state)
    state = call(
        state,
        tokens=[(from_core, pairs)],
        units=[],
        loops=[(own_blocks, own_blocks, 0, 2, 2)],
    )
    known_units, known_blocks = 2, 2 * own_blocks
    sent = []
    for slot in range(slots):
        for chain in range(2):
            arrived = [(across[chain], known_units)]
            if slot + 1 < slots:
                line[chain], *state = tie(ahead[chain], *state)
                if slot + 2 < slots:
                    ahead[chain] = onward(line[chain])
                across[chain] = swap(line[chain], 0, CORES)
                arrived.append((line[chain], known_units + 1))
            count = len(arrived)
            last = slot + 1 == slots and chain == 1
            state = call(
                state,
                tokens=[],
                units=arrived,
                loops=[(0, known_blocks, known_units, count, count)],
                sends=[own_blocks, 2 * own_blocks] if last else [],
            )
            state, sent = state[:3], sent + list(state[3:])
            known_units += count
            take = slot if chain == 0 and slot < CHUNKS - 1 else CHUNKS - 1 if last else None
            if take is not None:
                loops = [(known_blocks, 1, 0, known_units // 2 * 2, 2)]
                if known_units % 2:
                    loops.append((known_blocks, 1, known_units - 1, 1, 1))
                state = call(
                    state,
                    tokens=[(chunks[take], known_blocks * rows)],
                    units=[],
                    loops=loops,
                    sends=[3 * own_blocks] if last else [],
                )
                state, sent = state[:3], sent + list(state[3:])
                known_blocks += 1

    from_core = swap(sent[0], 0, 1)
    from_side = swap(sent[1], 1, 0)
    from_diagonal = swap(sent[2], 1, 1)
    return pl.pallas_call(
        functools.partial(blocks_kernel, tops, rank),
        out_shape=jax.ShapeDtypeStruct((SEG_DEV, experts, rank * rank), jnp.bfloat16),
        in_specs=[VMEM] * 6,
        out_specs=VMEM,
        scratch_shapes=[
            pltpu.VMEM((pairs, 2 * rank), jnp.float32),
            pltpu.VMEM((tops, rank, tokens), jnp.float32),
            pltpu.VMEM((rank, experts, tokens), jnp.float32),
        ],
        compiler_params=pltpu.CompilerParams(vmem_limit_bytes=32 * MIB),
        cost_estimate=QUICK,
    )(routes.T, basis, state[2], from_core, from_side, from_diagonal)


def solution(mesh):
    placed = (
        P(("groups", "expert"), None),
        P(("groups", "expert"), None, None),
        P(("groups", "expert"), None),
        P(("groups", "expert")),
        P(),
        P("expert", None, None),
    )
    return jax.shard_map(
        local,
        mesh=mesh,
        in_specs=placed,
        out_specs=P(("groups", "expert"), None, None),
        check_vma=False,
    )
```

```python
import functools

import jax
import jax.numpy as jnp
import numpy as np
from jax import lax
from jax.experimental import pallas as pl
from jax.experimental.pallas import tpu as pltpu
from jax.sharding import PartitionSpec as P

SEG_DEV = 2
CORES = 2
SIDES = 2
QUAD = 4
PIECES = 4
LANES = 128
ALIGN = 16
DIGIT = 32
BOTH = ("groups", "expert")
MIB = 1024 * 1024
VMEM = pl.BlockSpec(memory_space=pltpu.VMEM)
SMEM = pl.BlockSpec(memory_space=pltpu.SMEM)
HBM = pl.BlockSpec(memory_space=pl.ANY)
QUICK = pl.CostEstimate(flops=1, bytes_accessed=1, transcendentals=0)
NT = (((1,), (1,)), ((), ()))


def columns_of(ref, who, width):
    return ref.at[..., pl.ds(pl.multiple_of(who * width, width), width)]


def key_column(routes_row):
    count = routes_row.shape[1]
    keys = routes_row * count + lax.broadcasted_iota(jnp.int32, (1, count), 1)
    return jnp.broadcast_to(keys.astype(jnp.float32), (8, count)).T[:, 0:1]


def ranks(column, keys):
    total = jnp.zeros(keys.shape, jnp.float32)
    for first in range(0, column.shape[0], 128):
        smaller = jnp.where(column[first : first + 128] < keys, 1.0, 0.0)
        total = total + jnp.sum(smaller, axis=0, keepdims=True)
    return total


def sort_kernel(
    who_ref,
    routes_ref,
    weight_ref,
    grads_ref,
    mine_ref,
    core_ref,
    starts_ref,
    head_ref,
    order_ref,
    piece_ref,
    next_ref,
    stage,
    sems,
):
    width = mine_ref.shape[1]
    copies = [
        pltpu.make_async_copy(columns_of(grads_ref, who_ref[2], width), stage, sems.at[0]),
        pltpu.make_async_copy(columns_of(weight_ref, who_ref[0], width), mine_ref, sems.at[1]),
        pltpu.make_async_copy(columns_of(weight_ref, who_ref[1], width), core_ref, sems.at[2]),
    ]
    for copy in copies:
        copy.start()
    routes = routes_ref[...]
    pairs = routes.shape[1]
    column = key_column(routes)
    keys = routes * pairs + lax.broadcasted_iota(jnp.int32, (1, pairs), 1)
    place = ranks(column, keys.astype(jnp.float32)).astype(jnp.int32)
    firsts = lax.broadcasted_iota(jnp.int32, starts_ref.shape, 1) * pairs
    starts = ranks(column, firsts.astype(jnp.float32)).astype(jnp.int32)
    starts_ref[...] = starts
    wide = head_ref.shape[1] - starts.shape[1]
    digits = [starts // DIGIT, starts % DIGIT]
    digits = [jnp.pad(d.astype(jnp.float32), ((0, 0), (0, wide))) for d in digits]
    row = lax.broadcasted_iota(jnp.int32, head_ref.shape, 0)
    head = jnp.where(row == 0, digits[0], jnp.where(row == 1, digits[1], 0.0))
    head_ref[...] = head.astype(jnp.bfloat16)
    rows = next_ref.shape[0]
    for first in range(0, pairs, rows):
        ids = first + lax.broadcasted_iota(jnp.int32, (rows, pairs), 0)
        order_ref[first : first + rows, :] = jnp.where(place == ids, 1.0, 0.0).astype(jnp.bfloat16)
    for copy in copies:
        copy.wait()
    sorted_rows = jnp.dot(
        order_ref[0 : 2 * rows, :],
        stage[...].reshape(pairs, width),
        preferred_element_type=jnp.float32,
    ).astype(jnp.bfloat16)
    piece_ref[0:rows, :] = sorted_rows[0:rows]
    piece_ref[rows:, :] = head_ref[...]
    next_ref[...] = sorted_rows[rows:]


def permute_kernel(plan, who_ref, order_ref, head_ref, grads_ref, *refs):
    outs, stage, sems = refs[:-2], refs[-2], refs[-1]
    pairs, width = order_ref.shape[0], outs[0].shape[1]
    devices = sorted({device for device, _, _ in plan})
    copies = {
        device: pltpu.make_async_copy(
            columns_of(grads_ref, who_ref[device], width), stage.at[i], sems.at[i]
        )
        for i, device in enumerate(devices)
    }
    for copy in copies.values():
        copy.start()
    for i, device in enumerate(devices):
        copies[device].wait()
        grads = stage[i].reshape(pairs, width)
        for out, (target, first, rows) in zip(outs, plan):
            if target == device:
                out[0:rows, :] = jnp.dot(
                    order_ref[first : first + rows, :], grads, preferred_element_type=jnp.float32
                ).astype(jnp.bfloat16)
                if out.shape[0] > rows:
                    out[rows:, :] = head_ref[...]


def basis_kernel(
    hidden_ref, proj_ref, segment_ref, routes_ref, turned_ref, out_ref, order_ref
):
    projected = lax.dot_general(
        hidden_ref[...], proj_ref[...], NT, preferred_element_type=jnp.float32
    )
    zero = jnp.zeros_like(projected)
    picked = [jnp.where(segment_ref[...] == s, projected, zero) for s in range(SEG_DEV)]
    even = jnp.concatenate([b for p in picked for b in (p, zero)], axis=1)
    odd = jnp.concatenate([b for p in picked for b in (zero, p)], axis=1)
    out_ref[...] = jnp.concatenate([even, odd], axis=0).astype(out_ref.dtype)
    pairs = routes_ref.shape[1]
    tops, tokens = turned_ref.shape
    column = key_column(routes_ref[...])
    at = [
        turned_ref[k : k + 1, :] * pairs + lax.broadcasted_iota(jnp.int32, (1, tokens), 1) * tops + k
        for k in range(tops)
    ]
    place = ranks(column, jnp.concatenate(at, axis=1).astype(jnp.float32)).astype(jnp.int32)
    for first in range(0, pairs, 256):
        ids = first + lax.broadcasted_iota(jnp.int32, (256, pairs), 0)
        order_ref[first : first + 256, :] = jnp.where(place == ids, 1.0, 0.0).astype(jnp.bfloat16)


def packed(total, first, pairs, rank):
    half = pairs // 2
    low = lax.broadcasted_iota(jnp.int32, (half, LANES), 1) < rank
    one = total[first : first + half, :]
    two = total[first + half : first + pairs, :]
    return jnp.where(low, one + pltpu.roll(one, rank, 1), two + pltpu.roll(two, rank, 1))


def partial_kernel(
    rank, pairs, window, new_tokens, new_units, tasks, fresh, sends, groups, bases_ref, *refs
):
    start_refs = dict(zip(groups, refs))
    refs = refs[len(groups) :]
    token_refs, refs = refs[: len(new_tokens)], refs[len(new_tokens) :]
    unit_refs, refs = refs[: len(new_units)], refs[len(new_units) :]
    if fresh:
        tokens, units, total = refs
        send_refs = ()
        total[...] = jnp.zeros_like(total)
    else:
        tokens, units, total = refs[3:6]
        send_refs = refs[6:]
    for ref, (first, count) in zip(token_refs, new_tokens):
        tokens[first : first + count, :] = ref[0:count, :]
    for ref, place in zip(unit_refs, new_units):
        units[place] = ref[...]
    cols = units.shape[1]
    held = cols // rank
    per_tile = LANES // rank
    low = lax.broadcasted_iota(jnp.int32, (1, LANES), 1) < rank

    def process(w, members):
        base = bases_ref[w]
        heres, offsets = [], []
        for g in members:
            at = jnp.minimum(start_refs[g][0, base] & -ALIGN, pairs - window)
            offsets.append(at)
            heres.append(pl.ds(pl.multiple_of(g * pairs + at, ALIGN), window))
        rows = [tokens[here, :] for here in heres]
        rows = jnp.concatenate(rows, axis=0) if len(rows) > 1 else rows[0]
        dense = lax.dot_general(rows, units[w], NT, preferred_element_type=jnp.float32)
        for n, g in enumerate(members):
            value = total[heres[n], :]
            number = offsets[n] + lax.broadcasted_iota(jnp.int32, (window, LANES), 0)
            for j in range(cols // LANES):
                edge = [start_refs[g][0, base + j * per_tile + i] for i in range(per_tile + 1)]
                inside = (number >= jnp.where(low, edge[0], edge[1])) & (
                    number < jnp.where(low, edge[1], edge[2])
                )
                part = dense[n * window : (n + 1) * window, j * LANES : (j + 1) * LANES]
                value = jnp.where(inside, part, value)
            total[heres[n], :] = value

    for task in tasks:
        if task[0] == "units":
            _, members, first_w, count = task

            def each(i, carry, members=members, first_w=first_w):
                process(first_w + i, members)
                return carry

        else:
            _, member, first_row, end_row, first_w, count = task

            def each(
                i, carry, member=member, first_row=first_row, end_row=end_row, first_w=first_w
            ):
                w = first_w + i
                base = bases_ref[w]
                touches = (start_refs[member][0, base] < end_row) & (
                    start_refs[member][0, base + held] > first_row
                )

                @pl.when(touches)
                def _():
                    process(w, [member])

                return carry

        lax.fori_loop(0, count, each, 0)
    for ref, g in zip(send_refs, sends):
        ref[...] = packed(total, g * pairs, pairs, rank).astype(ref.dtype)


def accumulate(
    state, bases, starts, tokens, units, tasks, rank, pairs, window, places=0, sends=()
):
    fresh = state is None
    operands = [bases, *starts.values(), *[a for a, _, _ in tokens], *[a for a, _ in units]]
    specs = [SMEM] * (1 + len(starts)) + [VMEM] * (len(tokens) + len(units))
    if fresh:
        width = units[0][0].shape[1]
        shapes = [
            jax.ShapeDtypeStruct((QUAD * pairs, width), jnp.bfloat16),
            jax.ShapeDtypeStruct((places, *units[0][0].shape), jnp.bfloat16),
            jax.ShapeDtypeStruct((QUAD * pairs, LANES), jnp.float32),
        ]
        aliases = {}
    else:
        aliases = {len(operands) + i: i for i in range(3)}
        operands += state
        specs += [VMEM] * 3
        shapes = [jax.ShapeDtypeStruct(a.shape, a.dtype) for a in state]
    shapes += [jax.ShapeDtypeStruct((pairs // 2, LANES), jnp.bfloat16)] * len(sends)
    out = pl.pallas_call(
        functools.partial(
            partial_kernel,
            rank,
            pairs,
            window,
            [(first, count) for _, first, count in tokens],
            [p for _, p in units],
            tasks,
            fresh,
            sends,
            list(starts),
        ),
        out_shape=shapes,
        in_specs=specs,
        out_specs=[VMEM] * len(shapes),
        input_output_aliases=aliases,
        compiler_params=pltpu.CompilerParams(vmem_limit_bytes=20 * MIB),
        cost_estimate=QUICK,
    )(*operands)
    return list(out[:3]), list(out[3:])


def blocks_kernel(
    tops, rank, routes_ref, basis_ref, order_ref, total_ref, b_ref, c_ref, d_ref, out_ref, turned, spread
):
    half = b_ref.shape[0]
    tokens = 2 * half // tops
    value = packed(total_ref, 0, 2 * half, rank)
    for ref in (b_ref, c_ref, d_ref):
        value = value + ref[...].astype(jnp.float32)
    value = value.T
    value = jnp.concatenate([value[0:rank], value[rank : 2 * rank]], axis=1).astype(jnp.bfloat16)
    turned[...] = jnp.dot(value, order_ref[...], preferred_element_type=jnp.float32)
    experts = out_ref.shape[1]

    def expand(tile, carry):
        first = pl.multiple_of(tile * 8, 8)
        ids = first + lax.broadcasted_iota(jnp.int32, (8, tokens), 0)
        masks = [routes_ref[k : k + 1, :] == ids for k in range(tops)]
        for r in range(rank):
            value = jnp.zeros((8, tokens), jnp.float32)
            for k in range(tops):
                row = turned[r : r + 1, k * tokens : (k + 1) * tokens]
                value = jnp.where(masks[k], row, value)
            spread[r, pl.ds(first, 8), :] = value
        return carry

    lax.fori_loop(0, experts // 8, expand, 0)
    for pair in range(rank // 2):
        both = jnp.concatenate([spread[2 * pair], spread[2 * pair + 1]], axis=1)
        block = jnp.dot(
            both.astype(jnp.bfloat16), basis_ref[...], preferred_element_type=jnp.float32
        ).astype(jnp.bfloat16)
        for s in range(SEG_DEV):
            out_ref[s, :, pl.ds(pair * 2 * rank, 2 * rank)] = block[
                :, s * 2 * rank : (s + 1) * 2 * rank
            ]


def local(hidden_in, out_grads, routes, segments, in_proj, out_proj):
    tokens, tops = routes.shape
    exp_here, rank, width = out_proj.shape
    owners, groups = lax.axis_size("expert"), lax.axis_size("groups")
    experts = exp_here * owners
    pairs = tokens * tops
    capacity = max(2, 3 * pairs // (2 * experts))
    window = min(pairs, -(-(exp_here * capacity + ALIGN - 1) // ALIGN) * ALIGN)
    quarter = width // QUAD
    cols = exp_here * rank
    rows = pairs // PIECES
    group, index = lax.axis_index("groups"), lax.axis_index("expert")
    core = index % CORES
    slots = owners // CORES // 2
    mine = (group % SIDES) * CORES + core
    who = jnp.stack([mine, mine ^ 1, mine ^ 2, mine ^ 3]).astype(jnp.int32)
    ring = [0, *range(1, slots, 2), *range((slots - 1) // 2 * 2, 0, -2)]
    following = {a: b for a, b in zip(ring, ring[1:] + ring[:1])}
    before = {b: a for a, b in following.items()}

    def swap(array, side, bit):
        table = [
            (g * owners + e, (g ^ side) * owners + (e ^ bit))
            for g in range(groups)
            for e in range(owners)
        ]
        return lax.ppermute(array, BOTH, table)

    def onward(array, bit=0):
        wide = 2 * CORES
        table = [(e, following[e // wide] * wide + (e % wide ^ bit)) for e in range(owners)]
        return lax.ppermute(array, "expert", table)

    def tie(*arrays):
        return lax.optimization_barrier(arrays)

    rows_of = []
    for e in range(owners):
        z, y, c = e // (2 * CORES), e // CORES % 2, e % CORES
        named = [(z, y, c), (z, y, 1 - c)]
        here = z
        for slot in range(slots):
            after = before[here]
            for flip in (0, 1):
                named.append((here, 1 - y, c ^ flip))
                if slot + 1 < slots:
                    named.append((after, y, c ^ flip))
            here = after
        rows_of.append([((a * 2 + b) * CORES + d) * exp_here for a, b, d in named])
    places = len(rows_of[0])
    bases = lax.dynamic_index_in_dim(
        jnp.asarray(np.array(rows_of, np.int32)), index, axis=0, keepdims=False
    )

    flat_routes = routes.reshape(1, pairs)
    unit_shape = jax.ShapeDtypeStruct((cols, quarter), jnp.bfloat16)
    order_shape = jax.ShapeDtypeStruct((pairs, pairs), jnp.bfloat16)

    def rows_shape(count):
        return jax.ShapeDtypeStruct((count, quarter), jnp.bfloat16)

    stage = pltpu.VMEM((tokens, tops, quarter), jnp.bfloat16)
    edges = -(-(experts + 1) // LANES) * LANES
    mine_unit, core_unit, own_starts, head, order, *first_pieces = pl.pallas_call(
        sort_kernel,
        out_shape=[
            unit_shape,
            unit_shape,
            jax.ShapeDtypeStruct((1, edges), jnp.int32),
            rows_shape(ALIGN),
            order_shape,
            rows_shape(rows + ALIGN),
            rows_shape(rows),
        ],
        in_specs=[SMEM, VMEM, HBM, HBM],
        out_specs=[HBM, HBM, VMEM, VMEM, VMEM, VMEM, VMEM],
        scratch_shapes=[stage, pltpu.SemaphoreType.DMA((3,))],
        compiler_params=pltpu.CompilerParams(vmem_limit_bytes=60 * MIB),
        cost_estimate=QUICK,
    )(who, flat_routes, out_proj.reshape(cols, width), out_grads)

    def permuted(plan, headed, *after):
        count = len({device for device, _, _ in plan})
        held, *_ = tie(who, *after)
        return pl.pallas_call(
            functools.partial(permute_kernel, plan),
            out_shape=[
                rows_shape(many + (ALIGN if n in headed else 0))
                for n, (_, _, many) in enumerate(plan)
            ],
            in_specs=[SMEM, VMEM, VMEM, HBM],
            out_specs=[VMEM] * len(plan),
            scratch_shapes=[
                pltpu.VMEM((count, tokens, tops, quarter), jnp.bfloat16),
                pltpu.SemaphoreType.DMA((count,)),
            ],
            compiler_params=pltpu.CompilerParams(vmem_limit_bytes=56 * MIB),
            cost_estimate=QUICK,
        )(held, order, head, out_grads)

    def starts_in(block, count):
        digits = block[count : count + 2, :edges].astype(jnp.int32)
        return (digits[0] * DIGIT + digits[1]).reshape(1, edges)

    other_unit = swap(core_unit, 0, 1)
    pieces = [
        *first_pieces,
        *permuted([(2, n * rows, rows) for n in range(2, PIECES)], [], other_unit),
    ]

    def send_piece(number):
        return swap(pieces[number], 1, number // PIECES)

    flying = [
        [send_piece(0), swap(mine_unit, 0, CORES), onward(mine_unit)],
        [send_piece(1), swap(core_unit, 0, CORES + 1), onward(core_unit, 1)],
    ]
    own_tokens, for_core = permuted([(0, 0, pairs), (1, 0, pairs)], [1], *pieces[2:])
    pieces += permuted([(3, n * rows, rows) for n in range(PIECES)], [0], own_tokens)
    from_core = swap(for_core, 0, 1)
    local_segments, *_ = tie(segments, *pieces[PIECES:])
    basis, order_back = pl.pallas_call(
        basis_kernel,
        out_shape=[
            jax.ShapeDtypeStruct((2 * tokens, SEG_DEV * 2 * rank), jnp.bfloat16),
            order_shape,
        ],
        in_specs=[VMEM] * 5,
        out_specs=[VMEM] * 2,
        compiler_params=pltpu.CompilerParams(vmem_limit_bytes=16 * MIB),
        cost_estimate=QUICK,
    )(
        hidden_in,
        in_proj,
        (local_segments - index * SEG_DEV).reshape(tokens, 1),
        flat_routes,
        routes.T,
    )

    call = functools.partial(
        accumulate, bases=bases, rank=rank, pairs=pairs, window=window, places=places
    )
    steps = 2 * slots
    core_step = min(4, steps - 1)
    units = [(mine_unit, 0), (other_unit, 1)]
    known_units = 0
    members = [0]
    starts = {0: own_starts}
    state, sent = None, []
    held = [own_tokens, basis, order_back]
    for event in [[0, 1], *[[n] for n in range(2, steps)]]:
        arrived, waiting = [], []
        for step in event:
            chain = step % 2
            piece, across, ahead = flying[chain]
            upcoming = [None, None, None]
            if ahead is not None:
                number = step + 2
                if number < 2 * PIECES:
                    pieces[number], piece, across, ahead, *held = tie(
                        pieces[number], piece, across, ahead, *held
                    )
                    upcoming[0] = send_piece(number)
                else:
                    across, ahead, *held = tie(across, ahead, *held)
                upcoming[1] = swap(ahead, 0, CORES)
                if step + 4 < steps:
                    upcoming[2] = onward(ahead)
            flying[chain] = upcoming
            units.append((across, known_units + len(units)))
            if ahead is not None:
                units.append((ahead, known_units + len(units)))
            if piece is not None:
                waiting.append((piece, step))
        if state is None:
            own_tokens, basis, order_back = held
            arrived.append((own_tokens, 0, pairs))
        else:
            state = held
        tasks = [("units", list(members), known_units, len(units))]
        known_units += len(units)
        if event[0] == core_step:
            starts[1] = starts_in(from_core, pairs)
            arrived.append((from_core, pairs, pairs))
            tasks.append(("units", [1], 0, known_units))
            members.append(1)
        for piece, number in waiting:
            g, part = 2 + number // PIECES, number % PIECES
            arrived.append((piece, g * pairs + part * rows, rows))
            if part == 0:
                starts[g] = starts_in(piece, rows)
                members.append(g)
            tasks.append(("piece", g, part * rows, (part + 1) * rows, 0, known_units))
        last = event[-1] + 1 == steps
        state, out = call(
            state,
            starts=starts,
            tokens=arrived,
            units=units,
            tasks=tasks,
            sends=[1, 2, 3] if last else [],
        )
        sent += out
        held = state
        units = []

    from_core = swap(sent[0], 0, 1)
    from_side = swap(sent[1], 1, 0)
    from_diagonal = swap(sent[2], 1, 1)
    return pl.pallas_call(
        functools.partial(blocks_kernel, tops, rank),
        out_shape=jax.ShapeDtypeStruct((SEG_DEV, experts, rank * rank), jnp.bfloat16),
        in_specs=[VMEM] * 7,
        out_specs=VMEM,
        scratch_shapes=[
            pltpu.VMEM((rank, pairs), jnp.float32),
            pltpu.VMEM((rank, experts, tokens), jnp.float32),
        ],
        compiler_params=pltpu.CompilerParams(vmem_limit_bytes=32 * MIB),
        cost_estimate=QUICK,
    )(routes.T, basis, order_back, state[2], from_core, from_side, from_diagonal)


def solution(mesh):
    placed = (
        P(("groups", "expert"), None),
        P(("groups", "expert"), None, None),
        P(("groups", "expert"), None),
        P(("groups", "expert")),
        P(),
        P("expert", None, None),
    )
    return jax.shard_map(
        local,
        mesh=mesh,
        in_specs=placed,
        out_specs=P(("groups", "expert"), None, None),
        check_vma=False,
    )
```

```python
import functools

import jax
import jax.numpy as jnp
import numpy as np
from jax import lax
from jax.experimental import pallas as pl
from jax.experimental.pallas import tpu as pltpu
from jax.sharding import PartitionSpec as P

SEG_DEV = 2
CORES = 2
SIDES = 2
QUAD = 4
PIECES = 4
LANES = 128
ALIGN = 16
DIGIT = 32
BOTH = ("groups", "expert")
MIB = 1024 * 1024
VMEM = pl.BlockSpec(memory_space=pltpu.VMEM)
SMEM = pl.BlockSpec(memory_space=pltpu.SMEM)
HBM = pl.BlockSpec(memory_space=pl.ANY)
QUICK = pl.CostEstimate(flops=1, bytes_accessed=1, transcendentals=0)
SHORT = pl.CostEstimate(flops=6 * 10**8, bytes_accessed=1, transcendentals=0)
NT = (((1,), (1,)), ((), ()))


def in_vmem(array):
    return pltpu.with_memory_space_constraint(array, pltpu.VMEM)


def in_hbm(array):
    return pltpu.with_memory_space_constraint(array, pltpu.HBM)


def place_in_quad(flip):
    side, core = lax.axis_index("groups") % SIDES, lax.axis_index("expert") % CORES
    return (side ^ (flip // CORES)) * CORES + (core ^ (flip % CORES))


def columns_of(flip, width):
    return pl.ds(pl.multiple_of(place_in_quad(flip) * width, width), width)


def row_of(routes):
    tops, tokens = routes.shape
    pairs = tops * tokens
    lane = lax.broadcasted_iota(jnp.int32, (tokens, pairs), 1)
    token = lax.broadcasted_iota(jnp.int32, (tokens, pairs), 0)
    spread = jnp.where(lane // tops == token, 1.0, 0.0).astype(jnp.bfloat16)
    values = routes.astype(jnp.float32).astype(jnp.bfloat16)
    every = jnp.dot(values, spread, preferred_element_type=jnp.float32)
    lane = lax.broadcasted_iota(jnp.int32, (tops, pairs), 1)
    k = lax.broadcasted_iota(jnp.int32, (tops, pairs), 0)
    return jnp.sum(jnp.where(lane % tops == k, every, 0.0), axis=0, keepdims=True).astype(jnp.int32)


def key_column(routes_row):
    count = routes_row.shape[1]
    keys = routes_row * count + lax.broadcasted_iota(jnp.int32, (1, count), 1)
    return jnp.broadcast_to(keys.astype(jnp.float32), (8, count)).T[:, 0:1]


def ranks(column, keys):
    total = jnp.zeros(keys.shape, jnp.float32)
    for first in range(0, column.shape[0], 128):
        smaller = jnp.where(column[first : first + 128] < keys, 1.0, 0.0)
        total = total + jnp.sum(smaller, axis=0, keepdims=True)
    return total


def sort_kernel(
    routes_ref,
    weight_ref,
    grads_ref,
    held_ref,
    mine_ref,
    core_ref,
    starts_ref,
    head_ref,
    order_ref,
    piece_ref,
    next_ref,
    stage,
    sems,
):
    width = mine_ref.shape[1]
    count = sems.shape[0] - 1
    part = grads_ref.shape[0] // count
    copies = [pltpu.make_async_copy(weight_ref, stage, sems.at[count])]
    for n in range(count):
        here = pl.ds(n * part, part)
        copies.append(pltpu.make_async_copy(grads_ref.at[here], held_ref.at[here], sems.at[n]))
    for copy in copies:
        copy.start()
    routes = row_of(routes_ref[...])
    pairs = routes.shape[1]
    column = key_column(routes)
    keys = routes * pairs + lax.broadcasted_iota(jnp.int32, (1, pairs), 1)
    place = ranks(column, keys.astype(jnp.float32)).astype(jnp.int32)
    firsts = lax.broadcasted_iota(jnp.int32, starts_ref.shape, 1) * pairs
    starts = ranks(column, firsts.astype(jnp.float32)).astype(jnp.int32)
    starts_ref[...] = starts
    wide = head_ref.shape[1] - starts.shape[1]
    digits = [starts // DIGIT, starts % DIGIT]
    digits = [jnp.pad(d.astype(jnp.float32), ((0, 0), (0, wide))) for d in digits]
    row = lax.broadcasted_iota(jnp.int32, head_ref.shape, 0)
    head = jnp.where(row == 0, digits[0], jnp.where(row == 1, digits[1], 0.0))
    head_ref[...] = head.astype(jnp.bfloat16)
    rows = next_ref.shape[0]
    for first in range(0, pairs, rows):
        ids = first + lax.broadcasted_iota(jnp.int32, (rows, pairs), 0)
        order_ref[first : first + rows, :] = jnp.where(place == ids, 1.0, 0.0).astype(jnp.bfloat16)
    copies[0].wait()
    mine_ref[...] = stage[:, columns_of(0, width)]
    core_ref[...] = stage[:, columns_of(1, width)]
    for copy in copies[1:]:
        copy.wait()
    sorted_rows = jnp.dot(
        order_ref[0 : 2 * rows, :],
        held_ref[:, :, columns_of(2, width)].reshape(pairs, width),
        preferred_element_type=jnp.float32,
    ).astype(jnp.bfloat16)
    piece_ref[0:rows, :] = sorted_rows[0:rows]
    piece_ref[rows:, :] = head_ref[...]
    next_ref[...] = sorted_rows[rows:]


def permute_kernel(plan, order_ref, head_ref, grads_ref, *outs):
    pairs, width = order_ref.shape[0], outs[0].shape[1]
    for device in sorted({device for device, _, _ in plan}):
        grads = grads_ref[:, :, columns_of(device, width)].reshape(pairs, width)
        for out, (target, first, rows) in zip(outs, plan):
            if target == device:
                out[0:rows, :] = jnp.dot(
                    order_ref[first : first + rows, :], grads, preferred_element_type=jnp.float32
                ).astype(jnp.bfloat16)
                if out.shape[0] > rows:
                    out[rows:, :] = head_ref[...]


def basis_kernel(
    hidden_ref, proj_ref, segment_ref, routes_ref, out_ref, order_ref
):
    projected = lax.dot_general(
        hidden_ref[...], proj_ref[...], NT, preferred_element_type=jnp.float32
    )
    zero = jnp.zeros_like(projected)
    picked = [jnp.where(segment_ref[...] == s, projected, zero) for s in range(SEG_DEV)]
    even = jnp.concatenate([b for p in picked for b in (p, zero)], axis=1)
    odd = jnp.concatenate([b for p in picked for b in (zero, p)], axis=1)
    out_ref[...] = jnp.concatenate([even, odd], axis=0).astype(out_ref.dtype)
    tops, tokens = routes_ref.shape
    pairs = tops * tokens
    column = key_column(row_of(routes_ref[...]))
    at = [
        routes_ref[k : k + 1, :] * pairs + lax.broadcasted_iota(jnp.int32, (1, tokens), 1) * tops + k
        for k in range(tops)
    ]
    place = ranks(column, jnp.concatenate(at, axis=1).astype(jnp.float32)).astype(jnp.int32)
    for first in range(0, pairs, 256):
        ids = first + lax.broadcasted_iota(jnp.int32, (256, pairs), 0)
        order_ref[first : first + 256, :] = jnp.where(place == ids, 1.0, 0.0).astype(jnp.bfloat16)


def packed(total, first, pairs, rank):
    half = pairs // 2
    low = lax.broadcasted_iota(jnp.int32, (half, LANES), 1) < rank
    one = total[first : first + half, :]
    two = total[first + half : first + pairs, :]
    return jnp.where(low, one + pltpu.roll(one, rank, 1), two + pltpu.roll(two, rank, 1))


def partial_kernel(
    rank, pairs, window, new_tokens, new_units, tasks, fresh, sends, groups, bases_ref, *refs
):
    start_refs = dict(zip(groups, refs))
    refs = refs[len(groups) :]
    token_refs, refs = refs[: len(new_tokens)], refs[len(new_tokens) :]
    unit_refs, refs = refs[: len(new_units)], refs[len(new_units) :]
    if fresh:
        tokens, units, total = refs
        send_refs = ()
        total[...] = jnp.zeros_like(total)
    else:
        tokens, units, total = refs[3:6]
        send_refs = refs[6:]
    for ref, (first, count) in zip(token_refs, new_tokens):
        tokens[first : first + count, :] = ref[0:count, :]
    for ref, place in zip(unit_refs, new_units):
        units[place] = ref[...]
    cols = units.shape[1]
    held = cols // rank
    per_tile = LANES // rank
    low = lax.broadcasted_iota(jnp.int32, (1, LANES), 1) < rank

    device = lax.axis_index("expert")

    def process(w, members):
        base = bases_ref[device, w]
        heres, offsets = [], []
        for g in members:
            at = jnp.minimum(start_refs[g][0, base] & -ALIGN, pairs - window)
            offsets.append(at)
            heres.append(pl.ds(pl.multiple_of(g * pairs + at, ALIGN), window))
        rows = [tokens[here, :] for here in heres]
        rows = jnp.concatenate(rows, axis=0) if len(rows) > 1 else rows[0]
        dense = lax.dot_general(rows, units[w], NT, preferred_element_type=jnp.float32)
        for n, g in enumerate(members):
            value = total[heres[n], :]
            number = offsets[n] + lax.broadcasted_iota(jnp.int32, (window, LANES), 0)
            for j in range(cols // LANES):
                edge = [start_refs[g][0, base + j * per_tile + i] for i in range(per_tile + 1)]
                inside = (number >= jnp.where(low, edge[0], edge[1])) & (
                    number < jnp.where(low, edge[1], edge[2])
                )
                part = dense[n * window : (n + 1) * window, j * LANES : (j + 1) * LANES]
                value = jnp.where(inside, part, value)
            total[heres[n], :] = value

    for task in tasks:
        if task[0] == "units":
            _, members, first_w, count = task

            def each(i, carry, members=members, first_w=first_w):
                process(first_w + i, members)
                return carry

        else:
            _, member, first_row, end_row, first_w, count = task

            def each(
                i, carry, member=member, first_row=first_row, end_row=end_row, first_w=first_w
            ):
                w = first_w + i
                base = bases_ref[device, w]
                touches = (start_refs[member][0, base] < end_row) & (
                    start_refs[member][0, base + held] > first_row
                )

                @pl.when(touches)
                def _():
                    process(w, [member])

                return carry

        lax.fori_loop(0, count, each, 0)
    for ref, g in zip(send_refs, sends):
        ref[...] = packed(total, g * pairs, pairs, rank).astype(ref.dtype)


def accumulate(
    state, bases, starts, tokens, units, tasks, rank, pairs, window, places=0, sends=()
):
    fresh = state is None
    operands = [bases, *starts.values(), *[a for a, _, _ in tokens], *[a for a, _ in units]]
    specs = [SMEM] * (1 + len(starts)) + [VMEM] * (len(tokens) + len(units))
    if fresh:
        width = units[0][0].shape[1]
        shapes = [
            pltpu.VMEM((QUAD * pairs, width), jnp.bfloat16),
            pltpu.VMEM((places, *units[0][0].shape), jnp.bfloat16),
            pltpu.VMEM((QUAD * pairs, LANES), jnp.float32),
        ]
        aliases = {}
    else:
        aliases = {len(operands) + i: i for i in range(3)}
        operands += [in_vmem(a) for a in state]
        specs += [VMEM] * 3
        shapes = [pltpu.VMEM(a.shape, a.dtype) for a in state]
    shapes += [pltpu.VMEM((pairs // 2, LANES), jnp.bfloat16)] * len(sends)
    out = pl.pallas_call(
        functools.partial(
            partial_kernel,
            rank,
            pairs,
            window,
            [(first, count) for _, first, count in tokens],
            [p for _, p in units],
            tasks,
            fresh,
            sends,
            list(starts),
        ),
        out_shape=shapes,
        in_specs=specs,
        out_specs=[VMEM] * len(shapes),
        input_output_aliases=aliases,
        compiler_params=pltpu.CompilerParams(vmem_limit_bytes=16 * MIB),
        cost_estimate=SHORT,
    )(*operands)
    return list(out[:3]), list(out[3:])


def blocks_kernel(
    tops, rank, routes_ref, basis_ref, order_ref, total_ref, b_ref, c_ref, d_ref, out_ref, turned, spread
):
    half = b_ref.shape[0]
    tokens = 2 * half // tops
    value = packed(total_ref, 0, 2 * half, rank)
    for ref in (b_ref, c_ref, d_ref):
        value = value + ref[...].astype(jnp.float32)
    value = value.T
    value = jnp.concatenate([value[0:rank], value[rank : 2 * rank]], axis=1).astype(jnp.bfloat16)
    turned[...] = jnp.dot(value, order_ref[...], preferred_element_type=jnp.float32)
    experts = out_ref.shape[1]

    def expand(tile, carry):
        first = pl.multiple_of(tile * 8, 8)
        ids = first + lax.broadcasted_iota(jnp.int32, (8, tokens), 0)
        masks = [routes_ref[k : k + 1, :] == ids for k in range(tops)]
        for r in range(rank):
            value = jnp.zeros((8, tokens), jnp.float32)
            for k in range(tops):
                row = turned[r : r + 1, k * tokens : (k + 1) * tokens]
                value = jnp.where(masks[k], row, value)
            spread[r, pl.ds(first, 8), :] = value
        return carry

    lax.fori_loop(0, experts // 8, expand, 0)
    for pair in range(rank // 2):
        both = jnp.concatenate([spread[2 * pair], spread[2 * pair + 1]], axis=1)
        block = jnp.dot(
            both.astype(jnp.bfloat16), basis_ref[...], preferred_element_type=jnp.float32
        ).astype(jnp.bfloat16)
        for s in range(SEG_DEV):
            out_ref[s, :, pl.ds(pair * 2 * rank, 2 * rank)] = block[
                :, s * 2 * rank : (s + 1) * 2 * rank
            ]


def local(hidden_in, out_grads, routes, segments, in_proj, out_proj):
    tokens, tops = routes.shape
    exp_here, rank, width = out_proj.shape
    owners, groups = lax.axis_size("expert"), lax.axis_size("groups")
    experts = exp_here * owners
    pairs = tokens * tops
    capacity = max(2, 3 * pairs // (2 * experts))
    window = min(pairs, -(-(exp_here * capacity + ALIGN - 1) // ALIGN) * ALIGN)
    quarter = width // QUAD
    cols = exp_here * rank
    rows = pairs // PIECES
    index = lax.axis_index("expert")
    slots = owners // CORES // 2
    ring = [0, *range(1, slots, 2), *range((slots - 1) // 2 * 2, 0, -2)]
    following = {a: b for a, b in zip(ring, ring[1:] + ring[:1])}
    before = {b: a for a, b in following.items()}

    def swap(array, side, bit):
        table = [
            (g * owners + e, (g ^ side) * owners + (e ^ bit))
            for g in range(groups)
            for e in range(owners)
        ]
        return lax.ppermute(array, BOTH, table)

    def onward(array, bit=0):
        wide = 2 * CORES
        table = [(e, following[e // wide] * wide + (e % wide ^ bit)) for e in range(owners)]
        return lax.ppermute(array, "expert", table)

    def tie(*arrays):
        return lax.optimization_barrier(arrays)

    rows_of = []
    for e in range(owners):
        z, y, c = e // (2 * CORES), e // CORES % 2, e % CORES
        named = [(z, y, c), (z, y, 1 - c)]
        here = z
        for slot in range(slots):
            after = before[here]
            for flip in (0, 1):
                named.append((here, 1 - y, c ^ flip))
                if slot + 1 < slots:
                    named.append((after, y, c ^ flip))
            here = after
        rows_of.append([((a * 2 + b) * CORES + d) * exp_here for a, b, d in named])
    places = len(rows_of[0])
    bases = jnp.asarray(np.array(rows_of, np.int32))

    unit_shape = pltpu.VMEM((cols, quarter), jnp.bfloat16)
    order_shape = pltpu.VMEM((pairs, pairs), jnp.bfloat16)

    def rows_shape(count):
        return pltpu.VMEM((count, quarter), jnp.bfloat16)

    by_rank = routes.T
    edges = -(-(experts + 1) // LANES) * LANES
    held_grads, mine_unit, core_unit, own_starts, head, order, *first_pieces = pl.pallas_call(
        sort_kernel,
        out_shape=[
            pltpu.VMEM(out_grads.shape, jnp.bfloat16),
            unit_shape,
            unit_shape,
            jax.ShapeDtypeStruct((1, edges), jnp.int32),
            rows_shape(ALIGN),
            order_shape,
            rows_shape(rows + ALIGN),
            rows_shape(rows),
        ],
        in_specs=[VMEM, HBM, HBM],
        out_specs=[VMEM] * 8,
        scratch_shapes=[
            pltpu.VMEM((cols, width), jnp.bfloat16),
            pltpu.SemaphoreType.DMA((9,)),
        ],
        compiler_params=pltpu.CompilerParams(vmem_limit_bytes=24 * MIB),
        cost_estimate=QUICK,
    )(by_rank, in_hbm(out_proj.reshape(cols, width)), in_hbm(out_grads))

    def permuted(plan, headed, *after):
        held, *_ = tie(order, *after)
        return pl.pallas_call(
            functools.partial(permute_kernel, plan),
            out_shape=[
                rows_shape(many + (ALIGN if n in headed else 0))
                for n, (_, _, many) in enumerate(plan)
            ],
            in_specs=[VMEM] * 3,
            out_specs=[VMEM] * len(plan),
            compiler_params=pltpu.CompilerParams(vmem_limit_bytes=24 * MIB),
            cost_estimate=QUICK,
        )(in_vmem(held), head, in_vmem(held_grads))

    def starts_in(block, count):
        digits = block[count : count + 2, :edges].astype(jnp.int32)
        return (digits[0] * DIGIT + digits[1]).reshape(1, edges)

    other_unit = swap(core_unit, 0, 1)
    pieces = [
        *first_pieces,
        *permuted([(2, n * rows, rows) for n in range(2, PIECES)], [], other_unit),
    ]

    def send_piece(number):
        return swap(pieces[number], 1, number // PIECES)

    flying = [
        [send_piece(0), swap(mine_unit, 0, CORES), onward(mine_unit)],
        [send_piece(1), swap(core_unit, 0, CORES + 1), onward(core_unit, 1)],
    ]
    own_tokens, for_core = permuted([(0, 0, pairs), (1, 0, pairs)], [1], *pieces[2:])
    pieces += permuted([(3, n * rows, rows) for n in range(PIECES)], [0], own_tokens)
    from_core = swap(for_core, 0, 1)
    local_segments, *_ = tie(segments, *pieces[PIECES:])
    basis, order_back = pl.pallas_call(
        basis_kernel,
        out_shape=[
            pltpu.VMEM((2 * tokens, SEG_DEV * 2 * rank), jnp.bfloat16),
            order_shape,
        ],
        in_specs=[VMEM] * 4,
        out_specs=[VMEM] * 2,
        compiler_params=pltpu.CompilerParams(vmem_limit_bytes=16 * MIB),
        cost_estimate=QUICK,
    )(
        hidden_in,
        in_proj,
        (local_segments - index * SEG_DEV).reshape(tokens, 1),
        by_rank,
    )

    call = functools.partial(
        accumulate, bases=bases, rank=rank, pairs=pairs, window=window, places=places
    )
    steps = 2 * slots
    core_step = min(4, steps - 1)
    units = [(mine_unit, 0), (other_unit, 1)]
    known_units = 0
    members = [0]
    starts = {0: own_starts}
    state, sent = None, []
    held = [own_tokens, basis, order_back]
    for event in [[0, 1], *[[n] for n in range(2, steps)]]:
        arrived, waiting = [], []
        for step in event:
            chain = step % 2
            piece, across, ahead = flying[chain]
            upcoming = [None, None, None]
            if ahead is not None:
                number = step + 2
                if number < 2 * PIECES:
                    pieces[number], piece, across, ahead, *held = tie(
                        pieces[number], piece, across, ahead, *held
                    )
                    upcoming[0] = send_piece(number)
                else:
                    across, ahead, *held = tie(across, ahead, *held)
                upcoming[1] = swap(ahead, 0, CORES)
                if step + 4 < steps:
                    upcoming[2] = onward(ahead)
            flying[chain] = upcoming
            units.append((across, known_units + len(units)))
            if ahead is not None:
                units.append((ahead, known_units + len(units)))
            if piece is not None:
                waiting.append((piece, step))
        if state is None:
            own_tokens, basis, order_back = held
            arrived.append((own_tokens, 0, pairs))
        else:
            state = held
        tasks = [("units", list(members), known_units, len(units))]
        known_units += len(units)
        if event[0] == core_step:
            starts[1] = starts_in(from_core, pairs)
            arrived.append((from_core, pairs, pairs))
            tasks.append(("units", [1], 0, known_units))
            members.append(1)
        for piece, number in waiting:
            g, part = 2 + number // PIECES, number % PIECES
            arrived.append((piece, g * pairs + part * rows, rows))
            if part == 0:
                starts[g] = starts_in(piece, rows)
                members.append(g)
            tasks.append(("piece", g, part * rows, (part + 1) * rows, 0, known_units))
        last = event[-1] + 1 == steps
        state, out = call(
            state,
            starts=starts,
            tokens=arrived,
            units=units,
            tasks=tasks,
            sends=[1, 2, 3] if last else [],
        )
        sent += out
        held = state
        units = []

    from_core = swap(sent[0], 0, 1)
    from_side = swap(sent[1], 1, 0)
    from_diagonal = swap(sent[2], 1, 1)
    return pl.pallas_call(
        functools.partial(blocks_kernel, tops, rank),
        out_shape=jax.ShapeDtypeStruct((SEG_DEV, experts, rank * rank), jnp.bfloat16),
        in_specs=[VMEM] * 7,
        out_specs=VMEM,
        scratch_shapes=[
            pltpu.VMEM((rank, pairs), jnp.float32),
            pltpu.VMEM((rank, experts, tokens), jnp.float32),
        ],
        compiler_params=pltpu.CompilerParams(vmem_limit_bytes=32 * MIB),
        cost_estimate=QUICK,
    )(by_rank, basis, in_vmem(order_back), in_vmem(state[2]), from_core, from_side, from_diagonal)


def solution(mesh):
    placed = (
        P(("groups", "expert"), None),
        P(("groups", "expert"), None, None),
        P(("groups", "expert"), None),
        P(("groups", "expert")),
        P(),
        P("expert", None, None),
    )
    return jax.shard_map(
        local,
        mesh=mesh,
        in_specs=placed,
        out_specs=P(("groups", "expert"), None, None),
        check_vma=False,
    )
```

```python
import functools

import jax
import jax.numpy as jnp
import numpy as np
from jax import lax
from jax.experimental import pallas as pl
from jax.experimental.pallas import tpu as pltpu
from jax.sharding import PartitionSpec as P

SEG_DEV = 2
CORES = 2
SIDES = 2
QUAD = 4
PIECES = 4
LANES = 128
ALIGN = 16
DIGIT = 32
BOTH = ("groups", "expert")
MIB = 1024 * 1024
VMEM = pl.BlockSpec(memory_space=pltpu.VMEM)
SMEM = pl.BlockSpec(memory_space=pltpu.SMEM)
HBM = pl.BlockSpec(memory_space=pl.ANY)
QUICK = pl.CostEstimate(flops=1, bytes_accessed=1, transcendentals=0)
SHORT = pl.CostEstimate(flops=10**9, bytes_accessed=1, transcendentals=0)
NT = (((1,), (1,)), ((), ()))


def in_vmem(array):
    return pltpu.with_memory_space_constraint(array, pltpu.VMEM)


def in_hbm(array):
    return pltpu.with_memory_space_constraint(array, pltpu.HBM)


def place_in_quad(flip):
    side, core = lax.axis_index("groups") % SIDES, lax.axis_index("expert") % CORES
    return (side ^ (flip // CORES)) * CORES + (core ^ (flip % CORES))


def columns_of(flip, width):
    return pl.ds(pl.multiple_of(place_in_quad(flip) * width, width), width)


def row_of(routes):
    tops, tokens = routes.shape
    pairs = tops * tokens
    lane = lax.broadcasted_iota(jnp.int32, (tokens, pairs), 1)
    token = lax.broadcasted_iota(jnp.int32, (tokens, pairs), 0)
    spread = jnp.where(lane // tops == token, 1.0, 0.0).astype(jnp.bfloat16)
    values = routes.astype(jnp.float32).astype(jnp.bfloat16)
    every = jnp.dot(values, spread, preferred_element_type=jnp.float32)
    lane = lax.broadcasted_iota(jnp.int32, (tops, pairs), 1)
    k = lax.broadcasted_iota(jnp.int32, (tops, pairs), 0)
    return jnp.sum(jnp.where(lane % tops == k, every, 0.0), axis=0, keepdims=True).astype(jnp.int32)


def key_column(routes_row):
    count = routes_row.shape[1]
    keys = routes_row * count + lax.broadcasted_iota(jnp.int32, (1, count), 1)
    return jnp.broadcast_to(keys.astype(jnp.float32), (8, count)).T[:, 0:1]


def ranks(column, keys):
    total = jnp.zeros(keys.shape, jnp.float32)
    for first in range(0, column.shape[0], 128):
        smaller = jnp.where(column[first : first + 128] < keys, 1.0, 0.0)
        total = total + jnp.sum(smaller, axis=0, keepdims=True)
    return total


def sort_kernel(
    routes_ref,
    weight_ref,
    grads_ref,
    held_ref,
    mine_ref,
    core_ref,
    starts_ref,
    head_ref,
    order_ref,
    piece_ref,
    stage,
    sems,
):
    width = mine_ref.shape[1]
    count = sems.shape[0] - 1
    part = grads_ref.shape[0] // count
    copies = [pltpu.make_async_copy(weight_ref, stage, sems.at[count])]
    for n in range(count):
        here = pl.ds(n * part, part)
        copies.append(pltpu.make_async_copy(grads_ref.at[here], held_ref.at[here], sems.at[n]))
    for copy in copies:
        copy.start()
    routes = row_of(routes_ref[...])
    pairs = routes.shape[1]
    column = key_column(routes)
    keys = routes * pairs + lax.broadcasted_iota(jnp.int32, (1, pairs), 1)
    place = ranks(column, keys.astype(jnp.float32)).astype(jnp.int32)
    firsts = lax.broadcasted_iota(jnp.int32, starts_ref.shape, 1) * pairs
    starts = ranks(column, firsts.astype(jnp.float32)).astype(jnp.int32)
    starts_ref[...] = starts
    wide = head_ref.shape[1] - starts.shape[1]
    digits = [starts // DIGIT, starts % DIGIT]
    digits = [jnp.pad(d.astype(jnp.float32), ((0, 0), (0, wide))) for d in digits]
    row = lax.broadcasted_iota(jnp.int32, head_ref.shape, 0)
    head = jnp.where(row == 0, digits[0], jnp.where(row == 1, digits[1], 0.0))
    head_ref[...] = head.astype(jnp.bfloat16)
    rows = piece_ref.shape[0] - ALIGN
    for first in range(0, pairs, rows):
        ids = first + lax.broadcasted_iota(jnp.int32, (rows, pairs), 0)
        order_ref[first : first + rows, :] = jnp.where(place == ids, 1.0, 0.0).astype(jnp.bfloat16)
    copies[0].wait()
    mine_ref[...] = stage[:, columns_of(0, width)]
    core_ref[...] = stage[:, columns_of(1, width)]
    for copy in copies[1:]:
        copy.wait()
    piece_ref[0:rows, :] = jnp.dot(
        order_ref[0:rows, :],
        held_ref[:, :, columns_of(2, width)].reshape(pairs, width),
        preferred_element_type=jnp.float32,
    ).astype(jnp.bfloat16)
    piece_ref[rows:, :] = head_ref[...]


def join_kernel(one_ref, two_ref, out_ref):
    half = one_ref.shape[0]
    out_ref[0:half, :] = one_ref[...]
    out_ref[half:, :] = two_ref[...]


def permute_kernel(plan, order_ref, head_ref, grads_ref, *outs):
    pairs, width = order_ref.shape[0], outs[0].shape[1]
    for device in sorted({device for device, _, _ in plan}):
        grads = grads_ref[:, :, columns_of(device, width)].reshape(pairs, width)
        for out, (target, first, rows) in zip(outs, plan):
            if target == device:
                out[0:rows, :] = jnp.dot(
                    order_ref[first : first + rows, :], grads, preferred_element_type=jnp.float32
                ).astype(jnp.bfloat16)
                if out.shape[0] > rows:
                    out[rows:, :] = head_ref[...]


def basis_kernel(
    hidden_ref, proj_ref, segment_ref, routes_ref, out_ref, order_ref, hidden, proj, sems
):
    count = sems.shape[0] - 1
    part = hidden.shape[0] // count
    copies = [pltpu.make_async_copy(proj_ref, proj, sems.at[count])]
    for n in range(count):
        here = pl.ds(n * part, part)
        copies.append(pltpu.make_async_copy(hidden_ref.at[here], hidden.at[here], sems.at[n]))
    for copy in copies:
        copy.start()
    tops, tokens = routes_ref.shape
    pairs = tops * tokens
    column = key_column(row_of(routes_ref[...]))
    at = [
        routes_ref[k : k + 1, :] * pairs + lax.broadcasted_iota(jnp.int32, (1, tokens), 1) * tops + k
        for k in range(tops)
    ]
    place = ranks(column, jnp.concatenate(at, axis=1).astype(jnp.float32)).astype(jnp.int32)
    for first in range(0, pairs, 256):
        ids = first + lax.broadcasted_iota(jnp.int32, (256, pairs), 0)
        order_ref[first : first + 256, :] = jnp.where(place == ids, 1.0, 0.0).astype(jnp.bfloat16)
    segment = (segment_ref[...] - lax.axis_index("expert") * SEG_DEV).astype(jnp.float32)
    segment = jnp.broadcast_to(segment, (8, tokens)).T[:, 0:1]
    for copy in copies:
        copy.wait()
    projected = lax.dot_general(hidden[...], proj[...], NT, preferred_element_type=jnp.float32)
    zero = jnp.zeros_like(projected)
    picked = [jnp.where(segment == float(s), projected, zero) for s in range(SEG_DEV)]
    even = jnp.concatenate([b for p in picked for b in (p, zero)], axis=1)
    odd = jnp.concatenate([b for p in picked for b in (zero, p)], axis=1)
    out_ref[...] = jnp.concatenate([even, odd], axis=0).astype(out_ref.dtype)


def packed(total, first, pairs, rank):
    half = pairs // 2
    low = lax.broadcasted_iota(jnp.int32, (half, LANES), 1) < rank
    one = total[first : first + half, :]
    two = total[first + half : first + pairs, :]
    return jnp.where(low, one + pltpu.roll(one, rank, 1), two + pltpu.roll(two, rank, 1))


def partial_kernel(
    rank, pairs, window, new_tokens, new_units, tasks, fresh, sends, groups, bases_ref, *refs
):
    start_refs = dict(zip(groups, refs))
    refs = refs[len(groups) :]
    token_refs, refs = refs[: len(new_tokens)], refs[len(new_tokens) :]
    unit_refs, refs = refs[: len(new_units)], refs[len(new_units) :]
    if fresh:
        tokens, units, total = refs
        send_refs = ()
        total[...] = jnp.zeros_like(total)
    else:
        tokens, units, total = refs[3:6]
        send_refs = refs[6:]
    for ref, (first, count) in zip(token_refs, new_tokens):
        tokens[first : first + count, :] = ref[0:count, :]
    cols = units.shape[1]
    for ref, place in zip(unit_refs, new_units):
        for half in range(CORES):
            units[place + half] = ref[half * cols : (half + 1) * cols, :]
    held = cols // rank
    per_tile = LANES // rank
    low = lax.broadcasted_iota(jnp.int32, (1, LANES), 1) < rank

    device = lax.axis_index("expert")

    def process(w, members):
        base = bases_ref[device, w]
        heres, offsets = [], []
        for g in members:
            at = jnp.minimum(start_refs[g][0, base] & -ALIGN, pairs - window)
            offsets.append(at)
            heres.append(pl.ds(pl.multiple_of(g * pairs + at, ALIGN), window))
        rows = [tokens[here, :] for here in heres]
        rows = jnp.concatenate(rows, axis=0) if len(rows) > 1 else rows[0]
        dense = lax.dot_general(rows, units[w], NT, preferred_element_type=jnp.float32)
        for n, g in enumerate(members):
            value = total[heres[n], :]
            number = offsets[n] + lax.broadcasted_iota(jnp.int32, (window, LANES), 0)
            for j in range(cols // LANES):
                edge = [start_refs[g][0, base + j * per_tile + i] for i in range(per_tile + 1)]
                inside = (number >= jnp.where(low, edge[0], edge[1])) & (
                    number < jnp.where(low, edge[1], edge[2])
                )
                part = dense[n * window : (n + 1) * window, j * LANES : (j + 1) * LANES]
                value = jnp.where(inside, part, value)
            total[heres[n], :] = value

    for task in tasks:
        if task[0] == "units":
            _, members, first_w, count = task

            def each(i, carry, members=members, first_w=first_w):
                process(first_w + i, members)
                return carry

        else:
            _, member, first_row, end_row, first_w, count = task

            def each(
                i, carry, member=member, first_row=first_row, end_row=end_row, first_w=first_w
            ):
                w = first_w + i
                base = bases_ref[device, w]
                touches = (start_refs[member][0, base] < end_row) & (
                    start_refs[member][0, base + held] > first_row
                )

                @pl.when(touches)
                def _():
                    process(w, [member])

                return carry

        lax.fori_loop(0, count, each, 0)
    for ref, g in zip(send_refs, sends):
        ref[...] = packed(total, g * pairs, pairs, rank).astype(ref.dtype)


def accumulate(
    state, bases, starts, tokens, units, tasks, rank, pairs, window, places=0, sends=(), cost=QUICK
):
    fresh = state is None
    operands = [bases, *starts.values(), *[a for a, _, _ in tokens], *[a for a, _ in units]]
    specs = [SMEM] * (1 + len(starts)) + [VMEM] * (len(tokens) + len(units))
    if fresh:
        width = units[0][0].shape[1]
        shapes = [
            pltpu.VMEM((QUAD * pairs, width), jnp.bfloat16),
            pltpu.VMEM((places, units[0][0].shape[0] // CORES, width), jnp.bfloat16),
            pltpu.VMEM((QUAD * pairs, LANES), jnp.float32),
        ]
        aliases = {}
    else:
        aliases = {len(operands) + i: i for i in range(3)}
        operands += [in_vmem(a) for a in state]
        specs += [VMEM] * 3
        shapes = [pltpu.VMEM(a.shape, a.dtype) for a in state]
    shapes += [pltpu.VMEM((pairs // 2, LANES), jnp.bfloat16)] * len(sends)
    out = pl.pallas_call(
        functools.partial(
            partial_kernel,
            rank,
            pairs,
            window,
            [(first, count) for _, first, count in tokens],
            [p for _, p in units],
            tasks,
            fresh,
            sends,
            list(starts),
        ),
        out_shape=shapes,
        in_specs=specs,
        out_specs=[VMEM] * len(shapes),
        input_output_aliases=aliases,
        compiler_params=pltpu.CompilerParams(vmem_limit_bytes=8 * MIB),
        cost_estimate=cost,
    )(*operands)
    return list(out[:3]), list(out[3:])


def blocks_kernel(
    tops, rank, routes_ref, basis_ref, order_ref, total_ref, b_ref, c_ref, d_ref, out_ref, turned, spread
):
    half = b_ref.shape[0]
    tokens = 2 * half // tops
    value = packed(total_ref, 0, 2 * half, rank)
    for ref in (b_ref, c_ref, d_ref):
        value = value + ref[...].astype(jnp.float32)
    value = value.T
    value = jnp.concatenate([value[0:rank], value[rank : 2 * rank]], axis=1).astype(jnp.bfloat16)
    turned[...] = jnp.dot(value, order_ref[...], preferred_element_type=jnp.float32)
    experts = out_ref.shape[1]

    def expand(tile, carry):
        first = pl.multiple_of(tile * 8, 8)
        ids = first + lax.broadcasted_iota(jnp.int32, (8, tokens), 0)
        masks = [routes_ref[k : k + 1, :] == ids for k in range(tops)]
        for r in range(rank):
            value = jnp.zeros((8, tokens), jnp.float32)
            for k in range(tops):
                row = turned[r : r + 1, k * tokens : (k + 1) * tokens]
                value = jnp.where(masks[k], row, value)
            spread[r, pl.ds(first, 8), :] = value
        return carry

    lax.fori_loop(0, experts // 8, expand, 0)
    for pair in range(rank // 2):
        both = jnp.concatenate([spread[2 * pair], spread[2 * pair + 1]], axis=1)
        block = jnp.dot(
            both.astype(jnp.bfloat16), basis_ref[...], preferred_element_type=jnp.float32
        ).astype(jnp.bfloat16)
        for s in range(SEG_DEV):
            out_ref[s, :, pl.ds(pair * 2 * rank, 2 * rank)] = block[
                :, s * 2 * rank : (s + 1) * 2 * rank
            ]


def local(hidden_in, out_grads, routes, segments, in_proj, out_proj):
    tokens, tops = routes.shape
    exp_here, rank, width = out_proj.shape
    owners, groups = lax.axis_size("expert"), lax.axis_size("groups")
    experts = exp_here * owners
    pairs = tokens * tops
    capacity = max(2, 3 * pairs // (2 * experts))
    window = min(pairs, -(-(exp_here * capacity + ALIGN - 1) // ALIGN) * ALIGN)
    quarter = width // QUAD
    cols = exp_here * rank
    rows = pairs // PIECES
    index = lax.axis_index("expert")
    slots = owners // CORES // 2
    ring = [0, *range(1, slots, 2), *range((slots - 1) // 2 * 2, 0, -2)]
    following = {a: b for a, b in zip(ring, ring[1:] + ring[:1])}
    before = {b: a for a, b in following.items()}

    def swap(array, side, bit):
        table = [
            (g * owners + e, (g ^ side) * owners + (e ^ bit))
            for g in range(groups)
            for e in range(owners)
        ]
        return lax.ppermute(array, BOTH, table)

    def along(array, table):
        wide = 2 * CORES
        pairs_of = [(e, table[e // wide] * wide + e % wide) for e in range(owners)]
        return lax.ppermute(array, "expert", pairs_of)

    def tie(*arrays):
        return lax.optimization_barrier(arrays)

    ahead, back = slots // 2, (slots - 1) // 2
    landing = [0]
    for n in range(1, ahead + 1):
        landing += [n] + ([-n] if n <= back else [])
    known_first = [(n, 0) for n in landing[:-1]] + [(n, 1) for n in landing[:-2]]
    known_next = [(landing[-1], 0), (landing[-2], 1)]
    arrival = known_first + known_next + [(landing[-1], 1)]

    def source(z, n):
        for _ in range(abs(n)):
            z = before[z] if n > 0 else following[z]
        return z

    rows_of = [
        [
            ((source(e // (2 * CORES), n) * 2 + (e // CORES % 2 ^ crossed)) * CORES + (e % CORES ^ flip))
            * exp_here
            for n, crossed in arrival
            for flip in (0, 1)
        ]
        for e in range(owners)
    ]
    places = len(rows_of[0])
    bases = jnp.asarray(np.array(rows_of, np.int32))

    unit_shape = pltpu.VMEM((cols, quarter), jnp.bfloat16)
    order_shape = pltpu.VMEM((pairs, pairs), jnp.bfloat16)

    def rows_shape(count):
        return pltpu.VMEM((count, quarter), jnp.bfloat16)

    by_rank = routes.T
    edges = -(-(experts + 1) // LANES) * LANES
    held_grads, mine_unit, core_unit, own_starts, head, order, first_piece = pl.pallas_call(
        sort_kernel,
        out_shape=[
            pltpu.VMEM(out_grads.shape, jnp.bfloat16),
            unit_shape,
            unit_shape,
            jax.ShapeDtypeStruct((1, edges), jnp.int32),
            rows_shape(ALIGN),
            order_shape,
            rows_shape(2 * rows + ALIGN),
        ],
        in_specs=[VMEM, HBM, HBM],
        out_specs=[VMEM] * 7,
        scratch_shapes=[
            pltpu.VMEM((cols, width), jnp.bfloat16),
            pltpu.SemaphoreType.DMA((9,)),
        ],
        compiler_params=pltpu.CompilerParams(vmem_limit_bytes=12 * MIB),
        cost_estimate=QUICK,
    )(by_rank, in_hbm(out_proj.reshape(cols, width)), in_hbm(out_grads))

    def permuted(plan, headed, *after):
        held, *_ = tie(order, *after)
        return pl.pallas_call(
            functools.partial(permute_kernel, plan),
            out_shape=[
                rows_shape(many + (ALIGN if n in headed else 0))
                for n, (_, _, many) in enumerate(plan)
            ],
            in_specs=[VMEM] * 3,
            out_specs=[VMEM] * len(plan),
            compiler_params=pltpu.CompilerParams(vmem_limit_bytes=12 * MIB),
            cost_estimate=QUICK,
        )(in_vmem(held), head, in_vmem(held_grads))

    def starts_in(block, count):
        digits = block[count : count + 2, :edges].astype(jnp.int32)
        return (digits[0] * DIGIT + digits[1]).reshape(1, edges)

    side_pieces = [swap(first_piece, 1, 0)]
    other_unit = swap(core_unit, 0, 1)
    unit = pl.pallas_call(
        join_kernel,
        out_shape=pltpu.VMEM((CORES * cols, quarter), jnp.bfloat16),
        in_specs=[VMEM] * 2,
        out_specs=VMEM,
        compiler_params=pltpu.CompilerParams(vmem_limit_bytes=4 * MIB),
        cost_estimate=QUICK,
    )(mine_unit, other_unit)
    (second_piece,) = permuted([(2, 2 * rows, 2 * rows)], [], unit)
    own_tokens, *for_core = permuted(
        [(0, 0, pairs), (1, 0, 2 * rows), (1, 2 * rows, 2 * rows)], [1], second_piece
    )
    third_piece, last_piece = permuted(
        [(3, 0, 3 * rows), (3, 3 * rows, rows)], [0], own_tokens
    )
    from_core = [swap(piece, 0, 1) for piece in for_core]
    side_pieces.append(swap(second_piece, 1, 0))
    diagonal_pieces = [swap(third_piece, 1, 1), swap(last_piece, 1, 1)]
    local_segments, *_ = tie(segments, last_piece)
    basis, order_back = pl.pallas_call(
        basis_kernel,
        out_shape=[
            pltpu.VMEM((2 * tokens, SEG_DEV * 2 * rank), jnp.bfloat16),
            order_shape,
        ],
        in_specs=[HBM, HBM, VMEM, VMEM],
        out_specs=[VMEM] * 2,
        scratch_shapes=[
            pltpu.VMEM(hidden_in.shape, jnp.bfloat16),
            pltpu.VMEM(in_proj.shape, jnp.bfloat16),
            pltpu.SemaphoreType.DMA((5,)),
        ],
        compiler_params=pltpu.CompilerParams(vmem_limit_bytes=12 * MIB),
        cost_estimate=QUICK,
    )(in_hbm(hidden_in), in_hbm(in_proj), local_segments.reshape(1, tokens), by_rank)

    call = functools.partial(
        accumulate, bases=bases, rank=rank, pairs=pairs, window=window, places=places
    )
    place_of = {name: CORES * n for n, name in enumerate(arrival)}
    held = {(0, 0): unit}
    crossings = []
    state = None

    def cross(name):
        held[name, 1] = swap(held[name, 0], 0, CORES)
        crossings.append((name, 1))

    held[1, 0] = along(unit, following)
    cross(0)
    if back:
        held[-1, 0] = along(unit, before)
    for name in landing[1:]:
        final = name == landing[-1]
        if final:
            state, _ = call(
                None,
                starts={0: own_starts, 2: starts_in(side_pieces[0], 2 * rows)},
                tokens=[
                    (own_tokens, 0, pairs),
                    (side_pieces[0], 2 * pairs, 2 * rows),
                    (side_pieces[1], 2 * pairs + 2 * rows, 2 * rows),
                ],
                units=[(held[n], place_of[n]) for n in known_first],
                tasks=[("units", [0, 2], 0, CORES * len(known_first))],
                cost=SHORT,
            )
            old = crossings[-1:]
        else:
            old = crossings[-2:-1]
        if old and state is None:
            side_pieces[0], *old_units = tie(side_pieces[0], *[held[n] for n in old])
            held.update(zip(old, old_units))
        tied = tie(held[name, 0], *[held[n] for n in old], *(state or []), basis, order_back)
        held[name, 0], *tied = tied
        for n in old:
            held[n], *tied = tied
        if state is not None:
            state, tied = tied[:3], tied[3:]
        basis, order_back = tied
        cross(name)
        if name > 0 and name < ahead:
            held[name + 1, 0] = along(held[name, 0], following)
        if name < 0 and -name < back:
            held[name - 1, 0] = along(held[name, 0], before)

    starts = {
        0: own_starts,
        1: starts_in(from_core[0], 2 * rows),
        2: starts_in(side_pieces[0], 2 * rows),
    }
    first = CORES * len(known_first)
    state, _ = call(
        state,
        starts=starts,
        tokens=[
            (from_core[0], pairs, 2 * rows),
            (from_core[1], pairs + 2 * rows, 2 * rows),
        ],
        units=[(held[n], place_of[n]) for n in known_next],
        tasks=[
            ("units", [0, 2], first, CORES * len(known_next)),
            ("units", [1], 0, first + CORES * len(known_next)),
        ],
    )
    starts[3] = starts_in(diagonal_pieces[0], 3 * rows)
    state, _ = call(
        state,
        starts=starts,
        tokens=[(diagonal_pieces[0], 3 * pairs, 3 * rows)],
        units=[],
        tasks=[("piece", 3, 0, 3 * rows, 0, places - CORES)],
    )
    state, sent = call(
        state,
        starts=starts,
        tokens=[(diagonal_pieces[1], 3 * pairs + 3 * rows, rows)],
        units=[(held[arrival[-1]], places - CORES)],
        tasks=[
            ("units", [0, 1, 2, 3], places - CORES, CORES),
            ("piece", 3, 3 * rows, 4 * rows, 0, places - CORES),
        ],
        sends=[1, 2, 3],
    )

    from_core = swap(sent[0], 0, 1)
    from_side = swap(sent[1], 1, 0)
    from_diagonal = swap(sent[2], 1, 1)
    return pl.pallas_call(
        functools.partial(blocks_kernel, tops, rank),
        out_shape=jax.ShapeDtypeStruct((SEG_DEV, experts, rank * rank), jnp.bfloat16),
        in_specs=[VMEM] * 7,
        out_specs=VMEM,
        scratch_shapes=[
            pltpu.VMEM((rank, pairs), jnp.float32),
            pltpu.VMEM((rank, experts, tokens), jnp.float32),
        ],
        compiler_params=pltpu.CompilerParams(vmem_limit_bytes=32 * MIB),
        cost_estimate=QUICK,
    )(by_rank, basis, in_vmem(order_back), in_vmem(state[2]), from_core, from_side, from_diagonal)


def solution(mesh):
    placed = (
        P(("groups", "expert"), None),
        P(("groups", "expert"), None, None),
        P(("groups", "expert"), None),
        P(("groups", "expert")),
        P(),
        P("expert", None, None),
    )
    return jax.shard_map(
        local,
        mesh=mesh,
        in_specs=placed,
        out_specs=P(("groups", "expert"), None, None),
        check_vma=False,
    )
```

```python
import functools

import jax
import jax.numpy as jnp
import numpy as np
from jax import lax
from jax.experimental import pallas as pl
from jax.experimental.pallas import tpu as pltpu
from jax.sharding import PartitionSpec as P

SEG_DEV = 2
CORES = 2
SIDES = 2
QUAD = 4
PIECES = 4
LANES = 128
ALIGN = 16
DIGIT = 32
BOTH = ("groups", "expert")
MIB = 1024 * 1024
VMEM = pl.BlockSpec(memory_space=pltpu.VMEM)
SMEM = pl.BlockSpec(memory_space=pltpu.SMEM)
HBM = pl.BlockSpec(memory_space=pl.ANY)
QUICK = pl.CostEstimate(flops=1, bytes_accessed=1, transcendentals=0)
SHORT = pl.CostEstimate(flops=10**9, bytes_accessed=1, transcendentals=0)
NT = (((1,), (1,)), ((), ()))


def in_vmem(array):
    return pltpu.with_memory_space_constraint(array, pltpu.VMEM)


def in_hbm(array):
    return pltpu.with_memory_space_constraint(array, pltpu.HBM)


def place_in_quad(flip):
    side, core = lax.axis_index("groups") % SIDES, lax.axis_index("expert") % CORES
    return (side ^ (flip // CORES)) * CORES + (core ^ (flip % CORES))


def columns_of(flip, width):
    return pl.ds(pl.multiple_of(place_in_quad(flip) * width, width), width)


def row_of(routes):
    tops, tokens = routes.shape
    pairs = tops * tokens
    lane = lax.broadcasted_iota(jnp.int32, (tokens, pairs), 1)
    token = lax.broadcasted_iota(jnp.int32, (tokens, pairs), 0)
    spread = jnp.where(lane // tops == token, 1.0, 0.0).astype(jnp.bfloat16)
    values = routes.astype(jnp.float32).astype(jnp.bfloat16)
    every = jnp.dot(values, spread, preferred_element_type=jnp.float32)
    lane = lax.broadcasted_iota(jnp.int32, (tops, pairs), 1)
    k = lax.broadcasted_iota(jnp.int32, (tops, pairs), 0)
    return jnp.sum(jnp.where(lane % tops == k, every, 0.0), axis=0, keepdims=True).astype(jnp.int32)


def key_column(routes_row):
    count = routes_row.shape[1]
    keys = routes_row * count + lax.broadcasted_iota(jnp.int32, (1, count), 1)
    return jnp.broadcast_to(keys.astype(jnp.float32), (8, count)).T[:, 0:1]


def ranks(column, keys):
    total = jnp.zeros(keys.shape, jnp.float32)
    for first in range(0, column.shape[0], 128):
        smaller = jnp.where(column[first : first + 128] < keys, 1.0, 0.0)
        total = total + jnp.sum(smaller, axis=0, keepdims=True)
    return total


def sort_kernel(
    routes_ref,
    grads_ref,
    held_ref,
    starts_ref,
    head_ref,
    order_ref,
    piece_ref,
    sems,
):
    width = piece_ref.shape[1]
    count = sems.shape[0]
    part = grads_ref.shape[0] // count
    copies = []
    for n in range(count):
        here = pl.ds(n * part, part)
        copies.append(pltpu.make_async_copy(grads_ref.at[here], held_ref.at[here], sems.at[n]))
    for copy in copies:
        copy.start()
    routes = row_of(routes_ref[...])
    pairs = routes.shape[1]
    column = key_column(routes)
    keys = routes * pairs + lax.broadcasted_iota(jnp.int32, (1, pairs), 1)
    place = ranks(column, keys.astype(jnp.float32)).astype(jnp.int32)
    firsts = lax.broadcasted_iota(jnp.int32, starts_ref.shape, 1) * pairs
    starts = ranks(column, firsts.astype(jnp.float32)).astype(jnp.int32)
    starts_ref[...] = starts
    wide = head_ref.shape[1] - starts.shape[1]
    digits = [starts // DIGIT, starts % DIGIT]
    digits = [jnp.pad(d.astype(jnp.float32), ((0, 0), (0, wide))) for d in digits]
    row = lax.broadcasted_iota(jnp.int32, head_ref.shape, 0)
    head = jnp.where(row == 0, digits[0], jnp.where(row == 1, digits[1], 0.0))
    head_ref[...] = head.astype(jnp.bfloat16)
    rows = piece_ref.shape[0] - ALIGN
    for first in range(0, pairs, rows):
        ids = first + lax.broadcasted_iota(jnp.int32, (rows, pairs), 0)
        order_ref[first : first + rows, :] = jnp.where(place == ids, 1.0, 0.0).astype(jnp.bfloat16)
    for copy in copies:
        copy.wait()
    piece_ref[0:rows, :] = jnp.dot(
        order_ref[0:rows, :],
        held_ref[:, :, columns_of(2, width)].reshape(pairs, width),
        preferred_element_type=jnp.float32,
    ).astype(jnp.bfloat16)
    piece_ref[rows:, :] = head_ref[...]


def weights_kernel(weight_ref, mine_ref, core_ref, stage, sems):
    rows, width = mine_ref.shape
    count = sems.shape[0]
    part = rows // count
    copies = [
        pltpu.make_async_copy(
            weight_ref.at[pl.ds(n * part, part)], stage.at[pl.ds(n * part, part)], sems.at[n]
        )
        for n in range(count)
    ]
    for copy in copies:
        copy.start()
    for copy in copies:
        copy.wait()
    core_ref[...] = stage[:, columns_of(1, width)]
    mine_ref[...] = stage[:, columns_of(0, width)]


def join_kernel(one_ref, two_ref, out_ref):
    half = one_ref.shape[0]
    out_ref[0:half, :] = one_ref[...]
    out_ref[half:, :] = two_ref[...]


def permute_kernel(plan, order_ref, head_ref, grads_ref, *outs):
    pairs, width = order_ref.shape[0], outs[0].shape[1]
    for device in sorted({device for device, _, _ in plan}):
        grads = grads_ref[:, :, columns_of(device, width)].reshape(pairs, width)
        for out, (target, first, rows) in zip(outs, plan):
            if target == device:
                out[0:rows, :] = jnp.dot(
                    order_ref[first : first + rows, :], grads, preferred_element_type=jnp.float32
                ).astype(jnp.bfloat16)
                if out.shape[0] > rows:
                    out[rows:, :] = head_ref[...]


def basis_kernel(
    hidden_ref, proj_ref, segment_ref, routes_ref, out_ref, order_ref, hidden, proj, sems
):
    count = sems.shape[0] - 1
    part = hidden.shape[0] // count
    copies = [pltpu.make_async_copy(proj_ref, proj, sems.at[count])]
    for n in range(count):
        here = pl.ds(n * part, part)
        copies.append(pltpu.make_async_copy(hidden_ref.at[here], hidden.at[here], sems.at[n]))
    for copy in copies:
        copy.start()
    tops, tokens = routes_ref.shape
    pairs = tops * tokens
    column = key_column(row_of(routes_ref[...]))
    at = [
        routes_ref[k : k + 1, :] * pairs + lax.broadcasted_iota(jnp.int32, (1, tokens), 1) * tops + k
        for k in range(tops)
    ]
    place = ranks(column, jnp.concatenate(at, axis=1).astype(jnp.float32)).astype(jnp.int32)
    for first in range(0, pairs, 256):
        ids = first + lax.broadcasted_iota(jnp.int32, (256, pairs), 0)
        order_ref[first : first + 256, :] = jnp.where(place == ids, 1.0, 0.0).astype(jnp.bfloat16)
    segment = (segment_ref[...] - lax.axis_index("expert") * SEG_DEV).astype(jnp.float32)
    segment = jnp.broadcast_to(segment, (8, tokens)).T[:, 0:1]
    for copy in copies:
        copy.wait()
    projected = lax.dot_general(hidden[...], proj[...], NT, preferred_element_type=jnp.float32)
    zero = jnp.zeros_like(projected)
    picked = [jnp.where(segment == float(s), projected, zero) for s in range(SEG_DEV)]
    even = jnp.concatenate([b for p in picked for b in (p, zero)], axis=1)
    odd = jnp.concatenate([b for p in picked for b in (zero, p)], axis=1)
    out_ref[...] = jnp.concatenate([even, odd], axis=0).astype(out_ref.dtype)


def packed(total, first, pairs, rank):
    half = pairs // 2
    low = lax.broadcasted_iota(jnp.int32, (half, LANES), 1) < rank
    one = total[first : first + half, :]
    two = total[first + half : first + pairs, :]
    return jnp.where(low, one + pltpu.roll(one, rank, 1), two + pltpu.roll(two, rank, 1))


def partial_kernel(
    rank, pairs, window, new_tokens, new_units, tasks, fresh, sends, groups, bases_ref, *refs
):
    start_refs = dict(zip(groups, refs))
    refs = refs[len(groups) :]
    token_refs, refs = refs[: len(new_tokens)], refs[len(new_tokens) :]
    unit_refs, refs = refs[: len(new_units)], refs[len(new_units) :]
    if fresh:
        tokens, units, total = refs
        send_refs = ()
        total[...] = jnp.zeros_like(total)
    else:
        tokens, units, total = refs[3:6]
        send_refs = refs[6:]
    for ref, (first, count) in zip(token_refs, new_tokens):
        tokens[first : first + count, :] = ref[0:count, :]
    cols = units.shape[1]
    for ref, place in zip(unit_refs, new_units):
        for half in range(CORES):
            units[place + half] = ref[half * cols : (half + 1) * cols, :]
    held = cols // rank
    per_tile = LANES // rank
    low = lax.broadcasted_iota(jnp.int32, (1, LANES), 1) < rank

    device = lax.axis_index("expert")

    def process(w, members):
        base = bases_ref[device, w]
        heres, offsets = [], []
        for g in members:
            at = jnp.minimum(start_refs[g][0, base] & -ALIGN, pairs - window)
            offsets.append(at)
            heres.append(pl.ds(pl.multiple_of(g * pairs + at, ALIGN), window))
        rows = [tokens[here, :] for here in heres]
        rows = jnp.concatenate(rows, axis=0) if len(rows) > 1 else rows[0]
        dense = lax.dot_general(rows, units[w], NT, preferred_element_type=jnp.float32)
        for n, g in enumerate(members):
            value = total[heres[n], :]
            number = offsets[n] + lax.broadcasted_iota(jnp.int32, (window, LANES), 0)
            for j in range(cols // LANES):
                edge = [start_refs[g][0, base + j * per_tile + i] for i in range(per_tile + 1)]
                inside = (number >= jnp.where(low, edge[0], edge[1])) & (
                    number < jnp.where(low, edge[1], edge[2])
                )
                part = dense[n * window : (n + 1) * window, j * LANES : (j + 1) * LANES]
                value = jnp.where(inside, part, value)
            total[heres[n], :] = value

    for task in tasks:
        if task[0] == "units":
            _, members, first_w, count = task

            def each(i, carry, members=members, first_w=first_w):
                process(first_w + i, members)
                return carry

        else:
            _, member, first_row, end_row, first_w, count = task

            def each(
                i, carry, member=member, first_row=first_row, end_row=end_row, first_w=first_w
            ):
                w = first_w + i
                base = bases_ref[device, w]
                touches = (start_refs[member][0, base] < end_row) & (
                    start_refs[member][0, base + held] > first_row
                )

                @pl.when(touches)
                def _():
                    process(w, [member])

                return carry

        lax.fori_loop(0, count, each, 0)
    for ref, g in zip(send_refs, sends):
        ref[...] = packed(total, g * pairs, pairs, rank).astype(ref.dtype)


def accumulate(
    state, bases, starts, tokens, units, tasks, rank, pairs, window, places=0, sends=(), cost=QUICK
):
    fresh = state is None
    operands = [bases, *starts.values(), *[a for a, _, _ in tokens], *[a for a, _ in units]]
    specs = [SMEM] * (1 + len(starts)) + [VMEM] * (len(tokens) + len(units))
    if fresh:
        width = units[0][0].shape[1]
        shapes = [
            pltpu.VMEM((QUAD * pairs, width), jnp.bfloat16),
            pltpu.VMEM((places, units[0][0].shape[0] // CORES, width), jnp.bfloat16),
            pltpu.VMEM((QUAD * pairs, LANES), jnp.float32),
        ]
        aliases = {}
    else:
        aliases = {len(operands) + i: i for i in range(3)}
        operands += [in_vmem(a) for a in state]
        specs += [VMEM] * 3
        shapes = [pltpu.VMEM(a.shape, a.dtype) for a in state]
    shapes += [pltpu.VMEM((pairs // 2, LANES), jnp.bfloat16)] * len(sends)
    out = pl.pallas_call(
        functools.partial(
            partial_kernel,
            rank,
            pairs,
            window,
            [(first, count) for _, first, count in tokens],
            [p for _, p in units],
            tasks,
            fresh,
            sends,
            list(starts),
        ),
        out_shape=shapes,
        in_specs=specs,
        out_specs=[VMEM] * len(shapes),
        input_output_aliases=aliases,
        compiler_params=pltpu.CompilerParams(vmem_limit_bytes=8 * MIB),
        cost_estimate=cost,
    )(*operands)
    return list(out[:3]), list(out[3:])


def blocks_kernel(
    tops, rank, routes_ref, basis_ref, order_ref, total_ref, b_ref, c_ref, d_ref, out_ref, turned, spread
):
    half = b_ref.shape[0]
    tokens = 2 * half // tops
    value = packed(total_ref, 0, 2 * half, rank)
    for ref in (b_ref, c_ref, d_ref):
        value = value + ref[...].astype(jnp.float32)
    value = value.T
    value = jnp.concatenate([value[0:rank], value[rank : 2 * rank]], axis=1).astype(jnp.bfloat16)
    turned[...] = jnp.dot(value, order_ref[...], preferred_element_type=jnp.float32)
    experts = out_ref.shape[1]

    def expand(tile, carry):
        first = pl.multiple_of(tile * 8, 8)
        ids = first + lax.broadcasted_iota(jnp.int32, (8, tokens), 0)
        masks = [routes_ref[k : k + 1, :] == ids for k in range(tops)]
        for r in range(rank):
            value = jnp.zeros((8, tokens), jnp.float32)
            for k in range(tops):
                row = turned[r : r + 1, k * tokens : (k + 1) * tokens]
                value = jnp.where(masks[k], row, value)
            spread[r, pl.ds(first, 8), :] = value
        return carry

    lax.fori_loop(0, experts // 8, expand, 0)
    for pair in range(rank // 2):
        both = jnp.concatenate([spread[2 * pair], spread[2 * pair + 1]], axis=1)
        block = jnp.dot(
            both.astype(jnp.bfloat16), basis_ref[...], preferred_element_type=jnp.float32
        ).astype(jnp.bfloat16)
        for s in range(SEG_DEV):
            out_ref[s, :, pl.ds(pair * 2 * rank, 2 * rank)] = block[
                :, s * 2 * rank : (s + 1) * 2 * rank
            ]


def local(hidden_in, out_grads, routes, segments, in_proj, out_proj):
    tokens, tops = routes.shape
    exp_here, rank, width = out_proj.shape
    owners, groups = lax.axis_size("expert"), lax.axis_size("groups")
    experts = exp_here * owners
    pairs = tokens * tops
    capacity = max(2, 3 * pairs // (2 * experts))
    window = min(pairs, -(-(exp_here * capacity + ALIGN - 1) // ALIGN) * ALIGN)
    quarter = width // QUAD
    cols = exp_here * rank
    rows = pairs // PIECES
    index = lax.axis_index("expert")
    slots = owners // CORES // 2
    ring = [0, *range(1, slots, 2), *range((slots - 1) // 2 * 2, 0, -2)]
    following = {a: b for a, b in zip(ring, ring[1:] + ring[:1])}
    before = {b: a for a, b in following.items()}

    def swap(array, side, bit):
        table = [
            (g * owners + e, (g ^ side) * owners + (e ^ bit))
            for g in range(groups)
            for e in range(owners)
        ]
        return lax.ppermute(array, BOTH, table)

    def along(array, table):
        wide = 2 * CORES
        pairs_of = [(e, table[e // wide] * wide + e % wide) for e in range(owners)]
        return lax.ppermute(array, "expert", pairs_of)

    def tie(*arrays):
        return lax.optimization_barrier(arrays)

    final = slots - 1
    first_names = [(n, 0) for n in range(final)] + [(n, 1) for n in range(final - 1)]
    next_names = [(final, 0), (final - 1, 1)]
    arrival = first_names + next_names + [(final, 1)]

    def source(z, hops):
        for _ in range(hops):
            z = before[z]
        return z

    rows_of = [
        [
            ((source(e // (2 * CORES), n) * 2 + (e // CORES % 2 ^ y)) * CORES + (e % CORES ^ c)) * exp_here
            for n, y in arrival
            for c in range(CORES)
        ]
        for e in range(owners)
    ]
    places = CORES * len(arrival)
    bases = jnp.asarray(np.array(rows_of, np.int32))

    unit_shape = pltpu.VMEM((cols, quarter), jnp.bfloat16)
    order_shape = pltpu.VMEM((pairs, pairs), jnp.bfloat16)

    def rows_shape(count):
        return pltpu.VMEM((count, quarter), jnp.bfloat16)

    mine_unit, core_unit = pl.pallas_call(
        weights_kernel,
        out_shape=[unit_shape, unit_shape],
        in_specs=[HBM],
        out_specs=[VMEM] * 2,
        scratch_shapes=[pltpu.VMEM((cols, width), jnp.bfloat16), pltpu.SemaphoreType.DMA((4,))],
        compiler_params=pltpu.CompilerParams(vmem_limit_bytes=8 * MIB),
        cost_estimate=QUICK,
    )(in_hbm(out_proj.reshape(cols, width)))
    other_unit = swap(core_unit, 0, 1)
    unit = pl.pallas_call(
        join_kernel,
        out_shape=pltpu.VMEM((CORES * cols, quarter), jnp.bfloat16),
        in_specs=[VMEM] * 2,
        out_specs=VMEM,
        compiler_params=pltpu.CompilerParams(vmem_limit_bytes=4 * MIB),
        cost_estimate=QUICK,
    )(mine_unit, other_unit)
    held = {(0, 0): unit, (1, 0): along(unit, following), (0, 1): swap(unit, 0, CORES)}

    by_rank, _ = tie(routes.T, unit)
    edges = -(-(experts + 1) // LANES) * LANES
    held_grads, own_starts, head, order, first_piece = pl.pallas_call(
        sort_kernel,
        out_shape=[
            pltpu.VMEM(out_grads.shape, jnp.bfloat16),
            jax.ShapeDtypeStruct((1, edges), jnp.int32),
            rows_shape(ALIGN),
            order_shape,
            rows_shape(2 * rows + ALIGN),
        ],
        in_specs=[VMEM, HBM],
        out_specs=[VMEM] * 5,
        scratch_shapes=[pltpu.SemaphoreType.DMA((8,))],
        compiler_params=pltpu.CompilerParams(vmem_limit_bytes=12 * MIB),
        cost_estimate=QUICK,
    )(by_rank, in_hbm(out_grads))

    def permuted(plan, headed, *after):
        held, *_ = tie(order, *after)
        return pl.pallas_call(
            functools.partial(permute_kernel, plan),
            out_shape=[
                rows_shape(many + (ALIGN if n in headed else 0))
                for n, (_, _, many) in enumerate(plan)
            ],
            in_specs=[VMEM] * 3,
            out_specs=[VMEM] * len(plan),
            compiler_params=pltpu.CompilerParams(vmem_limit_bytes=12 * MIB),
            cost_estimate=QUICK,
        )(in_vmem(held), head, in_vmem(held_grads))

    def starts_in(block, count):
        digits = block[count : count + 2, :edges].astype(jnp.int32)
        return (digits[0] * DIGIT + digits[1]).reshape(1, edges)

    side_pieces = [swap(first_piece, 1, 0)]
    (second_piece,) = permuted([(2, 2 * rows, 2 * rows)], [])
    own_tokens, *for_core = permuted(
        [(0, 0, pairs), (1, 0, 2 * rows), (1, 2 * rows, 2 * rows)], [1], second_piece
    )
    third_piece, last_piece = permuted(
        [(3, 0, 3 * rows), (3, 3 * rows, rows)], [0], own_tokens
    )
    from_core = [swap(piece, 0, 1) for piece in for_core]
    side_pieces.append(swap(second_piece, 1, 0))
    diagonal_pieces = [swap(third_piece, 1, 1), swap(last_piece, 1, 1)]
    local_segments, *_ = tie(segments, last_piece)
    basis, order_back = pl.pallas_call(
        basis_kernel,
        out_shape=[
            pltpu.VMEM((2 * tokens, SEG_DEV * 2 * rank), jnp.bfloat16),
            order_shape,
        ],
        in_specs=[HBM, HBM, VMEM, VMEM],
        out_specs=[VMEM] * 2,
        scratch_shapes=[
            pltpu.VMEM(hidden_in.shape, jnp.bfloat16),
            pltpu.VMEM(in_proj.shape, jnp.bfloat16),
            pltpu.SemaphoreType.DMA((5,)),
        ],
        compiler_params=pltpu.CompilerParams(vmem_limit_bytes=12 * MIB),
        cost_estimate=QUICK,
    )(in_hbm(hidden_in), in_hbm(in_proj), local_segments.reshape(1, tokens), by_rank)

    call = functools.partial(
        accumulate, bases=bases, rank=rank, pairs=pairs, window=window, places=places
    )
    place_of = {name: CORES * n for n, name in enumerate(arrival)}
    starts = {0: own_starts}
    members = []
    known_units = 0
    state = None

    def work(names, tokens, sends=(), cost=QUICK):
        nonlocal state, known_units
        tasks, arrived = [], []
        if names and members:
            tasks.append(("units", list(members), known_units, CORES * len(names)))
        known_units += CORES * len(names)
        for group, piece, first, count in tokens:
            arrived.append((piece, group * pairs + first, count))
            if first == 0:
                members.append(group)
                if group:
                    starts[group] = starts_in(piece, count)
            if count == pairs:
                tasks.append(("units", [group], 0, known_units))
            else:
                tasks.append(("piece", group, first, first + count, 0, known_units))
        state, out = call(
            state,
            starts=starts,
            tokens=arrived,
            units=[(held[n], place_of[n]) for n in names],
            tasks=tasks,
            sends=sends,
            cost=cost,
        )
        return out

    for n in range(1, slots):
        tied = [held[n, 0], held[n - 1, 1]]
        if n == final - 1:
            tied += [side_pieces[0], basis, order_back]
        if n == final:
            work(
                first_names,
                [(0, own_tokens, 0, pairs)]
                + [(2, piece, part * 2 * rows, 2 * rows) for part, piece in enumerate(side_pieces)],
            )
            tied += state
        held[n, 0], held[n - 1, 1], *tied = tie(*tied)
        if n == final - 1:
            side_pieces[0], basis, order_back = tied
        if n == final:
            state = tied
        else:
            held[n + 1, 0] = along(held[n, 0], following)
        held[n, 1] = swap(held[n, 0], 0, CORES)

    work(
        next_names,
        [(1, piece, part * 2 * rows, 2 * rows) for part, piece in enumerate(from_core)],
    )
    work([], [(3, diagonal_pieces[0], 0, 3 * rows)])
    sent = work([arrival[-1]], [(3, diagonal_pieces[1], 3 * rows, rows)], sends=[1, 2, 3])

    from_core = swap(sent[0], 0, 1)
    from_side = swap(sent[1], 1, 0)
    from_diagonal = swap(sent[2], 1, 1)
    return pl.pallas_call(
        functools.partial(blocks_kernel, tops, rank),
        out_shape=jax.ShapeDtypeStruct((SEG_DEV, experts, rank * rank), jnp.bfloat16),
        in_specs=[VMEM] * 7,
        out_specs=VMEM,
        scratch_shapes=[
            pltpu.VMEM((rank, pairs), jnp.float32),
            pltpu.VMEM((rank, experts, tokens), jnp.float32),
        ],
        compiler_params=pltpu.CompilerParams(vmem_limit_bytes=32 * MIB),
        cost_estimate=QUICK,
    )(by_rank, basis, in_vmem(order_back), in_vmem(state[2]), from_core, from_side, from_diagonal)


def solution(mesh):
    placed = (
        P(("groups", "expert"), None),
        P(("groups", "expert"), None, None),
        P(("groups", "expert"), None),
        P(("groups", "expert")),
        P(),
        P("expert", None, None),
    )
    return jax.shard_map(
        local,
        mesh=mesh,
        in_specs=placed,
        out_specs=P(("groups", "expert"), None, None),
        check_vma=False,
    )
```

```python
import functools

import jax
import jax.numpy as jnp
import numpy as np
from jax import lax
from jax.experimental import pallas as pl
from jax.experimental.pallas import tpu as pltpu
from jax.sharding import PartitionSpec as P

SEG_DEV = 2
CORES = 2
SIDES = 2
QUAD = 4
PIECES = 4
LANES = 128
ALIGN = 16
DIGIT = 32
BOTH = ("groups", "expert")
MIB = 1024 * 1024
VMEM = pl.BlockSpec(memory_space=pltpu.VMEM)
SMEM = pl.BlockSpec(memory_space=pltpu.SMEM)
HBM = pl.BlockSpec(memory_space=pl.ANY)
QUICK = pl.CostEstimate(flops=1, bytes_accessed=1, transcendentals=0)
SHORT = pl.CostEstimate(flops=10**9, bytes_accessed=1, transcendentals=0)
NT = (((1,), (1,)), ((), ()))


def in_vmem(array):
    return pltpu.with_memory_space_constraint(array, pltpu.VMEM)


def in_hbm(array):
    return pltpu.with_memory_space_constraint(array, pltpu.HBM)


def place_in_quad(flip):
    side, core = lax.axis_index("groups") % SIDES, lax.axis_index("expert") % CORES
    return (side ^ (flip // CORES)) * CORES + (core ^ (flip % CORES))


def columns_of(flip, width):
    return pl.ds(pl.multiple_of(place_in_quad(flip) * width, width), width)


def row_of(routes):
    tops, tokens = routes.shape
    pairs = tops * tokens
    lane = lax.broadcasted_iota(jnp.int32, (tokens, pairs), 1)
    token = lax.broadcasted_iota(jnp.int32, (tokens, pairs), 0)
    spread = jnp.where(lane // tops == token, 1.0, 0.0).astype(jnp.bfloat16)
    values = routes.astype(jnp.float32).astype(jnp.bfloat16)
    every = jnp.dot(values, spread, preferred_element_type=jnp.float32)
    lane = lax.broadcasted_iota(jnp.int32, (tops, pairs), 1)
    k = lax.broadcasted_iota(jnp.int32, (tops, pairs), 0)
    return jnp.sum(jnp.where(lane % tops == k, every, 0.0), axis=0, keepdims=True).astype(jnp.int32)


def key_column(routes_row):
    count = routes_row.shape[1]
    keys = routes_row * count + lax.broadcasted_iota(jnp.int32, (1, count), 1)
    return jnp.broadcast_to(keys.astype(jnp.float32), (8, count)).T[:, 0:1]


def ranks(column, keys):
    total = jnp.zeros(keys.shape, jnp.float32)
    for first in range(0, column.shape[0], 128):
        smaller = jnp.where(column[first : first + 128] < keys, 1.0, 0.0)
        total = total + jnp.sum(smaller, axis=0, keepdims=True)
    return total


def sort_kernel(
    routes_ref,
    grads_ref,
    held_ref,
    starts_ref,
    head_ref,
    order_ref,
    piece_ref,
    sems,
):
    width = piece_ref.shape[1]
    count = sems.shape[0]
    part = grads_ref.shape[0] // count
    copies = []
    for n in range(count):
        here = pl.ds(n * part, part)
        copies.append(pltpu.make_async_copy(grads_ref.at[here], held_ref.at[here], sems.at[n]))
    for copy in copies:
        copy.start()
    routes = row_of(routes_ref[...])
    pairs = routes.shape[1]
    column = key_column(routes)
    keys = routes * pairs + lax.broadcasted_iota(jnp.int32, (1, pairs), 1)
    place = ranks(column, keys.astype(jnp.float32)).astype(jnp.int32)
    firsts = lax.broadcasted_iota(jnp.int32, starts_ref.shape, 1) * pairs
    starts = ranks(column, firsts.astype(jnp.float32)).astype(jnp.int32)
    starts_ref[...] = starts
    wide = head_ref.shape[1] - starts.shape[1]
    digits = [starts // DIGIT, starts % DIGIT]
    digits = [jnp.pad(d.astype(jnp.float32), ((0, 0), (0, wide))) for d in digits]
    row = lax.broadcasted_iota(jnp.int32, head_ref.shape, 0)
    head = jnp.where(row == 0, digits[0], jnp.where(row == 1, digits[1], 0.0))
    head_ref[...] = head.astype(jnp.bfloat16)
    rows = piece_ref.shape[0] - ALIGN
    for first in range(0, pairs, rows):
        ids = first + lax.broadcasted_iota(jnp.int32, (rows, pairs), 0)
        order_ref[first : first + rows, :] = jnp.where(place == ids, 1.0, 0.0).astype(jnp.bfloat16)
    for copy in copies:
        copy.wait()
    piece_ref[0:rows, :] = jnp.dot(
        order_ref[0:rows, :],
        held_ref[:, :, columns_of(2, width)].reshape(pairs, width),
        preferred_element_type=jnp.float32,
    ).astype(jnp.bfloat16)
    piece_ref[rows:, :] = head_ref[...]


def weights_kernel(weight_ref, mine_ref, core_ref, stage, sems):
    rows, width = mine_ref.shape
    count = sems.shape[0]
    part = rows // count
    copies = [
        pltpu.make_async_copy(
            weight_ref.at[pl.ds(n * part, part)], stage.at[pl.ds(n * part, part)], sems.at[n]
        )
        for n in range(count)
    ]
    for copy in copies:
        copy.start()
    for copy in copies:
        copy.wait()
    core_ref[...] = stage[:, columns_of(1, width)]
    mine_ref[...] = stage[:, columns_of(0, width)]


def join_kernel(one_ref, two_ref, out_ref):
    half = one_ref.shape[0]
    out_ref[0:half, :] = one_ref[...]
    out_ref[half:, :] = two_ref[...]


def permute_kernel(plan, order_ref, head_ref, grads_ref, *outs):
    pairs, width = order_ref.shape[0], outs[0].shape[1]
    for device in sorted({device for device, _, _ in plan}):
        grads = grads_ref[:, :, columns_of(device, width)].reshape(pairs, width)
        for out, (target, first, rows) in zip(outs, plan):
            if target == device:
                out[0:rows, :] = jnp.dot(
                    order_ref[first : first + rows, :], grads, preferred_element_type=jnp.float32
                ).astype(jnp.bfloat16)
                if out.shape[0] > rows:
                    out[rows:, :] = head_ref[...]


def basis_kernel(
    hidden_ref, proj_ref, segment_ref, routes_ref, out_ref, order_ref, hidden, proj, sems
):
    count = sems.shape[0] - 1
    part = hidden.shape[0] // count
    copies = [pltpu.make_async_copy(proj_ref, proj, sems.at[count])]
    for n in range(count):
        here = pl.ds(n * part, part)
        copies.append(pltpu.make_async_copy(hidden_ref.at[here], hidden.at[here], sems.at[n]))
    for copy in copies:
        copy.start()
    tops, tokens = routes_ref.shape
    pairs = tops * tokens
    column = key_column(row_of(routes_ref[...]))
    at = [
        routes_ref[k : k + 1, :] * pairs + lax.broadcasted_iota(jnp.int32, (1, tokens), 1) * tops + k
        for k in range(tops)
    ]
    place = ranks(column, jnp.concatenate(at, axis=1).astype(jnp.float32)).astype(jnp.int32)
    for first in range(0, pairs, 256):
        ids = first + lax.broadcasted_iota(jnp.int32, (256, pairs), 0)
        order_ref[first : first + 256, :] = jnp.where(place == ids, 1.0, 0.0).astype(jnp.bfloat16)
    segment = (segment_ref[...] - lax.axis_index("expert") * SEG_DEV).astype(jnp.float32)
    segment = jnp.broadcast_to(segment, (8, tokens)).T[:, 0:1]
    for copy in copies:
        copy.wait()
    projected = lax.dot_general(hidden[...], proj[...], NT, preferred_element_type=jnp.float32)
    zero = jnp.zeros_like(projected)
    picked = [jnp.where(segment == float(s), projected, zero) for s in range(SEG_DEV)]
    even = jnp.concatenate([b for p in picked for b in (p, zero)], axis=1)
    odd = jnp.concatenate([b for p in picked for b in (zero, p)], axis=1)
    out_ref[...] = jnp.concatenate([even, odd], axis=0).astype(out_ref.dtype)


def packed(total, first, pairs, rank):
    half = pairs // 2
    low = lax.broadcasted_iota(jnp.int32, (half, LANES), 1) < rank
    one = total[first : first + half, :]
    two = total[first + half : first + pairs, :]
    return jnp.where(low, one + pltpu.roll(one, rank, 1), two + pltpu.roll(two, rank, 1))


def partial_kernel(
    rank, pairs, window, new_tokens, new_units, tasks, fresh, sends, groups, bases_ref, *refs
):
    start_refs = dict(zip(groups, refs))
    refs = refs[len(groups) :]
    token_refs, refs = refs[: len(new_tokens)], refs[len(new_tokens) :]
    unit_refs, refs = refs[: len(new_units)], refs[len(new_units) :]
    if fresh:
        tokens, units, total = refs
        send_refs = ()
        total[...] = jnp.zeros_like(total)
    else:
        tokens, units, total = refs[3:6]
        send_refs = refs[6:]
    for ref, (first, count) in zip(token_refs, new_tokens):
        tokens[first : first + count, :] = ref[0:count, :]
    cols = units.shape[1]
    for ref, place in zip(unit_refs, new_units):
        for half in range(CORES):
            units[place + half] = ref[half * cols : (half + 1) * cols, :]
    held = cols // rank
    per_tile = LANES // rank
    low = lax.broadcasted_iota(jnp.int32, (1, LANES), 1) < rank

    device = lax.axis_index("expert")

    def process(w, members):
        base = bases_ref[device, w]
        heres, offsets = [], []
        for g in members:
            at = jnp.minimum(start_refs[g][0, base] & -ALIGN, pairs - window)
            offsets.append(at)
            heres.append(pl.ds(pl.multiple_of(g * pairs + at, ALIGN), window))
        rows = [tokens[here, :] for here in heres]
        rows = jnp.concatenate(rows, axis=0) if len(rows) > 1 else rows[0]
        dense = lax.dot_general(rows, units[w], NT, preferred_element_type=jnp.float32)
        for n, g in enumerate(members):
            value = total[heres[n], :]
            number = offsets[n] + lax.broadcasted_iota(jnp.int32, (window, LANES), 0)
            for j in range(cols // LANES):
                edge = [start_refs[g][0, base + j * per_tile + i] for i in range(per_tile + 1)]
                inside = (number >= jnp.where(low, edge[0], edge[1])) & (
                    number < jnp.where(low, edge[1], edge[2])
                )
                part = dense[n * window : (n + 1) * window, j * LANES : (j + 1) * LANES]
                value = jnp.where(inside, part, value)
            total[heres[n], :] = value

    for task in tasks:
        if task[0] == "units":
            _, members, first_w, count = task

            def each(i, carry, members=members, first_w=first_w):
                process(first_w + i, members)
                return carry

        else:
            _, member, first_row, end_row, first_w, count = task

            def each(
                i, carry, member=member, first_row=first_row, end_row=end_row, first_w=first_w
            ):
                w = first_w + i
                base = bases_ref[device, w]
                touches = (start_refs[member][0, base] < end_row) & (
                    start_refs[member][0, base + held] > first_row
                )

                @pl.when(touches)
                def _():
                    process(w, [member])

                return carry

        lax.fori_loop(0, count, each, 0)
    for ref, g in zip(send_refs, sends):
        ref[...] = packed(total, g * pairs, pairs, rank).astype(ref.dtype)


def accumulate(
    state, bases, starts, tokens, units, tasks, rank, pairs, window, places=0, sends=(), cost=QUICK
):
    fresh = state is None
    operands = [bases, *starts.values(), *[a for a, _, _ in tokens], *[a for a, _ in units]]
    specs = [SMEM] * (1 + len(starts)) + [VMEM] * (len(tokens) + len(units))
    if fresh:
        width = units[0][0].shape[1]
        shapes = [
            pltpu.VMEM((QUAD * pairs, width), jnp.bfloat16),
            pltpu.VMEM((places, units[0][0].shape[0] // CORES, width), jnp.bfloat16),
            pltpu.VMEM((QUAD * pairs, LANES), jnp.float32),
        ]
        aliases = {}
    else:
        aliases = {len(operands) + i: i for i in range(3)}
        operands += [in_vmem(a) for a in state]
        specs += [VMEM] * 3
        shapes = [pltpu.VMEM(a.shape, a.dtype) for a in state]
    shapes += [pltpu.VMEM((pairs // 2, LANES), jnp.bfloat16)] * len(sends)
    out = pl.pallas_call(
        functools.partial(
            partial_kernel,
            rank,
            pairs,
            window,
            [(first, count) for _, first, count in tokens],
            [p for _, p in units],
            tasks,
            fresh,
            sends,
            list(starts),
        ),
        out_shape=shapes,
        in_specs=specs,
        out_specs=[VMEM] * len(shapes),
        input_output_aliases=aliases,
        compiler_params=pltpu.CompilerParams(vmem_limit_bytes=8 * MIB),
        cost_estimate=cost,
    )(*operands)
    return list(out[:3]), list(out[3:])


def blocks_kernel(
    tops, rank, routes_ref, basis_ref, order_ref, total_ref, b_ref, c_ref, d_ref, out_ref, turned, spread
):
    half = b_ref.shape[0]
    tokens = 2 * half // tops
    value = packed(total_ref, 0, 2 * half, rank)
    for ref in (b_ref, c_ref, d_ref):
        value = value + ref[...].astype(jnp.float32)
    value = value.T
    value = jnp.concatenate([value[0:rank], value[rank : 2 * rank]], axis=1).astype(jnp.bfloat16)
    turned[...] = jnp.dot(value, order_ref[...], preferred_element_type=jnp.float32)
    experts = out_ref.shape[1]

    def expand(tile, carry):
        first = pl.multiple_of(tile * 8, 8)
        ids = first + lax.broadcasted_iota(jnp.int32, (8, tokens), 0)
        masks = [routes_ref[k : k + 1, :] == ids for k in range(tops)]
        for r in range(rank):
            value = jnp.zeros((8, tokens), jnp.float32)
            for k in range(tops):
                row = turned[r : r + 1, k * tokens : (k + 1) * tokens]
                value = jnp.where(masks[k], row, value)
            spread[r, pl.ds(first, 8), :] = value
        return carry

    lax.fori_loop(0, experts // 8, expand, 0)
    for pair in range(rank // 2):
        both = jnp.concatenate([spread[2 * pair], spread[2 * pair + 1]], axis=1)
        block = jnp.dot(
            both.astype(jnp.bfloat16), basis_ref[...], preferred_element_type=jnp.float32
        ).astype(jnp.bfloat16)
        for s in range(SEG_DEV):
            out_ref[s, :, pl.ds(pair * 2 * rank, 2 * rank)] = block[
                :, s * 2 * rank : (s + 1) * 2 * rank
            ]


def local(hidden_in, out_grads, routes, segments, in_proj, out_proj):
    tokens, tops = routes.shape
    exp_here, rank, width = out_proj.shape
    owners, groups = lax.axis_size("expert"), lax.axis_size("groups")
    experts = exp_here * owners
    pairs = tokens * tops
    capacity = max(2, 3 * pairs // (2 * experts))
    window = min(pairs, -(-(exp_here * capacity + ALIGN - 1) // ALIGN) * ALIGN)
    quarter = width // QUAD
    cols = exp_here * rank
    rows = pairs // PIECES
    index = lax.axis_index("expert")
    slots = owners // CORES // 2
    ring = [0, *range(1, slots, 2), *range((slots - 1) // 2 * 2, 0, -2)]
    following = {a: b for a, b in zip(ring, ring[1:] + ring[:1])}
    before = {b: a for a, b in following.items()}

    def swap(array, side, bit):
        table = [
            (g * owners + e, (g ^ side) * owners + (e ^ bit))
            for g in range(groups)
            for e in range(owners)
        ]
        return lax.ppermute(array, BOTH, table)

    def along(array, table):
        wide = 2 * CORES
        pairs_of = [(e, table[e // wide] * wide + e % wide) for e in range(owners)]
        return lax.ppermute(array, "expert", pairs_of)

    def tie(*arrays):
        return lax.optimization_barrier(arrays)

    final = slots - 1
    first_names = [(n, 0) for n in range(final)] + [(n, 1) for n in range(final - 1)]
    arrival = first_names + [(final - 1, 1), (final, 1), (final, 0)]

    def source(z, hops):
        for _ in range(hops):
            z = before[z]
        return z

    rows_of = [
        [
            ((source(e // (2 * CORES), n) * 2 + (e // CORES % 2 ^ y)) * CORES + (e % CORES ^ c)) * exp_here
            for n, y in arrival
            for c in range(CORES)
        ]
        for e in range(owners)
    ]
    places = CORES * len(arrival)
    bases = jnp.asarray(np.array(rows_of, np.int32))

    unit_shape = pltpu.VMEM((cols, quarter), jnp.bfloat16)
    order_shape = pltpu.VMEM((pairs, pairs), jnp.bfloat16)

    def rows_shape(count):
        return pltpu.VMEM((count, quarter), jnp.bfloat16)

    mine_unit, core_unit = pl.pallas_call(
        weights_kernel,
        out_shape=[unit_shape, unit_shape],
        in_specs=[HBM],
        out_specs=[VMEM] * 2,
        scratch_shapes=[pltpu.VMEM((cols, width), jnp.bfloat16), pltpu.SemaphoreType.DMA((4,))],
        compiler_params=pltpu.CompilerParams(vmem_limit_bytes=8 * MIB),
        cost_estimate=QUICK,
    )(in_hbm(out_proj.reshape(cols, width)))
    other_unit = swap(core_unit, 0, 1)
    by_rank, _ = tie(routes.T, core_unit)
    edges = -(-(experts + 1) // LANES) * LANES
    held_grads, own_starts, head, order, first_piece = pl.pallas_call(
        sort_kernel,
        out_shape=[
            pltpu.VMEM(out_grads.shape, jnp.bfloat16),
            jax.ShapeDtypeStruct((1, edges), jnp.int32),
            rows_shape(ALIGN),
            order_shape,
            rows_shape(2 * rows + ALIGN),
        ],
        in_specs=[VMEM, HBM],
        out_specs=[VMEM] * 5,
        scratch_shapes=[pltpu.SemaphoreType.DMA((8,))],
        compiler_params=pltpu.CompilerParams(vmem_limit_bytes=12 * MIB),
        cost_estimate=QUICK,
    )(by_rank, in_hbm(out_grads))

    *joined, order = tie(mine_unit, other_unit, order)
    unit = pl.pallas_call(
        join_kernel,
        out_shape=pltpu.VMEM((CORES * cols, quarter), jnp.bfloat16),
        in_specs=[VMEM] * 2,
        out_specs=VMEM,
        compiler_params=pltpu.CompilerParams(vmem_limit_bytes=4 * MIB),
        cost_estimate=QUICK,
    )(*joined)
    held = {(0, 0): unit, (1, 0): along(unit, following), (0, 1): swap(unit, 0, CORES)}

    def permuted(plan, headed, *after):
        held, *_ = tie(order, *after)
        return pl.pallas_call(
            functools.partial(permute_kernel, plan),
            out_shape=[
                rows_shape(many + (ALIGN if n in headed else 0))
                for n, (_, _, many) in enumerate(plan)
            ],
            in_specs=[VMEM] * 3,
            out_specs=[VMEM] * len(plan),
            compiler_params=pltpu.CompilerParams(vmem_limit_bytes=12 * MIB),
            cost_estimate=QUICK,
        )(in_vmem(held), head, in_vmem(held_grads))

    def starts_in(block, count):
        digits = block[count : count + 2, :edges].astype(jnp.int32)
        return (digits[0] * DIGIT + digits[1]).reshape(1, edges)

    side_pieces = [swap(first_piece, 1, 0)]
    (second_piece,) = permuted([(2, 2 * rows, 2 * rows)], [], unit)
    own_tokens, *for_core = permuted(
        [(0, 0, pairs), (1, 0, 2 * rows), (1, 2 * rows, 2 * rows)], [1], second_piece
    )
    third_piece, last_piece = permuted(
        [(3, 0, 3 * rows), (3, 3 * rows, rows)], [0], own_tokens
    )
    from_core = [swap(piece, 0, 1) for piece in for_core]
    side_pieces.append(swap(second_piece, 1, 0))
    third_piece, last_piece, side_pieces[0] = tie(third_piece, last_piece, side_pieces[0])
    diagonal_pieces = [swap(third_piece, 1, 1), swap(last_piece, 1, 1)]
    local_segments, *_ = tie(segments, last_piece)
    basis, order_back = pl.pallas_call(
        basis_kernel,
        out_shape=[
            pltpu.VMEM((2 * tokens, SEG_DEV * 2 * rank), jnp.bfloat16),
            order_shape,
        ],
        in_specs=[HBM, HBM, VMEM, VMEM],
        out_specs=[VMEM] * 2,
        scratch_shapes=[
            pltpu.VMEM(hidden_in.shape, jnp.bfloat16),
            pltpu.VMEM(in_proj.shape, jnp.bfloat16),
            pltpu.SemaphoreType.DMA((5,)),
        ],
        compiler_params=pltpu.CompilerParams(vmem_limit_bytes=12 * MIB),
        cost_estimate=QUICK,
    )(in_hbm(hidden_in), in_hbm(in_proj), local_segments.reshape(1, tokens), by_rank)

    call = functools.partial(
        accumulate, bases=bases, rank=rank, pairs=pairs, window=window, places=places
    )
    place_of = {name: CORES * n for n, name in enumerate(arrival)}
    starts = {0: own_starts}
    members = []
    known_units = 0
    state = None

    def work(names, complete=(), partial=(), sends=(), cost=QUICK):
        nonlocal state, known_units
        tasks, arrived = [], []
        for group, blocks in complete:
            first = 0
            for piece, count in blocks:
                arrived.append((piece, group * pairs + first, count))
                first += count
            if group:
                starts[group] = starts_in(*blocks[0])
            members.append(group)
        if names:
            tasks.append(("units", list(members), known_units, CORES * len(names)))
        known_units += CORES * len(names)
        for group, piece, first, count in partial:
            arrived.append((piece, group * pairs + first, count))
            if first == 0:
                starts[group] = starts_in(piece, count)
                members.append(group)
            tasks.append(("piece", group, first, first + count, 0, known_units))
        state, out = call(
            state,
            starts=starts,
            tokens=arrived,
            units=[(held[n], place_of[n]) for n in names],
            tasks=tasks,
            sends=sends,
            cost=cost,
        )
        return out

    for n in range(1, slots):
        if n == final:
            break
        tied = [held[n, 0], held[n - 1, 1]]
        if n == 1:
            tied.append(side_pieces[0])
        if n == final - 1:
            tied += [basis, order_back]
        held[n, 0], held[n - 1, 1], *tied = tie(*tied)
        if n == 1:
            side_pieces[0], *tied = tied
        if n == final - 1:
            basis, order_back = tied
            half = 2 * rows
            work(
                first_names,
                complete=[
                    (0, [(own_tokens, pairs)]),
                    (1, [(piece, half) for piece in from_core]),
                    (2, [(piece, half) for piece in side_pieces]),
                ],
            )
        held[n + 1, 0] = along(held[n, 0], following)
        held[n, 1] = swap(held[n, 0], 0, CORES)
    held[final, 1] = along(held[0, 1], before)

    work([(final - 1, 1)], partial=[(3, diagonal_pieces[0], 0, 3 * rows)])
    work([(final, 1)], cost=SHORT)
    sent = work(
        [(final, 0)], partial=[(3, diagonal_pieces[1], 3 * rows, rows)], sends=[1, 2, 3], cost=SHORT
    )

    from_core = swap(sent[0], 0, 1)
    from_side = swap(sent[1], 1, 0)
    from_diagonal = swap(sent[2], 1, 1)
    return pl.pallas_call(
        functools.partial(blocks_kernel, tops, rank),
        out_shape=jax.ShapeDtypeStruct((SEG_DEV, experts, rank * rank), jnp.bfloat16),
        in_specs=[VMEM] * 7,
        out_specs=VMEM,
        scratch_shapes=[
            pltpu.VMEM((rank, pairs), jnp.float32),
            pltpu.VMEM((rank, experts, tokens), jnp.float32),
        ],
        compiler_params=pltpu.CompilerParams(vmem_limit_bytes=32 * MIB),
        cost_estimate=QUICK,
    )(by_rank, basis, in_vmem(order_back), in_vmem(state[2]), from_core, from_side, from_diagonal)


def solution(mesh):
    placed = (
        P(("groups", "expert"), None),
        P(("groups", "expert"), None, None),
        P(("groups", "expert"), None),
        P(("groups", "expert")),
        P(),
        P("expert", None, None),
    )
    return jax.shard_map(
        local,
        mesh=mesh,
        in_specs=placed,
        out_specs=P(("groups", "expert"), None, None),
        check_vma=False,
    )
```

```python
import functools

import jax
import jax.numpy as jnp
import numpy as np
from jax import lax
from jax.experimental import pallas as pl
from jax.experimental.pallas import tpu as pltpu
from jax.sharding import PartitionSpec as P

SEG_DEV = 2
CORES = 2
SIDES = 2
QUAD = 4
PIECES = 4
LANES = 128
ALIGN = 16
DIGIT = 32
BOTH = ("groups", "expert")
MIB = 1024 * 1024
VMEM = pl.BlockSpec(memory_space=pltpu.VMEM)
SMEM = pl.BlockSpec(memory_space=pltpu.SMEM)
HBM = pl.BlockSpec(memory_space=pl.ANY)
QUICK = pl.CostEstimate(flops=1, bytes_accessed=1, transcendentals=0)
SHORT = pl.CostEstimate(flops=10**9, bytes_accessed=1, transcendentals=0)
NT = (((1,), (1,)), ((), ()))


def in_vmem(array):
    return pltpu.with_memory_space_constraint(array, pltpu.VMEM)


def in_hbm(array):
    return pltpu.with_memory_space_constraint(array, pltpu.HBM)


def place_in_quad(flip):
    side, core = lax.axis_index("groups") % SIDES, lax.axis_index("expert") % CORES
    return (side ^ (flip // CORES)) * CORES + (core ^ (flip % CORES))


def columns_of(flip, width):
    return pl.ds(pl.multiple_of(place_in_quad(flip) * width, width), width)


def row_of(routes):
    tops, tokens = routes.shape
    pairs = tops * tokens
    lane = lax.broadcasted_iota(jnp.int32, (tokens, pairs), 1)
    token = lax.broadcasted_iota(jnp.int32, (tokens, pairs), 0)
    spread = jnp.where(lane // tops == token, 1.0, 0.0).astype(jnp.bfloat16)
    values = routes.astype(jnp.float32).astype(jnp.bfloat16)
    every = jnp.dot(values, spread, preferred_element_type=jnp.float32)
    lane = lax.broadcasted_iota(jnp.int32, (tops, pairs), 1)
    k = lax.broadcasted_iota(jnp.int32, (tops, pairs), 0)
    return jnp.sum(jnp.where(lane % tops == k, every, 0.0), axis=0, keepdims=True).astype(jnp.int32)


def key_column(routes_row):
    count = routes_row.shape[1]
    keys = routes_row * count + lax.broadcasted_iota(jnp.int32, (1, count), 1)
    return jnp.broadcast_to(keys.astype(jnp.float32), (8, count)).T[:, 0:1]


def ranks(column, keys):
    total = jnp.zeros(keys.shape, jnp.float32)
    for first in range(0, column.shape[0], 128):
        smaller = jnp.where(column[first : first + 128] < keys, 1.0, 0.0)
        total = total + jnp.sum(smaller, axis=0, keepdims=True)
    return total


def sort_kernel(
    routes_ref,
    grads_ref,
    held_ref,
    starts_ref,
    head_ref,
    order_ref,
    piece_ref,
    sems,
):
    width = piece_ref.shape[1]
    count = sems.shape[0]
    part = grads_ref.shape[0] // count
    copies = []
    for n in range(count):
        here = pl.ds(n * part, part)
        copies.append(pltpu.make_async_copy(grads_ref.at[here], held_ref.at[here], sems.at[n]))
    for copy in copies:
        copy.start()
    routes = row_of(routes_ref[...])
    pairs = routes.shape[1]
    column = key_column(routes)
    keys = routes * pairs + lax.broadcasted_iota(jnp.int32, (1, pairs), 1)
    place = ranks(column, keys.astype(jnp.float32)).astype(jnp.int32)
    firsts = lax.broadcasted_iota(jnp.int32, starts_ref.shape, 1) * pairs
    starts = ranks(column, firsts.astype(jnp.float32)).astype(jnp.int32)
    starts_ref[...] = starts
    wide = head_ref.shape[1] - starts.shape[1]
    digits = [starts // DIGIT, starts % DIGIT]
    digits = [jnp.pad(d.astype(jnp.float32), ((0, 0), (0, wide))) for d in digits]
    row = lax.broadcasted_iota(jnp.int32, head_ref.shape, 0)
    head = jnp.where(row == 0, digits[0], jnp.where(row == 1, digits[1], 0.0))
    head_ref[...] = head.astype(jnp.bfloat16)
    rows = piece_ref.shape[0] - ALIGN
    for first in range(0, pairs, rows):
        ids = first + lax.broadcasted_iota(jnp.int32, (rows, pairs), 0)
        order_ref[first : first + rows, :] = jnp.where(place == ids, 1.0, 0.0).astype(jnp.bfloat16)
    for copy in copies:
        copy.wait()
    piece_ref[0:rows, :] = jnp.dot(
        order_ref[0:rows, :],
        held_ref[:, :, columns_of(2, width)].reshape(pairs, width),
        preferred_element_type=jnp.float32,
    ).astype(jnp.bfloat16)
    piece_ref[rows:, :] = head_ref[...]


def weights_kernel(weight_ref, mine_ref, core_ref, stage, sems):
    rows, width = mine_ref.shape
    count = sems.shape[0]
    part = rows // count
    copies = [
        pltpu.make_async_copy(
            weight_ref.at[pl.ds(n * part, part)], stage.at[pl.ds(n * part, part)], sems.at[n]
        )
        for n in range(count)
    ]
    for copy in copies:
        copy.start()
    for copy in copies:
        copy.wait()
    core_ref[...] = stage[:, columns_of(1, width)]
    mine_ref[...] = stage[:, columns_of(0, width)]


def join_kernel(one_ref, two_ref, out_ref):
    half = one_ref.shape[0]
    out_ref[0:half, :] = one_ref[...]
    out_ref[half:, :] = two_ref[...]


def permute_kernel(plan, order_ref, head_ref, grads_ref, *outs):
    pairs, width = order_ref.shape[0], outs[0].shape[1]
    for device in sorted({device for device, _, _ in plan}):
        grads = grads_ref[:, :, columns_of(device, width)].reshape(pairs, width)
        for out, (target, first, rows) in zip(outs, plan):
            if target == device:
                out[0:rows, :] = jnp.dot(
                    order_ref[first : first + rows, :], grads, preferred_element_type=jnp.float32
                ).astype(jnp.bfloat16)
                if out.shape[0] > rows:
                    out[rows:, :] = head_ref[...]


def basis_kernel(
    hidden_ref, proj_ref, segment_ref, routes_ref, out_ref, order_ref, hidden, proj, sems
):
    count = sems.shape[0] - 1
    part = hidden.shape[0] // count
    copies = [pltpu.make_async_copy(proj_ref, proj, sems.at[count])]
    for n in range(count):
        here = pl.ds(n * part, part)
        copies.append(pltpu.make_async_copy(hidden_ref.at[here], hidden.at[here], sems.at[n]))
    for copy in copies:
        copy.start()
    tops, tokens = routes_ref.shape
    pairs = tops * tokens
    column = key_column(row_of(routes_ref[...]))
    at = [
        routes_ref[k : k + 1, :] * pairs + lax.broadcasted_iota(jnp.int32, (1, tokens), 1) * tops + k
        for k in range(tops)
    ]
    place = ranks(column, jnp.concatenate(at, axis=1).astype(jnp.float32)).astype(jnp.int32)
    for first in range(0, pairs, 256):
        ids = first + lax.broadcasted_iota(jnp.int32, (256, pairs), 0)
        order_ref[first : first + 256, :] = jnp.where(place == ids, 1.0, 0.0).astype(jnp.bfloat16)
    segment = (segment_ref[...] - lax.axis_index("expert") * SEG_DEV).astype(jnp.float32)
    segment = jnp.broadcast_to(segment, (8, tokens)).T[:, 0:1]
    for copy in copies:
        copy.wait()
    projected = lax.dot_general(hidden[...], proj[...], NT, preferred_element_type=jnp.float32)
    zero = jnp.zeros_like(projected)
    picked = [jnp.where(segment == float(s), projected, zero) for s in range(SEG_DEV)]
    even = jnp.concatenate([b for p in picked for b in (p, zero)], axis=1)
    odd = jnp.concatenate([b for p in picked for b in (zero, p)], axis=1)
    out_ref[...] = jnp.concatenate([even, odd], axis=0).astype(out_ref.dtype)


def packed(total, first, pairs, rank):
    half = pairs // 2
    low = lax.broadcasted_iota(jnp.int32, (half, LANES), 1) < rank
    one = total[first : first + half, :]
    two = total[first + half : first + pairs, :]
    return jnp.where(low, one + pltpu.roll(one, rank, 1), two + pltpu.roll(two, rank, 1))


def partial_kernel(
    rank, pairs, window, new_tokens, new_units, tasks, fresh, sends, groups, bases_ref, *refs
):
    start_refs = dict(zip(groups, refs))
    refs = refs[len(groups) :]
    token_refs, refs = refs[: len(new_tokens)], refs[len(new_tokens) :]
    unit_refs, refs = refs[: len(new_units)], refs[len(new_units) :]
    if fresh:
        tokens, units, total = refs
        send_refs = ()
        total[...] = jnp.zeros_like(total)
    else:
        tokens, units, total = refs[3:6]
        send_refs = refs[6:]
    for ref, (first, count) in zip(token_refs, new_tokens):
        tokens[first : first + count, :] = ref[0:count, :]
    cols = units.shape[1]
    for ref, place in zip(unit_refs, new_units):
        for half in range(CORES):
            units[place + half] = ref[half * cols : (half + 1) * cols, :]
    held = cols // rank
    per_tile = LANES // rank
    low = lax.broadcasted_iota(jnp.int32, (1, LANES), 1) < rank

    device = lax.axis_index("expert")

    def process(w, members):
        base = bases_ref[device, w]
        heres, offsets = [], []
        for g in members:
            at = jnp.minimum(start_refs[g][0, base] & -ALIGN, pairs - window)
            offsets.append(at)
            heres.append(pl.ds(pl.multiple_of(g * pairs + at, ALIGN), window))
        rows = [tokens[here, :] for here in heres]
        rows = jnp.concatenate(rows, axis=0) if len(rows) > 1 else rows[0]
        dense = lax.dot_general(rows, units[w], NT, preferred_element_type=jnp.float32)
        for n, g in enumerate(members):
            value = total[heres[n], :]
            number = offsets[n] + lax.broadcasted_iota(jnp.int32, (window, LANES), 0)
            for j in range(cols // LANES):
                edge = [start_refs[g][0, base + j * per_tile + i] for i in range(per_tile + 1)]
                inside = (number >= jnp.where(low, edge[0], edge[1])) & (
                    number < jnp.where(low, edge[1], edge[2])
                )
                part = dense[n * window : (n + 1) * window, j * LANES : (j + 1) * LANES]
                value = jnp.where(inside, part, value)
            total[heres[n], :] = value

    for task in tasks:
        if task[0] == "units":
            _, members, first_w, count = task

            def each(i, carry, members=members, first_w=first_w):
                process(first_w + i, members)
                return carry

        else:
            _, member, first_row, end_row, first_w, count = task

            def each(
                i, carry, member=member, first_row=first_row, end_row=end_row, first_w=first_w
            ):
                w = first_w + i
                base = bases_ref[device, w]
                touches = (start_refs[member][0, base] < end_row) & (
                    start_refs[member][0, base + held] > first_row
                )

                @pl.when(touches)
                def _():
                    process(w, [member])

                return carry

        lax.fori_loop(0, count, each, 0)
    for ref, g in zip(send_refs, sends):
        ref[...] = packed(total, g * pairs, pairs, rank).astype(ref.dtype)


def accumulate(
    state, bases, starts, tokens, units, tasks, rank, pairs, window, places=0, sends=(), cost=QUICK
):
    fresh = state is None
    operands = [bases, *starts.values(), *[a for a, _, _ in tokens], *[a for a, _ in units]]
    specs = [SMEM] * (1 + len(starts)) + [VMEM] * (len(tokens) + len(units))
    if fresh:
        width = units[0][0].shape[1]
        shapes = [
            pltpu.VMEM((QUAD * pairs, width), jnp.bfloat16),
            pltpu.VMEM((places, units[0][0].shape[0] // CORES, width), jnp.bfloat16),
            pltpu.VMEM((QUAD * pairs, LANES), jnp.float32),
        ]
        aliases = {}
    else:
        aliases = {len(operands) + i: i for i in range(3)}
        operands += [in_vmem(a) for a in state]
        specs += [VMEM] * 3
        shapes = [pltpu.VMEM(a.shape, a.dtype) for a in state]
    shapes += [pltpu.VMEM((pairs // 2, LANES), jnp.bfloat16)] * len(sends)
    out = pl.pallas_call(
        functools.partial(
            partial_kernel,
            rank,
            pairs,
            window,
            [(first, count) for _, first, count in tokens],
            [p for _, p in units],
            tasks,
            fresh,
            sends,
            list(starts),
        ),
        out_shape=shapes,
        in_specs=specs,
        out_specs=[VMEM] * len(shapes),
        input_output_aliases=aliases,
        compiler_params=pltpu.CompilerParams(vmem_limit_bytes=8 * MIB),
        cost_estimate=cost,
    )(*operands)
    return list(out[:3]), list(out[3:])


def late_kernel(
    rank, pairs, window, place, groups, bases_ref, *refs
):
    start_refs, (tokens, unit_ref), outs = refs[:groups], refs[groups : groups + 2], refs[groups + 2 :]
    cols = unit_ref.shape[0] // CORES
    per_tile = LANES // rank
    low = lax.broadcasted_iota(jnp.int32, (1, LANES), 1) < rank
    device = lax.axis_index("expert")
    first_core = device % CORES == 0
    folded = []
    for half in range(CORES):
        base = bases_ref[device, place + half]
        offsets, rows = [], []
        for g in range(groups):
            at = jnp.minimum(start_refs[g][0, base] & -ALIGN, pairs - window)
            offsets.append(at)
            rows.append(tokens[pl.ds(pl.multiple_of(g * pairs + at, ALIGN), window), :])
        dense = lax.dot_general(
            jnp.concatenate(rows, axis=0),
            unit_ref[half * cols : (half + 1) * cols, :],
            NT,
            preferred_element_type=jnp.float32,
        )
        found = []
        for g in range(groups):
            value = jnp.zeros((window, LANES), jnp.float32)
            number = offsets[g] + lax.broadcasted_iota(jnp.int32, (window, LANES), 0)
            for j in range(cols // LANES):
                edge = [start_refs[g][0, base + j * per_tile + i] for i in range(per_tile + 1)]
                inside = (number >= jnp.where(low, edge[0], edge[1])) & (
                    number < jnp.where(low, edge[1], edge[2])
                )
                part = dense[g * window : (g + 1) * window, j * LANES : (j + 1) * LANES]
                value = jnp.where(inside, part, value)
            found.append(value + pltpu.roll(value, rank, 1))
        folded.append(found)
    for g, out in enumerate(outs):
        one, two = folded[0][g], folded[1][g]
        zero = jnp.where(first_core, one, two)
        other = jnp.where(first_core, two, one)
        out[...] = jnp.where(low, zero, other).astype(out.dtype)


def expand(routes_ref, turned, spread, first, tiles):
    tops, tokens = routes_ref.shape
    rank = turned.shape[0]

    def one(tile, carry):
        here = pl.multiple_of(tile * 8, 8)
        ids = first + here + lax.broadcasted_iota(jnp.int32, (8, tokens), 0)
        masks = [routes_ref[k : k + 1, :] == ids for k in range(tops)]
        for r in range(rank):
            value = jnp.zeros((8, tokens), jnp.float32)
            for k in range(tops):
                row = turned[r : r + 1, k * tokens : (k + 1) * tokens]
                value = jnp.where(masks[k], row, value)
            spread[r, pl.ds(here, 8), :] = value
        return carry

    lax.fori_loop(0, tiles, one, 0)


def blocks_kernel(
    rank, routes_ref, basis_ref, order_ref, total_ref, b_ref, c_ref, d_ref, out_ref, turned, spread
):
    half = b_ref.shape[0]
    value = packed(total_ref, 0, 2 * half, rank)
    for ref in (b_ref, c_ref, d_ref):
        value = value + ref[...].astype(jnp.float32)
    value = value.T
    value = jnp.concatenate([value[0:rank], value[rank : 2 * rank]], axis=1).astype(jnp.bfloat16)
    turned[...] = jnp.dot(value, order_ref[...], preferred_element_type=jnp.float32)
    experts = out_ref.shape[1]
    expand(routes_ref, turned, spread, 0, experts // 8)
    for pair in range(rank // 2):
        both = jnp.concatenate([spread[2 * pair], spread[2 * pair + 1]], axis=1)
        block = jnp.dot(
            both.astype(jnp.bfloat16), basis_ref[...], preferred_element_type=jnp.float32
        ).astype(jnp.bfloat16)
        for s in range(SEG_DEV):
            out_ref[s, :, pl.ds(pair * 2 * rank, 2 * rank)] = block[
                :, s * 2 * rank : (s + 1) * 2 * rank
            ]


def last_kernel(
    rank,
    place,
    count,
    held,
    bases_ref,
    starts_ref,
    routes_ref,
    basis_ref,
    order_ref,
    turned_ref,
    own_ref,
    b_ref,
    c_ref,
    d_ref,
    _,
    out_ref,
    turned,
    spread,
    block,
    sem,
):
    window = own_ref.shape[0]
    pairs = order_ref.shape[0]
    value = own_ref[...]
    for ref in (b_ref, c_ref, d_ref):
        value = value + ref[...].astype(jnp.float32)
    value = value.T.astype(jnp.bfloat16)
    first = bases_ref[lax.axis_index("expert"), place] // count * count
    unit = bases_ref[lax.axis_index("expert"), place] // (CORES * held) * (CORES * held)
    total = turned_ref[...]
    for core in range(CORES):
        at = jnp.minimum(starts_ref[0, unit + core * held] & -ALIGN, pairs - window)
        rows = order_ref[pl.ds(pl.multiple_of(at, ALIGN), window), :]
        total = total + jnp.dot(
            value[core * rank : (core + 1) * rank], rows, preferred_element_type=jnp.float32
        )
    turned[...] = total
    expand(routes_ref, turned, spread, first, count // 8)
    lines = [
        jnp.concatenate([spread[2 * pair], spread[2 * pair + 1]], axis=1) for pair in range(rank // 2)
    ]
    made = jnp.dot(
        jnp.concatenate(lines, axis=0).astype(jnp.bfloat16),
        basis_ref[...],
        preferred_element_type=jnp.float32,
    ).astype(jnp.bfloat16)
    for pair in range(rank // 2):
        for s in range(SEG_DEV):
            block[s, :, pl.ds(pair * 2 * rank, 2 * rank)] = made[
                pair * count : (pair + 1) * count, s * 2 * rank : (s + 1) * 2 * rank
            ]
    copy = pltpu.make_async_copy(
        block, out_ref.at[:, pl.ds(pl.multiple_of(first, count), count), :], sem
    )
    copy.start()
    copy.wait()


def local(hidden_in, out_grads, routes, segments, in_proj, out_proj):
    tokens, tops = routes.shape
    exp_here, rank, width = out_proj.shape
    owners, groups = lax.axis_size("expert"), lax.axis_size("groups")
    experts = exp_here * owners
    pairs = tokens * tops
    capacity = max(2, 3 * pairs // (2 * experts))
    window = min(pairs, -(-(exp_here * capacity + ALIGN - 1) // ALIGN) * ALIGN)
    quarter = width // QUAD
    cols = exp_here * rank
    rows = pairs // PIECES
    index = lax.axis_index("expert")
    slots = owners // CORES // 2
    ring = [0, *range(1, slots, 2), *range((slots - 1) // 2 * 2, 0, -2)]
    following = {a: b for a, b in zip(ring, ring[1:] + ring[:1])}
    before = {b: a for a, b in following.items()}

    def swap(array, side, bit):
        table = [
            (g * owners + e, (g ^ side) * owners + (e ^ bit))
            for g in range(groups)
            for e in range(owners)
        ]
        return lax.ppermute(array, BOTH, table)

    def along(array, table):
        wide = 2 * CORES
        pairs_of = [(e, table[e // wide] * wide + e % wide) for e in range(owners)]
        return lax.ppermute(array, "expert", pairs_of)

    def tie(*arrays):
        return lax.optimization_barrier(arrays)

    final = slots - 1
    first_names = [(n, 0) for n in range(final)] + [(n, 1) for n in range(final - 1)]
    arrival = first_names + [(final - 1, 1), (final, 1), (final, 0)]

    def source(z, hops):
        for _ in range(hops):
            z = before[z]
        return z

    rows_of = [
        [
            ((source(e // (2 * CORES), n) * 2 + (e // CORES % 2 ^ y)) * CORES + (e % CORES ^ c)) * exp_here
            for n, y in arrival
            for c in range(CORES)
        ]
        for e in range(owners)
    ]
    places = CORES * len(arrival)
    bases = jnp.asarray(np.array(rows_of, np.int32))

    unit_shape = pltpu.VMEM((cols, quarter), jnp.bfloat16)
    order_shape = pltpu.VMEM((pairs, pairs), jnp.bfloat16)

    def rows_shape(count):
        return pltpu.VMEM((count, quarter), jnp.bfloat16)

    mine_unit, core_unit = pl.pallas_call(
        weights_kernel,
        out_shape=[unit_shape, unit_shape],
        in_specs=[HBM],
        out_specs=[VMEM] * 2,
        scratch_shapes=[pltpu.VMEM((cols, width), jnp.bfloat16), pltpu.SemaphoreType.DMA((4,))],
        compiler_params=pltpu.CompilerParams(vmem_limit_bytes=8 * MIB),
        cost_estimate=QUICK,
    )(in_hbm(out_proj.reshape(cols, width)))
    other_unit = swap(core_unit, 0, 1)
    by_rank, _ = tie(routes.T, core_unit)
    edges = -(-(experts + 1) // LANES) * LANES
    held_grads, own_starts, head, order, first_piece = pl.pallas_call(
        sort_kernel,
        out_shape=[
            pltpu.VMEM(out_grads.shape, jnp.bfloat16),
            jax.ShapeDtypeStruct((1, edges), jnp.int32),
            rows_shape(ALIGN),
            order_shape,
            rows_shape(2 * rows + ALIGN),
        ],
        in_specs=[VMEM, HBM],
        out_specs=[VMEM] * 5,
        scratch_shapes=[pltpu.SemaphoreType.DMA((8,))],
        compiler_params=pltpu.CompilerParams(vmem_limit_bytes=12 * MIB),
        cost_estimate=QUICK,
    )(by_rank, in_hbm(out_grads))

    *joined, order = tie(mine_unit, other_unit, order)
    unit = pl.pallas_call(
        join_kernel,
        out_shape=pltpu.VMEM((CORES * cols, quarter), jnp.bfloat16),
        in_specs=[VMEM] * 2,
        out_specs=VMEM,
        compiler_params=pltpu.CompilerParams(vmem_limit_bytes=4 * MIB),
        cost_estimate=QUICK,
    )(*joined)
    held = {(0, 0): unit, (1, 0): along(unit, following), (0, 1): swap(unit, 0, CORES)}

    def permuted(plan, headed, *after):
        held, *_ = tie(order, *after)
        return pl.pallas_call(
            functools.partial(permute_kernel, plan),
            out_shape=[
                rows_shape(many + (ALIGN if n in headed else 0))
                for n, (_, _, many) in enumerate(plan)
            ],
            in_specs=[VMEM] * 3,
            out_specs=[VMEM] * len(plan),
            compiler_params=pltpu.CompilerParams(vmem_limit_bytes=12 * MIB),
            cost_estimate=QUICK,
        )(in_vmem(held), head, in_vmem(held_grads))

    def starts_in(block, count):
        digits = block[count : count + 2, :edges].astype(jnp.int32)
        return (digits[0] * DIGIT + digits[1]).reshape(1, edges)

    side_pieces = [swap(first_piece, 1, 0)]
    (second_piece,) = permuted([(2, 2 * rows, 2 * rows)], [], unit)
    own_tokens, *for_core = permuted(
        [(0, 0, pairs), (1, 0, 2 * rows), (1, 2 * rows, 2 * rows)], [1], second_piece
    )
    third_piece, last_piece = permuted(
        [(3, 0, 3 * rows), (3, 3 * rows, rows)], [0], own_tokens
    )
    from_core = [swap(piece, 0, 1) for piece in for_core]
    side_pieces.append(swap(second_piece, 1, 0))
    third_piece, last_piece, side_pieces[0] = tie(third_piece, last_piece, side_pieces[0])
    diagonal_pieces = [swap(third_piece, 1, 1), swap(last_piece, 1, 1)]
    local_segments, *_ = tie(segments, last_piece)
    basis, order_back = pl.pallas_call(
        basis_kernel,
        out_shape=[
            pltpu.VMEM((2 * tokens, SEG_DEV * 2 * rank), jnp.bfloat16),
            order_shape,
        ],
        in_specs=[HBM, HBM, VMEM, VMEM],
        out_specs=[VMEM] * 2,
        scratch_shapes=[
            pltpu.VMEM(hidden_in.shape, jnp.bfloat16),
            pltpu.VMEM(in_proj.shape, jnp.bfloat16),
            pltpu.SemaphoreType.DMA((5,)),
        ],
        compiler_params=pltpu.CompilerParams(vmem_limit_bytes=12 * MIB),
        cost_estimate=QUICK,
    )(in_hbm(hidden_in), in_hbm(in_proj), local_segments.reshape(1, tokens), by_rank)

    call = functools.partial(
        accumulate, bases=bases, rank=rank, pairs=pairs, window=window, places=places
    )
    place_of = {name: CORES * n for n, name in enumerate(arrival)}
    starts = {0: own_starts}
    members = []
    known_units = 0
    state = None

    def work(names, complete=(), partial=(), sends=(), cost=QUICK):
        nonlocal state, known_units
        tasks, arrived = [], []
        for group, blocks in complete:
            first = 0
            for piece, count in blocks:
                arrived.append((piece, group * pairs + first, count))
                first += count
            if group:
                starts[group] = starts_in(*blocks[0])
            members.append(group)
        if names:
            tasks.append(("units", list(members), known_units, CORES * len(names)))
        known_units += CORES * len(names)
        for group, piece, first, count in partial:
            arrived.append((piece, group * pairs + first, count))
            if first == 0:
                starts[group] = starts_in(piece, count)
                members.append(group)
            tasks.append(("piece", group, first, first + count, 0, known_units))
        state, out = call(
            state,
            starts=starts,
            tokens=arrived,
            units=[(held[n], place_of[n]) for n in names],
            tasks=tasks,
            sends=sends,
            cost=cost,
        )
        return out

    for n in range(1, slots):
        if n == final:
            break
        tied = [held[n, 0], held[n - 1, 1]]
        if n == 1:
            tied.append(side_pieces[0])
        if n == final - 1:
            tied += [basis, order_back]
        held[n, 0], held[n - 1, 1], *tied = tie(*tied)
        if n == 1:
            side_pieces[0], *tied = tied
        if n == final - 1:
            basis, order_back = tied
            half = 2 * rows
            work(
                first_names,
                complete=[
                    (0, [(own_tokens, pairs)]),
                    (1, [(piece, half) for piece in from_core]),
                    (2, [(piece, half) for piece in side_pieces]),
                ],
            )
        held[n + 1, 0] = along(held[n, 0], following)
        held[n, 1] = swap(held[n, 0], 0, CORES)
    held[final, 1] = along(held[0, 1], before)

    work([(final - 1, 1)], partial=[(3, diagonal_pieces[0], 0, 3 * rows)])
    sent = work(
        [(final, 1)], partial=[(3, diagonal_pieces[1], 3 * rows, rows)], sends=[1, 2, 3], cost=SHORT
    )

    def returned(arrays):
        return [
            swap(array, side, bit) for array, (side, bit) in zip(arrays, ((0, 1), (1, 0), (1, 1)))
        ]

    early = returned(sent)
    place = places - CORES
    own_late, *sent = pl.pallas_call(
        functools.partial(late_kernel, rank, pairs, window, place, QUAD),
        out_shape=[pltpu.VMEM((window, LANES), jnp.float32)]
        + [pltpu.VMEM((window, LANES), jnp.bfloat16)] * (QUAD - 1),
        in_specs=[SMEM] * (1 + QUAD) + [VMEM] * 2,
        out_specs=[VMEM] * QUAD,
        compiler_params=pltpu.CompilerParams(vmem_limit_bytes=8 * MIB),
        cost_estimate=QUICK,
    )(bases, *[starts[g] for g in range(QUAD)], in_vmem(state[0]), held[final, 0])
    late = returned(sent)
    *early, own_late = tie(*early, own_late)
    out, turned = pl.pallas_call(
        functools.partial(blocks_kernel, rank),
        out_shape=[
            jax.ShapeDtypeStruct((SEG_DEV, experts, rank * rank), jnp.bfloat16),
            pltpu.VMEM((rank, pairs), jnp.float32),
        ],
        in_specs=[VMEM] * 7,
        out_specs=[VMEM] * 2,
        scratch_shapes=[pltpu.VMEM((rank, experts, tokens), jnp.float32)],
        compiler_params=pltpu.CompilerParams(vmem_limit_bytes=32 * MIB),
        cost_estimate=QUICK,
    )(by_rank, basis, in_vmem(order_back), in_vmem(state[2]), *early)
    count = 2 * CORES * exp_here
    return pl.pallas_call(
        functools.partial(last_kernel, rank, place, count, exp_here),
        out_shape=jax.ShapeDtypeStruct(out.shape, out.dtype),
        in_specs=[SMEM] * 2 + [VMEM] * 8 + [HBM],
        out_specs=HBM,
        scratch_shapes=[
            pltpu.VMEM((rank, pairs), jnp.float32),
            pltpu.VMEM((rank, count, tokens), jnp.float32),
            pltpu.VMEM((SEG_DEV, count, rank * rank), jnp.bfloat16),
            pltpu.SemaphoreType.DMA,
        ],
        input_output_aliases={10: 0},
        compiler_params=pltpu.CompilerParams(vmem_limit_bytes=16 * MIB),
        cost_estimate=QUICK,
    )(bases, own_starts, by_rank, basis, in_vmem(order_back), in_vmem(turned), own_late, *late, out)


def solution(mesh):
    placed = (
        P(("groups", "expert"), None),
        P(("groups", "expert"), None, None),
        P(("groups", "expert"), None),
        P(("groups", "expert")),
        P(),
        P("expert", None, None),
    )
    return jax.shard_map(
        local,
        mesh=mesh,
        in_specs=placed,
        out_specs=P(("groups", "expert"), None, None),
        check_vma=False,
    )
```

```python
import functools

import jax
import jax.numpy as jnp
import numpy as np
from jax import lax
from jax.experimental import pallas as pl
from jax.experimental.pallas import tpu as pltpu
from jax.sharding import PartitionSpec as P

SEG_DEV = 2
O = {'p1': 'core_unit', 'z1': 'none', 'p2': 'unit', 'cores': 2, 'core_in': 'none', 'y0': 'unit', 'basis': [], 'ev1': ['y0', 'side0'], 'diag': ['side0'], 'ev2': ['basis'], 'w': ['core'], 'last': ['z2'], 'ka': 0, 'z3_ka': 0, 'w_ka': 1, 'k0': 0, 'k1': 0, 'k2': 1, 'order': 'w'}
CORES = 2
SIDES = 2
QUAD = 4
PIECES = 4
LANES = 128
ALIGN = 16
DIGIT = 32
BOTH = ("groups", "expert")
MIB = 1024 * 1024
VMEM = pl.BlockSpec(memory_space=pltpu.VMEM)
SMEM = pl.BlockSpec(memory_space=pltpu.SMEM)
HBM = pl.BlockSpec(memory_space=pl.ANY)
QUICK = pl.CostEstimate(flops=1, bytes_accessed=1, transcendentals=0)
SHORT = pl.CostEstimate(flops=10**9, bytes_accessed=1, transcendentals=0)
NT = (((1,), (1,)), ((), ()))


def in_vmem(array):
    return pltpu.with_memory_space_constraint(array, pltpu.VMEM)


def in_hbm(array):
    return pltpu.with_memory_space_constraint(array, pltpu.HBM)


def place_in_quad(flip):
    side, core = lax.axis_index("groups") % SIDES, lax.axis_index("expert") % CORES
    return (side ^ (flip // CORES)) * CORES + (core ^ (flip % CORES))


def columns_of(flip, width):
    return pl.ds(pl.multiple_of(place_in_quad(flip) * width, width), width)


def row_of(routes):
    tops, tokens = routes.shape
    pairs = tops * tokens
    lane = lax.broadcasted_iota(jnp.int32, (tokens, pairs), 1)
    token = lax.broadcasted_iota(jnp.int32, (tokens, pairs), 0)
    spread = jnp.where(lane // tops == token, 1.0, 0.0).astype(jnp.bfloat16)
    values = routes.astype(jnp.float32).astype(jnp.bfloat16)
    every = jnp.dot(values, spread, preferred_element_type=jnp.float32)
    lane = lax.broadcasted_iota(jnp.int32, (tops, pairs), 1)
    k = lax.broadcasted_iota(jnp.int32, (tops, pairs), 0)
    return jnp.sum(jnp.where(lane % tops == k, every, 0.0), axis=0, keepdims=True).astype(jnp.int32)


def key_column(routes_row):
    count = routes_row.shape[1]
    keys = routes_row * count + lax.broadcasted_iota(jnp.int32, (1, count), 1)
    return jnp.broadcast_to(keys.astype(jnp.float32), (8, count)).T[:, 0:1]


def ranks(column, keys):
    total = jnp.zeros(keys.shape, jnp.float32)
    for first in range(0, column.shape[0], 128):
        smaller = jnp.where(column[first : first + 128] < keys, 1.0, 0.0)
        total = total + jnp.sum(smaller, axis=0, keepdims=True)
    return total


def sort_kernel(
    routes_ref,
    grads_ref,
    held_ref,
    starts_ref,
    head_ref,
    order_ref,
    piece_ref,
    sems,
):
    width = piece_ref.shape[1]
    count = sems.shape[0]
    part = grads_ref.shape[0] // count
    copies = []
    for n in range(count):
        here = pl.ds(n * part, part)
        copies.append(pltpu.make_async_copy(grads_ref.at[here], held_ref.at[here], sems.at[n]))
    for copy in copies:
        copy.start()
    routes = row_of(routes_ref[...])
    pairs = routes.shape[1]
    column = key_column(routes)
    keys = routes * pairs + lax.broadcasted_iota(jnp.int32, (1, pairs), 1)
    place = ranks(column, keys.astype(jnp.float32)).astype(jnp.int32)
    firsts = lax.broadcasted_iota(jnp.int32, starts_ref.shape, 1) * pairs
    starts = ranks(column, firsts.astype(jnp.float32)).astype(jnp.int32)
    starts_ref[...] = starts
    wide = head_ref.shape[1] - starts.shape[1]
    digits = [starts // DIGIT, starts % DIGIT]
    digits = [jnp.pad(d.astype(jnp.float32), ((0, 0), (0, wide))) for d in digits]
    row = lax.broadcasted_iota(jnp.int32, head_ref.shape, 0)
    head = jnp.where(row == 0, digits[0], jnp.where(row == 1, digits[1], 0.0))
    head_ref[...] = head.astype(jnp.bfloat16)
    rows = piece_ref.shape[0] - ALIGN
    for first in range(0, pairs, rows):
        ids = first + lax.broadcasted_iota(jnp.int32, (rows, pairs), 0)
        order_ref[first : first + rows, :] = jnp.where(place == ids, 1.0, 0.0).astype(jnp.bfloat16)
    for copy in copies:
        copy.wait()
    piece_ref[0:rows, :] = jnp.dot(
        order_ref[0:rows, :],
        held_ref[:, :, columns_of(2, width)].reshape(pairs, width),
        preferred_element_type=jnp.float32,
    ).astype(jnp.bfloat16)
    piece_ref[rows:, :] = head_ref[...]


def weights_kernel(weight_ref, mine_ref, core_ref, stage, sems):
    rows, width = mine_ref.shape
    count = sems.shape[0]
    part = rows // count
    copies = [
        pltpu.make_async_copy(
            weight_ref.at[pl.ds(n * part, part)], stage.at[pl.ds(n * part, part)], sems.at[n]
        )
        for n in range(count)
    ]
    for copy in copies:
        copy.start()
    for copy in copies:
        copy.wait()
    core_ref[...] = stage[:, columns_of(1, width)]
    mine_ref[...] = stage[:, columns_of(0, width)]


def join_kernel(one_ref, two_ref, out_ref):
    half = one_ref.shape[0]
    out_ref[0:half, :] = one_ref[...]
    out_ref[half:, :] = two_ref[...]


def permute_kernel(plan, order_ref, head_ref, grads_ref, *outs):
    pairs, width = order_ref.shape[0], outs[0].shape[1]
    for device in sorted({device for device, _, _ in plan}):
        grads = grads_ref[:, :, columns_of(device, width)].reshape(pairs, width)
        for out, (target, first, rows) in zip(outs, plan):
            if target == device:
                out[0:rows, :] = jnp.dot(
                    order_ref[first : first + rows, :], grads, preferred_element_type=jnp.float32
                ).astype(jnp.bfloat16)
                if out.shape[0] > rows:
                    out[rows:, :] = head_ref[...]


def basis_kernel(
    hidden_ref, proj_ref, segment_ref, routes_ref, out_ref, order_ref, hidden, proj, sems
):
    count = sems.shape[0] - 1
    part = hidden.shape[0] // count
    copies = [pltpu.make_async_copy(proj_ref, proj, sems.at[count])]
    for n in range(count):
        here = pl.ds(n * part, part)
        copies.append(pltpu.make_async_copy(hidden_ref.at[here], hidden.at[here], sems.at[n]))
    for copy in copies:
        copy.start()
    tops, tokens = routes_ref.shape
    pairs = tops * tokens
    column = key_column(row_of(routes_ref[...]))
    at = [
        routes_ref[k : k + 1, :] * pairs + lax.broadcasted_iota(jnp.int32, (1, tokens), 1) * tops + k
        for k in range(tops)
    ]
    place = ranks(column, jnp.concatenate(at, axis=1).astype(jnp.float32)).astype(jnp.int32)
    for first in range(0, pairs, 256):
        ids = first + lax.broadcasted_iota(jnp.int32, (256, pairs), 0)
        order_ref[first : first + 256, :] = jnp.where(place == ids, 1.0, 0.0).astype(jnp.bfloat16)
    segment = (segment_ref[...] - lax.axis_index("expert") * SEG_DEV).astype(jnp.float32)
    segment = jnp.broadcast_to(segment, (8, tokens)).T[:, 0:1]
    for copy in copies:
        copy.wait()
    projected = lax.dot_general(hidden[...], proj[...], NT, preferred_element_type=jnp.float32)
    zero = jnp.zeros_like(projected)
    picked = [jnp.where(segment == float(s), projected, zero) for s in range(SEG_DEV)]
    even = jnp.concatenate([b for p in picked for b in (p, zero)], axis=1)
    odd = jnp.concatenate([b for p in picked for b in (zero, p)], axis=1)
    out_ref[...] = jnp.concatenate([even, odd], axis=0).astype(out_ref.dtype)


def packed(total, first, pairs, rank):
    half = pairs // 2
    low = lax.broadcasted_iota(jnp.int32, (half, LANES), 1) < rank
    one = total[first : first + half, :]
    two = total[first + half : first + pairs, :]
    return jnp.where(low, one + pltpu.roll(one, rank, 1), two + pltpu.roll(two, rank, 1))


def partial_kernel(
    rank, pairs, window, new_tokens, new_units, tasks, fresh, sends, groups, bases_ref, *refs
):
    start_refs = dict(zip(groups, refs))
    refs = refs[len(groups) :]
    token_refs, refs = refs[: len(new_tokens)], refs[len(new_tokens) :]
    unit_refs, refs = refs[: len(new_units)], refs[len(new_units) :]
    if fresh:
        tokens, units, total = refs
        send_refs = ()
        total[...] = jnp.zeros_like(total)
    else:
        tokens, units, total = refs[3:6]
        send_refs = refs[6:]
    for ref, (first, count) in zip(token_refs, new_tokens):
        tokens[first : first + count, :] = ref[0:count, :]
    cols = units.shape[1]
    for ref, place in zip(unit_refs, new_units):
        for half in range(CORES):
            units[place + half] = ref[half * cols : (half + 1) * cols, :]
    held = cols // rank
    per_tile = LANES // rank
    low = lax.broadcasted_iota(jnp.int32, (1, LANES), 1) < rank

    device = lax.axis_index("expert")

    def process(w, members):
        base = bases_ref[device, w]
        heres, offsets = [], []
        for g in members:
            at = jnp.minimum(start_refs[g][0, base] & -ALIGN, pairs - window)
            offsets.append(at)
            heres.append(pl.ds(pl.multiple_of(g * pairs + at, ALIGN), window))
        rows = [tokens[here, :] for here in heres]
        rows = jnp.concatenate(rows, axis=0) if len(rows) > 1 else rows[0]
        dense = lax.dot_general(rows, units[w], NT, preferred_element_type=jnp.float32)
        for n, g in enumerate(members):
            value = total[heres[n], :]
            number = offsets[n] + lax.broadcasted_iota(jnp.int32, (window, LANES), 0)
            for j in range(cols // LANES):
                edge = [start_refs[g][0, base + j * per_tile + i] for i in range(per_tile + 1)]
                inside = (number >= jnp.where(low, edge[0], edge[1])) & (
                    number < jnp.where(low, edge[1], edge[2])
                )
                part = dense[n * window : (n + 1) * window, j * LANES : (j + 1) * LANES]
                value = jnp.where(inside, part, value)
            total[heres[n], :] = value

    for task in tasks:
        if task[0] == "units":
            _, members, first_w, count = task

            def each(i, carry, members=members, first_w=first_w):
                process(first_w + i, members)
                return carry

        else:
            _, member, first_row, end_row, first_w, count = task

            def each(
                i, carry, member=member, first_row=first_row, end_row=end_row, first_w=first_w
            ):
                w = first_w + i
                base = bases_ref[device, w]
                touches = (start_refs[member][0, base] < end_row) & (
                    start_refs[member][0, base + held] > first_row
                )

                @pl.when(touches)
                def _():
                    process(w, [member])

                return carry

        lax.fori_loop(0, count, each, 0)
    for ref, g in zip(send_refs, sends):
        ref[...] = packed(total, g * pairs, pairs, rank).astype(ref.dtype)


def accumulate(
    state, bases, starts, tokens, units, tasks, rank, pairs, window, places=0, sends=(), cost=QUICK
):
    fresh = state is None
    operands = [bases, *starts.values(), *[a for a, _, _ in tokens], *[a for a, _ in units]]
    specs = [SMEM] * (1 + len(starts)) + [VMEM] * (len(tokens) + len(units))
    if fresh:
        width = units[0][0].shape[1]
        shapes = [
            pltpu.VMEM((QUAD * pairs, width), jnp.bfloat16),
            pltpu.VMEM((places, units[0][0].shape[0] // CORES, width), jnp.bfloat16),
            pltpu.VMEM((QUAD * pairs, LANES), jnp.float32),
        ]
        aliases = {}
    else:
        aliases = {len(operands) + i: i for i in range(3)}
        operands += [in_vmem(a) for a in state]
        specs += [VMEM] * 3
        shapes = [pltpu.VMEM(a.shape, a.dtype) for a in state]
    shapes += [pltpu.VMEM((pairs // 2, LANES), jnp.bfloat16)] * len(sends)
    out = pl.pallas_call(
        functools.partial(
            partial_kernel,
            rank,
            pairs,
            window,
            [(first, count) for _, first, count in tokens],
            [p for _, p in units],
            tasks,
            fresh,
            sends,
            list(starts),
        ),
        out_shape=shapes,
        in_specs=specs,
        out_specs=[VMEM] * len(shapes),
        input_output_aliases=aliases,
        compiler_params=pltpu.CompilerParams(vmem_limit_bytes=8 * MIB),
        cost_estimate=cost,
    )(*operands)
    return list(out[:3]), list(out[3:])


def late_kernel(
    rank, pairs, window, place, groups, bases_ref, *refs
):
    start_refs, (tokens, unit_ref), outs = refs[:groups], refs[groups : groups + 2], refs[groups + 2 :]
    cols = unit_ref.shape[0] // CORES
    per_tile = LANES // rank
    low = lax.broadcasted_iota(jnp.int32, (1, LANES), 1) < rank
    device = lax.axis_index("expert")
    first_core = device % CORES == 0
    folded = []
    for half in range(CORES):
        base = bases_ref[device, place + half]
        offsets, rows = [], []
        for g in range(groups):
            at = jnp.minimum(start_refs[g][0, base] & -ALIGN, pairs - window)
            offsets.append(at)
            rows.append(tokens[pl.ds(pl.multiple_of(g * pairs + at, ALIGN), window), :])
        dense = lax.dot_general(
            jnp.concatenate(rows, axis=0),
            unit_ref[half * cols : (half + 1) * cols, :],
            NT,
            preferred_element_type=jnp.float32,
        )
        found = []
        for g in range(groups):
            value = jnp.zeros((window, LANES), jnp.float32)
            number = offsets[g] + lax.broadcasted_iota(jnp.int32, (window, LANES), 0)
            for j in range(cols // LANES):
                edge = [start_refs[g][0, base + j * per_tile + i] for i in range(per_tile + 1)]
                inside = (number >= jnp.where(low, edge[0], edge[1])) & (
                    number < jnp.where(low, edge[1], edge[2])
                )
                part = dense[g * window : (g + 1) * window, j * LANES : (j + 1) * LANES]
                value = jnp.where(inside, part, value)
            found.append(value + pltpu.roll(value, rank, 1))
        folded.append(found)
    for g, out in enumerate(outs):
        one, two = folded[0][g], folded[1][g]
        zero = jnp.where(first_core, one, two)
        other = jnp.where(first_core, two, one)
        out[...] = jnp.where(low, zero, other).astype(out.dtype)


def expand(routes_ref, turned, lines, first, tiles):
    tops, tokens = routes_ref.shape
    rank = turned.shape[0]

    def one(tile, carry):
        here = pl.multiple_of(tile * 8, 8)
        ids = first + here + lax.broadcasted_iota(jnp.int32, (8, tokens), 0)
        masks = [routes_ref[k : k + 1, :] == ids for k in range(tops)]
        for r in range(rank):
            value = jnp.zeros((8, tokens), jnp.float32)
            for k in range(tops):
                row = turned[r : r + 1, k * tokens : (k + 1) * tokens]
                value = jnp.where(masks[k], row, value)
            side = r % 2 * tokens
            lines[r // 2, pl.ds(here, 8), side : side + tokens] = value
        return carry

    lax.fori_loop(0, tiles, one, 0)


def form(lines, basis_ref, first, count, out_ref, rank):
    experts, width = lines.shape[1:]
    made = jnp.dot(
        lines[first : first + count].reshape(count * experts, width).astype(jnp.bfloat16),
        basis_ref[...],
        preferred_element_type=jnp.float32,
    ).astype(jnp.bfloat16)
    for pair in range(count):
        for s in range(SEG_DEV):
            out_ref[s, :, pl.ds((first + pair) * 2 * rank, 2 * rank)] = made[
                pair * experts : (pair + 1) * experts, s * 2 * rank : (s + 1) * 2 * rank
            ]


def blocks_kernel(
    rank, routes_ref, basis_ref, order_ref, total_ref, b_ref, c_ref, d_ref, out_ref, turned, lines
):
    half = b_ref.shape[0]
    value = packed(total_ref, 0, 2 * half, rank)
    for ref in (b_ref, c_ref, d_ref):
        value = value + ref[...].astype(jnp.float32)
    value = value.T
    value = jnp.concatenate([value[0:rank], value[rank : 2 * rank]], axis=1).astype(jnp.bfloat16)
    turned[...] = jnp.dot(value, order_ref[...], preferred_element_type=jnp.float32)
    expand(routes_ref, turned, lines, 0, lines.shape[1] // 8)
    for first in range(0, rank // 2, 8):
        form(lines, basis_ref, first, 8, out_ref, rank)


def last_kernel(
    rank,
    place,
    count,
    held,
    bases_ref,
    starts_ref,
    routes_ref,
    basis_ref,
    order_ref,
    turned_ref,
    own_ref,
    b_ref,
    c_ref,
    d_ref,
    _,
    out_ref,
    turned,
    lines,
    block,
    sem,
):
    window = own_ref.shape[0]
    pairs = order_ref.shape[0]
    value = own_ref[...]
    for ref in (b_ref, c_ref, d_ref):
        value = value + ref[...].astype(jnp.float32)
    value = value.T.astype(jnp.bfloat16)
    first = bases_ref[lax.axis_index("expert"), place] // count * count
    unit = bases_ref[lax.axis_index("expert"), place] // (CORES * held) * (CORES * held)
    total = turned_ref[...]
    for core in range(CORES):
        at = jnp.minimum(starts_ref[0, unit + core * held] & -ALIGN, pairs - window)
        rows = order_ref[pl.ds(pl.multiple_of(at, ALIGN), window), :]
        total = total + jnp.dot(
            value[core * rank : (core + 1) * rank], rows, preferred_element_type=jnp.float32
        )
    turned[...] = total
    expand(routes_ref, turned, lines, first, count // 8)
    form(lines, basis_ref, 0, rank // 2, block, rank)
    copy = pltpu.make_async_copy(
        block, out_ref.at[:, pl.ds(pl.multiple_of(first, count), count), :], sem
    )
    copy.start()
    copy.wait()


def local(hidden_in, out_grads, routes, segments, in_proj, out_proj):
    tokens, tops = routes.shape
    exp_here, rank, width = out_proj.shape
    owners, groups = lax.axis_size("expert"), lax.axis_size("groups")
    experts = exp_here * owners
    pairs = tokens * tops
    capacity = max(2, 3 * pairs // (2 * experts))
    window = min(pairs, -(-(exp_here * capacity + ALIGN - 1) // ALIGN) * ALIGN)
    quarter = width // QUAD
    cols = exp_here * rank
    rows = pairs // PIECES
    index = lax.axis_index("expert")
    slots = owners // CORES // 2
    ring = [0, *range(1, slots, 2), *range((slots - 1) // 2 * 2, 0, -2)]
    following = {a: b for a, b in zip(ring, ring[1:] + ring[:1])}
    before = {b: a for a, b in following.items()}

    def swap(array, side, bit):
        table = [
            (g * owners + e, (g ^ side) * owners + (e ^ bit))
            for g in range(groups)
            for e in range(owners)
        ]
        return lax.ppermute(array, BOTH, table)

    def along(array, table):
        wide = 2 * CORES
        pairs_of = [(e, table[e // wide] * wide + e % wide) for e in range(owners)]
        return lax.ppermute(array, "expert", pairs_of)

    def tie(*arrays):
        return lax.optimization_barrier(arrays)

    final = slots - 1
    names_a = [(n, 0) for n in range(final - 1)] + [(0, 1)]
    names_b = [(final - 1, 0)] + [(n, 1) for n in range(1, final - 1)]
    names_c = [(final, 1)] if O["order"] == "w" else [(final - 1, 1)]
    names_d = [(final - 1, 1)] if O["order"] == "w" else [(final, 1)]
    arrival = names_a + names_b + names_c + names_d + [(final, 0)]

    def source(z, hops):
        for _ in range(hops):
            z = before[z]
        return z

    rows_of = [
        [
            ((source(e // (2 * CORES), n) * 2 + (e // CORES % 2 ^ y)) * CORES + (e % CORES ^ c)) * exp_here
            for n, y in arrival
            for c in range(CORES)
        ]
        for e in range(owners)
    ]
    places = CORES * len(arrival)
    bases = jnp.asarray(np.array(rows_of, np.int32))

    unit_shape = pltpu.VMEM((cols, quarter), jnp.bfloat16)
    order_shape = pltpu.VMEM((pairs, pairs), jnp.bfloat16)

    def rows_shape(count):
        return pltpu.VMEM((count, quarter), jnp.bfloat16)

    mine_unit, core_unit = pl.pallas_call(
        weights_kernel,
        out_shape=[unit_shape, unit_shape],
        in_specs=[HBM],
        out_specs=[VMEM] * 2,
        scratch_shapes=[pltpu.VMEM((cols, width), jnp.bfloat16), pltpu.SemaphoreType.DMA((4,))],
        compiler_params=pltpu.CompilerParams(vmem_limit_bytes=8 * MIB),
        cost_estimate=QUICK,
    )(in_hbm(out_proj.reshape(cols, width)))
    other_unit = swap(core_unit, 0, 1)
    unit = pl.pallas_call(
        join_kernel,
        out_shape=pltpu.VMEM((CORES * cols, quarter), jnp.bfloat16),
        in_specs=[VMEM] * 2,
        out_specs=VMEM,
        compiler_params=pltpu.CompilerParams(vmem_limit_bytes=4 * MIB),
        cost_estimate=QUICK,
    )(mine_unit, other_unit)
    by_rank = routes.T
    if O["p1"] == "core_unit":
        by_rank, _ = tie(by_rank, core_unit)
    elif O["p1"] == "unit":
        by_rank, _ = tie(by_rank, unit)
    edges = -(-(experts + 1) // LANES) * LANES
    held_grads, own_starts, head, order, first_piece = pl.pallas_call(
        sort_kernel,
        out_shape=[
            pltpu.VMEM(out_grads.shape, jnp.bfloat16),
            jax.ShapeDtypeStruct((1, edges), jnp.int32),
            rows_shape(ALIGN),
            order_shape,
            rows_shape(2 * rows + ALIGN),
        ],
        in_specs=[VMEM, HBM],
        out_specs=[VMEM] * 5,
        scratch_shapes=[pltpu.SemaphoreType.DMA((8,))],
        compiler_params=pltpu.CompilerParams(vmem_limit_bytes=12 * MIB),
        cost_estimate=QUICK,
    )(by_rank, in_hbm(out_grads))

    def permuted(plan, headed, *after):
        held, *_ = tie(order, *after)
        return pl.pallas_call(
            functools.partial(permute_kernel, plan),
            out_shape=[
                rows_shape(many + (ALIGN if n in headed else 0))
                for n, (_, _, many) in enumerate(plan)
            ],
            in_specs=[VMEM] * 3,
            out_specs=[VMEM] * len(plan),
            compiler_params=pltpu.CompilerParams(vmem_limit_bytes=12 * MIB),
            cost_estimate=QUICK,
        )(in_vmem(held), head, in_vmem(held_grads))

    def starts_in(block, count):
        digits = block[count : count + 2, :edges].astype(jnp.int32)
        return (digits[0] * DIGIT + digits[1]).reshape(1, edges)

    side_pieces = [swap(first_piece, 1, 0)]
    ring_unit = unit
    if O["z1"] == "first":
        ring_unit, _ = tie(unit, first_piece)
    held = {(0, 0): unit, (1, 0): along(ring_unit, following)}
    p2after = {"none": [], "unit": [unit], "z1": [held[1, 0]]}[O["p2"]]
    (second_piece,) = permuted([(2, 2 * rows, 2 * rows)], [], *p2after)
    second_send = second_piece
    half = 2 * rows
    if O["cores"] == 2:
        own_tokens, *for_core = permuted([(0, 0, pairs), (1, 0, half), (1, half, half)], [1], second_piece)
        core_counts = [half, half]
    else:
        own_tokens, *for_core = permuted([(0, 0, pairs), (1, 0, pairs)], [1], second_piece)
        core_counts = [pairs]
    third_piece, last_piece = permuted([(3, 0, 3 * rows), (3, 3 * rows, rows)], [0], own_tokens)
    if O["core_in"] == "ev1":
        *for_core, held[1, 0] = tie(*for_core, held[1, 0])
    from_core = [swap(piece, 0, 1) for piece in for_core]
    y0_in = unit
    if O["y0"] == "first":
        y0_in, _ = tie(unit, first_piece)
    elif O["y0"] == "second":
        y0_in, _ = tie(unit, second_piece)
    elif O["y0"] == "own":
        y0_in, _ = tie(unit, own_tokens)
    elif O["y0"] == "core":
        y0_in, *from_core = tie(unit, *from_core)
    held[0, 1] = swap(y0_in, 0, CORES)
    side_pieces.append(swap(second_send, 1, 0))
    basis_in = [last_piece]
    if "z1" in O["basis"]:
        basis_in.append(held[1, 0])
    if "core" in O["basis"]:
        basis_in += from_core
    local_segments, *basis_out = tie(segments, *basis_in)
    if "core" in O["basis"]:
        from_core = basis_out[len(basis_out) - len(from_core):]
    basis, order_back = pl.pallas_call(
        basis_kernel,
        out_shape=[
            pltpu.VMEM((2 * tokens, SEG_DEV * 2 * rank), jnp.bfloat16),
            order_shape,
        ],
        in_specs=[HBM, HBM, VMEM, VMEM],
        out_specs=[VMEM] * 2,
        scratch_shapes=[
            pltpu.VMEM(hidden_in.shape, jnp.bfloat16),
            pltpu.VMEM(in_proj.shape, jnp.bfloat16),
            pltpu.SemaphoreType.DMA((5,)),
        ],
        compiler_params=pltpu.CompilerParams(vmem_limit_bytes=12 * MIB),
        cost_estimate=QUICK,
    )(in_hbm(hidden_in), in_hbm(in_proj), local_segments.reshape(1, tokens), by_rank)

    call = functools.partial(
        accumulate, bases=bases, rank=rank, pairs=pairs, window=window, places=places
    )
    place_of = {name: CORES * n for n, name in enumerate(arrival)}
    starts = {0: own_starts}
    members = []
    known_units = 0
    state = None

    def work(names, complete=(), partial=(), sends=(), cost=QUICK):
        nonlocal state, known_units
        tasks, arrived = [], []
        for group, blocks in complete:
            first = 0
            for piece, count in blocks:
                arrived.append((piece, group * pairs + first, count))
                first += count
            if group:
                starts[group] = starts_in(*blocks[0])
            members.append(group)
        fresh = [group for group, _ in complete]
        if fresh and known_units:
            tasks.append(("units", fresh, 0, known_units))
        if names:
            tasks.append(("units", list(members), known_units, CORES * len(names)))
        known_units += CORES * len(names)
        for group, piece, first, count in partial:
            arrived.append((piece, group * pairs + first, count))
            if first == 0:
                starts[group] = starts_in(piece, count)
                members.append(group)
            tasks.append(("piece", group, first, first + count, 0, known_units))
        state, out = call(
            state,
            starts=starts,
            tokens=arrived,
            units=[(held[n], place_of[n]) for n in names],
            tasks=tasks,
            sends=sends,
            cost=cost,
        )
        return out

    def group_tie(names, array):
        nonlocal basis, from_core
        items = []
        for name in names:
            if name == "y0":
                items.append(held[0, 1])
            if name == "y1":
                items.append(held[1, 1])
            if name == "z1":
                items.append(held[1, 0])
            if name == "z2":
                items.append(held[near])
            if name == "side0":
                items.append(side_pieces[0])
            if name == "side1":
                items.append(side_pieces[1])
            if name == "basis":
                items.append(basis)
            if name == "core":
                items += from_core
        out = tie(array, *items)
        out = list(out)
        array, out = out[0], out[1:]
        for name in names:
            if name == "y0":
                held[0, 1] = out.pop(0)
            if name == "y1":
                held[1, 1] = out.pop(0)
            if name == "z1":
                held[1, 0] = out.pop(0)
            if name == "z2":
                held[near] = out.pop(0)
            if name == "side0":
                side_pieces[0] = out.pop(0)
            if name == "side1":
                side_pieces[1] = out.pop(0)
            if name == "basis":
                basis = out.pop(0)
            if name == "core":
                from_core = [out.pop(0) for _ in from_core]
        return array

    held[1, 0] = group_tie(O["ev1"], held[1, 0])
    for n in range(1, final - 1):
        held[n + 1, 0] = along(held[n, 0], following)
        held[n, 1] = swap(held[n, 0], 0, CORES)
    third_piece = group_tie(O["diag"], third_piece)
    diagonal_pieces = [swap(third_piece, 1, 1)]
    near = (final - 1, 0)
    held[near] = group_tie(O["ev2"], held[near])
    COST = {0: QUICK, 1: SHORT}
    work(
        names_a,
        complete=[(0, [(own_tokens, pairs)]), (1, list(zip(from_core, core_counts)))],
        cost=COST[O["ka"]],
    )
    if O["z3_ka"]:
        held[near], *state = tie(held[near], *state)
    back_unit = group_tie(O["w"], held[0, 1])
    if O["w_ka"]:
        back_unit, *state = tie(back_unit, *state)
    held[final, 1] = along(back_unit, before)
    held[final, 0] = along(held[near], following)
    held[final - 1, 1] = swap(held[near], 0, CORES)
    last_piece = group_tie(O["last"], last_piece)
    diagonal_pieces.append(swap(last_piece, 1, 1))
    work(names_b, complete=[(2, [(piece, half) for piece in side_pieces])], cost=COST[O["k0"]])
    work(names_c, partial=[(3, diagonal_pieces[0], 0, 3 * rows)], cost=COST[O["k1"]])
    sent = work(
        names_d, partial=[(3, diagonal_pieces[1], 3 * rows, rows)], sends=[1, 2, 3], cost=COST[O["k2"]]
    )

    def returned(arrays):
        return [
            swap(array, side, bit) for array, (side, bit) in zip(arrays, ((0, 1), (1, 0), (1, 1)))
        ]

    early = returned(sent)
    place = places - CORES
    own_late, *sent = pl.pallas_call(
        functools.partial(late_kernel, rank, pairs, window, place, QUAD),
        out_shape=[pltpu.VMEM((window, LANES), jnp.float32)]
        + [pltpu.VMEM((window, LANES), jnp.bfloat16)] * (QUAD - 1),
        in_specs=[SMEM] * (1 + QUAD) + [VMEM] * 2,
        out_specs=[VMEM] * QUAD,
        compiler_params=pltpu.CompilerParams(vmem_limit_bytes=8 * MIB),
        cost_estimate=QUICK,
    )(bases, *[starts[g] for g in range(QUAD)], in_vmem(state[0]), held[final, 0])
    late = returned(sent)
    *early, own_late = tie(*early, own_late)
    out, turned = pl.pallas_call(
        functools.partial(blocks_kernel, rank),
        out_shape=[
            jax.ShapeDtypeStruct((SEG_DEV, experts, rank * rank), jnp.bfloat16),
            pltpu.VMEM((rank, pairs), jnp.float32),
        ],
        in_specs=[VMEM] * 7,
        out_specs=[VMEM] * 2,
        scratch_shapes=[pltpu.VMEM((rank // 2, experts, 2 * tokens), jnp.float32)],
        compiler_params=pltpu.CompilerParams(vmem_limit_bytes=32 * MIB),
        cost_estimate=QUICK,
    )(by_rank, basis, in_vmem(order_back), in_vmem(state[2]), *early)
    count = 2 * CORES * exp_here
    return pl.pallas_call(
        functools.partial(last_kernel, rank, place, count, exp_here),
        out_shape=jax.ShapeDtypeStruct(out.shape, out.dtype),
        in_specs=[SMEM] * 2 + [VMEM] * 8 + [HBM],
        out_specs=HBM,
        scratch_shapes=[
            pltpu.VMEM((rank, pairs), jnp.float32),
            pltpu.VMEM((rank // 2, count, 2 * tokens), jnp.float32),
            pltpu.VMEM((SEG_DEV, count, rank * rank), jnp.bfloat16),
            pltpu.SemaphoreType.DMA,
        ],
        input_output_aliases={10: 0},
        compiler_params=pltpu.CompilerParams(vmem_limit_bytes=16 * MIB),
        cost_estimate=QUICK,
    )(bases, own_starts, by_rank, basis, in_vmem(order_back), in_vmem(turned), own_late, *late, out)


def solution(mesh):
    placed = (
        P(("groups", "expert"), None),
        P(("groups", "expert"), None, None),
        P(("groups", "expert"), None),
        P(("groups", "expert")),
        P(),
        P("expert", None, None),
    )
    return jax.shard_map(
        local,
        mesh=mesh,
        in_specs=placed,
        out_specs=P(("groups", "expert"), None, None),
        check_vma=False,
    )
```

```python
import functools

import jax
import jax.numpy as jnp
import numpy as np
from jax import lax
from jax.experimental import pallas as pl
from jax.experimental.pallas import tpu as pltpu
from jax.sharding import PartitionSpec as P

SEG_DEV = 2
O = {'p1': 'core_unit', 'z1': 'none', 'p2': 'unit', 'cores': 2, 'core_in': 'none', 'y0': 'unit', 'basis': [], 'ev1': ['y0', 'side0'], 'diag': ['side0'], 'ev2': ['basis'], 'w': ['z2'], 'last': ['z2'], 'ka': 0, 'z3_ka': 0, 'w_ka': 1, 'k0': 0, 'k1': 0, 'k2': 1, 'y2': 'c'}
CORES = 2
SIDES = 2
QUAD = 4
PIECES = 4
LANES = 128
ALIGN = 16
DIGIT = 32
BOTH = ("groups", "expert")
MIB = 1024 * 1024
VMEM = pl.BlockSpec(memory_space=pltpu.VMEM)
SMEM = pl.BlockSpec(memory_space=pltpu.SMEM)
HBM = pl.BlockSpec(memory_space=pl.ANY)
QUICK = pl.CostEstimate(flops=1, bytes_accessed=1, transcendentals=0)
SHORT = pl.CostEstimate(flops=10**9, bytes_accessed=1, transcendentals=0)
NT = (((1,), (1,)), ((), ()))


def in_vmem(array):
    return pltpu.with_memory_space_constraint(array, pltpu.VMEM)


def in_hbm(array):
    return pltpu.with_memory_space_constraint(array, pltpu.HBM)


def place_in_quad(flip):
    side, core = lax.axis_index("groups") % SIDES, lax.axis_index("expert") % CORES
    return (side ^ (flip // CORES)) * CORES + (core ^ (flip % CORES))


def columns_of(flip, width):
    return pl.ds(pl.multiple_of(place_in_quad(flip) * width, width), width)


def row_of(routes):
    tops, tokens = routes.shape
    pairs = tops * tokens
    lane = lax.broadcasted_iota(jnp.int32, (tokens, pairs), 1)
    token = lax.broadcasted_iota(jnp.int32, (tokens, pairs), 0)
    spread = jnp.where(lane // tops == token, 1.0, 0.0).astype(jnp.bfloat16)
    values = routes.astype(jnp.float32).astype(jnp.bfloat16)
    every = jnp.dot(values, spread, preferred_element_type=jnp.float32)
    lane = lax.broadcasted_iota(jnp.int32, (tops, pairs), 1)
    k = lax.broadcasted_iota(jnp.int32, (tops, pairs), 0)
    return jnp.sum(jnp.where(lane % tops == k, every, 0.0), axis=0, keepdims=True).astype(jnp.int32)


def key_column(routes_row):
    count = routes_row.shape[1]
    keys = routes_row * count + lax.broadcasted_iota(jnp.int32, (1, count), 1)
    return jnp.broadcast_to(keys.astype(jnp.float32), (8, count)).T[:, 0:1]


def ranks(column, keys):
    total = jnp.zeros(keys.shape, jnp.float32)
    for first in range(0, column.shape[0], 128):
        smaller = jnp.where(column[first : first + 128] < keys, 1.0, 0.0)
        total = total + jnp.sum(smaller, axis=0, keepdims=True)
    return total


def sort_kernel(
    routes_ref,
    grads_ref,
    held_ref,
    starts_ref,
    head_ref,
    order_ref,
    piece_ref,
    sems,
):
    width = piece_ref.shape[1]
    count = sems.shape[0]
    part = grads_ref.shape[0] // count
    copies = []
    for n in range(count):
        here = pl.ds(n * part, part)
        copies.append(pltpu.make_async_copy(grads_ref.at[here], held_ref.at[here], sems.at[n]))
    for copy in copies:
        copy.start()
    routes = row_of(routes_ref[...])
    pairs = routes.shape[1]
    column = key_column(routes)
    keys = routes * pairs + lax.broadcasted_iota(jnp.int32, (1, pairs), 1)
    place = ranks(column, keys.astype(jnp.float32)).astype(jnp.int32)
    firsts = lax.broadcasted_iota(jnp.int32, starts_ref.shape, 1) * pairs
    starts = ranks(column, firsts.astype(jnp.float32)).astype(jnp.int32)
    starts_ref[...] = starts
    wide = head_ref.shape[1] - starts.shape[1]
    digits = [starts // DIGIT, starts % DIGIT]
    digits = [jnp.pad(d.astype(jnp.float32), ((0, 0), (0, wide))) for d in digits]
    row = lax.broadcasted_iota(jnp.int32, head_ref.shape, 0)
    head = jnp.where(row == 0, digits[0], jnp.where(row == 1, digits[1], 0.0))
    head_ref[...] = head.astype(jnp.bfloat16)
    rows = piece_ref.shape[0] - ALIGN
    for first in range(0, pairs, rows):
        ids = first + lax.broadcasted_iota(jnp.int32, (rows, pairs), 0)
        order_ref[first : first + rows, :] = jnp.where(place == ids, 1.0, 0.0).astype(jnp.bfloat16)
    for copy in copies:
        copy.wait()
    piece_ref[0:rows, :] = jnp.dot(
        order_ref[0:rows, :],
        held_ref[:, :, columns_of(2, width)].reshape(pairs, width),
        preferred_element_type=jnp.float32,
    ).astype(jnp.bfloat16)
    piece_ref[rows:, :] = head_ref[...]


def weights_kernel(weight_ref, mine_ref, core_ref, stage, sems):
    rows, width = mine_ref.shape
    count = sems.shape[0]
    part = rows // count
    copies = [
        pltpu.make_async_copy(
            weight_ref.at[pl.ds(n * part, part)], stage.at[pl.ds(n * part, part)], sems.at[n]
        )
        for n in range(count)
    ]
    for copy in copies:
        copy.start()
    for copy in copies:
        copy.wait()
    core_ref[...] = stage[:, columns_of(1, width)]
    mine_ref[...] = stage[:, columns_of(0, width)]


def join_kernel(one_ref, two_ref, out_ref):
    half = one_ref.shape[0]
    out_ref[0:half, :] = one_ref[...]
    out_ref[half:, :] = two_ref[...]


def permute_kernel(plan, order_ref, head_ref, grads_ref, *outs):
    pairs, width = order_ref.shape[0], outs[0].shape[1]
    for device in sorted({device for device, _, _ in plan}):
        grads = grads_ref[:, :, columns_of(device, width)].reshape(pairs, width)
        for out, (target, first, rows) in zip(outs, plan):
            if target == device:
                out[0:rows, :] = jnp.dot(
                    order_ref[first : first + rows, :], grads, preferred_element_type=jnp.float32
                ).astype(jnp.bfloat16)
                if out.shape[0] > rows:
                    out[rows:, :] = head_ref[...]


def basis_kernel(
    hidden_ref, proj_ref, segment_ref, routes_ref, out_ref, order_ref, hidden, proj, sems
):
    count = sems.shape[0] - 1
    part = hidden.shape[0] // count
    copies = [pltpu.make_async_copy(proj_ref, proj, sems.at[count])]
    for n in range(count):
        here = pl.ds(n * part, part)
        copies.append(pltpu.make_async_copy(hidden_ref.at[here], hidden.at[here], sems.at[n]))
    for copy in copies:
        copy.start()
    tops, tokens = routes_ref.shape
    pairs = tops * tokens
    column = key_column(row_of(routes_ref[...]))
    at = [
        routes_ref[k : k + 1, :] * pairs + lax.broadcasted_iota(jnp.int32, (1, tokens), 1) * tops + k
        for k in range(tops)
    ]
    place = ranks(column, jnp.concatenate(at, axis=1).astype(jnp.float32)).astype(jnp.int32)
    for first in range(0, pairs, 256):
        ids = first + lax.broadcasted_iota(jnp.int32, (256, pairs), 0)
        order_ref[first : first + 256, :] = jnp.where(place == ids, 1.0, 0.0).astype(jnp.bfloat16)
    segment = (segment_ref[...] - lax.axis_index("expert") * SEG_DEV).astype(jnp.float32)
    segment = jnp.broadcast_to(segment, (8, tokens)).T[:, 0:1]
    for copy in copies:
        copy.wait()
    projected = lax.dot_general(hidden[...], proj[...], NT, preferred_element_type=jnp.float32)
    zero = jnp.zeros_like(projected)
    picked = [jnp.where(segment == float(s), projected, zero) for s in range(SEG_DEV)]
    even = jnp.concatenate([b for p in picked for b in (p, zero)], axis=1)
    odd = jnp.concatenate([b for p in picked for b in (zero, p)], axis=1)
    out_ref[...] = jnp.concatenate([even, odd], axis=0).astype(out_ref.dtype)


def packed(total, first, pairs, rank):
    half = pairs // 2
    low = lax.broadcasted_iota(jnp.int32, (half, LANES), 1) < rank
    one = total[first : first + half, :]
    two = total[first + half : first + pairs, :]
    return jnp.where(low, one + pltpu.roll(one, rank, 1), two + pltpu.roll(two, rank, 1))


def partial_kernel(
    rank, pairs, window, new_tokens, new_units, tasks, fresh, sends, groups, bases_ref, *refs
):
    start_refs = dict(zip(groups, refs))
    refs = refs[len(groups) :]
    token_refs, refs = refs[: len(new_tokens)], refs[len(new_tokens) :]
    unit_refs, refs = refs[: len(new_units)], refs[len(new_units) :]
    if fresh:
        tokens, units, total = refs
        send_refs = ()
        total[...] = jnp.zeros_like(total)
    else:
        tokens, units, total = refs[3:6]
        send_refs = refs[6:]
    for ref, (first, count) in zip(token_refs, new_tokens):
        tokens[first : first + count, :] = ref[0:count, :]
    cols = units.shape[1]
    for ref, place in zip(unit_refs, new_units):
        for half in range(CORES):
            units[place + half] = ref[half * cols : (half + 1) * cols, :]
    held = cols // rank
    per_tile = LANES // rank
    low = lax.broadcasted_iota(jnp.int32, (1, LANES), 1) < rank

    device = lax.axis_index("expert")

    def process(w, members):
        base = bases_ref[device, w]
        heres, offsets = [], []
        for g in members:
            at = jnp.minimum(start_refs[g][0, base] & -ALIGN, pairs - window)
            offsets.append(at)
            heres.append(pl.ds(pl.multiple_of(g * pairs + at, ALIGN), window))
        rows = [tokens[here, :] for here in heres]
        rows = jnp.concatenate(rows, axis=0) if len(rows) > 1 else rows[0]
        dense = lax.dot_general(rows, units[w], NT, preferred_element_type=jnp.float32)
        for n, g in enumerate(members):
            value = total[heres[n], :]
            number = offsets[n] + lax.broadcasted_iota(jnp.int32, (window, LANES), 0)
            for j in range(cols // LANES):
                edge = [start_refs[g][0, base + j * per_tile + i] for i in range(per_tile + 1)]
                inside = (number >= jnp.where(low, edge[0], edge[1])) & (
                    number < jnp.where(low, edge[1], edge[2])
                )
                part = dense[n * window : (n + 1) * window, j * LANES : (j + 1) * LANES]
                value = jnp.where(inside, part, value)
            total[heres[n], :] = value

    for task in tasks:
        if task[0] == "units":
            _, members, first_w, count = task

            def each(i, carry, members=members, first_w=first_w):
                process(first_w + i, members)
                return carry

        else:
            _, member, first_row, end_row, first_w, count = task

            def each(
                i, carry, member=member, first_row=first_row, end_row=end_row, first_w=first_w
            ):
                w = first_w + i
                base = bases_ref[device, w]
                touches = (start_refs[member][0, base] < end_row) & (
                    start_refs[member][0, base + held] > first_row
                )

                @pl.when(touches)
                def _():
                    process(w, [member])

                return carry

        lax.fori_loop(0, count, each, 0)
    for ref, g in zip(send_refs, sends):
        ref[...] = packed(total, g * pairs, pairs, rank).astype(ref.dtype)


def accumulate(
    state, bases, starts, tokens, units, tasks, rank, pairs, window, places=0, sends=(), cost=QUICK
):
    fresh = state is None
    operands = [bases, *starts.values(), *[a for a, _, _ in tokens], *[a for a, _ in units]]
    specs = [SMEM] * (1 + len(starts)) + [VMEM] * (len(tokens) + len(units))
    if fresh:
        width = units[0][0].shape[1]
        shapes = [
            pltpu.VMEM((QUAD * pairs, width), jnp.bfloat16),
            pltpu.VMEM((places, units[0][0].shape[0] // CORES, width), jnp.bfloat16),
            pltpu.VMEM((QUAD * pairs, LANES), jnp.float32),
        ]
        aliases = {}
    else:
        aliases = {len(operands) + i: i for i in range(3)}
        operands += [in_vmem(a) for a in state]
        specs += [VMEM] * 3
        shapes = [pltpu.VMEM(a.shape, a.dtype) for a in state]
    shapes += [pltpu.VMEM((pairs // 2, LANES), jnp.bfloat16)] * len(sends)
    out = pl.pallas_call(
        functools.partial(
            partial_kernel,
            rank,
            pairs,
            window,
            [(first, count) for _, first, count in tokens],
            [p for _, p in units],
            tasks,
            fresh,
            sends,
            list(starts),
        ),
        out_shape=shapes,
        in_specs=specs,
        out_specs=[VMEM] * len(shapes),
        input_output_aliases=aliases,
        compiler_params=pltpu.CompilerParams(vmem_limit_bytes=8 * MIB),
        cost_estimate=cost,
    )(*operands)
    return list(out[:3]), list(out[3:])


def late_kernel(rank, pairs, window, place, groups, bases_ref, *refs):
    start_refs, tokens, refs = refs[:groups], refs[groups], refs[groups + 1 :]
    unit_refs, outs = refs[:2], refs[2:]
    per_tile = LANES // rank
    low = lax.broadcasted_iota(jnp.int32, (1, LANES), 1) < rank
    device = lax.axis_index("expert")
    first_core = device % CORES == 0
    for u, unit_ref in enumerate(unit_refs):
        cols = unit_ref.shape[0] // CORES
        folded = []
        for half in range(CORES):
            base = bases_ref[device, place + u * CORES + half]
            offsets, rows = [], []
            for g in range(groups):
                at = jnp.minimum(start_refs[g][0, base] & -ALIGN, pairs - window)
                offsets.append(at)
                rows.append(tokens[pl.ds(pl.multiple_of(g * pairs + at, ALIGN), window), :])
            dense = lax.dot_general(
                jnp.concatenate(rows, axis=0),
                unit_ref[half * cols : (half + 1) * cols, :],
                NT,
                preferred_element_type=jnp.float32,
            )
            found = []
            for g in range(groups):
                value = jnp.zeros((window, LANES), jnp.float32)
                number = offsets[g] + lax.broadcasted_iota(jnp.int32, (window, LANES), 0)
                for j in range(cols // LANES):
                    edge = [start_refs[g][0, base + j * per_tile + i] for i in range(per_tile + 1)]
                    inside = (number >= jnp.where(low, edge[0], edge[1])) & (
                        number < jnp.where(low, edge[1], edge[2])
                    )
                    part = dense[g * window : (g + 1) * window, j * LANES : (j + 1) * LANES]
                    value = jnp.where(inside, part, value)
                found.append(value + pltpu.roll(value, rank, 1))
            folded.append(found)
        for g, out in enumerate(outs):
            one, two = folded[0][g], folded[1][g]
            zero = jnp.where(first_core, one, two)
            other = jnp.where(first_core, two, one)
            out[u * window : (u + 1) * window, :] = jnp.where(low, zero, other).astype(out.dtype)


def expand(routes_ref, turned, lines, first, tiles):
    tops, tokens = routes_ref.shape
    rank = turned.shape[0]

    def one(tile, carry):
        here = pl.multiple_of(tile * 8, 8)
        ids = first + here + lax.broadcasted_iota(jnp.int32, (8, tokens), 0)
        masks = [routes_ref[k : k + 1, :] == ids for k in range(tops)]
        for r in range(rank):
            value = jnp.zeros((8, tokens), jnp.float32)
            for k in range(tops):
                row = turned[r : r + 1, k * tokens : (k + 1) * tokens]
                value = jnp.where(masks[k], row, value)
            side = r % 2 * tokens
            lines[r // 2, pl.ds(here, 8), side : side + tokens] = value
        return carry

    lax.fori_loop(0, tiles, one, 0)


def form(lines, basis_ref, first, count, out_ref, rank):
    experts, width = lines.shape[1:]
    made = jnp.dot(
        lines[first : first + count].reshape(count * experts, width).astype(jnp.bfloat16),
        basis_ref[...],
        preferred_element_type=jnp.float32,
    ).astype(jnp.bfloat16)
    for pair in range(count):
        for s in range(SEG_DEV):
            out_ref[s, :, pl.ds((first + pair) * 2 * rank, 2 * rank)] = made[
                pair * experts : (pair + 1) * experts, s * 2 * rank : (s + 1) * 2 * rank
            ]


def blocks_kernel(
    rank, routes_ref, basis_ref, order_ref, total_ref, b_ref, c_ref, d_ref, out_ref, turned, lines
):
    half = b_ref.shape[0]
    value = packed(total_ref, 0, 2 * half, rank)
    for ref in (b_ref, c_ref, d_ref):
        value = value + ref[...].astype(jnp.float32)
    value = value.T
    value = jnp.concatenate([value[0:rank], value[rank : 2 * rank]], axis=1).astype(jnp.bfloat16)
    turned[...] = jnp.dot(value, order_ref[...], preferred_element_type=jnp.float32)
    expand(routes_ref, turned, lines, 0, lines.shape[1] // 8)
    for first in range(0, rank // 2, 8):
        form(lines, basis_ref, first, 8, out_ref, rank)


def last_kernel(
    rank,
    place,
    count,
    held,
    bases_ref,
    starts_ref,
    routes_ref,
    basis_ref,
    order_ref,
    turned_ref,
    own_ref,
    b_ref,
    c_ref,
    d_ref,
    _,
    out_ref,
    turned,
    lines,
    block,
    sem,
):
    window = own_ref.shape[0] // 2
    pairs = order_ref.shape[0]
    value = own_ref[...]
    for ref in (b_ref, c_ref, d_ref):
        value = value + ref[...].astype(jnp.float32)
    value = value.T.astype(jnp.bfloat16)
    device = lax.axis_index("expert")
    first = bases_ref[device, place] // count * count
    total = turned_ref[...]
    for u in range(2):
        unit = bases_ref[device, place + u * CORES] // (CORES * held) * (CORES * held)
        for core in range(CORES):
            at = jnp.minimum(starts_ref[0, unit + core * held] & -ALIGN, pairs - window)
            total = total + jnp.dot(
                value[core * rank : (core + 1) * rank, u * window : (u + 1) * window],
                order_ref[pl.ds(pl.multiple_of(at, ALIGN), window), :],
                preferred_element_type=jnp.float32,
            )
    turned[...] = total
    expand(routes_ref, turned, lines, first, count // 8)
    form(lines, basis_ref, 0, rank // 2, block, rank)
    copy = pltpu.make_async_copy(
        block, out_ref.at[:, pl.ds(pl.multiple_of(first, count), count), :], sem
    )
    copy.start()
    copy.wait()


def local(hidden_in, out_grads, routes, segments, in_proj, out_proj):
    tokens, tops = routes.shape
    exp_here, rank, width = out_proj.shape
    owners, groups = lax.axis_size("expert"), lax.axis_size("groups")
    experts = exp_here * owners
    pairs = tokens * tops
    capacity = max(2, 3 * pairs // (2 * experts))
    window = min(pairs, -(-(exp_here * capacity + ALIGN - 1) // ALIGN) * ALIGN)
    quarter = width // QUAD
    cols = exp_here * rank
    rows = pairs // PIECES
    index = lax.axis_index("expert")
    slots = owners // CORES // 2
    ring = [0, *range(1, slots, 2), *range((slots - 1) // 2 * 2, 0, -2)]
    following = {a: b for a, b in zip(ring, ring[1:] + ring[:1])}
    before = {b: a for a, b in following.items()}

    def swap(array, side, bit):
        table = [
            (g * owners + e, (g ^ side) * owners + (e ^ bit))
            for g in range(groups)
            for e in range(owners)
        ]
        return lax.ppermute(array, BOTH, table)

    def along(array, table):
        wide = 2 * CORES
        pairs_of = [(e, table[e // wide] * wide + e % wide) for e in range(owners)]
        return lax.ppermute(array, "expert", pairs_of)

    def tie(*arrays):
        return lax.optimization_barrier(arrays)

    final = slots - 1
    names_a = [(n, 0) for n in range(final - 1)] + [(0, 1)]
    names_b = [(final - 1, 0)] + [(n, 1) for n in range(1, final - 1)]
    names_c = [(final - 1, 1)]
    arrival = names_a + names_b + names_c + [(final, 0), (final, 1)]

    def source(z, hops):
        for _ in range(hops):
            z = before[z]
        return z

    rows_of = [
        [
            ((source(e // (2 * CORES), n) * 2 + (e // CORES % 2 ^ y)) * CORES + (e % CORES ^ c)) * exp_here
            for n, y in arrival
            for c in range(CORES)
        ]
        for e in range(owners)
    ]
    places = CORES * len(arrival)
    bases = jnp.asarray(np.array(rows_of, np.int32))

    unit_shape = pltpu.VMEM((cols, quarter), jnp.bfloat16)
    order_shape = pltpu.VMEM((pairs, pairs), jnp.bfloat16)

    def rows_shape(count):
        return pltpu.VMEM((count, quarter), jnp.bfloat16)

    mine_unit, core_unit = pl.pallas_call(
        weights_kernel,
        out_shape=[unit_shape, unit_shape],
        in_specs=[HBM],
        out_specs=[VMEM] * 2,
        scratch_shapes=[pltpu.VMEM((cols, width), jnp.bfloat16), pltpu.SemaphoreType.DMA((4,))],
        compiler_params=pltpu.CompilerParams(vmem_limit_bytes=8 * MIB),
        cost_estimate=QUICK,
    )(in_hbm(out_proj.reshape(cols, width)))
    other_unit = swap(core_unit, 0, 1)
    unit = pl.pallas_call(
        join_kernel,
        out_shape=pltpu.VMEM((CORES * cols, quarter), jnp.bfloat16),
        in_specs=[VMEM] * 2,
        out_specs=VMEM,
        compiler_params=pltpu.CompilerParams(vmem_limit_bytes=4 * MIB),
        cost_estimate=QUICK,
    )(mine_unit, other_unit)
    by_rank = routes.T
    if O["p1"] == "core_unit":
        by_rank, _ = tie(by_rank, core_unit)
    elif O["p1"] == "unit":
        by_rank, _ = tie(by_rank, unit)
    edges = -(-(experts + 1) // LANES) * LANES
    held_grads, own_starts, head, order, first_piece = pl.pallas_call(
        sort_kernel,
        out_shape=[
            pltpu.VMEM(out_grads.shape, jnp.bfloat16),
            jax.ShapeDtypeStruct((1, edges), jnp.int32),
            rows_shape(ALIGN),
            order_shape,
            rows_shape(2 * rows + ALIGN),
        ],
        in_specs=[VMEM, HBM],
        out_specs=[VMEM] * 5,
        scratch_shapes=[pltpu.SemaphoreType.DMA((8,))],
        compiler_params=pltpu.CompilerParams(vmem_limit_bytes=12 * MIB),
        cost_estimate=QUICK,
    )(by_rank, in_hbm(out_grads))

    def permuted(plan, headed, *after):
        held, *_ = tie(order, *after)
        return pl.pallas_call(
            functools.partial(permute_kernel, plan),
            out_shape=[
                rows_shape(many + (ALIGN if n in headed else 0))
                for n, (_, _, many) in enumerate(plan)
            ],
            in_specs=[VMEM] * 3,
            out_specs=[VMEM] * len(plan),
            compiler_params=pltpu.CompilerParams(vmem_limit_bytes=12 * MIB),
            cost_estimate=QUICK,
        )(in_vmem(held), head, in_vmem(held_grads))

    def starts_in(block, count):
        digits = block[count : count + 2, :edges].astype(jnp.int32)
        return (digits[0] * DIGIT + digits[1]).reshape(1, edges)

    side_pieces = [swap(first_piece, 1, 0)]
    ring_unit = unit
    if O["z1"] == "first":
        ring_unit, _ = tie(unit, first_piece)
    held = {(0, 0): unit, (1, 0): along(ring_unit, following)}
    p2after = {"none": [], "unit": [unit], "z1": [held[1, 0]]}[O["p2"]]
    (second_piece,) = permuted([(2, 2 * rows, 2 * rows)], [], *p2after)
    second_send = second_piece
    half = 2 * rows
    if O["cores"] == 2:
        own_tokens, *for_core = permuted([(0, 0, pairs), (1, 0, half), (1, half, half)], [1], second_piece)
        core_counts = [half, half]
    else:
        own_tokens, *for_core = permuted([(0, 0, pairs), (1, 0, pairs)], [1], second_piece)
        core_counts = [pairs]
    third_piece, last_piece = permuted([(3, 0, 3 * rows), (3, 3 * rows, rows)], [0], own_tokens)
    if O["core_in"] == "ev1":
        *for_core, held[1, 0] = tie(*for_core, held[1, 0])
    from_core = [swap(piece, 0, 1) for piece in for_core]
    y0_in = unit
    if O["y0"] == "first":
        y0_in, _ = tie(unit, first_piece)
    elif O["y0"] == "second":
        y0_in, _ = tie(unit, second_piece)
    elif O["y0"] == "own":
        y0_in, _ = tie(unit, own_tokens)
    elif O["y0"] == "core":
        y0_in, *from_core = tie(unit, *from_core)
    held[0, 1] = swap(y0_in, 0, CORES)
    side_pieces.append(swap(second_send, 1, 0))
    basis_in = [last_piece]
    if "z1" in O["basis"]:
        basis_in.append(held[1, 0])
    if "core" in O["basis"]:
        basis_in += from_core
    local_segments, *basis_out = tie(segments, *basis_in)
    if "core" in O["basis"]:
        from_core = basis_out[len(basis_out) - len(from_core):]
    basis, order_back = pl.pallas_call(
        basis_kernel,
        out_shape=[
            pltpu.VMEM((2 * tokens, SEG_DEV * 2 * rank), jnp.bfloat16),
            order_shape,
        ],
        in_specs=[HBM, HBM, VMEM, VMEM],
        out_specs=[VMEM] * 2,
        scratch_shapes=[
            pltpu.VMEM(hidden_in.shape, jnp.bfloat16),
            pltpu.VMEM(in_proj.shape, jnp.bfloat16),
            pltpu.SemaphoreType.DMA((5,)),
        ],
        compiler_params=pltpu.CompilerParams(vmem_limit_bytes=12 * MIB),
        cost_estimate=QUICK,
    )(in_hbm(hidden_in), in_hbm(in_proj), local_segments.reshape(1, tokens), by_rank)

    call = functools.partial(
        accumulate, bases=bases, rank=rank, pairs=pairs, window=window, places=places
    )
    place_of = {name: CORES * n for n, name in enumerate(arrival)}
    starts = {0: own_starts}
    members = []
    known_units = 0
    state = None

    def work(names, complete=(), partial=(), sends=(), cost=QUICK):
        nonlocal state, known_units
        tasks, arrived = [], []
        for group, blocks in complete:
            first = 0
            for piece, count in blocks:
                arrived.append((piece, group * pairs + first, count))
                first += count
            if group:
                starts[group] = starts_in(*blocks[0])
            members.append(group)
        fresh = [group for group, _ in complete]
        if fresh and known_units:
            tasks.append(("units", fresh, 0, known_units))
        if names:
            tasks.append(("units", list(members), known_units, CORES * len(names)))
        known_units += CORES * len(names)
        for group, piece, first, count in partial:
            arrived.append((piece, group * pairs + first, count))
            if first == 0:
                starts[group] = starts_in(piece, count)
                members.append(group)
            tasks.append(("piece", group, first, first + count, 0, known_units))
        state, out = call(
            state,
            starts=starts,
            tokens=arrived,
            units=[(held[n], place_of[n]) for n in names],
            tasks=tasks,
            sends=sends,
            cost=cost,
        )
        return out

    def group_tie(names, array):
        nonlocal basis, from_core
        items = []
        for name in names:
            if name == "y0":
                items.append(held[0, 1])
            if name == "y1":
                items.append(held[1, 1])
            if name == "z1":
                items.append(held[1, 0])
            if name == "z2":
                items.append(held[near])
            if name == "side0":
                items.append(side_pieces[0])
            if name == "side1":
                items.append(side_pieces[1])
            if name == "basis":
                items.append(basis)
            if name == "core":
                items += from_core
        out = tie(array, *items)
        out = list(out)
        array, out = out[0], out[1:]
        for name in names:
            if name == "y0":
                held[0, 1] = out.pop(0)
            if name == "y1":
                held[1, 1] = out.pop(0)
            if name == "z1":
                held[1, 0] = out.pop(0)
            if name == "z2":
                held[near] = out.pop(0)
            if name == "side0":
                side_pieces[0] = out.pop(0)
            if name == "side1":
                side_pieces[1] = out.pop(0)
            if name == "basis":
                basis = out.pop(0)
            if name == "core":
                from_core = [out.pop(0) for _ in from_core]
        return array

    held[1, 0] = group_tie(O["ev1"], held[1, 0])
    for n in range(1, final - 1):
        held[n + 1, 0] = along(held[n, 0], following)
        held[n, 1] = swap(held[n, 0], 0, CORES)
    third_piece = group_tie(O["diag"], third_piece)
    diagonal_pieces = [swap(third_piece, 1, 1)]
    near = (final - 1, 0)
    held[near] = group_tie(O["ev2"], held[near])
    COST = {0: QUICK, 1: SHORT}
    work(
        names_a,
        complete=[(0, [(own_tokens, pairs)]), (1, list(zip(from_core, core_counts)))],
        cost=COST[O["ka"]],
    )
    if O["z3_ka"]:
        held[near], *state = tie(held[near], *state)
    back_unit = group_tie(O["w"], held[0, 1])
    if O["w_ka"]:
        back_unit, *state = tie(back_unit, *state)
    held[final, 1] = along(back_unit, before)
    held[final, 0] = along(held[near], following)
    held[final - 1, 1] = swap(held[near], 0, CORES)
    last_piece = group_tie(O["last"], last_piece)
    diagonal_pieces.append(swap(last_piece, 1, 1))
    work(names_b, complete=[(2, [(piece, half) for piece in side_pieces])], cost=COST[O["k0"]])
    sent = work(
        names_c if O["y2"] == "c" else [], partial=[(3, diagonal_pieces[0], 0, 3 * rows)], sends=[1, 2] if O["y2"] == "c" else [], cost=COST[O["k1"]]
    )
    sent = sent + work(
        [] if O["y2"] == "c" else names_c, partial=[(3, diagonal_pieces[1], 3 * rows, rows)], sends=[3] if O["y2"] == "c" else [1, 2, 3], cost=COST[O["k2"]]
    )

    def returned(arrays):
        return [
            swap(array, side, bit) for array, (side, bit) in zip(arrays, ((0, 1), (1, 0), (1, 1)))
        ]

    early = returned(sent)
    place = places - 2 * CORES
    own_late, *sent = pl.pallas_call(
        functools.partial(late_kernel, rank, pairs, window, place, QUAD),
        out_shape=[pltpu.VMEM((2 * window, LANES), jnp.float32)]
        + [pltpu.VMEM((2 * window, LANES), jnp.bfloat16)] * (QUAD - 1),
        in_specs=[SMEM] * (1 + QUAD) + [VMEM] * 3,
        out_specs=[VMEM] * QUAD,
        compiler_params=pltpu.CompilerParams(vmem_limit_bytes=8 * MIB),
        cost_estimate=QUICK,
    )(bases, *[starts[g] for g in range(QUAD)], in_vmem(state[0]), held[final, 0], held[final, 1])
    late = returned(sent)
    *early, own_late = tie(*early, own_late)
    out, turned = pl.pallas_call(
        functools.partial(blocks_kernel, rank),
        out_shape=[
            jax.ShapeDtypeStruct((SEG_DEV, experts, rank * rank), jnp.bfloat16),
            pltpu.VMEM((rank, pairs), jnp.float32),
        ],
        in_specs=[VMEM] * 7,
        out_specs=[VMEM] * 2,
        scratch_shapes=[pltpu.VMEM((rank // 2, experts, 2 * tokens), jnp.float32)],
        compiler_params=pltpu.CompilerParams(vmem_limit_bytes=32 * MIB),
        cost_estimate=QUICK,
    )(by_rank, basis, in_vmem(order_back), in_vmem(state[2]), *early)
    count = 2 * CORES * exp_here
    return pl.pallas_call(
        functools.partial(last_kernel, rank, place, count, exp_here),
        out_shape=jax.ShapeDtypeStruct(out.shape, out.dtype),
        in_specs=[SMEM] * 2 + [VMEM] * 8 + [HBM],
        out_specs=HBM,
        scratch_shapes=[
            pltpu.VMEM((rank, pairs), jnp.float32),
            pltpu.VMEM((rank // 2, count, 2 * tokens), jnp.float32),
            pltpu.VMEM((SEG_DEV, count, rank * rank), jnp.bfloat16),
            pltpu.SemaphoreType.DMA,
        ],
        input_output_aliases={10: 0},
        compiler_params=pltpu.CompilerParams(vmem_limit_bytes=16 * MIB),
        cost_estimate=QUICK,
    )(bases, own_starts, by_rank, basis, in_vmem(order_back), in_vmem(turned), own_late, *late, out)


def solution(mesh):
    placed = (
        P(("groups", "expert"), None),
        P(("groups", "expert"), None, None),
        P(("groups", "expert"), None),
        P(("groups", "expert")),
        P(),
        P("expert", None, None),
    )
    return jax.shard_map(
        local,
        mesh=mesh,
        in_specs=placed,
        out_specs=P(("groups", "expert"), None, None),
        check_vma=False,
    )
```

```python
import functools

import jax
import jax.numpy as jnp
import numpy as np
from jax import lax
from jax.experimental import pallas as pl
from jax.experimental.pallas import tpu as pltpu
from jax.sharding import PartitionSpec as P

SEG_DEV = 2
O = {'p1': 'core_unit', 'z1': 'none', 'p2': 'unit', 'cores': 2, 'core_in': 'none', 'y0': 'unit', 'basis': [], 'ev1': ['side0'], 'diag': ['side0'], 'ev2': ['basis', 'side0'], 'w': ['basis', 'core'], 'last': ['z2'], 'ka': 0, 'z3_ka': 0, 'w_ka': 0, 'k0': 1, 'k1': 0, 'k2': 1, 'y2': 'c'}
CORES = 2
SIDES = 2
QUAD = 4
PIECES = 4
LANES = 128
ALIGN = 16
DIGIT = 32
BOTH = ("groups", "expert")
MIB = 1024 * 1024
VMEM = pl.BlockSpec(memory_space=pltpu.VMEM)
SMEM = pl.BlockSpec(memory_space=pltpu.SMEM)
HBM = pl.BlockSpec(memory_space=pl.ANY)
QUICK = pl.CostEstimate(flops=1, bytes_accessed=1, transcendentals=0)
SHORT = pl.CostEstimate(flops=10**9, bytes_accessed=1, transcendentals=0)
NT = (((1,), (1,)), ((), ()))


def in_vmem(array):
    return pltpu.with_memory_space_constraint(array, pltpu.VMEM)


def in_hbm(array):
    return pltpu.with_memory_space_constraint(array, pltpu.HBM)


def place_in_quad(flip):
    side, core = lax.axis_index("groups") % SIDES, lax.axis_index("expert") % CORES
    return (side ^ (flip // CORES)) * CORES + (core ^ (flip % CORES))


def columns_of(flip, width):
    return pl.ds(pl.multiple_of(place_in_quad(flip) * width, width), width)


def row_of(routes):
    tops, tokens = routes.shape
    pairs = tops * tokens
    lane = lax.broadcasted_iota(jnp.int32, (tokens, pairs), 1)
    token = lax.broadcasted_iota(jnp.int32, (tokens, pairs), 0)
    spread = jnp.where(lane // tops == token, 1.0, 0.0).astype(jnp.bfloat16)
    values = routes.astype(jnp.float32).astype(jnp.bfloat16)
    every = jnp.dot(values, spread, preferred_element_type=jnp.float32)
    lane = lax.broadcasted_iota(jnp.int32, (tops, pairs), 1)
    k = lax.broadcasted_iota(jnp.int32, (tops, pairs), 0)
    return jnp.sum(jnp.where(lane % tops == k, every, 0.0), axis=0, keepdims=True).astype(jnp.int32)


def key_column(routes_row):
    count = routes_row.shape[1]
    keys = routes_row * count + lax.broadcasted_iota(jnp.int32, (1, count), 1)
    return jnp.broadcast_to(keys.astype(jnp.float32), (8, count)).T[:, 0:1]


def ranks(column, keys):
    total = jnp.zeros(keys.shape, jnp.float32)
    for first in range(0, column.shape[0], 128):
        smaller = jnp.where(column[first : first + 128] < keys, 1.0, 0.0)
        total = total + jnp.sum(smaller, axis=0, keepdims=True)
    return total


def sort_kernel(
    routes_ref,
    weight_ref,
    grads_ref,
    held_ref,
    mine_ref,
    core_ref,
    starts_ref,
    head_ref,
    order_ref,
    piece_ref,
    stage,
    sems,
):
    width = piece_ref.shape[1]
    count = sems.shape[0] - 1
    part = grads_ref.shape[0] // count
    copies = [pltpu.make_async_copy(weight_ref, stage, sems.at[count])]
    for n in range(count):
        here = pl.ds(n * part, part)
        copies.append(pltpu.make_async_copy(grads_ref.at[here], held_ref.at[here], sems.at[n]))
    for copy in copies:
        copy.start()
    routes = row_of(routes_ref[...])
    pairs = routes.shape[1]
    column = key_column(routes)
    keys = routes * pairs + lax.broadcasted_iota(jnp.int32, (1, pairs), 1)
    place = ranks(column, keys.astype(jnp.float32)).astype(jnp.int32)
    firsts = lax.broadcasted_iota(jnp.int32, starts_ref.shape, 1) * pairs
    starts = ranks(column, firsts.astype(jnp.float32)).astype(jnp.int32)
    starts_ref[...] = starts
    wide = head_ref.shape[1] - starts.shape[1]
    digits = [starts // DIGIT, starts % DIGIT]
    digits = [jnp.pad(d.astype(jnp.float32), ((0, 0), (0, wide))) for d in digits]
    row = lax.broadcasted_iota(jnp.int32, head_ref.shape, 0)
    head = jnp.where(row == 0, digits[0], jnp.where(row == 1, digits[1], 0.0))
    head_ref[...] = head.astype(jnp.bfloat16)
    rows = piece_ref.shape[0] - ALIGN
    for first in range(0, pairs, rows):
        ids = first + lax.broadcasted_iota(jnp.int32, (rows, pairs), 0)
        order_ref[first : first + rows, :] = jnp.where(place == ids, 1.0, 0.0).astype(jnp.bfloat16)
    copies[0].wait()
    core_ref[...] = stage[:, columns_of(1, width)]
    mine_ref[...] = stage[:, columns_of(0, width)]
    for copy in copies[1:]:
        copy.wait()
    piece_ref[0:rows, :] = jnp.dot(
        order_ref[0:rows, :],
        held_ref[:, :, columns_of(2, width)].reshape(pairs, width),
        preferred_element_type=jnp.float32,
    ).astype(jnp.bfloat16)
    piece_ref[rows:, :] = head_ref[...]


def join_kernel(one_ref, two_ref, out_ref):
    half = one_ref.shape[0]
    out_ref[0:half, :] = one_ref[...]
    out_ref[half:, :] = two_ref[...]


def permute_kernel(plan, order_ref, head_ref, grads_ref, *outs):
    pairs, width = order_ref.shape[0], outs[0].shape[1]
    for device in sorted({device for device, _, _ in plan}):
        grads = grads_ref[:, :, columns_of(device, width)].reshape(pairs, width)
        for out, (target, first, rows) in zip(outs, plan):
            if target == device:
                out[0:rows, :] = jnp.dot(
                    order_ref[first : first + rows, :], grads, preferred_element_type=jnp.float32
                ).astype(jnp.bfloat16)
                if out.shape[0] > rows:
                    out[rows:, :] = head_ref[...]


def basis_kernel(
    hidden_ref, proj_ref, segment_ref, routes_ref, out_ref, order_ref, hidden, proj, sems
):
    count = sems.shape[0] - 1
    part = hidden.shape[0] // count
    copies = [pltpu.make_async_copy(proj_ref, proj, sems.at[count])]
    for n in range(count):
        here = pl.ds(n * part, part)
        copies.append(pltpu.make_async_copy(hidden_ref.at[here], hidden.at[here], sems.at[n]))
    for copy in copies:
        copy.start()
    tops, tokens = routes_ref.shape
    pairs = tops * tokens
    column = key_column(row_of(routes_ref[...]))
    at = [
        routes_ref[k : k + 1, :] * pairs + lax.broadcasted_iota(jnp.int32, (1, tokens), 1) * tops + k
        for k in range(tops)
    ]
    place = ranks(column, jnp.concatenate(at, axis=1).astype(jnp.float32)).astype(jnp.int32)
    for first in range(0, pairs, 256):
        ids = first + lax.broadcasted_iota(jnp.int32, (256, pairs), 0)
        order_ref[first : first + 256, :] = jnp.where(place == ids, 1.0, 0.0).astype(jnp.bfloat16)
    segment = (segment_ref[...] - lax.axis_index("expert") * SEG_DEV).astype(jnp.float32)
    segment = jnp.broadcast_to(segment, (8, tokens)).T[:, 0:1]
    for copy in copies:
        copy.wait()
    projected = lax.dot_general(hidden[...], proj[...], NT, preferred_element_type=jnp.float32)
    zero = jnp.zeros_like(projected)
    picked = [jnp.where(segment == float(s), projected, zero) for s in range(SEG_DEV)]
    even = jnp.concatenate([b for p in picked for b in (p, zero)], axis=1)
    odd = jnp.concatenate([b for p in picked for b in (zero, p)], axis=1)
    out_ref[...] = jnp.concatenate([even, odd], axis=0).astype(out_ref.dtype)


def packed(total, first, pairs, rank):
    half = pairs // 2
    low = lax.broadcasted_iota(jnp.int32, (half, LANES), 1) < rank
    one = total[first : first + half, :]
    two = total[first + half : first + pairs, :]
    return jnp.where(low, one + pltpu.roll(one, rank, 1), two + pltpu.roll(two, rank, 1))


def partial_kernel(
    rank, pairs, window, new_tokens, new_units, tasks, fresh, sends, groups, bases_ref, *refs
):
    start_refs = dict(zip(groups, refs))
    refs = refs[len(groups) :]
    token_refs, refs = refs[: len(new_tokens)], refs[len(new_tokens) :]
    unit_refs, refs = refs[: len(new_units)], refs[len(new_units) :]
    if fresh:
        tokens, units, total = refs
        send_refs = ()
        total[...] = jnp.zeros_like(total)
    else:
        tokens, units, total = refs[3:6]
        send_refs = refs[6:]
    for ref, (first, count) in zip(token_refs, new_tokens):
        tokens[first : first + count, :] = ref[0:count, :]
    cols = units.shape[1]
    for ref, place in zip(unit_refs, new_units):
        for half in range(CORES):
            units[place + half] = ref[half * cols : (half + 1) * cols, :]
    held = cols // rank
    per_tile = LANES // rank
    low = lax.broadcasted_iota(jnp.int32, (1, LANES), 1) < rank

    device = lax.axis_index("expert")

    def process(w, members):
        base = bases_ref[device, w]
        heres, offsets = [], []
        for g in members:
            at = jnp.minimum(start_refs[g][0, base] & -ALIGN, pairs - window)
            offsets.append(at)
            heres.append(pl.ds(pl.multiple_of(g * pairs + at, ALIGN), window))
        rows = [tokens[here, :] for here in heres]
        rows = jnp.concatenate(rows, axis=0) if len(rows) > 1 else rows[0]
        dense = lax.dot_general(rows, units[w], NT, preferred_element_type=jnp.float32)
        for n, g in enumerate(members):
            value = total[heres[n], :]
            number = offsets[n] + lax.broadcasted_iota(jnp.int32, (window, LANES), 0)
            for j in range(cols // LANES):
                edge = [start_refs[g][0, base + j * per_tile + i] for i in range(per_tile + 1)]
                inside = (number >= jnp.where(low, edge[0], edge[1])) & (
                    number < jnp.where(low, edge[1], edge[2])
                )
                part = dense[n * window : (n + 1) * window, j * LANES : (j + 1) * LANES]
                value = jnp.where(inside, part, value)
            total[heres[n], :] = value

    for task in tasks:
        if task[0] == "units":
            _, members, first_w, count = task

            def each(i, carry, members=members, first_w=first_w):
                process(first_w + i, members)
                return carry

        else:
            _, member, first_row, end_row, first_w, count = task

            def each(
                i, carry, member=member, first_row=first_row, end_row=end_row, first_w=first_w
            ):
                w = first_w + i
                base = bases_ref[device, w]
                touches = (start_refs[member][0, base] < end_row) & (
                    start_refs[member][0, base + held] > first_row
                )

                @pl.when(touches)
                def _():
                    process(w, [member])

                return carry

        lax.fori_loop(0, count, each, 0)
    for ref, g in zip(send_refs, sends):
        ref[...] = packed(total, g * pairs, pairs, rank).astype(ref.dtype)


def accumulate(
    state, bases, starts, tokens, units, tasks, rank, pairs, window, places=0, sends=(), cost=QUICK
):
    fresh = state is None
    operands = [bases, *starts.values(), *[a for a, _, _ in tokens], *[a for a, _ in units]]
    specs = [SMEM] * (1 + len(starts)) + [VMEM] * (len(tokens) + len(units))
    if fresh:
        width = units[0][0].shape[1]
        shapes = [
            pltpu.VMEM((QUAD * pairs, width), jnp.bfloat16),
            pltpu.VMEM((places, units[0][0].shape[0] // CORES, width), jnp.bfloat16),
            pltpu.VMEM((QUAD * pairs, LANES), jnp.float32),
        ]
        aliases = {}
    else:
        aliases = {len(operands) + i: i for i in range(3)}
        operands += [in_vmem(a) for a in state]
        specs += [VMEM] * 3
        shapes = [pltpu.VMEM(a.shape, a.dtype) for a in state]
    shapes += [pltpu.VMEM((pairs // 2, LANES), jnp.bfloat16)] * len(sends)
    out = pl.pallas_call(
        functools.partial(
            partial_kernel,
            rank,
            pairs,
            window,
            [(first, count) for _, first, count in tokens],
            [p for _, p in units],
            tasks,
            fresh,
            sends,
            list(starts),
        ),
        out_shape=shapes,
        in_specs=specs,
        out_specs=[VMEM] * len(shapes),
        input_output_aliases=aliases,
        compiler_params=pltpu.CompilerParams(vmem_limit_bytes=8 * MIB),
        cost_estimate=cost,
    )(*operands)
    return list(out[:3]), list(out[3:])


def late_kernel(rank, pairs, window, place, groups, bases_ref, *refs):
    start_refs, tokens, refs = refs[:groups], refs[groups], refs[groups + 1 :]
    unit_refs, outs = refs[:2], refs[2:]
    per_tile = LANES // rank
    low = lax.broadcasted_iota(jnp.int32, (1, LANES), 1) < rank
    device = lax.axis_index("expert")
    first_core = device % CORES == 0
    for u, unit_ref in enumerate(unit_refs):
        cols = unit_ref.shape[0] // CORES
        folded = []
        for half in range(CORES):
            base = bases_ref[device, place + u * CORES + half]
            offsets, rows = [], []
            for g in range(groups):
                at = jnp.minimum(start_refs[g][0, base] & -ALIGN, pairs - window)
                offsets.append(at)
                rows.append(tokens[pl.ds(pl.multiple_of(g * pairs + at, ALIGN), window), :])
            dense = lax.dot_general(
                jnp.concatenate(rows, axis=0),
                unit_ref[half * cols : (half + 1) * cols, :],
                NT,
                preferred_element_type=jnp.float32,
            )
            found = []
            for g in range(groups):
                value = jnp.zeros((window, LANES), jnp.float32)
                number = offsets[g] + lax.broadcasted_iota(jnp.int32, (window, LANES), 0)
                for j in range(cols // LANES):
                    edge = [start_refs[g][0, base + j * per_tile + i] for i in range(per_tile + 1)]
                    inside = (number >= jnp.where(low, edge[0], edge[1])) & (
                        number < jnp.where(low, edge[1], edge[2])
                    )
                    part = dense[g * window : (g + 1) * window, j * LANES : (j + 1) * LANES]
                    value = jnp.where(inside, part, value)
                found.append(value + pltpu.roll(value, rank, 1))
            folded.append(found)
        for g, out in enumerate(outs):
            one, two = folded[0][g], folded[1][g]
            zero = jnp.where(first_core, one, two)
            other = jnp.where(first_core, two, one)
            out[u * window : (u + 1) * window, :] = jnp.where(low, zero, other).astype(out.dtype)


def expand(routes_ref, turned, lines, first, tiles):
    tops, tokens = routes_ref.shape
    rank = turned.shape[0]

    def one(tile, carry):
        here = pl.multiple_of(tile * 8, 8)
        ids = first + here + lax.broadcasted_iota(jnp.int32, (8, tokens), 0)
        masks = [routes_ref[k : k + 1, :] == ids for k in range(tops)]
        for r in range(rank):
            value = jnp.zeros((8, tokens), jnp.float32)
            for k in range(tops):
                row = turned[r : r + 1, k * tokens : (k + 1) * tokens]
                value = jnp.where(masks[k], row, value)
            side = r % 2 * tokens
            lines[r // 2, pl.ds(here, 8), side : side + tokens] = value
        return carry

    lax.fori_loop(0, tiles, one, 0)


def form(lines, basis_ref, first, count, out_ref, rank):
    experts, width = lines.shape[1:]
    made = jnp.dot(
        lines[first : first + count].reshape(count * experts, width).astype(jnp.bfloat16),
        basis_ref[...],
        preferred_element_type=jnp.float32,
    ).astype(jnp.bfloat16)
    for pair in range(count):
        for s in range(SEG_DEV):
            out_ref[s, :, pl.ds((first + pair) * 2 * rank, 2 * rank)] = made[
                pair * experts : (pair + 1) * experts, s * 2 * rank : (s + 1) * 2 * rank
            ]


def blocks_kernel(
    rank, routes_ref, basis_ref, order_ref, total_ref, b_ref, c_ref, d_ref, out_ref, turned, lines
):
    half = b_ref.shape[0]
    value = packed(total_ref, 0, 2 * half, rank)
    for ref in (b_ref, c_ref, d_ref):
        value = value + ref[...].astype(jnp.float32)
    value = value.T
    value = jnp.concatenate([value[0:rank], value[rank : 2 * rank]], axis=1).astype(jnp.bfloat16)
    turned[...] = jnp.dot(value, order_ref[...], preferred_element_type=jnp.float32)
    expand(routes_ref, turned, lines, 0, lines.shape[1] // 8)
    for first in range(0, rank // 2, 8):
        form(lines, basis_ref, first, 8, out_ref, rank)


def last_kernel(
    rank,
    place,
    count,
    held,
    bases_ref,
    starts_ref,
    routes_ref,
    basis_ref,
    order_ref,
    turned_ref,
    own_ref,
    b_ref,
    c_ref,
    d_ref,
    _,
    out_ref,
    turned,
    lines,
    block,
    sem,
):
    window = own_ref.shape[0] // 2
    pairs = order_ref.shape[0]
    value = own_ref[...]
    for ref in (b_ref, c_ref, d_ref):
        value = value + ref[...].astype(jnp.float32)
    value = value.T.astype(jnp.bfloat16)
    device = lax.axis_index("expert")
    first = bases_ref[device, place] // count * count
    total = turned_ref[...]
    for u in range(2):
        unit = bases_ref[device, place + u * CORES] // (CORES * held) * (CORES * held)
        for core in range(CORES):
            at = jnp.minimum(starts_ref[0, unit + core * held] & -ALIGN, pairs - window)
            total = total + jnp.dot(
                value[core * rank : (core + 1) * rank, u * window : (u + 1) * window],
                order_ref[pl.ds(pl.multiple_of(at, ALIGN), window), :],
                preferred_element_type=jnp.float32,
            )
    turned[...] = total
    expand(routes_ref, turned, lines, first, count // 8)
    form(lines, basis_ref, 0, rank // 2, block, rank)
    copy = pltpu.make_async_copy(
        block, out_ref.at[:, pl.ds(pl.multiple_of(first, count), count), :], sem
    )
    copy.start()
    copy.wait()


def local(hidden_in, out_grads, routes, segments, in_proj, out_proj):
    tokens, tops = routes.shape
    exp_here, rank, width = out_proj.shape
    owners, groups = lax.axis_size("expert"), lax.axis_size("groups")
    experts = exp_here * owners
    pairs = tokens * tops
    capacity = max(2, 3 * pairs // (2 * experts))
    window = min(pairs, -(-(exp_here * capacity + ALIGN - 1) // ALIGN) * ALIGN)
    quarter = width // QUAD
    cols = exp_here * rank
    rows = pairs // PIECES
    index = lax.axis_index("expert")
    slots = owners // CORES // 2
    ring = [0, *range(1, slots, 2), *range((slots - 1) // 2 * 2, 0, -2)]
    following = {a: b for a, b in zip(ring, ring[1:] + ring[:1])}
    before = {b: a for a, b in following.items()}

    def swap(array, side, bit):
        table = [
            (g * owners + e, (g ^ side) * owners + (e ^ bit))
            for g in range(groups)
            for e in range(owners)
        ]
        return lax.ppermute(array, BOTH, table)

    def along(array, table):
        wide = 2 * CORES
        pairs_of = [(e, table[e // wide] * wide + e % wide) for e in range(owners)]
        return lax.ppermute(array, "expert", pairs_of)

    def tie(*arrays):
        return lax.optimization_barrier(arrays)

    final = slots - 1
    names_a = [(n, 0) for n in range(final - 1)] + [(0, 1)]
    names_b = [(final - 1, 0)] + [(n, 1) for n in range(1, final - 1)]
    names_c = [(final - 1, 1)]
    arrival = names_a + names_b + names_c + [(final, 0), (final, 1)]

    def source(z, hops):
        for _ in range(hops):
            z = before[z]
        return z

    rows_of = [
        [
            ((source(e // (2 * CORES), n) * 2 + (e // CORES % 2 ^ y)) * CORES + (e % CORES ^ c)) * exp_here
            for n, y in arrival
            for c in range(CORES)
        ]
        for e in range(owners)
    ]
    places = CORES * len(arrival)
    bases = jnp.asarray(np.array(rows_of, np.int32))

    unit_shape = pltpu.VMEM((cols, quarter), jnp.bfloat16)
    order_shape = pltpu.VMEM((pairs, pairs), jnp.bfloat16)

    def rows_shape(count):
        return pltpu.VMEM((count, quarter), jnp.bfloat16)

    by_rank = routes.T
    edges = -(-(experts + 1) // LANES) * LANES
    held_grads, mine_unit, core_unit, own_starts, head, order, first_piece = pl.pallas_call(
        sort_kernel,
        out_shape=[
            pltpu.VMEM(out_grads.shape, jnp.bfloat16),
            unit_shape,
            unit_shape,
            jax.ShapeDtypeStruct((1, edges), jnp.int32),
            rows_shape(ALIGN),
            order_shape,
            rows_shape(2 * rows + ALIGN),
        ],
        in_specs=[VMEM, HBM, HBM],
        out_specs=[VMEM] * 7,
        scratch_shapes=[pltpu.VMEM((cols, width), jnp.bfloat16), pltpu.SemaphoreType.DMA((9,))],
        compiler_params=pltpu.CompilerParams(vmem_limit_bytes=12 * MIB),
        cost_estimate=QUICK,
    )(by_rank, in_hbm(out_proj.reshape(cols, width)), in_hbm(out_grads))
    other_unit = swap(core_unit, 0, 1)
    unit = pl.pallas_call(
        join_kernel,
        out_shape=pltpu.VMEM((CORES * cols, quarter), jnp.bfloat16),
        in_specs=[VMEM] * 2,
        out_specs=VMEM,
        compiler_params=pltpu.CompilerParams(vmem_limit_bytes=4 * MIB),
        cost_estimate=QUICK,
    )(mine_unit, other_unit)

    def permuted(plan, headed, *after):
        held, *_ = tie(order, *after)
        return pl.pallas_call(
            functools.partial(permute_kernel, plan),
            out_shape=[
                rows_shape(many + (ALIGN if n in headed else 0))
                for n, (_, _, many) in enumerate(plan)
            ],
            in_specs=[VMEM] * 3,
            out_specs=[VMEM] * len(plan),
            compiler_params=pltpu.CompilerParams(vmem_limit_bytes=12 * MIB),
            cost_estimate=QUICK,
        )(in_vmem(held), head, in_vmem(held_grads))

    def starts_in(block, count):
        digits = block[count : count + 2, :edges].astype(jnp.int32)
        return (digits[0] * DIGIT + digits[1]).reshape(1, edges)

    side_pieces = [swap(first_piece, 1, 0)]
    ring_unit = unit
    if O["z1"] == "first":
        ring_unit, _ = tie(unit, first_piece)
    held = {(0, 0): unit, (1, 0): along(ring_unit, following)}
    p2after = {"none": [], "unit": [unit], "z1": [held[1, 0]]}[O["p2"]]
    (second_piece,) = permuted([(2, 2 * rows, 2 * rows)], [], *p2after)
    second_send = second_piece
    half = 2 * rows
    if O["cores"] == 2:
        own_tokens, *for_core = permuted([(0, 0, pairs), (1, 0, half), (1, half, half)], [1], second_piece)
        core_counts = [half, half]
    else:
        own_tokens, *for_core = permuted([(0, 0, pairs), (1, 0, pairs)], [1], second_piece)
        core_counts = [pairs]
    third_piece, last_piece = permuted([(3, 0, 3 * rows), (3, 3 * rows, rows)], [0], own_tokens)
    if O["core_in"] == "ev1":
        *for_core, held[1, 0] = tie(*for_core, held[1, 0])
    from_core = [swap(piece, 0, 1) for piece in for_core]
    y0_in = unit
    if O["y0"] == "first":
        y0_in, _ = tie(unit, first_piece)
    elif O["y0"] == "second":
        y0_in, _ = tie(unit, second_piece)
    elif O["y0"] == "own":
        y0_in, _ = tie(unit, own_tokens)
    elif O["y0"] == "core":
        y0_in, *from_core = tie(unit, *from_core)
    held[0, 1] = swap(y0_in, 0, CORES)
    side_pieces.append(swap(second_send, 1, 0))
    basis_in = [last_piece]
    if "z1" in O["basis"]:
        basis_in.append(held[1, 0])
    if "core" in O["basis"]:
        basis_in += from_core
    local_segments, *basis_out = tie(segments, *basis_in)
    if "core" in O["basis"]:
        from_core = basis_out[len(basis_out) - len(from_core):]
    basis, order_back = pl.pallas_call(
        basis_kernel,
        out_shape=[
            pltpu.VMEM((2 * tokens, SEG_DEV * 2 * rank), jnp.bfloat16),
            order_shape,
        ],
        in_specs=[HBM, HBM, VMEM, VMEM],
        out_specs=[VMEM] * 2,
        scratch_shapes=[
            pltpu.VMEM(hidden_in.shape, jnp.bfloat16),
            pltpu.VMEM(in_proj.shape, jnp.bfloat16),
            pltpu.SemaphoreType.DMA((5,)),
        ],
        compiler_params=pltpu.CompilerParams(vmem_limit_bytes=12 * MIB),
        cost_estimate=QUICK,
    )(in_hbm(hidden_in), in_hbm(in_proj), local_segments.reshape(1, tokens), by_rank)

    call = functools.partial(
        accumulate, bases=bases, rank=rank, pairs=pairs, window=window, places=places
    )
    place_of = {name: CORES * n for n, name in enumerate(arrival)}
    starts = {0: own_starts}
    members = []
    known_units = 0
    state = None

    def work(names, complete=(), partial=(), sends=(), cost=QUICK):
        nonlocal state, known_units
        tasks, arrived = [], []
        for group, blocks in complete:
            first = 0
            for piece, count in blocks:
                arrived.append((piece, group * pairs + first, count))
                first += count
            if group:
                starts[group] = starts_in(*blocks[0])
            members.append(group)
        fresh = [group for group, _ in complete]
        if fresh and known_units:
            tasks.append(("units", fresh, 0, known_units))
        if names:
            tasks.append(("units", list(members), known_units, CORES * len(names)))
        known_units += CORES * len(names)
        for group, piece, first, count in partial:
            arrived.append((piece, group * pairs + first, count))
            if first == 0:
                starts[group] = starts_in(piece, count)
                members.append(group)
            tasks.append(("piece", group, first, first + count, 0, known_units))
        state, out = call(
            state,
            starts=starts,
            tokens=arrived,
            units=[(held[n], place_of[n]) for n in names],
            tasks=tasks,
            sends=sends,
            cost=cost,
        )
        return out

    def group_tie(names, array):
        nonlocal basis, from_core
        items = []
        for name in names:
            if name == "y0":
                items.append(held[0, 1])
            if name == "y1":
                items.append(held[1, 1])
            if name == "z1":
                items.append(held[1, 0])
            if name == "z2":
                items.append(held[near])
            if name == "side0":
                items.append(side_pieces[0])
            if name == "side1":
                items.append(side_pieces[1])
            if name == "basis":
                items.append(basis)
            if name == "core":
                items += from_core
        out = tie(array, *items)
        out = list(out)
        array, out = out[0], out[1:]
        for name in names:
            if name == "y0":
                held[0, 1] = out.pop(0)
            if name == "y1":
                held[1, 1] = out.pop(0)
            if name == "z1":
                held[1, 0] = out.pop(0)
            if name == "z2":
                held[near] = out.pop(0)
            if name == "side0":
                side_pieces[0] = out.pop(0)
            if name == "side1":
                side_pieces[1] = out.pop(0)
            if name == "basis":
                basis = out.pop(0)
            if name == "core":
                from_core = [out.pop(0) for _ in from_core]
        return array

    held[1, 0] = group_tie(O["ev1"], held[1, 0])
    for n in range(1, final - 1):
        held[n + 1, 0] = along(held[n, 0], following)
        held[n, 1] = swap(held[n, 0], 0, CORES)
    third_piece = group_tie(O["diag"], third_piece)
    diagonal_pieces = [swap(third_piece, 1, 1)]
    near = (final - 1, 0)
    held[near] = group_tie(O["ev2"], held[near])
    COST = {0: QUICK, 1: SHORT}
    work(
        names_a,
        complete=[(0, [(own_tokens, pairs)]), (1, list(zip(from_core, core_counts)))],
        cost=COST[O["ka"]],
    )
    if O["z3_ka"]:
        held[near], *state = tie(held[near], *state)
    back_unit = group_tie(O["w"], held[0, 1])
    if O["w_ka"]:
        back_unit, *state = tie(back_unit, *state)
    held[final, 1] = along(back_unit, before)
    held[final, 0] = along(held[near], following)
    held[final - 1, 1] = swap(held[near], 0, CORES)
    last_piece = group_tie(O["last"], last_piece)
    diagonal_pieces.append(swap(last_piece, 1, 1))
    work(names_b, complete=[(2, [(piece, half) for piece in side_pieces])], cost=COST[O["k0"]])
    sent = work(
        names_c if O["y2"] == "c" else [], partial=[(3, diagonal_pieces[0], 0, 3 * rows)], sends=[1, 2] if O["y2"] == "c" else [], cost=COST[O["k1"]]
    )
    sent = sent + work(
        [] if O["y2"] == "c" else names_c, partial=[(3, diagonal_pieces[1], 3 * rows, rows)], sends=[3] if O["y2"] == "c" else [1, 2, 3], cost=COST[O["k2"]]
    )

    def returned(arrays):
        return [
            swap(array, side, bit) for array, (side, bit) in zip(arrays, ((0, 1), (1, 0), (1, 1)))
        ]

    early = returned(sent)
    place = places - 2 * CORES
    own_late, *sent = pl.pallas_call(
        functools.partial(late_kernel, rank, pairs, window, place, QUAD),
        out_shape=[pltpu.VMEM((2 * window, LANES), jnp.float32)]
        + [pltpu.VMEM((2 * window, LANES), jnp.bfloat16)] * (QUAD - 1),
        in_specs=[SMEM] * (1 + QUAD) + [VMEM] * 3,
        out_specs=[VMEM] * QUAD,
        compiler_params=pltpu.CompilerParams(vmem_limit_bytes=8 * MIB),
        cost_estimate=QUICK,
    )(bases, *[starts[g] for g in range(QUAD)], in_vmem(state[0]), held[final, 0], held[final, 1])
    late = returned(sent)
    *early, own_late = tie(*early, own_late)
    out, turned = pl.pallas_call(
        functools.partial(blocks_kernel, rank),
        out_shape=[
            jax.ShapeDtypeStruct((SEG_DEV, experts, rank * rank), jnp.bfloat16),
            pltpu.VMEM((rank, pairs), jnp.float32),
        ],
        in_specs=[VMEM] * 7,
        out_specs=[VMEM] * 2,
        scratch_shapes=[pltpu.VMEM((rank // 2, experts, 2 * tokens), jnp.float32)],
        compiler_params=pltpu.CompilerParams(vmem_limit_bytes=32 * MIB),
        cost_estimate=QUICK,
    )(by_rank, basis, in_vmem(order_back), in_vmem(state[2]), *early)
    count = 2 * CORES * exp_here
    return pl.pallas_call(
        functools.partial(last_kernel, rank, place, count, exp_here),
        out_shape=jax.ShapeDtypeStruct(out.shape, out.dtype),
        in_specs=[SMEM] * 2 + [VMEM] * 8 + [HBM],
        out_specs=HBM,
        scratch_shapes=[
            pltpu.VMEM((rank, pairs), jnp.float32),
            pltpu.VMEM((rank // 2, count, 2 * tokens), jnp.float32),
            pltpu.VMEM((SEG_DEV, count, rank * rank), jnp.bfloat16),
            pltpu.SemaphoreType.DMA,
        ],
        input_output_aliases={10: 0},
        compiler_params=pltpu.CompilerParams(vmem_limit_bytes=16 * MIB),
        cost_estimate=QUICK,
    )(bases, own_starts, by_rank, basis, in_vmem(order_back), in_vmem(turned), own_late, *late, out)


def solution(mesh):
    placed = (
        P(("groups", "expert"), None),
        P(("groups", "expert"), None, None),
        P(("groups", "expert"), None),
        P(("groups", "expert")),
        P(),
        P("expert", None, None),
    )
    return jax.shard_map(
        local,
        mesh=mesh,
        in_specs=placed,
        out_specs=P(("groups", "expert"), None, None),
        check_vma=False,
    )
```

```python
import functools

import jax
import jax.numpy as jnp
import numpy as np
from jax import lax
from jax.experimental import pallas as pl
from jax.experimental.pallas import tpu as pltpu
from jax.sharding import PartitionSpec as P

SEG_DEV = 2
O = {'p1': 'core_unit', 'z1': 'none', 'p2': 'unit', 'cores': 1, 'core_in': 'none', 'y0': 'unit', 'basis': [], 'ev1': ['side0'], 'diag': ['side1'], 'ev2': ['basis', 'side0'], 'w': ['basis', 'core'], 'last': ['z2'], 'ka': 1, 'z3_ka': 0, 'w_ka': 0, 'k0': 1, 'k1': 0, 'k2': 1, 'y2': 'd', 'core_k': 'b', 'side_k': 'b'}
CORES = 2
SIDES = 2
QUAD = 4
PIECES = 4
LANES = 128
ALIGN = 16
DIGIT = 32
BOTH = ("groups", "expert")
MIB = 1024 * 1024
VMEM = pl.BlockSpec(memory_space=pltpu.VMEM)
SMEM = pl.BlockSpec(memory_space=pltpu.SMEM)
HBM = pl.BlockSpec(memory_space=pl.ANY)
QUICK = pl.CostEstimate(flops=1, bytes_accessed=1, transcendentals=0)
SHORT = pl.CostEstimate(flops=10**9, bytes_accessed=1, transcendentals=0)
NT = (((1,), (1,)), ((), ()))


def in_vmem(array):
    return pltpu.with_memory_space_constraint(array, pltpu.VMEM)


def in_hbm(array):
    return pltpu.with_memory_space_constraint(array, pltpu.HBM)


def place_in_quad(flip):
    side, core = lax.axis_index("groups") % SIDES, lax.axis_index("expert") % CORES
    return (side ^ (flip // CORES)) * CORES + (core ^ (flip % CORES))


def columns_of(flip, width):
    return pl.ds(pl.multiple_of(place_in_quad(flip) * width, width), width)


def row_of(routes):
    tops, tokens = routes.shape
    pairs = tops * tokens
    lane = lax.broadcasted_iota(jnp.int32, (tokens, pairs), 1)
    token = lax.broadcasted_iota(jnp.int32, (tokens, pairs), 0)
    spread = jnp.where(lane // tops == token, 1.0, 0.0).astype(jnp.bfloat16)
    values = routes.astype(jnp.float32).astype(jnp.bfloat16)
    every = jnp.dot(values, spread, preferred_element_type=jnp.float32)
    lane = lax.broadcasted_iota(jnp.int32, (tops, pairs), 1)
    k = lax.broadcasted_iota(jnp.int32, (tops, pairs), 0)
    return jnp.sum(jnp.where(lane % tops == k, every, 0.0), axis=0, keepdims=True).astype(jnp.int32)


def key_column(routes_row):
    count = routes_row.shape[1]
    keys = routes_row * count + lax.broadcasted_iota(jnp.int32, (1, count), 1)
    return jnp.broadcast_to(keys.astype(jnp.float32), (8, count)).T[:, 0:1]


def ranks(column, keys):
    total = jnp.zeros(keys.shape, jnp.float32)
    for first in range(0, column.shape[0], 128):
        smaller = jnp.where(column[first : first + 128] < keys, 1.0, 0.0)
        total = total + jnp.sum(smaller, axis=0, keepdims=True)
    return total


def sort_kernel(
    routes_ref,
    weight_ref,
    grads_ref,
    held_ref,
    mine_ref,
    core_ref,
    starts_ref,
    head_ref,
    order_ref,
    piece_ref,
    stage,
    sems,
):
    width = piece_ref.shape[1]
    count = sems.shape[0] - 1
    part = grads_ref.shape[0] // count
    copies = [pltpu.make_async_copy(weight_ref, stage, sems.at[count])]
    for n in range(count):
        here = pl.ds(n * part, part)
        copies.append(pltpu.make_async_copy(grads_ref.at[here], held_ref.at[here], sems.at[n]))
    for copy in copies:
        copy.start()
    routes = row_of(routes_ref[...])
    pairs = routes.shape[1]
    column = key_column(routes)
    keys = routes * pairs + lax.broadcasted_iota(jnp.int32, (1, pairs), 1)
    place = ranks(column, keys.astype(jnp.float32)).astype(jnp.int32)
    firsts = lax.broadcasted_iota(jnp.int32, starts_ref.shape, 1) * pairs
    starts = ranks(column, firsts.astype(jnp.float32)).astype(jnp.int32)
    starts_ref[...] = starts
    wide = head_ref.shape[1] - starts.shape[1]
    digits = [starts // DIGIT, starts % DIGIT]
    digits = [jnp.pad(d.astype(jnp.float32), ((0, 0), (0, wide))) for d in digits]
    row = lax.broadcasted_iota(jnp.int32, head_ref.shape, 0)
    head = jnp.where(row == 0, digits[0], jnp.where(row == 1, digits[1], 0.0))
    head_ref[...] = head.astype(jnp.bfloat16)
    rows = piece_ref.shape[0] - ALIGN
    for first in range(0, pairs, rows):
        ids = first + lax.broadcasted_iota(jnp.int32, (rows, pairs), 0)
        order_ref[first : first + rows, :] = jnp.where(place == ids, 1.0, 0.0).astype(jnp.bfloat16)
    copies[0].wait()
    core_ref[...] = stage[:, columns_of(1, width)]
    mine_ref[...] = stage[:, columns_of(0, width)]
    for copy in copies[1:]:
        copy.wait()
    piece_ref[0:rows, :] = jnp.dot(
        order_ref[0:rows, :],
        held_ref[:, :, columns_of(2, width)].reshape(pairs, width),
        preferred_element_type=jnp.float32,
    ).astype(jnp.bfloat16)
    piece_ref[rows:, :] = head_ref[...]


def join_kernel(one_ref, two_ref, out_ref):
    half = one_ref.shape[0]
    out_ref[0:half, :] = one_ref[...]
    out_ref[half:, :] = two_ref[...]


def permute_kernel(plan, order_ref, head_ref, grads_ref, *outs):
    pairs, width = order_ref.shape[0], outs[0].shape[1]
    for device in sorted({device for device, _, _ in plan}):
        grads = grads_ref[:, :, columns_of(device, width)].reshape(pairs, width)
        for out, (target, first, rows) in zip(outs, plan):
            if target == device:
                out[0:rows, :] = jnp.dot(
                    order_ref[first : first + rows, :], grads, preferred_element_type=jnp.float32
                ).astype(jnp.bfloat16)
                if out.shape[0] > rows:
                    out[rows:, :] = head_ref[...]


def basis_kernel(
    hidden_ref, proj_ref, segment_ref, routes_ref, out_ref, order_ref, hidden, proj, sems
):
    count = sems.shape[0] - 1
    part = hidden.shape[0] // count
    copies = [pltpu.make_async_copy(proj_ref, proj, sems.at[count])]
    for n in range(count):
        here = pl.ds(n * part, part)
        copies.append(pltpu.make_async_copy(hidden_ref.at[here], hidden.at[here], sems.at[n]))
    for copy in copies:
        copy.start()
    tops, tokens = routes_ref.shape
    pairs = tops * tokens
    column = key_column(row_of(routes_ref[...]))
    at = [
        routes_ref[k : k + 1, :] * pairs + lax.broadcasted_iota(jnp.int32, (1, tokens), 1) * tops + k
        for k in range(tops)
    ]
    place = ranks(column, jnp.concatenate(at, axis=1).astype(jnp.float32)).astype(jnp.int32)
    for first in range(0, pairs, 256):
        ids = first + lax.broadcasted_iota(jnp.int32, (256, pairs), 0)
        order_ref[first : first + 256, :] = jnp.where(place == ids, 1.0, 0.0).astype(jnp.bfloat16)
    segment = (segment_ref[...] - lax.axis_index("expert") * SEG_DEV).astype(jnp.float32)
    segment = jnp.broadcast_to(segment, (8, tokens)).T[:, 0:1]
    for copy in copies:
        copy.wait()
    projected = lax.dot_general(hidden[...], proj[...], NT, preferred_element_type=jnp.float32)
    zero = jnp.zeros_like(projected)
    picked = [jnp.where(segment == float(s), projected, zero) for s in range(SEG_DEV)]
    even = jnp.concatenate([b for p in picked for b in (p, zero)], axis=1)
    odd = jnp.concatenate([b for p in picked for b in (zero, p)], axis=1)
    out_ref[...] = jnp.concatenate([even, odd], axis=0).astype(out_ref.dtype)


def packed(total, first, pairs, rank):
    half = pairs // 2
    low = lax.broadcasted_iota(jnp.int32, (half, LANES), 1) < rank
    one = total[first : first + half, :]
    two = total[first + half : first + pairs, :]
    return jnp.where(low, one + pltpu.roll(one, rank, 1), two + pltpu.roll(two, rank, 1))


def partial_kernel(
    rank, pairs, window, new_tokens, new_units, tasks, fresh, sends, groups, bases_ref, *refs
):
    start_refs = dict(zip(groups, refs))
    refs = refs[len(groups) :]
    token_refs, refs = refs[: len(new_tokens)], refs[len(new_tokens) :]
    unit_refs, refs = refs[: len(new_units)], refs[len(new_units) :]
    if fresh:
        tokens, units, total = refs
        send_refs = ()
        total[...] = jnp.zeros_like(total)
    else:
        tokens, units, total = refs[3:6]
        send_refs = refs[6:]
    for ref, (first, count) in zip(token_refs, new_tokens):
        tokens[first : first + count, :] = ref[0:count, :]
    cols = units.shape[1]
    for ref, place in zip(unit_refs, new_units):
        for half in range(CORES):
            units[place + half] = ref[half * cols : (half + 1) * cols, :]
    held = cols // rank
    per_tile = LANES // rank
    low = lax.broadcasted_iota(jnp.int32, (1, LANES), 1) < rank

    device = lax.axis_index("expert")

    def process(w, members):
        base = bases_ref[device, w]
        heres, offsets = [], []
        for g in members:
            at = jnp.minimum(start_refs[g][0, base] & -ALIGN, pairs - window)
            offsets.append(at)
            heres.append(pl.ds(pl.multiple_of(g * pairs + at, ALIGN), window))
        rows = [tokens[here, :] for here in heres]
        rows = jnp.concatenate(rows, axis=0) if len(rows) > 1 else rows[0]
        dense = lax.dot_general(rows, units[w], NT, preferred_element_type=jnp.float32)
        for n, g in enumerate(members):
            value = total[heres[n], :]
            number = offsets[n] + lax.broadcasted_iota(jnp.int32, (window, LANES), 0)
            for j in range(cols // LANES):
                edge = [start_refs[g][0, base + j * per_tile + i] for i in range(per_tile + 1)]
                inside = (number >= jnp.where(low, edge[0], edge[1])) & (
                    number < jnp.where(low, edge[1], edge[2])
                )
                part = dense[n * window : (n + 1) * window, j * LANES : (j + 1) * LANES]
                value = jnp.where(inside, part, value)
            total[heres[n], :] = value

    for task in tasks:
        if task[0] == "units":
            _, members, first_w, count = task

            def each(i, carry, members=members, first_w=first_w):
                process(first_w + i, members)
                return carry

        else:
            _, member, first_row, end_row, first_w, count = task

            def each(
                i, carry, member=member, first_row=first_row, end_row=end_row, first_w=first_w
            ):
                w = first_w + i
                base = bases_ref[device, w]
                touches = (start_refs[member][0, base] < end_row) & (
                    start_refs[member][0, base + held] > first_row
                )

                @pl.when(touches)
                def _():
                    process(w, [member])

                return carry

        lax.fori_loop(0, count, each, 0)
    for ref, g in zip(send_refs, sends):
        ref[...] = packed(total, g * pairs, pairs, rank).astype(ref.dtype)


def accumulate(
    state, bases, starts, tokens, units, tasks, rank, pairs, window, places=0, sends=(), cost=QUICK
):
    fresh = state is None
    operands = [bases, *starts.values(), *[a for a, _, _ in tokens], *[a for a, _ in units]]
    specs = [SMEM] * (1 + len(starts)) + [VMEM] * (len(tokens) + len(units))
    if fresh:
        width = units[0][0].shape[1]
        shapes = [
            pltpu.VMEM((QUAD * pairs, width), jnp.bfloat16),
            pltpu.VMEM((places, units[0][0].shape[0] // CORES, width), jnp.bfloat16),
            pltpu.VMEM((QUAD * pairs, LANES), jnp.float32),
        ]
        aliases = {}
    else:
        aliases = {len(operands) + i: i for i in range(3)}
        operands += [in_vmem(a) for a in state]
        specs += [VMEM] * 3
        shapes = [pltpu.VMEM(a.shape, a.dtype) for a in state]
    shapes += [pltpu.VMEM((pairs // 2, LANES), jnp.bfloat16)] * len(sends)
    out = pl.pallas_call(
        functools.partial(
            partial_kernel,
            rank,
            pairs,
            window,
            [(first, count) for _, first, count in tokens],
            [p for _, p in units],
            tasks,
            fresh,
            sends,
            list(starts),
        ),
        out_shape=shapes,
        in_specs=specs,
        out_specs=[VMEM] * len(shapes),
        input_output_aliases=aliases,
        compiler_params=pltpu.CompilerParams(vmem_limit_bytes=8 * MIB),
        cost_estimate=cost,
    )(*operands)
    return list(out[:3]), list(out[3:])


def late_kernel(rank, pairs, window, place, groups, bases_ref, *refs):
    start_refs, tokens, refs = refs[:groups], refs[groups], refs[groups + 1 :]
    unit_refs, outs = refs[:2], refs[2:]
    per_tile = LANES // rank
    low = lax.broadcasted_iota(jnp.int32, (1, LANES), 1) < rank
    device = lax.axis_index("expert")
    first_core = device % CORES == 0
    for u, unit_ref in enumerate(unit_refs):
        cols = unit_ref.shape[0] // CORES
        folded = []
        for half in range(CORES):
            base = bases_ref[device, place + u * CORES + half]
            offsets, rows = [], []
            for g in range(groups):
                at = jnp.minimum(start_refs[g][0, base] & -ALIGN, pairs - window)
                offsets.append(at)
                rows.append(tokens[pl.ds(pl.multiple_of(g * pairs + at, ALIGN), window), :])
            dense = lax.dot_general(
                jnp.concatenate(rows, axis=0),
                unit_ref[half * cols : (half + 1) * cols, :],
                NT,
                preferred_element_type=jnp.float32,
            )
            found = []
            for g in range(groups):
                value = jnp.zeros((window, LANES), jnp.float32)
                number = offsets[g] + lax.broadcasted_iota(jnp.int32, (window, LANES), 0)
                for j in range(cols // LANES):
                    edge = [start_refs[g][0, base + j * per_tile + i] for i in range(per_tile + 1)]
                    inside = (number >= jnp.where(low, edge[0], edge[1])) & (
                        number < jnp.where(low, edge[1], edge[2])
                    )
                    part = dense[g * window : (g + 1) * window, j * LANES : (j + 1) * LANES]
                    value = jnp.where(inside, part, value)
                found.append(value + pltpu.roll(value, rank, 1))
            folded.append(found)
        for g, out in enumerate(outs):
            one, two = folded[0][g], folded[1][g]
            zero = jnp.where(first_core, one, two)
            other = jnp.where(first_core, two, one)
            out[u * window : (u + 1) * window, :] = jnp.where(low, zero, other).astype(out.dtype)


def expand(routes_ref, turned, lines, first, tiles):
    tops, tokens = routes_ref.shape
    rank = turned.shape[0]

    def one(tile, carry):
        here = pl.multiple_of(tile * 8, 8)
        ids = first + here + lax.broadcasted_iota(jnp.int32, (8, tokens), 0)
        masks = [routes_ref[k : k + 1, :] == ids for k in range(tops)]
        for r in range(rank):
            value = jnp.zeros((8, tokens), jnp.float32)
            for k in range(tops):
                row = turned[r : r + 1, k * tokens : (k + 1) * tokens]
                value = jnp.where(masks[k], row, value)
            side = r % 2 * tokens
            lines[r // 2, pl.ds(here, 8), side : side + tokens] = value
        return carry

    lax.fori_loop(0, tiles, one, 0)


def form(lines, basis_ref, first, count, out_ref, rank):
    experts, width = lines.shape[1:]
    made = jnp.dot(
        lines[first : first + count].reshape(count * experts, width).astype(jnp.bfloat16),
        basis_ref[...],
        preferred_element_type=jnp.float32,
    ).astype(jnp.bfloat16)
    for pair in range(count):
        for s in range(SEG_DEV):
            out_ref[s, :, pl.ds((first + pair) * 2 * rank, 2 * rank)] = made[
                pair * experts : (pair + 1) * experts, s * 2 * rank : (s + 1) * 2 * rank
            ]


def blocks_kernel(
    rank, routes_ref, basis_ref, order_ref, total_ref, b_ref, c_ref, d_ref, out_ref, turned, lines
):
    half = b_ref.shape[0]
    value = packed(total_ref, 0, 2 * half, rank)
    for ref in (b_ref, c_ref, d_ref):
        value = value + ref[...].astype(jnp.float32)
    value = value.T
    value = jnp.concatenate([value[0:rank], value[rank : 2 * rank]], axis=1).astype(jnp.bfloat16)
    turned[...] = jnp.dot(value, order_ref[...], preferred_element_type=jnp.float32)
    expand(routes_ref, turned, lines, 0, lines.shape[1] // 8)
    for first in range(0, rank // 2, 8):
        form(lines, basis_ref, first, 8, out_ref, rank)


def last_kernel(
    rank,
    place,
    count,
    held,
    bases_ref,
    starts_ref,
    routes_ref,
    basis_ref,
    order_ref,
    turned_ref,
    own_ref,
    b_ref,
    c_ref,
    d_ref,
    _,
    out_ref,
    turned,
    lines,
    block,
    sem,
):
    window = own_ref.shape[0] // 2
    pairs = order_ref.shape[0]
    value = own_ref[...]
    for ref in (b_ref, c_ref, d_ref):
        value = value + ref[...].astype(jnp.float32)
    value = value.T.astype(jnp.bfloat16)
    device = lax.axis_index("expert")
    first = bases_ref[device, place] // count * count
    total = turned_ref[...]
    for u in range(2):
        unit = bases_ref[device, place + u * CORES] // (CORES * held) * (CORES * held)
        for core in range(CORES):
            at = jnp.minimum(starts_ref[0, unit + core * held] & -ALIGN, pairs - window)
            total = total + jnp.dot(
                value[core * rank : (core + 1) * rank, u * window : (u + 1) * window],
                order_ref[pl.ds(pl.multiple_of(at, ALIGN), window), :],
                preferred_element_type=jnp.float32,
            )
    turned[...] = total
    expand(routes_ref, turned, lines, first, count // 8)
    form(lines, basis_ref, 0, rank // 2, block, rank)
    copy = pltpu.make_async_copy(
        block, out_ref.at[:, pl.ds(pl.multiple_of(first, count), count), :], sem
    )
    copy.start()
    copy.wait()


def local(hidden_in, out_grads, routes, segments, in_proj, out_proj):
    tokens, tops = routes.shape
    exp_here, rank, width = out_proj.shape
    owners, groups = lax.axis_size("expert"), lax.axis_size("groups")
    experts = exp_here * owners
    pairs = tokens * tops
    capacity = max(2, 3 * pairs // (2 * experts))
    window = min(pairs, -(-(exp_here * capacity + ALIGN - 1) // ALIGN) * ALIGN)
    quarter = width // QUAD
    cols = exp_here * rank
    rows = pairs // PIECES
    index = lax.axis_index("expert")
    slots = owners // CORES // 2
    ring = [0, *range(1, slots, 2), *range((slots - 1) // 2 * 2, 0, -2)]
    following = {a: b for a, b in zip(ring, ring[1:] + ring[:1])}
    before = {b: a for a, b in following.items()}

    def swap(array, side, bit):
        table = [
            (g * owners + e, (g ^ side) * owners + (e ^ bit))
            for g in range(groups)
            for e in range(owners)
        ]
        return lax.ppermute(array, BOTH, table)

    def along(array, table):
        wide = 2 * CORES
        pairs_of = [(e, table[e // wide] * wide + e % wide) for e in range(owners)]
        return lax.ppermute(array, "expert", pairs_of)

    def tie(*arrays):
        return lax.optimization_barrier(arrays)

    final = slots - 1
    names_a = [(n, 0) for n in range(final - 1)] + [(0, 1)]
    names_b = [(final - 1, 0)] + [(n, 1) for n in range(1, final - 1)]
    names_c = [(final - 1, 1)]
    arrival = names_a + names_b + names_c + [(final, 0), (final, 1)]

    def source(z, hops):
        for _ in range(hops):
            z = before[z]
        return z

    rows_of = [
        [
            ((source(e // (2 * CORES), n) * 2 + (e // CORES % 2 ^ y)) * CORES + (e % CORES ^ c)) * exp_here
            for n, y in arrival
            for c in range(CORES)
        ]
        for e in range(owners)
    ]
    places = CORES * len(arrival)
    bases = jnp.asarray(np.array(rows_of, np.int32))

    unit_shape = pltpu.VMEM((cols, quarter), jnp.bfloat16)
    order_shape = pltpu.VMEM((pairs, pairs), jnp.bfloat16)

    def rows_shape(count):
        return pltpu.VMEM((count, quarter), jnp.bfloat16)

    by_rank = routes.T
    edges = -(-(experts + 1) // LANES) * LANES
    held_grads, mine_unit, core_unit, own_starts, head, order, first_piece = pl.pallas_call(
        sort_kernel,
        out_shape=[
            pltpu.VMEM(out_grads.shape, jnp.bfloat16),
            unit_shape,
            unit_shape,
            jax.ShapeDtypeStruct((1, edges), jnp.int32),
            rows_shape(ALIGN),
            order_shape,
            rows_shape(2 * rows + ALIGN),
        ],
        in_specs=[VMEM, HBM, HBM],
        out_specs=[VMEM] * 7,
        scratch_shapes=[pltpu.VMEM((cols, width), jnp.bfloat16), pltpu.SemaphoreType.DMA((9,))],
        compiler_params=pltpu.CompilerParams(vmem_limit_bytes=12 * MIB),
        cost_estimate=QUICK,
    )(by_rank, in_hbm(out_proj.reshape(cols, width)), in_hbm(out_grads))
    other_unit = swap(core_unit, 0, 1)
    unit = pl.pallas_call(
        join_kernel,
        out_shape=pltpu.VMEM((CORES * cols, quarter), jnp.bfloat16),
        in_specs=[VMEM] * 2,
        out_specs=VMEM,
        compiler_params=pltpu.CompilerParams(vmem_limit_bytes=4 * MIB),
        cost_estimate=QUICK,
    )(mine_unit, other_unit)

    def permuted(plan, headed, *after):
        held, *_ = tie(order, *after)
        return pl.pallas_call(
            functools.partial(permute_kernel, plan),
            out_shape=[
                rows_shape(many + (ALIGN if n in headed else 0))
                for n, (_, _, many) in enumerate(plan)
            ],
            in_specs=[VMEM] * 3,
            out_specs=[VMEM] * len(plan),
            compiler_params=pltpu.CompilerParams(vmem_limit_bytes=12 * MIB),
            cost_estimate=QUICK,
        )(in_vmem(held), head, in_vmem(held_grads))

    def starts_in(block, count):
        digits = block[count : count + 2, :edges].astype(jnp.int32)
        return (digits[0] * DIGIT + digits[1]).reshape(1, edges)

    side_pieces = [swap(first_piece, 1, 0)]
    ring_unit = unit
    if O["z1"] == "first":
        ring_unit, _ = tie(unit, first_piece)
    held = {(0, 0): unit, (1, 0): along(ring_unit, following)}
    p2after = {"none": [], "unit": [unit], "z1": [held[1, 0]]}[O["p2"]]
    (second_piece,) = permuted([(2, 2 * rows, 2 * rows)], [], *p2after)
    second_send = second_piece
    half = 2 * rows
    if O["cores"] == 2:
        own_tokens, *for_core = permuted([(0, 0, pairs), (1, 0, half), (1, half, half)], [1], second_piece)
        core_counts = [half, half]
    else:
        own_tokens, *for_core = permuted([(0, 0, pairs), (1, 0, pairs)], [1], second_piece)
        core_counts = [pairs]
    third_piece, last_piece = permuted([(3, 0, 3 * rows), (3, 3 * rows, rows)], [0], own_tokens)
    if O["core_in"] == "ev1":
        *for_core, held[1, 0] = tie(*for_core, held[1, 0])
    from_core = [swap(piece, 0, 1) for piece in for_core]
    y0_in = unit
    if O["y0"] == "first":
        y0_in, _ = tie(unit, first_piece)
    elif O["y0"] == "second":
        y0_in, _ = tie(unit, second_piece)
    elif O["y0"] == "own":
        y0_in, _ = tie(unit, own_tokens)
    elif O["y0"] == "core":
        y0_in, *from_core = tie(unit, *from_core)
    held[0, 1] = swap(y0_in, 0, CORES)
    side_pieces.append(swap(second_send, 1, 0))
    basis_in = [last_piece]
    if "z1" in O["basis"]:
        basis_in.append(held[1, 0])
    if "core" in O["basis"]:
        basis_in += from_core
    local_segments, *basis_out = tie(segments, *basis_in)
    if "core" in O["basis"]:
        from_core = basis_out[len(basis_out) - len(from_core):]
    basis, order_back = pl.pallas_call(
        basis_kernel,
        out_shape=[
            pltpu.VMEM((2 * tokens, SEG_DEV * 2 * rank), jnp.bfloat16),
            order_shape,
        ],
        in_specs=[HBM, HBM, VMEM, VMEM],
        out_specs=[VMEM] * 2,
        scratch_shapes=[
            pltpu.VMEM(hidden_in.shape, jnp.bfloat16),
            pltpu.VMEM(in_proj.shape, jnp.bfloat16),
            pltpu.SemaphoreType.DMA((5,)),
        ],
        compiler_params=pltpu.CompilerParams(vmem_limit_bytes=12 * MIB),
        cost_estimate=QUICK,
    )(in_hbm(hidden_in), in_hbm(in_proj), local_segments.reshape(1, tokens), by_rank)

    call = functools.partial(
        accumulate, bases=bases, rank=rank, pairs=pairs, window=window, places=places
    )
    place_of = {name: CORES * n for n, name in enumerate(arrival)}
    starts = {0: own_starts}
    members = []
    known_units = 0
    state = None

    def work(names, complete=(), partial=(), sends=(), cost=QUICK):
        nonlocal state, known_units
        tasks, arrived = [], []
        for group, blocks in complete:
            first = 0
            for piece, count in blocks:
                arrived.append((piece, group * pairs + first, count))
                first += count
            if group:
                starts[group] = starts_in(*blocks[0])
            members.append(group)
        fresh = [group for group, _ in complete]
        if fresh and known_units:
            tasks.append(("units", fresh, 0, known_units))
        if names:
            tasks.append(("units", list(members), known_units, CORES * len(names)))
        known_units += CORES * len(names)
        for group, piece, first, count in partial:
            arrived.append((piece, group * pairs + first, count))
            if first == 0:
                starts[group] = starts_in(piece, count)
                members.append(group)
            tasks.append(("piece", group, first, first + count, 0, known_units))
        state, out = call(
            state,
            starts=starts,
            tokens=arrived,
            units=[(held[n], place_of[n]) for n in names],
            tasks=tasks,
            sends=sends,
            cost=cost,
        )
        return out

    def group_tie(names, array):
        nonlocal basis, from_core
        items = []
        for name in names:
            if name == "y0":
                items.append(held[0, 1])
            if name == "y1":
                items.append(held[1, 1])
            if name == "z1":
                items.append(held[1, 0])
            if name == "z2":
                items.append(held[near])
            if name == "side0":
                items.append(side_pieces[0])
            if name == "side1":
                items.append(side_pieces[1])
            if name == "basis":
                items.append(basis)
            if name == "core":
                items += from_core
        out = tie(array, *items)
        out = list(out)
        array, out = out[0], out[1:]
        for name in names:
            if name == "y0":
                held[0, 1] = out.pop(0)
            if name == "y1":
                held[1, 1] = out.pop(0)
            if name == "z1":
                held[1, 0] = out.pop(0)
            if name == "z2":
                held[near] = out.pop(0)
            if name == "side0":
                side_pieces[0] = out.pop(0)
            if name == "side1":
                side_pieces[1] = out.pop(0)
            if name == "basis":
                basis = out.pop(0)
            if name == "core":
                from_core = [out.pop(0) for _ in from_core]
        return array

    held[1, 0] = group_tie(O["ev1"], held[1, 0])
    for n in range(1, final - 1):
        held[n + 1, 0] = along(held[n, 0], following)
        held[n, 1] = swap(held[n, 0], 0, CORES)
    third_piece = group_tie(O["diag"], third_piece)
    diagonal_pieces = [swap(third_piece, 1, 1)]
    near = (final - 1, 0)
    held[near] = group_tie(O["ev2"], held[near])
    COST = {0: QUICK, 1: SHORT}
    work(
        names_a,
        complete=[(0, [(own_tokens, pairs)])]
        + ([(1, list(zip(from_core, core_counts)))] if O["core_k"] == "a" else [])
        + ([(2, [(piece, half) for piece in side_pieces])] if O["side_k"] == "a" else []),
        cost=COST[O["ka"]],
    )
    if O["z3_ka"]:
        held[near], *state = tie(held[near], *state)
    back_unit = group_tie(O["w"], held[0, 1])
    if O["w_ka"]:
        back_unit, *state = tie(back_unit, *state)
    held[final, 1] = along(back_unit, before)
    held[final, 0] = along(held[near], following)
    held[final - 1, 1] = swap(held[near], 0, CORES)
    last_piece = group_tie(O["last"], last_piece)
    diagonal_pieces.append(swap(last_piece, 1, 1))
    work(
        names_b,
        complete=([(1, list(zip(from_core, core_counts)))] if O["core_k"] == "b" else [])
        + ([(2, [(piece, half) for piece in side_pieces])] if O["side_k"] == "b" else []),
        cost=COST[O["k0"]],
    )
    sent = work(
        names_c if O["y2"] == "c" else [], partial=[(3, diagonal_pieces[0], 0, 3 * rows)], sends=[1, 2] if O["y2"] == "c" else [], cost=COST[O["k1"]]
    )
    sent = sent + work(
        [] if O["y2"] == "c" else names_c, partial=[(3, diagonal_pieces[1], 3 * rows, rows)], sends=[3] if O["y2"] == "c" else [1, 2, 3], cost=COST[O["k2"]]
    )

    def returned(arrays):
        return [
            swap(array, side, bit) for array, (side, bit) in zip(arrays, ((0, 1), (1, 0), (1, 1)))
        ]

    early = returned(sent)
    place = places - 2 * CORES
    own_late, *sent = pl.pallas_call(
        functools.partial(late_kernel, rank, pairs, window, place, QUAD),
        out_shape=[pltpu.VMEM((2 * window, LANES), jnp.float32)]
        + [pltpu.VMEM((2 * window, LANES), jnp.bfloat16)] * (QUAD - 1),
        in_specs=[SMEM] * (1 + QUAD) + [VMEM] * 3,
        out_specs=[VMEM] * QUAD,
        compiler_params=pltpu.CompilerParams(vmem_limit_bytes=8 * MIB),
        cost_estimate=QUICK,
    )(bases, *[starts[g] for g in range(QUAD)], in_vmem(state[0]), held[final, 0], held[final, 1])
    late = returned(sent)
    *early, own_late = tie(*early, own_late)
    out, turned = pl.pallas_call(
        functools.partial(blocks_kernel, rank),
        out_shape=[
            jax.ShapeDtypeStruct((SEG_DEV, experts, rank * rank), jnp.bfloat16),
            pltpu.VMEM((rank, pairs), jnp.float32),
        ],
        in_specs=[VMEM] * 7,
        out_specs=[VMEM] * 2,
        scratch_shapes=[pltpu.VMEM((rank // 2, experts, 2 * tokens), jnp.float32)],
        compiler_params=pltpu.CompilerParams(vmem_limit_bytes=32 * MIB),
        cost_estimate=QUICK,
    )(by_rank, basis, in_vmem(order_back), in_vmem(state[2]), *early)
    count = 2 * CORES * exp_here
    return pl.pallas_call(
        functools.partial(last_kernel, rank, place, count, exp_here),
        out_shape=jax.ShapeDtypeStruct(out.shape, out.dtype),
        in_specs=[SMEM] * 2 + [VMEM] * 8 + [HBM],
        out_specs=HBM,
        scratch_shapes=[
            pltpu.VMEM((rank, pairs), jnp.float32),
            pltpu.VMEM((rank // 2, count, 2 * tokens), jnp.float32),
            pltpu.VMEM((SEG_DEV, count, rank * rank), jnp.bfloat16),
            pltpu.SemaphoreType.DMA,
        ],
        input_output_aliases={10: 0},
        compiler_params=pltpu.CompilerParams(vmem_limit_bytes=16 * MIB),
        cost_estimate=QUICK,
    )(bases, own_starts, by_rank, basis, in_vmem(order_back), in_vmem(turned), own_late, *late, out)


def solution(mesh):
    placed = (
        P(("groups", "expert"), None),
        P(("groups", "expert"), None, None),
        P(("groups", "expert"), None),
        P(("groups", "expert")),
        P(),
        P("expert", None, None),
    )
    return jax.shard_map(
        local,
        mesh=mesh,
        in_specs=placed,
        out_specs=P(("groups", "expert"), None, None),
        check_vma=False,
    )
```

```python
import functools

import jax
import jax.numpy as jnp
import numpy as np
from jax import lax
from jax.experimental import pallas as pl
from jax.experimental.pallas import tpu as pltpu
from jax.sharding import PartitionSpec as P

SEG_DEV = 2
O = {'p1': 'core_unit', 'z1': 'none', 'p2': 'unit', 'cores': 1, 'core_in': 'none', 'y0': 'unit', 'basis': [], 'ev1': ['side0'], 'diag': ['side0'], 'ev2': ['basis', 'side0'], 'w': ['basis', 'core'], 'last': ['side1'], 'ka': 1, 'z3_ka': 0, 'w_ka': 0, 'k0': 1, 'k1': 0, 'k2': 1, 'y2': 'd', 'core_k': 'b', 'side_k': 'b'}
CORES = 2
SIDES = 2
QUAD = 4
PIECES = 4
LANES = 128
ALIGN = 16
DIGIT = 32
BOTH = ("groups", "expert")
MIB = 1024 * 1024
VMEM = pl.BlockSpec(memory_space=pltpu.VMEM)
SMEM = pl.BlockSpec(memory_space=pltpu.SMEM)
HBM = pl.BlockSpec(memory_space=pl.ANY)
QUICK = pl.CostEstimate(flops=1, bytes_accessed=1, transcendentals=0)
SHORT = pl.CostEstimate(flops=10**9, bytes_accessed=1, transcendentals=0)
NT = (((1,), (1,)), ((), ()))


def in_vmem(array):
    return pltpu.with_memory_space_constraint(array, pltpu.VMEM)


def in_hbm(array):
    return pltpu.with_memory_space_constraint(array, pltpu.HBM)


def place_in_quad(flip):
    side, core = lax.axis_index("groups") % SIDES, lax.axis_index("expert") % CORES
    return (side ^ (flip // CORES)) * CORES + (core ^ (flip % CORES))


def columns_of(flip, width):
    return pl.ds(pl.multiple_of(place_in_quad(flip) * width, width), width)


def row_of(routes):
    tops, tokens = routes.shape
    pairs = tops * tokens
    lane = lax.broadcasted_iota(jnp.int32, (tokens, pairs), 1)
    token = lax.broadcasted_iota(jnp.int32, (tokens, pairs), 0)
    spread = jnp.where(lane // tops == token, 1.0, 0.0).astype(jnp.bfloat16)
    values = routes.astype(jnp.float32).astype(jnp.bfloat16)
    every = jnp.dot(values, spread, preferred_element_type=jnp.float32)
    lane = lax.broadcasted_iota(jnp.int32, (tops, pairs), 1)
    k = lax.broadcasted_iota(jnp.int32, (tops, pairs), 0)
    return jnp.sum(jnp.where(lane % tops == k, every, 0.0), axis=0, keepdims=True).astype(jnp.int32)


def key_column(routes_row):
    count = routes_row.shape[1]
    keys = routes_row * count + lax.broadcasted_iota(jnp.int32, (1, count), 1)
    return jnp.broadcast_to(keys.astype(jnp.float32), (8, count)).T[:, 0:1]


def ranks(column, keys):
    total = jnp.zeros(keys.shape, jnp.float32)
    for first in range(0, column.shape[0], 128):
        smaller = jnp.where(column[first : first + 128] < keys, 1.0, 0.0)
        total = total + jnp.sum(smaller, axis=0, keepdims=True)
    return total


def sort_kernel(
    routes_ref,
    weight_ref,
    grads_ref,
    held_ref,
    mine_ref,
    core_ref,
    starts_ref,
    head_ref,
    order_ref,
    piece_ref,
    stage,
    sems,
):
    width = piece_ref.shape[1]
    count = sems.shape[0] - 1
    part = grads_ref.shape[0] // count
    copies = [pltpu.make_async_copy(weight_ref, stage, sems.at[count])]
    for n in range(count):
        here = pl.ds(n * part, part)
        copies.append(pltpu.make_async_copy(grads_ref.at[here], held_ref.at[here], sems.at[n]))
    for copy in copies:
        copy.start()
    routes = row_of(routes_ref[...])
    pairs = routes.shape[1]
    column = key_column(routes)
    keys = routes * pairs + lax.broadcasted_iota(jnp.int32, (1, pairs), 1)
    place = ranks(column, keys.astype(jnp.float32)).astype(jnp.int32)
    firsts = lax.broadcasted_iota(jnp.int32, starts_ref.shape, 1) * pairs
    starts = ranks(column, firsts.astype(jnp.float32)).astype(jnp.int32)
    starts_ref[...] = starts
    wide = head_ref.shape[1] - starts.shape[1]
    digits = [starts // DIGIT, starts % DIGIT]
    digits = [jnp.pad(d.astype(jnp.float32), ((0, 0), (0, wide))) for d in digits]
    row = lax.broadcasted_iota(jnp.int32, head_ref.shape, 0)
    head = jnp.where(row == 0, digits[0], jnp.where(row == 1, digits[1], 0.0))
    head_ref[...] = head.astype(jnp.bfloat16)
    rows = piece_ref.shape[0] - ALIGN
    for first in range(0, pairs, rows):
        ids = first + lax.broadcasted_iota(jnp.int32, (rows, pairs), 0)
        order_ref[first : first + rows, :] = jnp.where(place == ids, 1.0, 0.0).astype(jnp.bfloat16)
    copies[0].wait()
    core_ref[...] = stage[:, columns_of(1, width)]
    mine_ref[...] = stage[:, columns_of(0, width)]
    for copy in copies[1:]:
        copy.wait()
    piece_ref[0:rows, :] = jnp.dot(
        order_ref[0:rows, :],
        held_ref[:, :, columns_of(2, width)].reshape(pairs, width),
        preferred_element_type=jnp.float32,
    ).astype(jnp.bfloat16)
    piece_ref[rows:, :] = head_ref[...]


def join_kernel(one_ref, two_ref, out_ref):
    half = one_ref.shape[0]
    out_ref[0:half, :] = one_ref[...]
    out_ref[half:, :] = two_ref[...]


def permute_kernel(plan, order_ref, head_ref, grads_ref, *outs):
    pairs, width = order_ref.shape[0], outs[0].shape[1]
    for device in sorted({device for device, _, _ in plan}):
        grads = grads_ref[:, :, columns_of(device, width)].reshape(pairs, width)
        for out, (target, first, rows) in zip(outs, plan):
            if target == device:
                out[0:rows, :] = jnp.dot(
                    order_ref[first : first + rows, :], grads, preferred_element_type=jnp.float32
                ).astype(jnp.bfloat16)
                if out.shape[0] > rows:
                    out[rows:, :] = head_ref[...]


def basis_kernel(
    hidden_ref, proj_ref, segment_ref, routes_ref, out_ref, order_ref, hidden, proj, sems
):
    count = sems.shape[0] - 1
    part = hidden.shape[0] // count
    copies = [pltpu.make_async_copy(proj_ref, proj, sems.at[count])]
    for n in range(count):
        here = pl.ds(n * part, part)
        copies.append(pltpu.make_async_copy(hidden_ref.at[here], hidden.at[here], sems.at[n]))
    for copy in copies:
        copy.start()
    tops, tokens = routes_ref.shape
    pairs = tops * tokens
    column = key_column(row_of(routes_ref[...]))
    at = [
        routes_ref[k : k + 1, :] * pairs + lax.broadcasted_iota(jnp.int32, (1, tokens), 1) * tops + k
        for k in range(tops)
    ]
    place = ranks(column, jnp.concatenate(at, axis=1).astype(jnp.float32)).astype(jnp.int32)
    for first in range(0, pairs, 256):
        ids = first + lax.broadcasted_iota(jnp.int32, (256, pairs), 0)
        order_ref[first : first + 256, :] = jnp.where(place == ids, 1.0, 0.0).astype(jnp.bfloat16)
    segment = (segment_ref[...] - lax.axis_index("expert") * SEG_DEV).astype(jnp.float32)
    segment = jnp.broadcast_to(segment, (8, tokens)).T[:, 0:1]
    for copy in copies:
        copy.wait()
    projected = lax.dot_general(hidden[...], proj[...], NT, preferred_element_type=jnp.float32)
    zero = jnp.zeros_like(projected)
    picked = [jnp.where(segment == float(s), projected, zero) for s in range(SEG_DEV)]
    even = jnp.concatenate([b for p in picked for b in (p, zero)], axis=1)
    odd = jnp.concatenate([b for p in picked for b in (zero, p)], axis=1)
    out_ref[...] = jnp.concatenate([even, odd], axis=0).astype(out_ref.dtype)


def packed(total, first, pairs, rank):
    half = pairs // 2
    low = lax.broadcasted_iota(jnp.int32, (half, LANES), 1) < rank
    one = total[first : first + half, :]
    two = total[first + half : first + pairs, :]
    return jnp.where(low, one + pltpu.roll(one, rank, 1), two + pltpu.roll(two, rank, 1))


def partial_kernel(
    rank, pairs, window, new_tokens, new_units, tasks, fresh, sends, groups, bases_ref, *refs
):
    start_refs = dict(zip(groups, refs))
    refs = refs[len(groups) :]
    token_refs, refs = refs[: len(new_tokens)], refs[len(new_tokens) :]
    unit_refs, refs = refs[: len(new_units)], refs[len(new_units) :]
    if fresh:
        tokens, units, total = refs
        send_refs = ()
        total[...] = jnp.zeros_like(total)
    else:
        tokens, units, total = refs[3:6]
        send_refs = refs[6:]
    for ref, (first, count) in zip(token_refs, new_tokens):
        tokens[first : first + count, :] = ref[0:count, :]
    cols = units.shape[1]
    for ref, place in zip(unit_refs, new_units):
        for half in range(CORES):
            units[place + half] = ref[half * cols : (half + 1) * cols, :]
    held = cols // rank
    per_tile = LANES // rank
    low = lax.broadcasted_iota(jnp.int32, (1, LANES), 1) < rank

    device = lax.axis_index("expert")

    def process(w, members):
        base = bases_ref[device, w]
        heres, offsets = [], []
        for g in members:
            at = jnp.minimum(start_refs[g][0, base] & -ALIGN, pairs - window)
            offsets.append(at)
            heres.append(pl.ds(pl.multiple_of(g * pairs + at, ALIGN), window))
        rows = [tokens[here, :] for here in heres]
        rows = jnp.concatenate(rows, axis=0) if len(rows) > 1 else rows[0]
        dense = lax.dot_general(rows, units[w], NT, preferred_element_type=jnp.float32)
        for n, g in enumerate(members):
            value = total[heres[n], :]
            number = offsets[n] + lax.broadcasted_iota(jnp.int32, (window, LANES), 0)
            for j in range(cols // LANES):
                edge = [start_refs[g][0, base + j * per_tile + i] for i in range(per_tile + 1)]
                inside = (number >= jnp.where(low, edge[0], edge[1])) & (
                    number < jnp.where(low, edge[1], edge[2])
                )
                part = dense[n * window : (n + 1) * window, j * LANES : (j + 1) * LANES]
                value = jnp.where(inside, part, value)
            total[heres[n], :] = value

    for task in tasks:
        if task[0] == "units":
            _, members, first_w, count = task

            def each(i, carry, members=members, first_w=first_w):
                process(first_w + i, members)
                return carry

        else:
            _, member, first_row, end_row, first_w, count = task

            def each(
                i, carry, member=member, first_row=first_row, end_row=end_row, first_w=first_w
            ):
                w = first_w + i
                base = bases_ref[device, w]
                touches = (start_refs[member][0, base] < end_row) & (
                    start_refs[member][0, base + held] > first_row
                )

                @pl.when(touches)
                def _():
                    process(w, [member])

                return carry

        lax.fori_loop(0, count, each, 0)
    for ref, g in zip(send_refs, sends):
        ref[...] = packed(total, g * pairs, pairs, rank).astype(ref.dtype)


def accumulate(
    state, bases, starts, tokens, units, tasks, rank, pairs, window, places=0, sends=(), cost=QUICK
):
    fresh = state is None
    operands = [bases, *starts.values(), *[a for a, _, _ in tokens], *[a for a, _ in units]]
    specs = [SMEM] * (1 + len(starts)) + [VMEM] * (len(tokens) + len(units))
    if fresh:
        width = units[0][0].shape[1]
        shapes = [
            pltpu.VMEM((QUAD * pairs, width), jnp.bfloat16),
            pltpu.VMEM((places, units[0][0].shape[0] // CORES, width), jnp.bfloat16),
            pltpu.VMEM((QUAD * pairs, LANES), jnp.float32),
        ]
        aliases = {}
    else:
        aliases = {len(operands) + i: i for i in range(3)}
        operands += [in_vmem(a) for a in state]
        specs += [VMEM] * 3
        shapes = [pltpu.VMEM(a.shape, a.dtype) for a in state]
    shapes += [pltpu.VMEM((pairs // 2, LANES), jnp.bfloat16)] * len(sends)
    out = pl.pallas_call(
        functools.partial(
            partial_kernel,
            rank,
            pairs,
            window,
            [(first, count) for _, first, count in tokens],
            [p for _, p in units],
            tasks,
            fresh,
            sends,
            list(starts),
        ),
        out_shape=shapes,
        in_specs=specs,
        out_specs=[VMEM] * len(shapes),
        input_output_aliases=aliases,
        compiler_params=pltpu.CompilerParams(vmem_limit_bytes=8 * MIB),
        cost_estimate=cost,
    )(*operands)
    return list(out[:3]), list(out[3:])


def late_kernel(rank, pairs, window, place, groups, bases_ref, *refs):
    start_refs, tokens, refs = refs[:groups], refs[groups], refs[groups + 1 :]
    unit_refs, outs = refs[:2], refs[2:]
    per_tile = LANES // rank
    low = lax.broadcasted_iota(jnp.int32, (1, LANES), 1) < rank
    device = lax.axis_index("expert")
    first_core = device % CORES == 0
    for u, unit_ref in enumerate(unit_refs):
        cols = unit_ref.shape[0] // CORES
        folded = []
        for half in range(CORES):
            base = bases_ref[device, place + u * CORES + half]
            offsets, rows = [], []
            for g in range(groups):
                at = jnp.minimum(start_refs[g][0, base] & -ALIGN, pairs - window)
                offsets.append(at)
                rows.append(tokens[pl.ds(pl.multiple_of(g * pairs + at, ALIGN), window), :])
            dense = lax.dot_general(
                jnp.concatenate(rows, axis=0),
                unit_ref[half * cols : (half + 1) * cols, :],
                NT,
                preferred_element_type=jnp.float32,
            )
            found = []
            for g in range(groups):
                value = jnp.zeros((window, LANES), jnp.float32)
                number = offsets[g] + lax.broadcasted_iota(jnp.int32, (window, LANES), 0)
                for j in range(cols // LANES):
                    edge = [start_refs[g][0, base + j * per_tile + i] for i in range(per_tile + 1)]
                    inside = (number >= jnp.where(low, edge[0], edge[1])) & (
                        number < jnp.where(low, edge[1], edge[2])
                    )
                    part = dense[g * window : (g + 1) * window, j * LANES : (j + 1) * LANES]
                    value = jnp.where(inside, part, value)
                found.append(value + pltpu.roll(value, rank, 1))
            folded.append(found)
        for g, out in enumerate(outs):
            one, two = folded[0][g], folded[1][g]
            zero = jnp.where(first_core, one, two)
            other = jnp.where(first_core, two, one)
            out[u * window : (u + 1) * window, :] = jnp.where(low, zero, other).astype(out.dtype)


def expand(routes_ref, turned, lines, first, tiles):
    tops, tokens = routes_ref.shape
    rank = turned.shape[0]

    def one(tile, carry):
        here = pl.multiple_of(tile * 8, 8)
        ids = first + here + lax.broadcasted_iota(jnp.int32, (8, tokens), 0)
        masks = [routes_ref[k : k + 1, :] == ids for k in range(tops)]
        for r in range(rank):
            value = jnp.zeros((8, tokens), jnp.float32)
            for k in range(tops):
                row = turned[r : r + 1, k * tokens : (k + 1) * tokens]
                value = jnp.where(masks[k], row, value)
            side = r % 2 * tokens
            lines[r // 2, pl.ds(here, 8), side : side + tokens] = value
        return carry

    lax.fori_loop(0, tiles, one, 0)


def form(lines, basis_ref, first, count, out_ref, rank):
    experts, width = lines.shape[1:]
    made = jnp.dot(
        lines[first : first + count].reshape(count * experts, width).astype(jnp.bfloat16),
        basis_ref[...],
        preferred_element_type=jnp.float32,
    ).astype(jnp.bfloat16)
    for pair in range(count):
        for s in range(SEG_DEV):
            out_ref[s, :, pl.ds((first + pair) * 2 * rank, 2 * rank)] = made[
                pair * experts : (pair + 1) * experts, s * 2 * rank : (s + 1) * 2 * rank
            ]


def blocks_kernel(
    rank, routes_ref, basis_ref, order_ref, total_ref, b_ref, c_ref, d_ref, out_ref, turned, lines
):
    half = b_ref.shape[0]
    value = packed(total_ref, 0, 2 * half, rank)
    for ref in (b_ref, c_ref, d_ref):
        value = value + ref[...].astype(jnp.float32)
    value = value.T
    value = jnp.concatenate([value[0:rank], value[rank : 2 * rank]], axis=1).astype(jnp.bfloat16)
    turned[...] = jnp.dot(value, order_ref[...], preferred_element_type=jnp.float32)
    expand(routes_ref, turned, lines, 0, lines.shape[1] // 8)
    for first in range(0, rank // 2, 8):
        form(lines, basis_ref, first, 8, out_ref, rank)


def last_kernel(
    rank,
    place,
    count,
    held,
    bases_ref,
    starts_ref,
    routes_ref,
    basis_ref,
    order_ref,
    turned_ref,
    own_ref,
    b_ref,
    c_ref,
    d_ref,
    _,
    out_ref,
    turned,
    lines,
    block,
    sem,
):
    window = own_ref.shape[0] // 2
    pairs = order_ref.shape[0]
    value = own_ref[...]
    for ref in (b_ref, c_ref, d_ref):
        value = value + ref[...].astype(jnp.float32)
    value = value.T.astype(jnp.bfloat16)
    device = lax.axis_index("expert")
    first = bases_ref[device, place] // count * count
    total = turned_ref[...]
    for u in range(2):
        unit = bases_ref[device, place + u * CORES] // (CORES * held) * (CORES * held)
        for core in range(CORES):
            at = jnp.minimum(starts_ref[0, unit + core * held] & -ALIGN, pairs - window)
            total = total + jnp.dot(
                value[core * rank : (core + 1) * rank, u * window : (u + 1) * window],
                order_ref[pl.ds(pl.multiple_of(at, ALIGN), window), :],
                preferred_element_type=jnp.float32,
            )
    turned[...] = total
    expand(routes_ref, turned, lines, first, count // 8)
    form(lines, basis_ref, 0, rank // 2, block, rank)
    copy = pltpu.make_async_copy(
        block, out_ref.at[:, pl.ds(pl.multiple_of(first, count), count), :], sem
    )
    copy.start()
    copy.wait()


def local(hidden_in, out_grads, routes, segments, in_proj, out_proj):
    tokens, tops = routes.shape
    exp_here, rank, width = out_proj.shape
    owners, groups = lax.axis_size("expert"), lax.axis_size("groups")
    experts = exp_here * owners
    pairs = tokens * tops
    capacity = max(2, 3 * pairs // (2 * experts))
    window = min(pairs, -(-(exp_here * capacity + ALIGN - 1) // ALIGN) * ALIGN)
    quarter = width // QUAD
    cols = exp_here * rank
    rows = pairs // PIECES
    index = lax.axis_index("expert")
    slots = owners // CORES // 2
    ring = [0, *range(1, slots, 2), *range((slots - 1) // 2 * 2, 0, -2)]
    following = {a: b for a, b in zip(ring, ring[1:] + ring[:1])}
    before = {b: a for a, b in following.items()}

    def swap(array, side, bit):
        table = [
            (g * owners + e, (g ^ side) * owners + (e ^ bit))
            for g in range(groups)
            for e in range(owners)
        ]
        return lax.ppermute(array, BOTH, table)

    def along(array, table):
        wide = 2 * CORES
        pairs_of = [(e, table[e // wide] * wide + e % wide) for e in range(owners)]
        return lax.ppermute(array, "expert", pairs_of)

    def tie(*arrays):
        return lax.optimization_barrier(arrays)

    final = slots - 1
    names_a = [(n, 0) for n in range(final - 1)] + [(0, 1)]
    names_b = [(final - 1, 0)] + [(n, 1) for n in range(1, final - 1)]
    names_c = [(final - 1, 1)]
    arrival = names_a + names_b + names_c + [(final, 0), (final, 1)]

    def source(z, hops):
        for _ in range(hops):
            z = before[z]
        return z

    rows_of = [
        [
            ((source(e // (2 * CORES), n) * 2 + (e // CORES % 2 ^ y)) * CORES + (e % CORES ^ c)) * exp_here
            for n, y in arrival
            for c in range(CORES)
        ]
        for e in range(owners)
    ]
    places = CORES * len(arrival)
    bases = jnp.asarray(np.array(rows_of, np.int32))

    unit_shape = pltpu.VMEM((cols, quarter), jnp.bfloat16)
    order_shape = pltpu.VMEM((pairs, pairs), jnp.bfloat16)

    def rows_shape(count):
        return pltpu.VMEM((count, quarter), jnp.bfloat16)

    by_rank = routes.T
    edges = -(-(experts + 1) // LANES) * LANES
    held_grads, mine_unit, core_unit, own_starts, head, order, first_piece = pl.pallas_call(
        sort_kernel,
        out_shape=[
            pltpu.VMEM(out_grads.shape, jnp.bfloat16),
            unit_shape,
            unit_shape,
            jax.ShapeDtypeStruct((1, edges), jnp.int32),
            rows_shape(ALIGN),
            order_shape,
            rows_shape(2 * rows + ALIGN),
        ],
        in_specs=[VMEM, HBM, HBM],
        out_specs=[VMEM] * 7,
        scratch_shapes=[pltpu.VMEM((cols, width), jnp.bfloat16), pltpu.SemaphoreType.DMA((9,))],
        compiler_params=pltpu.CompilerParams(vmem_limit_bytes=12 * MIB),
        cost_estimate=QUICK,
    )(by_rank, in_hbm(out_proj.reshape(cols, width)), in_hbm(out_grads))
    other_unit = swap(core_unit, 0, 1)
    unit = pl.pallas_call(
        join_kernel,
        out_shape=pltpu.VMEM((CORES * cols, quarter), jnp.bfloat16),
        in_specs=[VMEM] * 2,
        out_specs=VMEM,
        compiler_params=pltpu.CompilerParams(vmem_limit_bytes=4 * MIB),
        cost_estimate=QUICK,
    )(mine_unit, other_unit)

    def permuted(plan, headed, *after):
        held, *_ = tie(order, *after)
        return pl.pallas_call(
            functools.partial(permute_kernel, plan),
            out_shape=[
                rows_shape(many + (ALIGN if n in headed else 0))
                for n, (_, _, many) in enumerate(plan)
            ],
            in_specs=[VMEM] * 3,
            out_specs=[VMEM] * len(plan),
            compiler_params=pltpu.CompilerParams(vmem_limit_bytes=12 * MIB),
            cost_estimate=QUICK,
        )(in_vmem(held), head, in_vmem(held_grads))

    def starts_in(block, count):
        digits = block[count : count + 2, :edges].astype(jnp.int32)
        return (digits[0] * DIGIT + digits[1]).reshape(1, edges)

    side_pieces = [swap(first_piece, 1, 0)]
    ring_unit = unit
    if O["z1"] == "first":
        ring_unit, _ = tie(unit, first_piece)
    held = {(0, 0): unit, (1, 0): along(ring_unit, following)}
    p2after = {"none": [], "unit": [unit], "z1": [held[1, 0]]}[O["p2"]]
    (second_piece,) = permuted([(2, 2 * rows, 2 * rows)], [], *p2after)
    second_send = second_piece
    half = 2 * rows
    if O["cores"] == 2:
        own_tokens, *for_core = permuted([(0, 0, pairs), (1, 0, half), (1, half, half)], [1], second_piece)
        core_counts = [half, half]
    else:
        own_tokens, *for_core = permuted([(0, 0, pairs), (1, 0, pairs)], [1], second_piece)
        core_counts = [pairs]
    third_piece, last_piece = permuted([(3, 0, 3 * rows), (3, 3 * rows, rows)], [0], own_tokens)
    if O["core_in"] == "ev1":
        *for_core, held[1, 0] = tie(*for_core, held[1, 0])
    from_core = [swap(piece, 0, 1) for piece in for_core]
    y0_in = unit
    if O["y0"] == "first":
        y0_in, _ = tie(unit, first_piece)
    elif O["y0"] == "second":
        y0_in, _ = tie(unit, second_piece)
    elif O["y0"] == "own":
        y0_in, _ = tie(unit, own_tokens)
    elif O["y0"] == "core":
        y0_in, *from_core = tie(unit, *from_core)
    held[0, 1] = swap(y0_in, 0, CORES)
    side_pieces.append(swap(second_send, 1, 0))
    basis_in = [last_piece]
    if "z1" in O["basis"]:
        basis_in.append(held[1, 0])
    if "core" in O["basis"]:
        basis_in += from_core
    local_segments, *basis_out = tie(segments, *basis_in)
    if "core" in O["basis"]:
        from_core = basis_out[len(basis_out) - len(from_core):]
    basis, order_back = pl.pallas_call(
        basis_kernel,
        out_shape=[
            pltpu.VMEM((2 * tokens, SEG_DEV * 2 * rank), jnp.bfloat16),
            order_shape,
        ],
        in_specs=[HBM, HBM, VMEM, VMEM],
        out_specs=[VMEM] * 2,
        scratch_shapes=[
            pltpu.VMEM(hidden_in.shape, jnp.bfloat16),
            pltpu.VMEM(in_proj.shape, jnp.bfloat16),
            pltpu.SemaphoreType.DMA((5,)),
        ],
        compiler_params=pltpu.CompilerParams(vmem_limit_bytes=12 * MIB),
        cost_estimate=QUICK,
    )(in_hbm(hidden_in), in_hbm(in_proj), local_segments.reshape(1, tokens), by_rank)

    call = functools.partial(
        accumulate, bases=bases, rank=rank, pairs=pairs, window=window, places=places
    )
    place_of = {name: CORES * n for n, name in enumerate(arrival)}
    starts = {0: own_starts}
    members = []
    known_units = 0
    state = None

    def work(names, complete=(), partial=(), sends=(), cost=QUICK):
        nonlocal state, known_units
        tasks, arrived = [], []
        for group, blocks in complete:
            first = 0
            for piece, count in blocks:
                arrived.append((piece, group * pairs + first, count))
                first += count
            if group:
                starts[group] = starts_in(*blocks[0])
            members.append(group)
        fresh = [group for group, _ in complete]
        if fresh and known_units:
            tasks.append(("units", fresh, 0, known_units))
        if names:
            tasks.append(("units", list(members), known_units, CORES * len(names)))
        known_units += CORES * len(names)
        for group, piece, first, count in partial:
            arrived.append((piece, group * pairs + first, count))
            if first == 0:
                starts[group] = starts_in(piece, count)
                members.append(group)
            tasks.append(("piece", group, first, first + count, 0, known_units))
        state, out = call(
            state,
            starts=starts,
            tokens=arrived,
            units=[(held[n], place_of[n]) for n in names],
            tasks=tasks,
            sends=sends,
            cost=cost,
        )
        return out

    def group_tie(names, array):
        nonlocal basis, from_core
        items = []
        for name in names:
            if name == "y0":
                items.append(held[0, 1])
            if name == "y1":
                items.append(held[1, 1])
            if name == "z1":
                items.append(held[1, 0])
            if name == "z2":
                items.append(held[near])
            if name == "side0":
                items.append(side_pieces[0])
            if name == "side1":
                items.append(side_pieces[1])
            if name == "basis":
                items.append(basis)
            if name == "core":
                items += from_core
        out = tie(array, *items)
        out = list(out)
        array, out = out[0], out[1:]
        for name in names:
            if name == "y0":
                held[0, 1] = out.pop(0)
            if name == "y1":
                held[1, 1] = out.pop(0)
            if name == "z1":
                held[1, 0] = out.pop(0)
            if name == "z2":
                held[near] = out.pop(0)
            if name == "side0":
                side_pieces[0] = out.pop(0)
            if name == "side1":
                side_pieces[1] = out.pop(0)
            if name == "basis":
                basis = out.pop(0)
            if name == "core":
                from_core = [out.pop(0) for _ in from_core]
        return array

    held[1, 0] = group_tie(O["ev1"], held[1, 0])
    for n in range(1, final - 1):
        held[n + 1, 0] = along(held[n, 0], following)
        held[n, 1] = swap(held[n, 0], 0, CORES)
    third_piece = group_tie(O["diag"], third_piece)
    diagonal_pieces = [swap(third_piece, 1, 1)]
    near = (final - 1, 0)
    held[near] = group_tie(O["ev2"], held[near])
    COST = {0: QUICK, 1: SHORT}
    work(
        names_a,
        complete=[(0, [(own_tokens, pairs)])]
        + ([(1, list(zip(from_core, core_counts)))] if O["core_k"] == "a" else [])
        + ([(2, [(piece, half) for piece in side_pieces])] if O["side_k"] == "a" else []),
        cost=COST[O["ka"]],
    )
    if O["z3_ka"]:
        held[near], *state = tie(held[near], *state)
    back_unit = group_tie(O["w"], held[0, 1])
    if O["w_ka"]:
        back_unit, *state = tie(back_unit, *state)
    held[final, 1] = along(back_unit, before)
    held[final, 0] = along(held[near], following)
    held[final - 1, 1] = swap(held[near], 0, CORES)
    last_piece = group_tie(O["last"], last_piece)
    diagonal_pieces.append(swap(last_piece, 1, 1))
    work(
        names_b,
        complete=([(1, list(zip(from_core, core_counts)))] if O["core_k"] == "b" else [])
        + ([(2, [(piece, half) for piece in side_pieces])] if O["side_k"] == "b" else []),
        cost=COST[O["k0"]],
    )
    sent = work(
        names_c if O["y2"] == "c" else [], partial=[(3, diagonal_pieces[0], 0, 3 * rows)], sends=[1, 2] if O["y2"] == "c" else [], cost=COST[O["k1"]]
    )
    sent = sent + work(
        [] if O["y2"] == "c" else names_c, partial=[(3, diagonal_pieces[1], 3 * rows, rows)], sends=[3] if O["y2"] == "c" else [1, 2, 3], cost=COST[O["k2"]]
    )

    def returned(arrays):
        return [
            swap(array, side, bit) for array, (side, bit) in zip(arrays, ((0, 1), (1, 0), (1, 1)))
        ]

    early = returned(sent)
    place = places - 2 * CORES
    own_late, *sent = pl.pallas_call(
        functools.partial(late_kernel, rank, pairs, window, place, QUAD),
        out_shape=[pltpu.VMEM((2 * window, LANES), jnp.float32)]
        + [pltpu.VMEM((2 * window, LANES), jnp.bfloat16)] * (QUAD - 1),
        in_specs=[SMEM] * (1 + QUAD) + [VMEM] * 3,
        out_specs=[VMEM] * QUAD,
        compiler_params=pltpu.CompilerParams(vmem_limit_bytes=8 * MIB),
        cost_estimate=QUICK,
    )(bases, *[starts[g] for g in range(QUAD)], in_vmem(state[0]), held[final, 0], held[final, 1])
    late = returned(sent)
    *early, own_late = tie(*early, own_late)
    out, turned = pl.pallas_call(
        functools.partial(blocks_kernel, rank),
        out_shape=[
            jax.ShapeDtypeStruct((SEG_DEV, experts, rank * rank), jnp.bfloat16),
            pltpu.VMEM((rank, pairs), jnp.float32),
        ],
        in_specs=[VMEM] * 7,
        out_specs=[VMEM] * 2,
        scratch_shapes=[pltpu.VMEM((rank // 2, experts, 2 * tokens), jnp.float32)],
        compiler_params=pltpu.CompilerParams(vmem_limit_bytes=32 * MIB),
        cost_estimate=QUICK,
    )(by_rank, basis, in_vmem(order_back), in_vmem(state[2]), *early)
    count = 2 * CORES * exp_here
    return pl.pallas_call(
        functools.partial(last_kernel, rank, place, count, exp_here),
        out_shape=jax.ShapeDtypeStruct(out.shape, out.dtype),
        in_specs=[SMEM] * 2 + [VMEM] * 8 + [HBM],
        out_specs=HBM,
        scratch_shapes=[
            pltpu.VMEM((rank, pairs), jnp.float32),
            pltpu.VMEM((rank // 2, count, 2 * tokens), jnp.float32),
            pltpu.VMEM((SEG_DEV, count, rank * rank), jnp.bfloat16),
            pltpu.SemaphoreType.DMA,
        ],
        input_output_aliases={10: 0},
        compiler_params=pltpu.CompilerParams(vmem_limit_bytes=16 * MIB),
        cost_estimate=QUICK,
    )(bases, own_starts, by_rank, basis, in_vmem(order_back), in_vmem(turned), own_late, *late, out)


def solution(mesh):
    placed = (
        P(("groups", "expert"), None),
        P(("groups", "expert"), None, None),
        P(("groups", "expert"), None),
        P(("groups", "expert")),
        P(),
        P("expert", None, None),
    )
    return jax.shard_map(
        local,
        mesh=mesh,
        in_specs=placed,
        out_specs=P(("groups", "expert"), None, None),
        check_vma=False,
    )
```

```python
import functools

import jax
import jax.numpy as jnp
import numpy as np
from jax import lax
from jax.experimental import pallas as pl
from jax.experimental.pallas import tpu as pltpu
from jax.sharding import PartitionSpec as P

SEG_DEV = 2
CORES = 2
SIDES = 2
QUAD = 4
PIECES = 4
LANES = 128
ALIGN = 16
DIGIT = 32
BOTH = ("groups", "expert")
MIB = 1024 * 1024
VMEM = pl.BlockSpec(memory_space=pltpu.VMEM)
SMEM = pl.BlockSpec(memory_space=pltpu.SMEM)
HBM = pl.BlockSpec(memory_space=pl.ANY)
QUICK = pl.CostEstimate(flops=1, bytes_accessed=1, transcendentals=0)
SHORT = pl.CostEstimate(flops=10**9, bytes_accessed=1, transcendentals=0)
NT = (((1,), (1,)), ((), ()))


def in_vmem(array):
    return pltpu.with_memory_space_constraint(array, pltpu.VMEM)


def in_hbm(array):
    return pltpu.with_memory_space_constraint(array, pltpu.HBM)


def place_in_quad(flip):
    side, core = lax.axis_index("groups") % SIDES, lax.axis_index("expert") % CORES
    return (side ^ (flip // CORES)) * CORES + (core ^ (flip % CORES))


def columns_of(flip, width):
    return pl.ds(pl.multiple_of(place_in_quad(flip) * width, width), width)


def row_of(routes):
    tops, tokens = routes.shape
    pairs = tops * tokens
    lane = lax.broadcasted_iota(jnp.int32, (tokens, pairs), 1)
    token = lax.broadcasted_iota(jnp.int32, (tokens, pairs), 0)
    spread = jnp.where(lane // tops == token, 1.0, 0.0).astype(jnp.bfloat16)
    values = routes.astype(jnp.float32).astype(jnp.bfloat16)
    every = jnp.dot(values, spread, preferred_element_type=jnp.float32)
    lane = lax.broadcasted_iota(jnp.int32, (tops, pairs), 1)
    k = lax.broadcasted_iota(jnp.int32, (tops, pairs), 0)
    return jnp.sum(jnp.where(lane % tops == k, every, 0.0), axis=0, keepdims=True).astype(jnp.int32)


def key_column(routes_row):
    count = routes_row.shape[1]
    keys = routes_row * count + lax.broadcasted_iota(jnp.int32, (1, count), 1)
    return jnp.broadcast_to(keys.astype(jnp.float32), (8, count)).T[:, 0:1]


def ranks(column, keys):
    total = jnp.zeros(keys.shape, jnp.float32)
    for first in range(0, column.shape[0], 128):
        smaller = jnp.where(column[first : first + 128] < keys, 1.0, 0.0)
        total = total + jnp.sum(smaller, axis=0, keepdims=True)
    return total


def sort_kernel(
    routes_ref,
    weight_ref,
    grads_ref,
    held_ref,
    mine_ref,
    core_ref,
    starts_ref,
    head_ref,
    order_ref,
    piece_ref,
    stage,
    sems,
):
    width = piece_ref.shape[1]
    count = sems.shape[0] - 1
    part = grads_ref.shape[0] // count
    copies = [pltpu.make_async_copy(weight_ref, stage, sems.at[count])]
    for n in range(count):
        here = pl.ds(n * part, part)
        copies.append(pltpu.make_async_copy(grads_ref.at[here], held_ref.at[here], sems.at[n]))
    for copy in copies:
        copy.start()
    routes = row_of(routes_ref[...])
    pairs = routes.shape[1]
    column = key_column(routes)
    keys = routes * pairs + lax.broadcasted_iota(jnp.int32, (1, pairs), 1)
    place = ranks(column, keys.astype(jnp.float32)).astype(jnp.int32)
    firsts = lax.broadcasted_iota(jnp.int32, starts_ref.shape, 1) * pairs
    starts = ranks(column, firsts.astype(jnp.float32)).astype(jnp.int32)
    starts_ref[...] = starts
    wide = head_ref.shape[1] - starts.shape[1]
    digits = [starts // DIGIT, starts % DIGIT]
    digits = [jnp.pad(d.astype(jnp.float32), ((0, 0), (0, wide))) for d in digits]
    row = lax.broadcasted_iota(jnp.int32, head_ref.shape, 0)
    head = jnp.where(row == 0, digits[0], jnp.where(row == 1, digits[1], 0.0))
    head_ref[...] = head.astype(jnp.bfloat16)
    rows = piece_ref.shape[0] - ALIGN
    for first in range(0, pairs, rows):
        ids = first + lax.broadcasted_iota(jnp.int32, (rows, pairs), 0)
        order_ref[first : first + rows, :] = jnp.where(place == ids, 1.0, 0.0).astype(jnp.bfloat16)
    copies[0].wait()
    core_ref[...] = stage[:, columns_of(1, width)]
    mine_ref[...] = stage[:, columns_of(0, width)]
    for copy in copies[1:]:
        copy.wait()
    piece_ref[0:rows, :] = jnp.dot(
        order_ref[0:rows, :],
        held_ref[:, :, columns_of(2, width)].reshape(pairs, width),
        preferred_element_type=jnp.float32,
    ).astype(jnp.bfloat16)
    piece_ref[rows:, :] = head_ref[...]


def join_kernel(one_ref, two_ref, out_ref):
    half = one_ref.shape[0]
    out_ref[0:half, :] = one_ref[...]
    out_ref[half:, :] = two_ref[...]


def permute_kernel(plan, order_ref, head_ref, grads_ref, *outs):
    pairs, width = order_ref.shape[0], outs[0].shape[1]
    for device in sorted({device for device, _, _ in plan}):
        grads = grads_ref[:, :, columns_of(device, width)].reshape(pairs, width)
        for out, (target, first, rows) in zip(outs, plan):
            if target == device:
                out[0:rows, :] = jnp.dot(
                    order_ref[first : first + rows, :], grads, preferred_element_type=jnp.float32
                ).astype(jnp.bfloat16)
                if out.shape[0] > rows:
                    out[rows:, :] = head_ref[...]


def basis_kernel(
    hidden_ref, proj_ref, segment_ref, routes_ref, out_ref, order_ref, hidden, proj, sems
):
    count = sems.shape[0] - 1
    part = hidden.shape[0] // count
    copies = [pltpu.make_async_copy(proj_ref, proj, sems.at[count])]
    for n in range(count):
        here = pl.ds(n * part, part)
        copies.append(pltpu.make_async_copy(hidden_ref.at[here], hidden.at[here], sems.at[n]))
    for copy in copies:
        copy.start()
    tops, tokens = routes_ref.shape
    pairs = tops * tokens
    column = key_column(row_of(routes_ref[...]))
    at = [
        routes_ref[k : k + 1, :] * pairs + lax.broadcasted_iota(jnp.int32, (1, tokens), 1) * tops + k
        for k in range(tops)
    ]
    place = ranks(column, jnp.concatenate(at, axis=1).astype(jnp.float32)).astype(jnp.int32)
    for first in range(0, pairs, 256):
        ids = first + lax.broadcasted_iota(jnp.int32, (256, pairs), 0)
        order_ref[first : first + 256, :] = jnp.where(place == ids, 1.0, 0.0).astype(jnp.bfloat16)
    segment = (segment_ref[...] - lax.axis_index("expert") * SEG_DEV).astype(jnp.float32)
    segment = jnp.broadcast_to(segment, (8, tokens)).T[:, 0:1]
    for copy in copies:
        copy.wait()
    projected = lax.dot_general(hidden[...], proj[...], NT, preferred_element_type=jnp.float32)
    zero = jnp.zeros_like(projected)
    picked = [jnp.where(segment == float(s), projected, zero) for s in range(SEG_DEV)]
    even = jnp.concatenate([b for p in picked for b in (p, zero)], axis=1)
    odd = jnp.concatenate([b for p in picked for b in (zero, p)], axis=1)
    out_ref[...] = jnp.concatenate([even, odd], axis=0).astype(out_ref.dtype)


def packed(total, first, pairs, rank):
    half = pairs // 2
    low = lax.broadcasted_iota(jnp.int32, (half, LANES), 1) < rank
    one = total[first : first + half, :]
    two = total[first + half : first + pairs, :]
    return jnp.where(low, one + pltpu.roll(one, rank, 1), two + pltpu.roll(two, rank, 1))


def partial_kernel(
    rank, pairs, window, new_tokens, new_units, tasks, fresh, sends, groups, bases_ref, *refs
):
    start_refs = dict(zip(groups, refs))
    refs = refs[len(groups) :]
    token_refs, refs = refs[: len(new_tokens)], refs[len(new_tokens) :]
    unit_refs, refs = refs[: len(new_units)], refs[len(new_units) :]
    if fresh:
        tokens, units, total = refs
        send_refs = ()
        total[...] = jnp.zeros_like(total)
    else:
        tokens, units, total = refs[3:6]
        send_refs = refs[6:]
    for ref, (first, count) in zip(token_refs, new_tokens):
        tokens[first : first + count, :] = ref[0:count, :]
    cols = units.shape[1]
    for ref, place in zip(unit_refs, new_units):
        for half in range(CORES):
            units[place + half] = ref[half * cols : (half + 1) * cols, :]
    held = cols // rank
    per_tile = LANES // rank
    low = lax.broadcasted_iota(jnp.int32, (1, LANES), 1) < rank

    device = lax.axis_index("expert")

    def process(w, members):
        base = bases_ref[device, w]
        heres, offsets = [], []
        for g in members:
            at = jnp.minimum(start_refs[g][0, base] & -ALIGN, pairs - window)
            offsets.append(at)
            heres.append(pl.ds(pl.multiple_of(g * pairs + at, ALIGN), window))
        rows = [tokens[here, :] for here in heres]
        rows = jnp.concatenate(rows, axis=0) if len(rows) > 1 else rows[0]
        dense = lax.dot_general(rows, units[w], NT, preferred_element_type=jnp.float32)
        for n, g in enumerate(members):
            value = total[heres[n], :]
            number = offsets[n] + lax.broadcasted_iota(jnp.int32, (window, LANES), 0)
            for j in range(cols // LANES):
                edge = [start_refs[g][0, base + j * per_tile + i] for i in range(per_tile + 1)]
                inside = (number >= jnp.where(low, edge[0], edge[1])) & (
                    number < jnp.where(low, edge[1], edge[2])
                )
                part = dense[n * window : (n + 1) * window, j * LANES : (j + 1) * LANES]
                value = jnp.where(inside, part, value)
            total[heres[n], :] = value

    for task in tasks:
        if task[0] == "units":
            _, members, first_w, count = task

            def each(i, carry, members=members, first_w=first_w):
                process(first_w + i, members)
                return carry

        else:
            _, member, first_row, end_row, first_w, count = task

            def each(
                i, carry, member=member, first_row=first_row, end_row=end_row, first_w=first_w
            ):
                w = first_w + i
                base = bases_ref[device, w]
                touches = (start_refs[member][0, base] < end_row) & (
                    start_refs[member][0, base + held] > first_row
                )

                @pl.when(touches)
                def _():
                    process(w, [member])

                return carry

        lax.fori_loop(0, count, each, 0)
    for ref, g in zip(send_refs, sends):
        ref[...] = packed(total, g * pairs, pairs, rank).astype(ref.dtype)


def accumulate(
    state, bases, starts, tokens, units, tasks, rank, pairs, window, places=0, sends=(), cost=QUICK
):
    fresh = state is None
    operands = [bases, *starts.values(), *[a for a, _, _ in tokens], *[a for a, _ in units]]
    specs = [SMEM] * (1 + len(starts)) + [VMEM] * (len(tokens) + len(units))
    if fresh:
        width = units[0][0].shape[1]
        shapes = [
            pltpu.VMEM((QUAD * pairs, width), jnp.bfloat16),
            pltpu.VMEM((places, units[0][0].shape[0] // CORES, width), jnp.bfloat16),
            pltpu.VMEM((QUAD * pairs, LANES), jnp.float32),
        ]
        aliases = {}
    else:
        aliases = {len(operands) + i: i for i in range(3)}
        operands += [in_vmem(a) for a in state]
        specs += [VMEM] * 3
        shapes = [pltpu.VMEM(a.shape, a.dtype) for a in state]
    shapes += [pltpu.VMEM((pairs // 2, LANES), jnp.bfloat16)] * len(sends)
    out = pl.pallas_call(
        functools.partial(
            partial_kernel,
            rank,
            pairs,
            window,
            [(first, count) for _, first, count in tokens],
            [p for _, p in units],
            tasks,
            fresh,
            sends,
            list(starts),
        ),
        out_shape=shapes,
        in_specs=specs,
        out_specs=[VMEM] * len(shapes),
        input_output_aliases=aliases,
        compiler_params=pltpu.CompilerParams(vmem_limit_bytes=8 * MIB),
        cost_estimate=cost,
    )(*operands)
    return list(out[:3]), list(out[3:])


def late_kernel(rank, pairs, window, place, groups, bases_ref, *refs):
    start_refs, tokens, refs = refs[:groups], refs[groups], refs[groups + 1 :]
    unit_refs, outs = refs[:2], refs[2:]
    per_tile = LANES // rank
    low = lax.broadcasted_iota(jnp.int32, (1, LANES), 1) < rank
    device = lax.axis_index("expert")
    first_core = device % CORES == 0
    for u, unit_ref in enumerate(unit_refs):
        cols = unit_ref.shape[0] // CORES
        folded = []
        for half in range(CORES):
            base = bases_ref[device, place + u * CORES + half]
            offsets, rows = [], []
            for g in range(groups):
                at = jnp.minimum(start_refs[g][0, base] & -ALIGN, pairs - window)
                offsets.append(at)
                rows.append(tokens[pl.ds(pl.multiple_of(g * pairs + at, ALIGN), window), :])
            dense = lax.dot_general(
                jnp.concatenate(rows, axis=0),
                unit_ref[half * cols : (half + 1) * cols, :],
                NT,
                preferred_element_type=jnp.float32,
            )
            found = []
            for g in range(groups):
                value = jnp.zeros((window, LANES), jnp.float32)
                number = offsets[g] + lax.broadcasted_iota(jnp.int32, (window, LANES), 0)
                for j in range(cols // LANES):
                    edge = [start_refs[g][0, base + j * per_tile + i] for i in range(per_tile + 1)]
                    inside = (number >= jnp.where(low, edge[0], edge[1])) & (
                        number < jnp.where(low, edge[1], edge[2])
                    )
                    part = dense[g * window : (g + 1) * window, j * LANES : (j + 1) * LANES]
                    value = jnp.where(inside, part, value)
                found.append(value + pltpu.roll(value, rank, 1))
            folded.append(found)
        for g, out in enumerate(outs):
            one, two = folded[0][g], folded[1][g]
            zero = jnp.where(first_core, one, two)
            other = jnp.where(first_core, two, one)
            out[u * window : (u + 1) * window, :] = jnp.where(low, zero, other).astype(out.dtype)


def expand(routes_ref, turned, lines, first, tiles):
    tops, tokens = routes_ref.shape
    rank = turned.shape[0]

    def one(tile, carry):
        here = pl.multiple_of(tile * 8, 8)
        ids = first + here + lax.broadcasted_iota(jnp.int32, (8, tokens), 0)
        masks = [routes_ref[k : k + 1, :] == ids for k in range(tops)]
        for r in range(rank):
            value = jnp.zeros((8, tokens), jnp.float32)
            for k in range(tops):
                row = turned[r : r + 1, k * tokens : (k + 1) * tokens]
                value = jnp.where(masks[k], row, value)
            side = r % 2 * tokens
            lines[r // 2, pl.ds(here, 8), side : side + tokens] = value
        return carry

    lax.fori_loop(0, tiles, one, 0)


def form(lines, basis_ref, first, count, out_ref, rank):
    experts, width = lines.shape[1:]
    made = jnp.dot(
        lines[first : first + count].reshape(count * experts, width).astype(jnp.bfloat16),
        basis_ref[...],
        preferred_element_type=jnp.float32,
    ).astype(jnp.bfloat16)
    for pair in range(count):
        for s in range(SEG_DEV):
            out_ref[s, :, pl.ds((first + pair) * 2 * rank, 2 * rank)] = made[
                pair * experts : (pair + 1) * experts, s * 2 * rank : (s + 1) * 2 * rank
            ]


def blocks_kernel(
    rank, routes_ref, basis_ref, order_ref, total_ref, b_ref, c_ref, d_ref, out_ref, turned, lines
):
    half = b_ref.shape[0]
    value = packed(total_ref, 0, 2 * half, rank)
    for ref in (b_ref, c_ref, d_ref):
        value = value + ref[...].astype(jnp.float32)
    value = value.T
    value = jnp.concatenate([value[0:rank], value[rank : 2 * rank]], axis=1).astype(jnp.bfloat16)
    turned[...] = jnp.dot(value, order_ref[...], preferred_element_type=jnp.float32)
    expand(routes_ref, turned, lines, 0, lines.shape[1] // 8)
    for first in range(0, rank // 2, 8):
        form(lines, basis_ref, first, 8, out_ref, rank)


def last_kernel(
    rank,
    place,
    count,
    held,
    bases_ref,
    starts_ref,
    routes_ref,
    basis_ref,
    order_ref,
    turned_ref,
    own_ref,
    b_ref,
    c_ref,
    d_ref,
    _,
    out_ref,
    turned,
    lines,
    block,
    sem,
):
    window = own_ref.shape[0] // 2
    pairs = order_ref.shape[0]
    value = own_ref[...]
    for ref in (b_ref, c_ref, d_ref):
        value = value + ref[...].astype(jnp.float32)
    value = value.T.astype(jnp.bfloat16)
    device = lax.axis_index("expert")
    first = bases_ref[device, place] // count * count
    total = turned_ref[...]
    for u in range(2):
        unit = bases_ref[device, place + u * CORES] // (CORES * held) * (CORES * held)
        for core in range(CORES):
            at = jnp.minimum(starts_ref[0, unit + core * held] & -ALIGN, pairs - window)
            total = total + jnp.dot(
                value[core * rank : (core + 1) * rank, u * window : (u + 1) * window],
                order_ref[pl.ds(pl.multiple_of(at, ALIGN), window), :],
                preferred_element_type=jnp.float32,
            )
    turned[...] = total
    expand(routes_ref, turned, lines, first, count // 8)
    form(lines, basis_ref, 0, rank // 2, block, rank)
    copy = pltpu.make_async_copy(
        block, out_ref.at[:, pl.ds(pl.multiple_of(first, count), count), :], sem
    )
    copy.start()
    copy.wait()


def local(hidden_in, out_grads, routes, segments, in_proj, out_proj):
    tokens, tops = routes.shape
    exp_here, rank, width = out_proj.shape
    owners, groups = lax.axis_size("expert"), lax.axis_size("groups")
    experts = exp_here * owners
    pairs = tokens * tops
    capacity = max(2, 3 * pairs // (2 * experts))
    window = min(pairs, -(-(exp_here * capacity + ALIGN - 1) // ALIGN) * ALIGN)
    quarter = width // QUAD
    cols = exp_here * rank
    rows = pairs // PIECES
    index = lax.axis_index("expert")
    slots = owners // CORES // 2
    ring = [0, *range(1, slots, 2), *range((slots - 1) // 2 * 2, 0, -2)]
    following = {a: b for a, b in zip(ring, ring[1:] + ring[:1])}
    before = {b: a for a, b in following.items()}

    def swap(array, side, bit):
        table = [
            (g * owners + e, (g ^ side) * owners + (e ^ bit))
            for g in range(groups)
            for e in range(owners)
        ]
        return lax.ppermute(array, BOTH, table)

    def along(array, table):
        wide = 2 * CORES
        pairs_of = [(e, table[e // wide] * wide + e % wide) for e in range(owners)]
        return lax.ppermute(array, "expert", pairs_of)

    def tie(*arrays):
        return lax.optimization_barrier(arrays)

    final = slots - 1
    names_a = [(n, 0) for n in range(final - 1)] + [(0, 1)]
    names_b = [(final - 1, 0)] + [(n, 1) for n in range(1, final - 1)]
    names_c = [(final - 1, 1)]
    arrival = names_a + names_b + names_c + [(final, 0), (final, 1)]

    def source(z, hops):
        for _ in range(hops):
            z = before[z]
        return z

    rows_of = [
        [
            ((source(e // (2 * CORES), n) * 2 + (e // CORES % 2 ^ y)) * CORES + (e % CORES ^ c)) * exp_here
            for n, y in arrival
            for c in range(CORES)
        ]
        for e in range(owners)
    ]
    places = CORES * len(arrival)
    bases = jnp.asarray(np.array(rows_of, np.int32))

    unit_shape = pltpu.VMEM((cols, quarter), jnp.bfloat16)
    order_shape = pltpu.VMEM((pairs, pairs), jnp.bfloat16)

    def rows_shape(count):
        return pltpu.VMEM((count, quarter), jnp.bfloat16)

    by_rank = routes.T
    edges = -(-(experts + 1) // LANES) * LANES
    held_grads, mine_unit, core_unit, own_starts, head, order, first_piece = pl.pallas_call(
        sort_kernel,
        out_shape=[
            pltpu.VMEM(out_grads.shape, jnp.bfloat16),
            unit_shape,
            unit_shape,
            jax.ShapeDtypeStruct((1, edges), jnp.int32),
            rows_shape(ALIGN),
            order_shape,
            rows_shape(2 * rows + ALIGN),
        ],
        in_specs=[VMEM, HBM, HBM],
        out_specs=[VMEM] * 7,
        scratch_shapes=[pltpu.VMEM((cols, width), jnp.bfloat16), pltpu.SemaphoreType.DMA((9,))],
        compiler_params=pltpu.CompilerParams(vmem_limit_bytes=12 * MIB),
        cost_estimate=QUICK,
    )(by_rank, in_hbm(out_proj.reshape(cols, width)), in_hbm(out_grads))
    other_unit = swap(core_unit, 0, 1)
    unit = pl.pallas_call(
        join_kernel,
        out_shape=pltpu.VMEM((CORES * cols, quarter), jnp.bfloat16),
        in_specs=[VMEM] * 2,
        out_specs=VMEM,
        compiler_params=pltpu.CompilerParams(vmem_limit_bytes=4 * MIB),
        cost_estimate=QUICK,
    )(mine_unit, other_unit)

    def permuted(plan, headed, *after):
        held, *_ = tie(order, *after)
        return pl.pallas_call(
            functools.partial(permute_kernel, plan),
            out_shape=[
                rows_shape(many + (ALIGN if n in headed else 0))
                for n, (_, _, many) in enumerate(plan)
            ],
            in_specs=[VMEM] * 3,
            out_specs=[VMEM] * len(plan),
            compiler_params=pltpu.CompilerParams(vmem_limit_bytes=12 * MIB),
            cost_estimate=QUICK,
        )(in_vmem(held), head, in_vmem(held_grads))

    def starts_in(block, count):
        digits = block[count : count + 2, :edges].astype(jnp.int32)
        return (digits[0] * DIGIT + digits[1]).reshape(1, edges)

    half = 2 * rows
    side_pieces = [swap(first_piece, 1, 0)]
    held = {(0, 0): unit, (1, 0): along(unit, following)}
    (second_piece,) = permuted([(2, half, half)], [], unit)
    own_tokens, for_core = permuted([(0, 0, pairs), (1, 0, pairs)], [1], second_piece)
    third_piece, last_piece = permuted([(3, 0, 3 * rows), (3, 3 * rows, rows)], [0], own_tokens)
    from_core = swap(for_core, 0, 1)
    held[0, 1] = swap(unit, 0, CORES)
    side_pieces.append(swap(second_piece, 1, 0))
    local_segments, _ = tie(segments, last_piece)
    basis, order_back = pl.pallas_call(
        basis_kernel,
        out_shape=[
            pltpu.VMEM((2 * tokens, SEG_DEV * 2 * rank), jnp.bfloat16),
            order_shape,
        ],
        in_specs=[HBM, HBM, VMEM, VMEM],
        out_specs=[VMEM] * 2,
        scratch_shapes=[
            pltpu.VMEM(hidden_in.shape, jnp.bfloat16),
            pltpu.VMEM(in_proj.shape, jnp.bfloat16),
            pltpu.SemaphoreType.DMA((5,)),
        ],
        compiler_params=pltpu.CompilerParams(vmem_limit_bytes=12 * MIB),
        cost_estimate=QUICK,
    )(in_hbm(hidden_in), in_hbm(in_proj), local_segments.reshape(1, tokens), by_rank)

    call = functools.partial(
        accumulate, bases=bases, rank=rank, pairs=pairs, window=window, places=places
    )
    place_of = {name: CORES * n for n, name in enumerate(arrival)}
    starts = {0: own_starts}
    members = []
    known_units = 0
    state = None

    def work(names, complete=(), partial=(), sends=(), cost=QUICK):
        nonlocal state, known_units
        tasks, arrived = [], []
        for group, blocks in complete:
            first = 0
            for piece, count in blocks:
                arrived.append((piece, group * pairs + first, count))
                first += count
            if group:
                starts[group] = starts_in(*blocks[0])
            members.append(group)
        fresh = [group for group, _ in complete]
        if fresh and known_units:
            tasks.append(("units", fresh, 0, known_units))
        if names:
            tasks.append(("units", list(members), known_units, CORES * len(names)))
        known_units += CORES * len(names)
        for group, piece, first, count in partial:
            arrived.append((piece, group * pairs + first, count))
            if first == 0:
                starts[group] = starts_in(piece, count)
                members.append(group)
            tasks.append(("piece", group, first, first + count, 0, known_units))
        state, out = call(
            state,
            starts=starts,
            tokens=arrived,
            units=[(held[n], place_of[n]) for n in names],
            tasks=tasks,
            sends=sends,
            cost=cost,
        )
        return out

    held[1, 0], side_pieces[0] = tie(held[1, 0], side_pieces[0])
    for n in range(1, final - 1):
        held[n + 1, 0] = along(held[n, 0], following)
        held[n, 1] = swap(held[n, 0], 0, CORES)
    third_piece, side_pieces[0] = tie(third_piece, side_pieces[0])
    diagonal_pieces = [swap(third_piece, 1, 1)]
    near = (final - 1, 0)
    held[near], basis, side_pieces[0] = tie(held[near], basis, side_pieces[0])
    work(names_a, complete=[(0, [(own_tokens, pairs)])], cost=SHORT)
    back_unit, basis, from_core = tie(held[0, 1], basis, from_core)
    held[final, 1] = along(back_unit, before)
    held[final, 0] = along(held[near], following)
    held[final - 1, 1] = swap(held[near], 0, CORES)
    last_piece, side_pieces[1] = tie(last_piece, side_pieces[1])
    diagonal_pieces.append(swap(last_piece, 1, 1))
    work(
        names_b,
        complete=[(1, [(from_core, pairs)]), (2, [(piece, half) for piece in side_pieces])],
        cost=SHORT,
    )
    work([], partial=[(3, diagonal_pieces[0], 0, 3 * rows)])
    sent = work(names_c, sends=[1, 2])
    sent = sent + work([], partial=[(3, diagonal_pieces[1], 3 * rows, rows)], sends=[3], cost=SHORT)

    def returned(arrays):
        return [
            swap(array, side, bit) for array, (side, bit) in zip(arrays, ((0, 1), (1, 0), (1, 1)))
        ]

    early = returned(sent)
    place = places - 2 * CORES
    own_late, *sent = pl.pallas_call(
        functools.partial(late_kernel, rank, pairs, window, place, QUAD),
        out_shape=[pltpu.VMEM((2 * window, LANES), jnp.float32)]
        + [pltpu.VMEM((2 * window, LANES), jnp.bfloat16)] * (QUAD - 1),
        in_specs=[SMEM] * (1 + QUAD) + [VMEM] * 3,
        out_specs=[VMEM] * QUAD,
        compiler_params=pltpu.CompilerParams(vmem_limit_bytes=8 * MIB),
        cost_estimate=QUICK,
    )(bases, *[starts[g] for g in range(QUAD)], in_vmem(state[0]), held[final, 0], held[final, 1])
    late = returned(sent)
    *early, own_late = tie(*early, own_late)
    out, turned = pl.pallas_call(
        functools.partial(blocks_kernel, rank),
        out_shape=[
            jax.ShapeDtypeStruct((SEG_DEV, experts, rank * rank), jnp.bfloat16),
            pltpu.VMEM((rank, pairs), jnp.float32),
        ],
        in_specs=[VMEM] * 7,
        out_specs=[VMEM] * 2,
        scratch_shapes=[pltpu.VMEM((rank // 2, experts, 2 * tokens), jnp.float32)],
        compiler_params=pltpu.CompilerParams(vmem_limit_bytes=32 * MIB),
        cost_estimate=QUICK,
    )(by_rank, basis, in_vmem(order_back), in_vmem(state[2]), *early)
    count = 2 * CORES * exp_here
    return pl.pallas_call(
        functools.partial(last_kernel, rank, place, count, exp_here),
        out_shape=jax.ShapeDtypeStruct(out.shape, out.dtype),
        in_specs=[SMEM] * 2 + [VMEM] * 8 + [HBM],
        out_specs=HBM,
        scratch_shapes=[
            pltpu.VMEM((rank, pairs), jnp.float32),
            pltpu.VMEM((rank // 2, count, 2 * tokens), jnp.float32),
            pltpu.VMEM((SEG_DEV, count, rank * rank), jnp.bfloat16),
            pltpu.SemaphoreType.DMA,
        ],
        input_output_aliases={10: 0},
        compiler_params=pltpu.CompilerParams(vmem_limit_bytes=16 * MIB),
        cost_estimate=QUICK,
    )(bases, own_starts, by_rank, basis, in_vmem(order_back), in_vmem(turned), own_late, *late, out)


def solution(mesh):
    placed = (
        P(("groups", "expert"), None),
        P(("groups", "expert"), None, None),
        P(("groups", "expert"), None),
        P(("groups", "expert")),
        P(),
        P("expert", None, None),
    )
    return jax.shard_map(
        local,
        mesh=mesh,
        in_specs=placed,
        out_specs=P(("groups", "expert"), None, None),
        check_vma=False,
    )
```

```python
import functools

import jax
import jax.numpy as jnp
import numpy as np
from jax import lax
from jax.experimental import pallas as pl
from jax.experimental.pallas import tpu as pltpu
from jax.sharding import PartitionSpec as P

SEG_DEV = 2
CORES = 2
SIDES = 2
QUAD = 4
PIECES = 4
LANES = 128
ALIGN = 16
DIGIT = 32
BOTH = ("groups", "expert")
MIB = 1024 * 1024
VMEM = pl.BlockSpec(memory_space=pltpu.VMEM)
SMEM = pl.BlockSpec(memory_space=pltpu.SMEM)
HBM = pl.BlockSpec(memory_space=pl.ANY)
QUICK = pl.CostEstimate(flops=1, bytes_accessed=1, transcendentals=0)
SHORT = pl.CostEstimate(flops=10**9, bytes_accessed=1, transcendentals=0)
NT = (((1,), (1,)), ((), ()))


def in_vmem(array):
    return pltpu.with_memory_space_constraint(array, pltpu.VMEM)


def in_hbm(array):
    return pltpu.with_memory_space_constraint(array, pltpu.HBM)


def place_in_quad(flip):
    side, core = lax.axis_index("groups") % SIDES, lax.axis_index("expert") % CORES
    return (side ^ (flip // CORES)) * CORES + (core ^ (flip % CORES))


def columns_of(flip, width):
    return pl.ds(pl.multiple_of(place_in_quad(flip) * width, width), width)


def row_of(routes):
    tops, tokens = routes.shape
    pairs = tops * tokens
    lane = lax.broadcasted_iota(jnp.int32, (tokens, pairs), 1)
    token = lax.broadcasted_iota(jnp.int32, (tokens, pairs), 0)
    spread = jnp.where(lane // tops == token, 1.0, 0.0).astype(jnp.bfloat16)
    values = routes.astype(jnp.float32).astype(jnp.bfloat16)
    every = jnp.dot(values, spread, preferred_element_type=jnp.float32)
    lane = lax.broadcasted_iota(jnp.int32, (tops, pairs), 1)
    k = lax.broadcasted_iota(jnp.int32, (tops, pairs), 0)
    return jnp.sum(jnp.where(lane % tops == k, every, 0.0), axis=0, keepdims=True).astype(jnp.int32)


def key_column(routes_row):
    count = routes_row.shape[1]
    keys = routes_row * count + lax.broadcasted_iota(jnp.int32, (1, count), 1)
    return jnp.broadcast_to(keys.astype(jnp.float32), (8, count)).T[:, 0:1]


def ranks(column, keys):
    total = jnp.zeros(keys.shape, jnp.float32)
    for first in range(0, column.shape[0], 128):
        smaller = jnp.where(column[first : first + 128] < keys, 1.0, 0.0)
        total = total + jnp.sum(smaller, axis=0, keepdims=True)
    return total


def sort_kernel(
    routes_ref,
    weight_ref,
    grads_ref,
    held_ref,
    mine_ref,
    core_ref,
    starts_ref,
    head_ref,
    order_ref,
    piece_ref,
    stage,
    sems,
):
    width = piece_ref.shape[1]
    count = sems.shape[0] - 1
    part = grads_ref.shape[0] // count
    copies = [pltpu.make_async_copy(weight_ref, stage, sems.at[count])]
    for n in range(count):
        here = pl.ds(n * part, part)
        copies.append(pltpu.make_async_copy(grads_ref.at[here], held_ref.at[here], sems.at[n]))
    for copy in copies:
        copy.start()
    routes = row_of(routes_ref[...])
    pairs = routes.shape[1]
    column = key_column(routes)
    keys = routes * pairs + lax.broadcasted_iota(jnp.int32, (1, pairs), 1)
    place = ranks(column, keys.astype(jnp.float32)).astype(jnp.int32)
    firsts = lax.broadcasted_iota(jnp.int32, starts_ref.shape, 1) * pairs
    starts = ranks(column, firsts.astype(jnp.float32)).astype(jnp.int32)
    starts_ref[...] = starts
    wide = head_ref.shape[1] - starts.shape[1]
    digits = [starts // DIGIT, starts % DIGIT]
    digits = [jnp.pad(d.astype(jnp.float32), ((0, 0), (0, wide))) for d in digits]
    row = lax.broadcasted_iota(jnp.int32, head_ref.shape, 0)
    head = jnp.where(row == 0, digits[0], jnp.where(row == 1, digits[1], 0.0))
    head_ref[...] = head.astype(jnp.bfloat16)
    rows = piece_ref.shape[0] - ALIGN
    for first in range(0, pairs, rows):
        ids = first + lax.broadcasted_iota(jnp.int32, (rows, pairs), 0)
        order_ref[first : first + rows, :] = jnp.where(place == ids, 1.0, 0.0).astype(jnp.bfloat16)
    copies[0].wait()
    core_ref[...] = stage[:, columns_of(1, width)]
    mine_ref[...] = stage[:, columns_of(0, width)]
    for copy in copies[1:]:
        copy.wait()
    piece_ref[0:rows, :] = jnp.dot(
        order_ref[0:rows, :],
        held_ref[:, :, columns_of(2, width)].reshape(pairs, width),
        preferred_element_type=jnp.float32,
    ).astype(jnp.bfloat16)
    piece_ref[rows:, :] = head_ref[...]


def join_kernel(one_ref, two_ref, out_ref):
    half = one_ref.shape[0]
    out_ref[0:half, :] = one_ref[...]
    out_ref[half:, :] = two_ref[...]


def permute_kernel(plan, order_ref, head_ref, grads_ref, *outs):
    pairs, width = order_ref.shape[0], outs[0].shape[1]
    for device in sorted({device for device, _, _ in plan}):
        grads = grads_ref[:, :, columns_of(device, width)].reshape(pairs, width)
        for out, (target, first, rows) in zip(outs, plan):
            if target == device:
                out[0:rows, :] = jnp.dot(
                    order_ref[first : first + rows, :], grads, preferred_element_type=jnp.float32
                ).astype(jnp.bfloat16)
                if out.shape[0] > rows:
                    out[rows:, :] = head_ref[...]


def basis_kernel(
    hidden_ref, proj_ref, segment_ref, routes_ref, out_ref, order_ref, hidden, proj, sems
):
    count = sems.shape[0] - 1
    part = hidden.shape[0] // count
    copies = [pltpu.make_async_copy(proj_ref, proj, sems.at[count])]
    for n in range(count):
        here = pl.ds(n * part, part)
        copies.append(pltpu.make_async_copy(hidden_ref.at[here], hidden.at[here], sems.at[n]))
    for copy in copies:
        copy.start()
    tops, tokens = routes_ref.shape
    pairs = tops * tokens
    column = key_column(row_of(routes_ref[...]))
    at = [
        routes_ref[k : k + 1, :] * pairs + lax.broadcasted_iota(jnp.int32, (1, tokens), 1) * tops + k
        for k in range(tops)
    ]
    place = ranks(column, jnp.concatenate(at, axis=1).astype(jnp.float32)).astype(jnp.int32)
    for first in range(0, pairs, 256):
        ids = first + lax.broadcasted_iota(jnp.int32, (256, pairs), 0)
        order_ref[first : first + 256, :] = jnp.where(place == ids, 1.0, 0.0).astype(jnp.bfloat16)
    segment = (segment_ref[...] - lax.axis_index("expert") * SEG_DEV).astype(jnp.float32)
    segment = jnp.broadcast_to(segment, (8, tokens)).T[:, 0:1]
    for copy in copies:
        copy.wait()
    projected = lax.dot_general(hidden[...], proj[...], NT, preferred_element_type=jnp.float32)
    zero = jnp.zeros_like(projected)
    picked = [jnp.where(segment == float(s), projected, zero) for s in range(SEG_DEV)]
    even = jnp.concatenate([b for p in picked for b in (p, zero)], axis=1)
    odd = jnp.concatenate([b for p in picked for b in (zero, p)], axis=1)
    out_ref[...] = jnp.concatenate([even, odd], axis=0).astype(out_ref.dtype)


def packed(total, first, pairs, rank):
    half = pairs // 2
    low = lax.broadcasted_iota(jnp.int32, (half, LANES), 1) < rank
    one = total[first : first + half, :]
    two = total[first + half : first + pairs, :]
    return jnp.where(low, one + pltpu.roll(one, rank, 1), two + pltpu.roll(two, rank, 1))


def partial_kernel(
    rank, pairs, window, new_tokens, new_units, tasks, fresh, sends, groups, bases_ref, *refs
):
    start_refs = dict(zip(groups, refs))
    refs = refs[len(groups) :]
    token_refs, refs = refs[: len(new_tokens)], refs[len(new_tokens) :]
    unit_refs, refs = refs[: len(new_units)], refs[len(new_units) :]
    if fresh:
        tokens, units, total = refs
        send_refs = ()
        total[...] = jnp.zeros_like(total)
    else:
        tokens, units, total = refs[3:6]
        send_refs = refs[6:]
    for ref, (first, count) in zip(token_refs, new_tokens):
        tokens[first : first + count, :] = ref[0:count, :]
    cols = units.shape[1]
    for ref, place in zip(unit_refs, new_units):
        for half in range(CORES):
            units[place + half] = ref[half * cols : (half + 1) * cols, :]
    held = cols // rank
    per_tile = LANES // rank
    low = lax.broadcasted_iota(jnp.int32, (1, LANES), 1) < rank

    device = lax.axis_index("expert")

    def process(w, members):
        base = bases_ref[device, w]
        heres, offsets = [], []
        for g in members:
            at = jnp.minimum(start_refs[g][0, base] & -ALIGN, pairs - window)
            offsets.append(at)
            heres.append(pl.ds(pl.multiple_of(g * pairs + at, ALIGN), window))
        rows = [tokens[here, :] for here in heres]
        rows = jnp.concatenate(rows, axis=0) if len(rows) > 1 else rows[0]
        dense = lax.dot_general(rows, units[w], NT, preferred_element_type=jnp.float32)
        for n, g in enumerate(members):
            value = total[heres[n], :]
            number = offsets[n] + lax.broadcasted_iota(jnp.int32, (window, LANES), 0)
            for j in range(cols // LANES):
                edge = [start_refs[g][0, base + j * per_tile + i] for i in range(per_tile + 1)]
                inside = (number >= jnp.where(low, edge[0], edge[1])) & (
                    number < jnp.where(low, edge[1], edge[2])
                )
                part = dense[n * window : (n + 1) * window, j * LANES : (j + 1) * LANES]
                value = jnp.where(inside, part, value)
            total[heres[n], :] = value

    for task in tasks:
        if task[0] == "units":
            _, members, first_w, count = task

            def each(i, carry, members=members, first_w=first_w):
                process(first_w + i, members)
                return carry

        else:
            _, member, first_row, end_row, first_w, count = task

            def each(
                i, carry, member=member, first_row=first_row, end_row=end_row, first_w=first_w
            ):
                w = first_w + i
                base = bases_ref[device, w]
                touches = (start_refs[member][0, base] < end_row) & (
                    start_refs[member][0, base + held] > first_row
                )

                @pl.when(touches)
                def _():
                    process(w, [member])

                return carry

        lax.fori_loop(0, count, each, 0)
    for ref, g in zip(send_refs, sends):
        ref[...] = packed(total, g * pairs, pairs, rank).astype(ref.dtype)


def accumulate(
    state, bases, starts, tokens, units, tasks, rank, pairs, window, places=0, sends=(), cost=QUICK
):
    fresh = state is None
    operands = [bases, *starts.values(), *[a for a, _, _ in tokens], *[a for a, _ in units]]
    specs = [SMEM] * (1 + len(starts)) + [VMEM] * (len(tokens) + len(units))
    if fresh:
        width = units[0][0].shape[1]
        shapes = [
            pltpu.VMEM((QUAD * pairs, width), jnp.bfloat16),
            pltpu.VMEM((places, units[0][0].shape[0] // CORES, width), jnp.bfloat16),
            pltpu.VMEM((QUAD * pairs, LANES), jnp.float32),
        ]
        aliases = {}
    else:
        aliases = {len(operands) + i: i for i in range(3)}
        operands += [in_vmem(a) for a in state]
        specs += [VMEM] * 3
        shapes = [pltpu.VMEM(a.shape, a.dtype) for a in state]
    shapes += [pltpu.VMEM((pairs // 2, LANES), jnp.bfloat16)] * len(sends)
    out = pl.pallas_call(
        functools.partial(
            partial_kernel,
            rank,
            pairs,
            window,
            [(first, count) for _, first, count in tokens],
            [p for _, p in units],
            tasks,
            fresh,
            sends,
            list(starts),
        ),
        out_shape=shapes,
        in_specs=specs,
        out_specs=[VMEM] * len(shapes),
        input_output_aliases=aliases,
        compiler_params=pltpu.CompilerParams(vmem_limit_bytes=8 * MIB),
        cost_estimate=cost,
    )(*operands)
    return list(out[:3]), list(out[3:])


def late_kernel(rank, pairs, window, place, groups, bases_ref, *refs):
    start_refs, tokens, refs = refs[:groups], refs[groups], refs[groups + 1 :]
    unit_refs, outs = refs[:2], refs[2:]
    per_tile = LANES // rank
    low = lax.broadcasted_iota(jnp.int32, (1, LANES), 1) < rank
    device = lax.axis_index("expert")
    first_core = device % CORES == 0
    for u, unit_ref in enumerate(unit_refs):
        cols = unit_ref.shape[0] // CORES
        folded = []
        for half in range(CORES):
            base = bases_ref[device, place + u * CORES + half]
            offsets, rows = [], []
            for g in range(groups):
                at = jnp.minimum(start_refs[g][0, base] & -ALIGN, pairs - window)
                offsets.append(at)
                rows.append(tokens[pl.ds(pl.multiple_of(g * pairs + at, ALIGN), window), :])
            dense = lax.dot_general(
                jnp.concatenate(rows, axis=0),
                unit_ref[half * cols : (half + 1) * cols, :],
                NT,
                preferred_element_type=jnp.float32,
            )
            found = []
            for g in range(groups):
                value = jnp.zeros((window, LANES), jnp.float32)
                number = offsets[g] + lax.broadcasted_iota(jnp.int32, (window, LANES), 0)
                for j in range(cols // LANES):
                    edge = [start_refs[g][0, base + j * per_tile + i] for i in range(per_tile + 1)]
                    inside = (number >= jnp.where(low, edge[0], edge[1])) & (
                        number < jnp.where(low, edge[1], edge[2])
                    )
                    part = dense[g * window : (g + 1) * window, j * LANES : (j + 1) * LANES]
                    value = jnp.where(inside, part, value)
                found.append(value + pltpu.roll(value, rank, 1))
            folded.append(found)
        for g, out in enumerate(outs):
            one, two = folded[0][g], folded[1][g]
            zero = jnp.where(first_core, one, two)
            other = jnp.where(first_core, two, one)
            out[u * window : (u + 1) * window, :] = jnp.where(low, zero, other).astype(out.dtype)


def expand(routes_ref, turned, lines, first, tiles):
    tops, tokens = routes_ref.shape
    rank = turned.shape[0]

    def one(tile, carry):
        here = pl.multiple_of(tile * 8, 8)
        ids = first + here + lax.broadcasted_iota(jnp.int32, (8, tokens), 0)
        masks = [routes_ref[k : k + 1, :] == ids for k in range(tops)]
        for r in range(rank):
            value = jnp.zeros((8, tokens), jnp.float32)
            for k in range(tops):
                row = turned[r : r + 1, k * tokens : (k + 1) * tokens]
                value = jnp.where(masks[k], row, value)
            side = r % 2 * tokens
            lines[r // 2, pl.ds(here, 8), side : side + tokens] = value
        return carry

    lax.fori_loop(0, tiles, one, 0)


def form(lines, basis_ref, first, count, out_ref, rank):
    experts, width = lines.shape[1:]
    made = jnp.dot(
        lines[first : first + count].reshape(count * experts, width).astype(jnp.bfloat16),
        basis_ref[...],
        preferred_element_type=jnp.float32,
    ).astype(jnp.bfloat16)
    for pair in range(count):
        for s in range(SEG_DEV):
            out_ref[s, :, pl.ds((first + pair) * 2 * rank, 2 * rank)] = made[
                pair * experts : (pair + 1) * experts, s * 2 * rank : (s + 1) * 2 * rank
            ]


def blocks_kernel(
    rank, routes_ref, basis_ref, order_ref, total_ref, b_ref, c_ref, d_ref, out_ref, turned, lines
):
    half = b_ref.shape[0]
    value = packed(total_ref, 0, 2 * half, rank)
    for ref in (b_ref, c_ref, d_ref):
        value = value + ref[...].astype(jnp.float32)
    value = value.T
    value = jnp.concatenate([value[0:rank], value[rank : 2 * rank]], axis=1).astype(jnp.bfloat16)
    turned[...] = jnp.dot(value, order_ref[...], preferred_element_type=jnp.float32)
    expand(routes_ref, turned, lines, 0, lines.shape[1] // 8)
    for first in range(0, rank // 2, 8):
        form(lines, basis_ref, first, 8, out_ref, rank)


def last_kernel(
    rank,
    place,
    count,
    held,
    bases_ref,
    starts_ref,
    routes_ref,
    basis_ref,
    order_ref,
    turned_ref,
    own_ref,
    b_ref,
    c_ref,
    d_ref,
    _,
    out_ref,
    turned,
    lines,
    block,
    sem,
):
    window = own_ref.shape[0] // 2
    pairs = order_ref.shape[0]
    value = own_ref[...]
    for ref in (b_ref, c_ref, d_ref):
        value = value + ref[...].astype(jnp.float32)
    value = value.T.astype(jnp.bfloat16)
    device = lax.axis_index("expert")
    first = bases_ref[device, place] // count * count
    total = turned_ref[...]
    for u in range(2):
        unit = bases_ref[device, place + u * CORES] // (CORES * held) * (CORES * held)
        for core in range(CORES):
            at = jnp.minimum(starts_ref[0, unit + core * held] & -ALIGN, pairs - window)
            total = total + jnp.dot(
                value[core * rank : (core + 1) * rank, u * window : (u + 1) * window],
                order_ref[pl.ds(pl.multiple_of(at, ALIGN), window), :],
                preferred_element_type=jnp.float32,
            )
    turned[...] = total
    expand(routes_ref, turned, lines, first, count // 8)
    form(lines, basis_ref, 0, rank // 2, block, rank)
    copy = pltpu.make_async_copy(
        block, out_ref.at[:, pl.ds(pl.multiple_of(first, count), count), :], sem
    )
    copy.start()
    copy.wait()


def local(hidden_in, out_grads, routes, segments, in_proj, out_proj):
    tokens, tops = routes.shape
    exp_here, rank, width = out_proj.shape
    owners, groups = lax.axis_size("expert"), lax.axis_size("groups")
    experts = exp_here * owners
    pairs = tokens * tops
    capacity = max(2, 3 * pairs // (2 * experts))
    window = min(pairs, -(-(exp_here * capacity + ALIGN - 1) // ALIGN) * ALIGN)
    quarter = width // QUAD
    cols = exp_here * rank
    rows = pairs // PIECES
    index = lax.axis_index("expert")
    slots = owners // CORES // 2
    ring = [0, *range(1, slots, 2), *range((slots - 1) // 2 * 2, 0, -2)]
    following = {a: b for a, b in zip(ring, ring[1:] + ring[:1])}
    before = {b: a for a, b in following.items()}

    def swap(array, side, bit):
        table = [
            (g * owners + e, (g ^ side) * owners + (e ^ bit))
            for g in range(groups)
            for e in range(owners)
        ]
        return lax.ppermute(array, BOTH, table)

    def along(array, table):
        wide = 2 * CORES
        pairs_of = [(e, table[e // wide] * wide + e % wide) for e in range(owners)]
        return lax.ppermute(array, "expert", pairs_of)

    def tie(*arrays):
        return lax.optimization_barrier(arrays)

    final = slots - 1
    names_a = [(n, 0) for n in range(final - 1)] + [(0, 1)]
    names_b = [(final - 1, 0)] + [(n, 1) for n in range(1, final - 1)]
    names_c = [(final - 1, 1)]
    arrival = names_a + names_b + names_c + [(final, 0), (final, 1)]

    def source(z, hops):
        for _ in range(hops):
            z = before[z]
        return z

    rows_of = [
        [
            ((source(e // (2 * CORES), n) * 2 + (e // CORES % 2 ^ y)) * CORES + (e % CORES ^ c)) * exp_here
            for n, y in arrival
            for c in range(CORES)
        ]
        for e in range(owners)
    ]
    places = CORES * len(arrival)
    bases = jnp.asarray(np.array(rows_of, np.int32))

    unit_shape = pltpu.VMEM((cols, quarter), jnp.bfloat16)
    order_shape = pltpu.VMEM((pairs, pairs), jnp.bfloat16)

    def rows_shape(count):
        return pltpu.VMEM((count, quarter), jnp.bfloat16)

    by_rank = routes.T
    edges = -(-(experts + 1) // LANES) * LANES
    held_grads, mine_unit, core_unit, own_starts, head, order, first_piece = pl.pallas_call(
        sort_kernel,
        out_shape=[
            pltpu.VMEM(out_grads.shape, jnp.bfloat16),
            unit_shape,
            unit_shape,
            jax.ShapeDtypeStruct((1, edges), jnp.int32),
            rows_shape(ALIGN),
            order_shape,
            rows_shape(2 * rows + ALIGN),
        ],
        in_specs=[VMEM, HBM, HBM],
        out_specs=[VMEM] * 7,
        scratch_shapes=[pltpu.VMEM((cols, width), jnp.bfloat16), pltpu.SemaphoreType.DMA((9,))],
        compiler_params=pltpu.CompilerParams(vmem_limit_bytes=12 * MIB),
        cost_estimate=QUICK,
    )(by_rank, in_hbm(out_proj.reshape(cols, width)), in_hbm(out_grads))
    other_unit = swap(core_unit, 0, 1)
    unit = pl.pallas_call(
        join_kernel,
        out_shape=pltpu.VMEM((CORES * cols, quarter), jnp.bfloat16),
        in_specs=[VMEM] * 2,
        out_specs=VMEM,
        compiler_params=pltpu.CompilerParams(vmem_limit_bytes=4 * MIB),
        cost_estimate=QUICK,
    )(mine_unit, other_unit)

    def permuted(plan, headed, *after):
        held, *_ = tie(order, *after)
        return pl.pallas_call(
            functools.partial(permute_kernel, plan),
            out_shape=[
                rows_shape(many + (ALIGN if n in headed else 0))
                for n, (_, _, many) in enumerate(plan)
            ],
            in_specs=[VMEM] * 3,
            out_specs=[VMEM] * len(plan),
            compiler_params=pltpu.CompilerParams(vmem_limit_bytes=12 * MIB),
            cost_estimate=QUICK,
        )(in_vmem(held), head, in_vmem(held_grads))

    def starts_in(block, count):
        digits = block[count : count + 2, :edges].astype(jnp.int32)
        return (digits[0] * DIGIT + digits[1]).reshape(1, edges)

    half = 2 * rows
    side_pieces = [swap(first_piece, 1, 0)]
    held = {(0, 0): unit, (1, 0): along(unit, following)}
    (second_piece,) = permuted([(2, half, half)], [], unit)
    own_tokens, for_core = permuted([(0, 0, pairs), (1, 0, pairs)], [1], second_piece)
    third_piece, last_piece = permuted([(3, 0, 3 * rows), (3, 3 * rows, rows)], [0], own_tokens)
    from_core = swap(for_core, 0, 1)
    held[0, 1] = swap(unit, 0, CORES)
    side_pieces.append(swap(second_piece, 1, 0))
    local_segments, _ = tie(segments, last_piece)
    basis, order_back = pl.pallas_call(
        basis_kernel,
        out_shape=[
            pltpu.VMEM((2 * tokens, SEG_DEV * 2 * rank), jnp.bfloat16),
            order_shape,
        ],
        in_specs=[HBM, HBM, VMEM, VMEM],
        out_specs=[VMEM] * 2,
        scratch_shapes=[
            pltpu.VMEM(hidden_in.shape, jnp.bfloat16),
            pltpu.VMEM(in_proj.shape, jnp.bfloat16),
            pltpu.SemaphoreType.DMA((5,)),
        ],
        compiler_params=pltpu.CompilerParams(vmem_limit_bytes=12 * MIB),
        cost_estimate=QUICK,
    )(in_hbm(hidden_in), in_hbm(in_proj), local_segments.reshape(1, tokens), by_rank)

    call = functools.partial(
        accumulate, bases=bases, rank=rank, pairs=pairs, window=window, places=places
    )
    place_of = {name: CORES * n for n, name in enumerate(arrival)}
    starts = {0: own_starts}
    members = []
    known_units = 0
    state = None

    def work(names, complete=(), partial=(), sends=(), cost=QUICK):
        nonlocal state, known_units
        tasks, arrived = [], []
        for group, blocks in complete:
            first = 0
            for piece, count in blocks:
                arrived.append((piece, group * pairs + first, count))
                first += count
            if group:
                starts[group] = starts_in(*blocks[0])
            members.append(group)
        fresh = [group for group, _ in complete]
        if fresh and known_units:
            tasks.append(("units", fresh, 0, known_units))
        if names:
            tasks.append(("units", list(members), known_units, CORES * len(names)))
        known_units += CORES * len(names)
        for group, piece, first, count in partial:
            arrived.append((piece, group * pairs + first, count))
            if first == 0:
                starts[group] = starts_in(piece, count)
                members.append(group)
            tasks.append(("piece", group, first, first + count, 0, known_units))
        state, out = call(
            state,
            starts=starts,
            tokens=arrived,
            units=[(held[n], place_of[n]) for n in names],
            tasks=tasks,
            sends=sends,
            cost=cost,
        )
        return out

    held[1, 0], side_pieces[0] = tie(held[1, 0], side_pieces[0])
    for n in range(1, final - 1):
        held[n + 1, 0] = along(held[n, 0], following)
        held[n, 1] = swap(held[n, 0], 0, CORES)
    third_piece, side_pieces[0] = tie(third_piece, side_pieces[0])
    diagonal_pieces = [swap(third_piece, 1, 1)]
    near = (final - 1, 0)
    held[near], basis, side_pieces[0] = tie(held[near], basis, side_pieces[0])
    work(names_a, complete=[(0, [(own_tokens, pairs)])], cost=SHORT)
    back_unit, basis, from_core = tie(held[0, 1], basis, from_core)
    held[final, 1] = along(back_unit, before)
    held[final, 0] = along(held[near], following)
    held[final - 1, 1] = swap(held[near], 0, CORES)
    last_piece, side_pieces[1] = tie(last_piece, side_pieces[1])
    diagonal_pieces.append(swap(last_piece, 1, 1))
    work(
        names_b,
        complete=[(1, [(from_core, pairs)]), (2, [(piece, half) for piece in side_pieces])],
        cost=SHORT,
    )
    work([], partial=[(3, diagonal_pieces[0], 0, 3 * rows)])
    sent = work(names_c, sends=[1, 2])
    sent = sent + work([], partial=[(3, diagonal_pieces[1], 3 * rows, rows)], sends=[3], cost=SHORT)

    def returned(arrays):
        return [
            swap(array, side, bit) for array, (side, bit) in zip(arrays, ((0, 1), (1, 0), (1, 1)))
        ]

    early = returned(sent)
    held_tokens, *early[:2] = tie(state[0], *early[:2])
    place = places - 2 * CORES
    own_late, *sent = pl.pallas_call(
        functools.partial(late_kernel, rank, pairs, window, place, QUAD),
        out_shape=[pltpu.VMEM((2 * window, LANES), jnp.float32)]
        + [pltpu.VMEM((2 * window, LANES), jnp.bfloat16)] * (QUAD - 1),
        in_specs=[SMEM] * (1 + QUAD) + [VMEM] * 3,
        out_specs=[VMEM] * QUAD,
        compiler_params=pltpu.CompilerParams(vmem_limit_bytes=8 * MIB),
        cost_estimate=QUICK,
    )(bases, *[starts[g] for g in range(QUAD)], in_vmem(held_tokens), held[final, 0], held[final, 1])
    late = returned(sent)
    *early, own_late = tie(*early, own_late)
    out, turned = pl.pallas_call(
        functools.partial(blocks_kernel, rank),
        out_shape=[
            jax.ShapeDtypeStruct((SEG_DEV, experts, rank * rank), jnp.bfloat16),
            pltpu.VMEM((rank, pairs), jnp.float32),
        ],
        in_specs=[VMEM] * 7,
        out_specs=[VMEM] * 2,
        scratch_shapes=[pltpu.VMEM((rank // 2, experts, 2 * tokens), jnp.float32)],
        compiler_params=pltpu.CompilerParams(vmem_limit_bytes=32 * MIB),
        cost_estimate=QUICK,
    )(by_rank, basis, in_vmem(order_back), in_vmem(state[2]), *early)
    count = 2 * CORES * exp_here
    return pl.pallas_call(
        functools.partial(last_kernel, rank, place, count, exp_here),
        out_shape=jax.ShapeDtypeStruct(out.shape, out.dtype),
        in_specs=[SMEM] * 2 + [VMEM] * 8 + [HBM],
        out_specs=HBM,
        scratch_shapes=[
            pltpu.VMEM((rank, pairs), jnp.float32),
            pltpu.VMEM((rank // 2, count, 2 * tokens), jnp.float32),
            pltpu.VMEM((SEG_DEV, count, rank * rank), jnp.bfloat16),
            pltpu.SemaphoreType.DMA,
        ],
        input_output_aliases={10: 0},
        compiler_params=pltpu.CompilerParams(vmem_limit_bytes=16 * MIB),
        cost_estimate=QUICK,
    )(bases, own_starts, by_rank, basis, in_vmem(order_back), in_vmem(turned), own_late, *late, out)


def solution(mesh):
    placed = (
        P(("groups", "expert"), None),
        P(("groups", "expert"), None, None),
        P(("groups", "expert"), None),
        P(("groups", "expert")),
        P(),
        P("expert", None, None),
    )
    return jax.shard_map(
        local,
        mesh=mesh,
        in_specs=placed,
        out_specs=P(("groups", "expert"), None, None),
        check_vma=False,
    )
```

```python
import functools

import jax
import jax.numpy as jnp
import numpy as np
from jax import lax
from jax.experimental import pallas as pl
from jax.experimental.pallas import tpu as pltpu
from jax.sharding import PartitionSpec as P

SEG_DEV = 2
CORES = 2
SIDES = 2
QUAD = 4
PIECES = 4
LANES = 128
ALIGN = 16
DIGIT = 32
BOTH = ("groups", "expert")
MIB = 1024 * 1024
VMEM = pl.BlockSpec(memory_space=pltpu.VMEM)
SMEM = pl.BlockSpec(memory_space=pltpu.SMEM)
HBM = pl.BlockSpec(memory_space=pl.ANY)
QUICK = pl.CostEstimate(flops=1, bytes_accessed=1, transcendentals=0)
SHORT = pl.CostEstimate(flops=10**9, bytes_accessed=1, transcendentals=0)
NT = (((1,), (1,)), ((), ()))


def in_vmem(array):
    return pltpu.with_memory_space_constraint(array, pltpu.VMEM)


def in_hbm(array):
    return pltpu.with_memory_space_constraint(array, pltpu.HBM)


def place_in_quad(flip):
    side, core = lax.axis_index("groups") % SIDES, lax.axis_index("expert") % CORES
    return (side ^ (flip // CORES)) * CORES + (core ^ (flip % CORES))


def columns_of(flip, width):
    return pl.ds(pl.multiple_of(place_in_quad(flip) * width, width), width)


def row_of(routes):
    tops, tokens = routes.shape
    pairs = tops * tokens
    lane = lax.broadcasted_iota(jnp.int32, (tokens, pairs), 1)
    token = lax.broadcasted_iota(jnp.int32, (tokens, pairs), 0)
    spread = jnp.where(lane // tops == token, 1.0, 0.0).astype(jnp.bfloat16)
    values = routes.astype(jnp.float32).astype(jnp.bfloat16)
    every = jnp.dot(values, spread, preferred_element_type=jnp.float32)
    lane = lax.broadcasted_iota(jnp.int32, (tops, pairs), 1)
    k = lax.broadcasted_iota(jnp.int32, (tops, pairs), 0)
    return jnp.sum(jnp.where(lane % tops == k, every, 0.0), axis=0, keepdims=True).astype(jnp.int32)


def key_column(routes_row):
    count = routes_row.shape[1]
    keys = routes_row * count + lax.broadcasted_iota(jnp.int32, (1, count), 1)
    return jnp.broadcast_to(keys.astype(jnp.float32), (8, count)).T[:, 0:1]


def ranks(column, keys):
    total = jnp.zeros(keys.shape, jnp.float32)
    for first in range(0, column.shape[0], 128):
        smaller = jnp.where(column[first : first + 128] < keys, 1.0, 0.0)
        total = total + jnp.sum(smaller, axis=0, keepdims=True)
    return total


def sort_kernel(
    routes_ref,
    weight_ref,
    grads_ref,
    held_ref,
    mine_ref,
    core_ref,
    starts_ref,
    head_ref,
    order_ref,
    piece_ref,
    stage,
    sems,
):
    width = piece_ref.shape[1]
    count = sems.shape[0] - 1
    part = grads_ref.shape[0] // count
    copies = [pltpu.make_async_copy(weight_ref, stage, sems.at[count])]
    for n in range(count):
        here = pl.ds(n * part, part)
        copies.append(pltpu.make_async_copy(grads_ref.at[here], held_ref.at[here], sems.at[n]))
    for copy in copies:
        copy.start()
    routes = row_of(routes_ref[...])
    pairs = routes.shape[1]
    column = key_column(routes)
    keys = routes * pairs + lax.broadcasted_iota(jnp.int32, (1, pairs), 1)
    place = ranks(column, keys.astype(jnp.float32)).astype(jnp.int32)
    firsts = lax.broadcasted_iota(jnp.int32, starts_ref.shape, 1) * pairs
    starts = ranks(column, firsts.astype(jnp.float32)).astype(jnp.int32)
    starts_ref[...] = starts
    wide = head_ref.shape[1] - starts.shape[1]
    digits = [starts // DIGIT, starts % DIGIT]
    digits = [jnp.pad(d.astype(jnp.float32), ((0, 0), (0, wide))) for d in digits]
    row = lax.broadcasted_iota(jnp.int32, head_ref.shape, 0)
    head = jnp.where(row == 0, digits[0], jnp.where(row == 1, digits[1], 0.0))
    head_ref[...] = head.astype(jnp.bfloat16)
    rows = piece_ref.shape[0] - ALIGN
    for first in range(0, pairs, rows):
        ids = first + lax.broadcasted_iota(jnp.int32, (rows, pairs), 0)
        order_ref[first : first + rows, :] = jnp.where(place == ids, 1.0, 0.0).astype(jnp.bfloat16)
    copies[0].wait()
    core_ref[...] = stage[:, columns_of(1, width)]
    mine_ref[...] = stage[:, columns_of(0, width)]
    for copy in copies[1:]:
        copy.wait()
    piece_ref[0:rows, :] = jnp.dot(
        order_ref[0:rows, :],
        held_ref[:, :, columns_of(2, width)].reshape(pairs, width),
        preferred_element_type=jnp.float32,
    ).astype(jnp.bfloat16)
    piece_ref[rows:, :] = head_ref[...]


def join_kernel(one_ref, two_ref, out_ref):
    half = one_ref.shape[0]
    out_ref[0:half, :] = one_ref[...]
    out_ref[half:, :] = two_ref[...]


def permute_kernel(plan, order_ref, head_ref, grads_ref, *outs):
    pairs, width = order_ref.shape[0], outs[0].shape[1]
    for device in sorted({device for device, _, _ in plan}):
        grads = grads_ref[:, :, columns_of(device, width)].reshape(pairs, width)
        for out, (target, first, rows) in zip(outs, plan):
            if target == device:
                out[0:rows, :] = jnp.dot(
                    order_ref[first : first + rows, :], grads, preferred_element_type=jnp.float32
                ).astype(jnp.bfloat16)
                if out.shape[0] > rows:
                    out[rows:, :] = head_ref[...]


def basis_kernel(
    hidden_ref, proj_ref, segment_ref, routes_ref, out_ref, order_ref, hidden, proj, sems
):
    count = sems.shape[0] - 1
    part = hidden.shape[0] // count
    copies = [pltpu.make_async_copy(proj_ref, proj, sems.at[count])]
    for n in range(count):
        here = pl.ds(n * part, part)
        copies.append(pltpu.make_async_copy(hidden_ref.at[here], hidden.at[here], sems.at[n]))
    for copy in copies:
        copy.start()
    tops, tokens = routes_ref.shape
    pairs = tops * tokens
    column = key_column(row_of(routes_ref[...]))
    at = [
        routes_ref[k : k + 1, :] * pairs + lax.broadcasted_iota(jnp.int32, (1, tokens), 1) * tops + k
        for k in range(tops)
    ]
    place = ranks(column, jnp.concatenate(at, axis=1).astype(jnp.float32)).astype(jnp.int32)
    for first in range(0, pairs, 256):
        ids = first + lax.broadcasted_iota(jnp.int32, (256, pairs), 0)
        order_ref[first : first + 256, :] = jnp.where(place == ids, 1.0, 0.0).astype(jnp.bfloat16)
    segment = (segment_ref[...] - lax.axis_index("expert") * SEG_DEV).astype(jnp.float32)
    segment = jnp.broadcast_to(segment, (8, tokens)).T[:, 0:1]
    for copy in copies:
        copy.wait()
    projected = lax.dot_general(hidden[...], proj[...], NT, preferred_element_type=jnp.float32)
    zero = jnp.zeros_like(projected)
    picked = [jnp.where(segment == float(s), projected, zero) for s in range(SEG_DEV)]
    even = jnp.concatenate([b for p in picked for b in (p, zero)], axis=1)
    odd = jnp.concatenate([b for p in picked for b in (zero, p)], axis=1)
    out_ref[...] = jnp.concatenate([even, odd], axis=0).astype(out_ref.dtype)


def packed(total, first, pairs, rank):
    half = pairs // 2
    low = lax.broadcasted_iota(jnp.int32, (half, LANES), 1) < rank
    one = total[first : first + half, :]
    two = total[first + half : first + pairs, :]
    return jnp.where(low, one + pltpu.roll(one, rank, 1), two + pltpu.roll(two, rank, 1))


def partial_kernel(
    rank, pairs, window, new_tokens, new_units, tasks, fresh, sends, groups, bases_ref, *refs
):
    start_refs = dict(zip(groups, refs))
    refs = refs[len(groups) :]
    token_refs, refs = refs[: len(new_tokens)], refs[len(new_tokens) :]
    unit_refs, refs = refs[: len(new_units)], refs[len(new_units) :]
    if fresh:
        tokens, units, total = refs
        send_refs = ()
        total[...] = jnp.zeros_like(total)
    else:
        tokens, units, total = refs[3:6]
        send_refs = refs[6:]
    for ref, (first, count) in zip(token_refs, new_tokens):
        tokens[first : first + count, :] = ref[0:count, :]
    cols = units.shape[1]
    for ref, place in zip(unit_refs, new_units):
        for half in range(CORES):
            units[place + half] = ref[half * cols : (half + 1) * cols, :]
    held = cols // rank
    per_tile = LANES // rank
    low = lax.broadcasted_iota(jnp.int32, (1, LANES), 1) < rank

    device = lax.axis_index("expert")

    def process(w, members):
        base = bases_ref[device, w]
        heres, offsets = [], []
        for g in members:
            at = jnp.minimum(start_refs[g][0, base] & -ALIGN, pairs - window)
            offsets.append(at)
            heres.append(pl.ds(pl.multiple_of(g * pairs + at, ALIGN), window))
        rows = [tokens[here, :] for here in heres]
        rows = jnp.concatenate(rows, axis=0) if len(rows) > 1 else rows[0]
        dense = lax.dot_general(rows, units[w], NT, preferred_element_type=jnp.float32)
        for n, g in enumerate(members):
            value = total[heres[n], :]
            number = offsets[n] + lax.broadcasted_iota(jnp.int32, (window, LANES), 0)
            for j in range(cols // LANES):
                edge = [start_refs[g][0, base + j * per_tile + i] for i in range(per_tile + 1)]
                inside = (number >= jnp.where(low, edge[0], edge[1])) & (
                    number < jnp.where(low, edge[1], edge[2])
                )
                part = dense[n * window : (n + 1) * window, j * LANES : (j + 1) * LANES]
                value = jnp.where(inside, part, value)
            total[heres[n], :] = value

    for task in tasks:
        if task[0] == "units":
            _, members, first_w, count = task

            def each(i, carry, members=members, first_w=first_w):
                process(first_w + i, members)
                return carry

        else:
            _, member, first_row, end_row, first_w, count = task

            def each(
                i, carry, member=member, first_row=first_row, end_row=end_row, first_w=first_w
            ):
                w = first_w + i
                base = bases_ref[device, w]
                touches = (start_refs[member][0, base] < end_row) & (
                    start_refs[member][0, base + held] > first_row
                )

                @pl.when(touches)
                def _():
                    process(w, [member])

                return carry

        lax.fori_loop(0, count, each, 0)
    for ref, g in zip(send_refs, sends):
        ref[...] = packed(total, g * pairs, pairs, rank).astype(ref.dtype)


def accumulate(
    state, bases, starts, tokens, units, tasks, rank, pairs, window, places=0, sends=(), cost=QUICK
):
    fresh = state is None
    operands = [bases, *starts.values(), *[a for a, _, _ in tokens], *[a for a, _ in units]]
    specs = [SMEM] * (1 + len(starts)) + [VMEM] * (len(tokens) + len(units))
    if fresh:
        width = units[0][0].shape[1]
        shapes = [
            pltpu.VMEM((QUAD * pairs, width), jnp.bfloat16),
            pltpu.VMEM((places, units[0][0].shape[0] // CORES, width), jnp.bfloat16),
            pltpu.VMEM((QUAD * pairs, LANES), jnp.float32),
        ]
        aliases = {}
    else:
        aliases = {len(operands) + i: i for i in range(3)}
        operands += [in_vmem(a) for a in state]
        specs += [VMEM] * 3
        shapes = [pltpu.VMEM(a.shape, a.dtype) for a in state]
    shapes += [pltpu.VMEM((pairs // 2, LANES), jnp.bfloat16)] * len(sends)
    out = pl.pallas_call(
        functools.partial(
            partial_kernel,
            rank,
            pairs,
            window,
            [(first, count) for _, first, count in tokens],
            [p for _, p in units],
            tasks,
            fresh,
            sends,
            list(starts),
        ),
        out_shape=shapes,
        in_specs=specs,
        out_specs=[VMEM] * len(shapes),
        input_output_aliases=aliases,
        compiler_params=pltpu.CompilerParams(vmem_limit_bytes=8 * MIB),
        cost_estimate=cost,
    )(*operands)
    return list(out[:3]), list(out[3:])


def late_kernel(rank, pairs, window, place, groups, bases_ref, *refs):
    start_refs, tokens, refs = refs[:groups], refs[groups], refs[groups + 1 :]
    unit_refs, outs = refs[:2], refs[2:]
    per_tile = LANES // rank
    low = lax.broadcasted_iota(jnp.int32, (1, LANES), 1) < rank
    device = lax.axis_index("expert")
    first_core = device % CORES == 0
    for u, unit_ref in enumerate(unit_refs):
        cols = unit_ref.shape[0] // CORES
        folded = []
        for half in range(CORES):
            base = bases_ref[device, place + u * CORES + half]
            offsets, rows = [], []
            for g in range(groups):
                at = jnp.minimum(start_refs[g][0, base] & -ALIGN, pairs - window)
                offsets.append(at)
                rows.append(tokens[pl.ds(pl.multiple_of(g * pairs + at, ALIGN), window), :])
            dense = lax.dot_general(
                jnp.concatenate(rows, axis=0),
                unit_ref[half * cols : (half + 1) * cols, :],
                NT,
                preferred_element_type=jnp.float32,
            )
            found = []
            for g in range(groups):
                value = jnp.zeros((window, LANES), jnp.float32)
                number = offsets[g] + lax.broadcasted_iota(jnp.int32, (window, LANES), 0)
                for j in range(cols // LANES):
                    edge = [start_refs[g][0, base + j * per_tile + i] for i in range(per_tile + 1)]
                    inside = (number >= jnp.where(low, edge[0], edge[1])) & (
                        number < jnp.where(low, edge[1], edge[2])
                    )
                    part = dense[g * window : (g + 1) * window, j * LANES : (j + 1) * LANES]
                    value = jnp.where(inside, part, value)
                found.append(value + pltpu.roll(value, rank, 1))
            folded.append(found)
        for g, out in enumerate(outs):
            one, two = folded[0][g], folded[1][g]
            zero = jnp.where(first_core, one, two)
            other = jnp.where(first_core, two, one)
            out[u * window : (u + 1) * window, :] = jnp.where(low, zero, other).astype(out.dtype)


def expand(routes_ref, turned, lines, first, tiles):
    tops, tokens = routes_ref.shape
    rank = turned.shape[0]

    def one(tile, carry):
        here = pl.multiple_of(tile * 8, 8)
        ids = first + here + lax.broadcasted_iota(jnp.int32, (8, tokens), 0)
        masks = [routes_ref[k : k + 1, :] == ids for k in range(tops)]
        for r in range(rank):
            value = jnp.zeros((8, tokens), jnp.float32)
            for k in range(tops):
                row = turned[r : r + 1, k * tokens : (k + 1) * tokens]
                value = jnp.where(masks[k], row, value)
            side = r % 2 * tokens
            lines[r // 2, pl.ds(here, 8), side : side + tokens] = value
        return carry

    lax.fori_loop(0, tiles, one, 0)


def form(lines, basis_ref, first, count, out_ref, rank):
    experts, width = lines.shape[1:]
    made = jnp.dot(
        lines[first : first + count].reshape(count * experts, width).astype(jnp.bfloat16),
        basis_ref[...],
        preferred_element_type=jnp.float32,
    ).astype(jnp.bfloat16)
    for pair in range(count):
        for s in range(SEG_DEV):
            out_ref[s, :, pl.ds((first + pair) * 2 * rank, 2 * rank)] = made[
                pair * experts : (pair + 1) * experts, s * 2 * rank : (s + 1) * 2 * rank
            ]


def blocks_kernel(
    rank, routes_ref, basis_ref, order_ref, total_ref, b_ref, c_ref, d_ref, out_ref, turned, lines
):
    half = b_ref.shape[0]
    value = packed(total_ref, 0, 2 * half, rank)
    for ref in (b_ref, c_ref, d_ref):
        value = value + ref[...].astype(jnp.float32)
    value = value.T
    value = jnp.concatenate([value[0:rank], value[rank : 2 * rank]], axis=1).astype(jnp.bfloat16)
    turned[...] = jnp.dot(value, order_ref[...], preferred_element_type=jnp.float32)
    expand(routes_ref, turned, lines, 0, lines.shape[1] // 8)
    for first in range(0, rank // 2, 8):
        form(lines, basis_ref, first, 8, out_ref, rank)


def last_kernel(
    rank,
    place,
    count,
    held,
    bases_ref,
    starts_ref,
    routes_ref,
    basis_ref,
    order_ref,
    turned_ref,
    own_ref,
    b_ref,
    c_ref,
    d_ref,
    _,
    out_ref,
    turned,
    lines,
    block,
    sem,
):
    window = own_ref.shape[0] // 2
    pairs = order_ref.shape[0]
    value = own_ref[...]
    for ref in (b_ref, c_ref, d_ref):
        value = value + ref[...].astype(jnp.float32)
    value = value.T.astype(jnp.bfloat16)
    device = lax.axis_index("expert")
    first = bases_ref[device, place] // count * count
    total = turned_ref[...]
    for u in range(2):
        unit = bases_ref[device, place + u * CORES] // (CORES * held) * (CORES * held)
        for core in range(CORES):
            at = jnp.minimum(starts_ref[0, unit + core * held] & -ALIGN, pairs - window)
            total = total + jnp.dot(
                value[core * rank : (core + 1) * rank, u * window : (u + 1) * window],
                order_ref[pl.ds(pl.multiple_of(at, ALIGN), window), :],
                preferred_element_type=jnp.float32,
            )
    turned[...] = total
    expand(routes_ref, turned, lines, first, count // 8)
    form(lines, basis_ref, 0, rank // 2, block, rank)
    copy = pltpu.make_async_copy(
        block, out_ref.at[:, pl.ds(pl.multiple_of(first, count), count), :], sem
    )
    copy.start()
    copy.wait()


def local(hidden_in, out_grads, routes, segments, in_proj, out_proj):
    tokens, tops = routes.shape
    exp_here, rank, width = out_proj.shape
    owners, groups = lax.axis_size("expert"), lax.axis_size("groups")
    experts = exp_here * owners
    pairs = tokens * tops
    capacity = max(2, 3 * pairs // (2 * experts))
    window = min(pairs, -(-(exp_here * capacity + ALIGN - 1) // ALIGN) * ALIGN)
    quarter = width // QUAD
    cols = exp_here * rank
    rows = pairs // PIECES
    index = lax.axis_index("expert")
    slots = owners // CORES // 2
    ring = [0, *range(1, slots, 2), *range((slots - 1) // 2 * 2, 0, -2)]
    following = {a: b for a, b in zip(ring, ring[1:] + ring[:1])}
    before = {b: a for a, b in following.items()}

    def swap(array, side, bit):
        table = [
            (g * owners + e, (g ^ side) * owners + (e ^ bit))
            for g in range(groups)
            for e in range(owners)
        ]
        return lax.ppermute(array, BOTH, table)

    def along(array, table):
        wide = 2 * CORES
        pairs_of = [(e, table[e // wide] * wide + e % wide) for e in range(owners)]
        return lax.ppermute(array, "expert", pairs_of)

    def tie(*arrays):
        return lax.optimization_barrier(arrays)

    final = slots - 1
    names_a = [(n, 0) for n in range(final - 1)] + [(0, 1)]
    names_b = [(final - 1, 0)] + [(n, 1) for n in range(1, final - 1)]
    names_c = [(final - 1, 1)]
    arrival = names_a + names_b + names_c + [(final, 0), (final, 1)]

    def source(z, hops):
        for _ in range(hops):
            z = before[z]
        return z

    rows_of = [
        [
            ((source(e // (2 * CORES), n) * 2 + (e // CORES % 2 ^ y)) * CORES + (e % CORES ^ c)) * exp_here
            for n, y in arrival
            for c in range(CORES)
        ]
        for e in range(owners)
    ]
    places = CORES * len(arrival)
    bases = jnp.asarray(np.array(rows_of, np.int32))

    unit_shape = pltpu.VMEM((cols, quarter), jnp.bfloat16)
    order_shape = pltpu.VMEM((pairs, pairs), jnp.bfloat16)

    def rows_shape(count):
        return pltpu.VMEM((count, quarter), jnp.bfloat16)

    by_rank = routes.T
    edges = -(-(experts + 1) // LANES) * LANES
    held_grads, mine_unit, core_unit, own_starts, head, order, first_piece = pl.pallas_call(
        sort_kernel,
        out_shape=[
            pltpu.VMEM(out_grads.shape, jnp.bfloat16),
            unit_shape,
            unit_shape,
            jax.ShapeDtypeStruct((1, edges), jnp.int32),
            rows_shape(ALIGN),
            order_shape,
            rows_shape(2 * rows + ALIGN),
        ],
        in_specs=[VMEM, HBM, HBM],
        out_specs=[VMEM] * 7,
        scratch_shapes=[pltpu.VMEM((cols, width), jnp.bfloat16), pltpu.SemaphoreType.DMA((9,))],
        compiler_params=pltpu.CompilerParams(vmem_limit_bytes=12 * MIB),
        cost_estimate=QUICK,
    )(by_rank, in_hbm(out_proj.reshape(cols, width)), in_hbm(out_grads))
    other_unit = swap(core_unit, 0, 1)
    unit = pl.pallas_call(
        join_kernel,
        out_shape=pltpu.VMEM((CORES * cols, quarter), jnp.bfloat16),
        in_specs=[VMEM] * 2,
        out_specs=VMEM,
        compiler_params=pltpu.CompilerParams(vmem_limit_bytes=4 * MIB),
        cost_estimate=QUICK,
    )(mine_unit, other_unit)

    def permuted(plan, headed, *after):
        held, *_ = tie(order, *after)
        return pl.pallas_call(
            functools.partial(permute_kernel, plan),
            out_shape=[
                rows_shape(many + (ALIGN if n in headed else 0))
                for n, (_, _, many) in enumerate(plan)
            ],
            in_specs=[VMEM] * 3,
            out_specs=[VMEM] * len(plan),
            compiler_params=pltpu.CompilerParams(vmem_limit_bytes=12 * MIB),
            cost_estimate=QUICK,
        )(in_vmem(held), head, in_vmem(held_grads))

    def starts_in(block, count):
        digits = block[count : count + 2, :edges].astype(jnp.int32)
        return (digits[0] * DIGIT + digits[1]).reshape(1, edges)

    half = 2 * rows
    side_pieces = [swap(first_piece, 1, 0)]
    held = {(0, 0): unit, (1, 0): along(unit, following)}
    (second_piece,) = permuted([(2, half, half)], [], unit)
    own_tokens, for_core = permuted([(0, 0, pairs), (1, 0, pairs)], [1], second_piece)
    third_piece, last_piece = permuted([(3, 0, 3 * rows), (3, 3 * rows, rows)], [0], own_tokens)
    from_core = swap(for_core, 0, 1)
    held[0, 1] = swap(unit, 0, CORES)
    side_pieces.append(swap(second_piece, 1, 0))
    local_segments, _ = tie(segments, last_piece)
    basis, order_back = pl.pallas_call(
        basis_kernel,
        out_shape=[
            pltpu.VMEM((2 * tokens, SEG_DEV * 2 * rank), jnp.bfloat16),
            order_shape,
        ],
        in_specs=[HBM, HBM, VMEM, VMEM],
        out_specs=[VMEM] * 2,
        scratch_shapes=[
            pltpu.VMEM(hidden_in.shape, jnp.bfloat16),
            pltpu.VMEM(in_proj.shape, jnp.bfloat16),
            pltpu.SemaphoreType.DMA((5,)),
        ],
        compiler_params=pltpu.CompilerParams(vmem_limit_bytes=12 * MIB),
        cost_estimate=QUICK,
    )(in_hbm(hidden_in), in_hbm(in_proj), local_segments.reshape(1, tokens), by_rank)

    call = functools.partial(
        accumulate, bases=bases, rank=rank, pairs=pairs, window=window, places=places
    )
    place_of = {name: CORES * n for n, name in enumerate(arrival)}
    starts = {0: own_starts}
    members = []
    known_units = 0
    state = None

    def work(names, complete=(), partial=(), sends=(), cost=QUICK):
        nonlocal state, known_units
        tasks, arrived = [], []
        for group, blocks in complete:
            first = 0
            for piece, count in blocks:
                arrived.append((piece, group * pairs + first, count))
                first += count
            if group:
                starts[group] = starts_in(*blocks[0])
            members.append(group)
        fresh = [group for group, _ in complete]
        if fresh and known_units:
            tasks.append(("units", fresh, 0, known_units))
        if names:
            tasks.append(("units", list(members), known_units, CORES * len(names)))
        known_units += CORES * len(names)
        for group, piece, first, count in partial:
            arrived.append((piece, group * pairs + first, count))
            if first == 0:
                starts[group] = starts_in(piece, count)
                members.append(group)
            tasks.append(("piece", group, first, first + count, 0, known_units))
        state, out = call(
            state,
            starts=starts,
            tokens=arrived,
            units=[(held[n], place_of[n]) for n in names],
            tasks=tasks,
            sends=sends,
            cost=cost,
        )
        return out

    held[1, 0], side_pieces[0] = tie(held[1, 0], side_pieces[0])
    for n in range(1, final - 1):
        held[n + 1, 0] = along(held[n, 0], following)
        held[n, 1] = swap(held[n, 0], 0, CORES)
    third_piece, side_pieces[0] = tie(third_piece, side_pieces[0])
    diagonal_pieces = [swap(third_piece, 1, 1)]
    near = (final - 1, 0)
    held[near], basis, side_pieces[0] = tie(held[near], basis, side_pieces[0])
    work(names_a, complete=[(0, [(own_tokens, pairs)])], cost=SHORT)
    back_unit, basis, from_core = tie(held[0, 1], basis, from_core)
    held[final, 1] = along(back_unit, before)
    held[final, 0] = along(held[near], following)
    crossing, from_core = tie(held[near], from_core)
    held[final - 1, 1] = swap(crossing, 0, CORES)
    last_piece, side_pieces[1] = tie(last_piece, side_pieces[1])
    diagonal_pieces.append(swap(last_piece, 1, 1))
    work(
        names_b,
        complete=[(1, [(from_core, pairs)]), (2, [(piece, half) for piece in side_pieces])],
        cost=SHORT,
    )
    work([], partial=[(3, diagonal_pieces[0], 0, 3 * rows)])
    sent = work(names_c, sends=[1, 2])
    sent = sent + work([], partial=[(3, diagonal_pieces[1], 3 * rows, rows)], sends=[3], cost=SHORT)

    def returned(arrays):
        return [
            swap(array, side, bit) for array, (side, bit) in zip(arrays, ((0, 1), (1, 0), (1, 1)))
        ]

    early = returned(sent)
    held_tokens, *early[:2] = tie(state[0], *early[:2])
    place = places - 2 * CORES
    own_late, *sent = pl.pallas_call(
        functools.partial(late_kernel, rank, pairs, window, place, QUAD),
        out_shape=[pltpu.VMEM((2 * window, LANES), jnp.float32)]
        + [pltpu.VMEM((2 * window, LANES), jnp.bfloat16)] * (QUAD - 1),
        in_specs=[SMEM] * (1 + QUAD) + [VMEM] * 3,
        out_specs=[VMEM] * QUAD,
        compiler_params=pltpu.CompilerParams(vmem_limit_bytes=8 * MIB),
        cost_estimate=QUICK,
    )(bases, *[starts[g] for g in range(QUAD)], in_vmem(held_tokens), held[final, 0], held[final, 1])
    late = returned(sent)
    *early, own_late = tie(*early, own_late)
    out, turned = pl.pallas_call(
        functools.partial(blocks_kernel, rank),
        out_shape=[
            jax.ShapeDtypeStruct((SEG_DEV, experts, rank * rank), jnp.bfloat16),
            pltpu.VMEM((rank, pairs), jnp.float32),
        ],
        in_specs=[VMEM] * 7,
        out_specs=[VMEM] * 2,
        scratch_shapes=[pltpu.VMEM((rank // 2, experts, 2 * tokens), jnp.float32)],
        compiler_params=pltpu.CompilerParams(vmem_limit_bytes=32 * MIB),
        cost_estimate=QUICK,
    )(by_rank, basis, in_vmem(order_back), in_vmem(state[2]), *early)
    count = 2 * CORES * exp_here
    return pl.pallas_call(
        functools.partial(last_kernel, rank, place, count, exp_here),
        out_shape=jax.ShapeDtypeStruct(out.shape, out.dtype),
        in_specs=[SMEM] * 2 + [VMEM] * 8 + [HBM],
        out_specs=HBM,
        scratch_shapes=[
            pltpu.VMEM((rank, pairs), jnp.float32),
            pltpu.VMEM((rank // 2, count, 2 * tokens), jnp.float32),
            pltpu.VMEM((SEG_DEV, count, rank * rank), jnp.bfloat16),
            pltpu.SemaphoreType.DMA,
        ],
        input_output_aliases={10: 0},
        compiler_params=pltpu.CompilerParams(vmem_limit_bytes=16 * MIB),
        cost_estimate=QUICK,
    )(bases, own_starts, by_rank, basis, in_vmem(order_back), in_vmem(turned), own_late, *late, out)


def solution(mesh):
    placed = (
        P(("groups", "expert"), None),
        P(("groups", "expert"), None, None),
        P(("groups", "expert"), None),
        P(("groups", "expert")),
        P(),
        P("expert", None, None),
    )
    return jax.shard_map(
        local,
        mesh=mesh,
        in_specs=placed,
        out_specs=P(("groups", "expert"), None, None),
        check_vma=False,
    )
```
